32 devices in a mesh: gx: 2 (over y), gy: 4 (over z), gz: 4 (over x, core).
Axes of the slice: x: 2, y: 2, z: 4, core: 2. Of those that a mesh axis runs over, the one named last changes fastest.
Arguments:
- residual_q2: bfloat16 [64, 64, 1024], P('gx', 'gy', 'gz'), may hold values from -6 to 6
- viscosity: float32 [32, 32, 512], P('gx', 'gy', 'gz'), may hold values from 0.001 to 1000
- pinned: int32 [32, 32, 512], P('gx', 'gy', 'gz'), may hold values 0 or 1
Outputs:
- scaled_correction: float32 [32, 32, 512], P('gx', 'gy', 'gz')
The draws below stay inside these ranges and needn't reach their ends.
All inputs are finite; a program needn't handle non-finite values. No bound on the sum of `pinned` on one device may be relied on, other than what follows from the above.
Results may differ from the reference program's by a relative error of at most 0.0003.
Values sent between devices are 32-bit elements; how exact they have to be, the bound alone decides.
No kernel may reach another device: no remote copies, remote signals or barrier semaphores. Data moves between devices by JAX's collectives and lax.ppermute only.
A program may use at most 192 MiB of HBM per device.

```python
import math
import jax
import jax.numpy as jnp
from jax import lax

NU = 3
NX = 32
NY = 32
NZ = 512


def plant(values, rng, smallest, high):
    place = [jax.random.randint(jax.random.fold_in(rng, axis), (), 0, length) for axis, length in enumerate(values.shape)]
    longest = values.shape.index(max(values.shape))
    neighbour = place[:longest] + [(place[longest] + 1) % values.shape[longest]] + place[longest + 1:]
    return values.at[tuple(place)].set(smallest).at[tuple(neighbour)].set(high)


def level_of(key, extent, split, smallest, largest):
    level = 1.0
    for dim, shards_of in split:
        heights = jax.random.uniform(jax.random.fold_in(jax.random.fold_in(key, 6), dim), (shards_of,), jnp.float32, smallest / len(split), largest / len(split))
        level = level * jnp.repeat(jnp.exp(heights), extent[dim] // shards_of).reshape((-1,) + (1,) * (len(extent) - 1 - dim))
    return level


def scatter_about(key, shape, deviation, most, pieces=(), dtype=jnp.bfloat16):
    result = deviation * jax.random.normal(key, shape, jnp.float32)
    if pieces:
        result = result * level_of(key, shape, pieces, -0.22, 0.18)
    return jnp.clip(result, -most, most).astype(dtype)


def setup_inputs(seed: int = 0) -> dict:
    key_of = jax.random.split(jax.random.key(seed), 4)
    residual_q2 = scatter_about(key_of[0], (2 * NX, 2 * NY, 2 * NZ), 1.0, 6.0, ((0, 2), (1, 4), (2, 4)))
    viscosity = jnp.clip(jnp.exp(math.log(1000.0) - 13.815511 * jax.random.uniform(key_of[1], (NX, NY, NZ), jnp.float32) ** level_of(key_of[1], (NX, NY, NZ), ((0, 2), (1, 4), (2, 4)), -0.2, 0.2)), 0.001, 1000.0)
    pinned = plant((jax.random.randint(key_of[2], (NX, NY, NZ), 0, 16) < 1).astype(jnp.int32), jax.random.fold_in(key_of[2], 1), 0, 1)
    return {"residual_q2": residual_q2, "viscosity": viscosity, "pinned": pinned}


OMEGA = 0.6

def coarsen(x):
    a, b, c = x.shape
    return x.reshape(a // 2, 2, b // 2, 2, c // 2, 2).sum(axis=(1, 3, 5))

def refine(x):
    return jnp.repeat(jnp.repeat(jnp.repeat(x, 2, 0), 2, 1), 2, 2)

def shifted(padded):
    return [padded[2:, 1:-1, 1:-1], padded[:-2, 1:-1, 1:-1], padded[1:-1, 2:, 1:-1], padded[1:-1, :-2, 1:-1], padded[1:-1, 1:-1, 2:], padded[1:-1, 1:-1, :-2]]

def couplings(fluid, factor):
    return [factor * 2.0 * fluid * near / (fluid + near) for near in shifted(jnp.pad(fluid, 1))]

def apply_op(field, weights, diag):
    total = diag * field
    for weight, near in zip(weights, shifted(jnp.pad(field, 1))):
        total = total - weight * near
    return total

def presmooth(rhs, weights, diag):
    corr = OMEGA * rhs / diag
    for sweep in range(NU - 1):
        corr = corr + OMEGA * (rhs - apply_op(corr, weights, diag)) / diag
    return corr

def postsmooth(corr, rhs, weights, diag):
    for sweep in range(NU):
        corr = corr + OMEGA * (rhs - apply_op(corr, weights, diag)) / diag
    return corr

def column_solve(rhs, weights, diag):
    lower = -weights[5]
    upper = -weights[4]
    across = diag + lower + upper
    solved = lax.linalg.tridiagonal_solve(lower, diag, upper, rhs[..., None])[..., 0]
    shift_col = jnp.sum(rhs, axis=2, keepdims=True) / jnp.sum(across, axis=2, keepdims=True)
    return solved + shift_col

def reference(residual_q2, viscosity, pinned):
    fluid1 = 1.0 / viscosity
    pin1 = 4.0 * pinned.astype(jnp.float32) * fluid1
    rhs1 = coarsen(residual_q2.astype(jnp.float32))
    fluid2 = coarsen(fluid1) / 8.0
    pin2 = coarsen(pin1) / 4.0
    fluid3 = coarsen(fluid2) / 8.0
    pin3 = coarsen(pin2) / 4.0
    weights1 = couplings(fluid1, 1.0)
    weights2 = couplings(fluid2, 2.0)
    weights3 = couplings(fluid3, 4.0)
    diag1 = sum(weights1) + pin1
    diag2 = sum(weights2) + pin2
    diag3 = sum(weights3) + pin3
    corr1 = presmooth(rhs1, weights1, diag1)
    rhs2 = coarsen(rhs1 - apply_op(corr1, weights1, diag1))
    corr2 = presmooth(rhs2, weights2, diag2)
    rhs3 = coarsen(rhs2 - apply_op(corr2, weights2, diag2))
    corr3 = column_solve(rhs3, weights3, diag3)
    corr3 = corr3 + column_solve(rhs3 - apply_op(corr3, weights3, diag3), weights3, diag3)
    corr2 = postsmooth(corr2 + refine(corr3), rhs2, weights2, diag2)
    corr1 = postsmooth(corr1 + refine(corr2), rhs1, weights1, diag1)
    return diag1 * corr1
```

```python
import functools

import jax
import jax.numpy as jnp
from jax import lax
from jax.experimental import pallas as pl
from jax.experimental.pallas import tpu as pltpu
from jax.sharding import PartitionSpec as P

NU = 3


OMEGA = 0.6


def with_halo(block, sides, width):
    for axis, dim in sides:
        count = lax.axis_size(axis)
        forward = [(i, i + 1) for i in range(count - 1)]
        backward = [(target, source) for source, target in forward]
        low = lax.ppermute(
            lax.slice_in_dim(block, block.shape[dim] - width, None, axis=dim), axis, forward
        )
        high = lax.ppermute(lax.slice_in_dim(block, 0, width, axis=dim), axis, backward)
        block = jnp.concatenate([low, block, high], axis=dim)
    return block


def coarsen(x):
    a, b, c = x.shape
    return x.reshape(a // 2, 2, b // 2, 2, c // 2, 2).sum(axis=(1, 3, 5))


def refine(x):
    return jnp.repeat(jnp.repeat(jnp.repeat(x, 2, 0), 2, 1), 2, 2)


def extended(field):
    return with_halo(field, (("gx", 0), ("gy", 1), ("gz", 2)), 1)


def shifted(padded):
    return [
        padded[2:, 1:-1, 1:-1],
        padded[:-2, 1:-1, 1:-1],
        padded[1:-1, 2:, 1:-1],
        padded[1:-1, :-2, 1:-1],
        padded[1:-1, 1:-1, 2:],
        padded[1:-1, 1:-1, :-2],
    ]


def neighbours(field):
    return shifted(extended(field))


def harmonic(fluid, near, factor):
    total = fluid + near
    return jnp.where(total > 0, factor * 2.0 * fluid * near / jnp.where(total > 0, total, 1.0), 0.0)


def couplings(fluid, factor):
    return [harmonic(fluid, near, factor) for near in neighbours(fluid)]


def apply_op(field, weights, diag):
    total = diag * field
    for weight, near in zip(weights, neighbours(field)):
        total = total - weight * near
    return total


def presmooth(rhs, weights, diag):
    corr = OMEGA * rhs / diag
    for sweep in range(NU - 1):
        corr = corr + OMEGA * (rhs - apply_op(corr, weights, diag)) / diag
    return corr


def postsmooth(corr, rhs, weights, diag):
    for sweep in range(NU):
        corr = corr + OMEGA * (rhs - apply_op(corr, weights, diag)) / diag
    return corr


def tridiag(coeffs, rhs):
    solved = lax.linalg.tridiagonal_solve(coeffs[0], coeffs[1], coeffs[2], rhs[..., None])[..., 0]
    last = rhs.ndim - 1
    shift_col = jnp.sum(rhs, axis=last, keepdims=True) / jnp.sum(
        coeffs[3], axis=last, keepdims=True
    )
    return solved + shift_col


def prepare_columns(weights, diag):
    lower = -weights[5]
    upper = -weights[4]
    across = diag + lower + upper
    return (
        lax.all_gather(lower, "gz", axis=2, tiled=True),
        lax.all_gather(diag, "gz", axis=2, tiled=True),
        lax.all_gather(upper, "gz", axis=2, tiled=True),
        lax.all_gather(across, "gz", axis=2, tiled=True),
    )


def column_solve(rhs, coeffs):
    depth = rhs.shape[2]
    whole = lax.all_gather(rhs, "gz", axis=2, tiled=True)
    solved = tridiag(coeffs, whole)
    return lax.dynamic_slice_in_dim(solved, lax.axis_index("gz") * depth, depth, 2)


def per_device(residual_q2, viscosity, pinned):
    fluid1 = 1.0 / viscosity
    pin1 = 4.0 * pinned.astype(jnp.float32) * fluid1
    rhs1 = coarsen(residual_q2.astype(jnp.float32))
    fluid2 = coarsen(fluid1) / 8.0
    pin2 = coarsen(pin1) / 4.0
    fluid3 = coarsen(fluid2) / 8.0
    pin3 = coarsen(pin2) / 4.0
    weights1 = couplings(fluid1, 1.0)
    weights2 = couplings(fluid2, 2.0)
    weights3 = couplings(fluid3, 4.0)
    diag1 = sum(weights1) + pin1
    diag2 = sum(weights2) + pin2
    diag3 = sum(weights3) + pin3
    coeffs = prepare_columns(weights3, diag3)
    corr1 = presmooth(rhs1, weights1, diag1)
    rhs2 = coarsen(rhs1 - apply_op(corr1, weights1, diag1))
    corr2 = presmooth(rhs2, weights2, diag2)
    rhs3 = coarsen(rhs2 - apply_op(corr2, weights2, diag2))
    corr3 = column_solve(rhs3, coeffs)
    corr3 = corr3 + column_solve(rhs3 - apply_op(corr3, weights3, diag3), coeffs)
    corr2 = postsmooth(corr2 + refine(corr3), rhs2, weights2, diag2)
    corr1 = postsmooth(corr1 + refine(corr2), rhs1, weights1, diag1)
    return diag1 * corr1


PLANE = (32, 32)
SPLIT = (2, 4)
ROWS = 8
LANES = 128
HALO = 18
SLAB = 56
NEAR = 8
F32 = jnp.float32


def iota(shape, dim):
    return lax.broadcasted_iota(jnp.int32, shape, dim)


def dot01(field, chosen, dims=(((1,), (0,)), ((), ()))):
    total = None
    rest = field
    for part in range(3):
        piece = rest.astype(jnp.bfloat16)
        term = lax.dot_general(piece, chosen, dims, preferred_element_type=F32)
        total = term if total is None else total + term
        if part < 2:
            rest = rest - piece.astype(F32)
    return total


def where01(condition):
    return jnp.where(condition, 1.0, 0.0).astype(jnp.bfloat16)


def loop(low, high, size, body):
    size = min(size, high - low)
    steps = -(-(high - low) // size)

    def step(index, carry):
        body(jnp.minimum(low + index * size, high - size), size)
        return carry

    lax.fori_loop(0, steps, step, 0)


class Level:
    def __init__(self, level):
        self.ny = PLANE[1] >> level
        self.xs = 4 >> level
        self.factor = float(2**level)

    def masks(self, shape):
        lane = iota(shape, 2)
        row = iota(shape, 1)
        within = (lane // self.ny) % self.xs
        y = lane % self.ny
        last_x = (row == ROWS - 1) & (within == self.xs - 1)
        return within, y == self.ny - 1, last_x

    def next_x(self, field):
        within = (iota(field.shape, 2) // self.ny) % self.xs
        moved = pltpu.roll(field, LANES - self.ny, 2)
        return jnp.where(within == self.xs - 1, pltpu.roll(moved, ROWS - 1, 1), moved)

    def last_x(self, field):
        within = (iota(field.shape, 2) // self.ny) % self.xs
        moved = pltpu.roll(field, self.ny, 2)
        return jnp.where(within == 0, pltpu.roll(moved, 1, 1), moved)

    def next_y(self, field):
        return pltpu.roll(field, LANES - 1, 2)

    def last_y(self, field):
        return pltpu.roll(field, 1, 2)

    def balance(self, field, wx, wy, wz):
        mid = field[1:-1]
        flow_x = wx * (self.next_x(mid) - mid)
        flow_y = wy * (self.next_y(mid) - mid)
        flow_z = wz * (field[1:] - field[:-1])
        return (
            (flow_x - self.last_x(flow_x))
            + (flow_y - self.last_y(flow_y))
            + (flow_z[1:] - flow_z[:-1])
        )


def mean_of(fluid, near, factor):
    total = fluid + near
    safe = jnp.where(total > 0, total, 1.0)
    return jnp.where(total > 0, (factor * 2.0) * fluid * near / safe, 0.0)


def set_level(level, low, high, size, fluid, pin, rhs, wx, wy, wz, gain, corr):
    def body(plane, count):
        wide = fluid[pl.ds(plane - 1, count + 2)]
        mid = wide[1:-1]
        within, end_y, end_x = level.masks(mid.shape)
        to_x = jnp.where(end_x, 0.0, mean_of(mid, level.next_x(mid), level.factor))
        to_y = jnp.where(end_y, 0.0, mean_of(mid, level.next_y(mid), level.factor))
        to_z = mean_of(wide[:-1], wide[1:], level.factor)
        diag = (
            (to_x + level.last_x(to_x))
            + (to_y + level.last_y(to_y))
            + (to_z[1:] + to_z[:-1])
            + pin[pl.ds(plane, count)]
        )
        some = diag > 0
        scale = jnp.where(some, OMEGA / jnp.where(some, diag, 1.0), 0.0)
        wx[pl.ds(plane, count)] = to_x
        wy[pl.ds(plane, count)] = to_y
        wz[pl.ds(plane, count)] = to_z[1:]
        gain[pl.ds(plane, count)] = scale
        if corr is not None:
            corr[pl.ds(plane, count)] = scale * rhs[pl.ds(plane, count)]

    loop(low, high, size, body)


def residual_of(level, plane, count, fields, corr):
    rhs, pin, wx, wy, wz = fields
    field = corr[pl.ds(plane - 1, count + 2)]
    spread = level.balance(
        field, wx[pl.ds(plane, count)], wy[pl.ds(plane, count)], wz[pl.ds(plane - 1, count + 1)]
    )
    mid = field[1:-1]
    return mid, (rhs[pl.ds(plane, count)] - pin[pl.ds(plane, count)] * mid) + spread


def sweep(level, low, high, size, fields, gain, source, target):
    def body(plane, count):
        mid, rest = residual_of(level, plane, count, fields, source)
        target[pl.ds(plane, count)] = mid + gain[pl.ds(plane, count)] * rest

    loop(low, high, size, body)


def pair_sum(field):
    half = field.reshape((field.shape[0] // 2, 2) + field.shape[1:])
    return half[:, 0] + half[:, 1]


def coarse_residual(level, low, high, size, fields, corr, target):
    assert (high - low) % size == 0 and size % 2 == 0

    def body(plane, count):
        _, rest = residual_of(level, plane, count, fields, corr)
        target[pl.ds((plane - low) // 2, count // 2)] = pair_sum(rest)

    loop(low, high, size, body)


def lanes_down(level):
    fine = iota((LANES, LANES), 0)
    coarse = iota((LANES, LANES), 1)
    ny, xs = PLANE[1] >> level, 4 >> level
    half = xs // 2
    same_x = ((fine // ny) % xs) // 2 == (coarse // (ny // 2)) % half
    same_y = (fine % ny) // 2 == coarse % (ny // 2)
    return where01((fine < ny * xs) & same_x & same_y)


def in_lanes(field, chosen):
    flat = field.reshape(field.shape[0] * ROWS, LANES)
    return dot01(flat, chosen).reshape(field.shape)


def prepare_kernel(res_ref, visc_ref, pin_ref, own_ref, top_ref, bottom_ref):
    bx, by, depth = visc_ref.shape
    cells = bx * by
    groups = bx // 4
    pick = where01(iota((depth, 2 * depth), 1) // 2 == iota((depth, 2 * depth), 0))
    deep = lax.dot_general(
        pick, res_ref[...], (((1,), (1,)), ((), ())), preferred_element_type=F32
    )

    def lane_of(x, y):
        return (x % 4) * (groups * by) + (x // 4) * by + y

    fine = iota((4 * cells, cells), 0)
    lane = iota((4 * cells, cells), 1)
    chosen = where01(lane_of(fine // (4 * by), (fine % (2 * by)) // 2) == lane)
    rhs = dot01(deep, chosen)
    fluid = 1.0 / visc_ref[...].reshape(cells, depth)
    pin = 4.0 * pin_ref[...].reshape(cells, depth).astype(F32) * fluid
    cell = iota((cells, cells), 0)
    lane = iota((cells, cells), 1)
    chosen = where01(lane_of(cell // by, cell % by) == lane)
    fluid = dot01(fluid.T, chosen)
    pin = dot01(pin.T, chosen)
    for index, field in enumerate((fluid, rhs, pin)):
        own_ref[index * depth : (index + 1) * depth] = field
        top_ref[index * HALO : (index + 1) * HALO] = field[depth - HALO :]
        bottom_ref[index * HALO : (index + 1) * HALO] = field[:HALO]
    empty = jnp.zeros((SLAB - 3 * HALO, LANES), F32)
    top_ref[3 * HALO :] = empty
    bottom_ref[3 * HALO :] = empty


def place(gathered, row, target, plane, groups, by):
    group = (iota((ROWS, LANES), 1) // by) % groups
    nx, ny = SPLIT
    for ix in range(nx):
        found = [gathered[ix * ny + iy, pl.ds(row, ROWS), :] for iy in range(ny)]
        for part in range(groups):
            total = found[part]
            for iy in range(ny):
                if iy != part:
                    moved = pltpu.roll(found[iy], (by * (iy - part)) % LANES, 1)
                    total = jnp.where(group == iy, moved, total)
            target[pl.ds(plane, ROWS), ix * groups + part, :] = total


def down_kernel(
    groups, by, depth, sizes,
    gathered,
    rhs1, pin1, wx1, wy1, wz1, gain1, corr1,
    rhs2, pin2, wx2, wy2, wz2, gain2, corr2,
    packed,
    fluid1, other1, fluid2, other2, sums,
):
    for index, target in enumerate((fluid1, rhs1, pin1)):
        def body(step, carry, index=index, target=target):
            row = pl.multiple_of(index * depth + step * ROWS, ROWS)
            place(gathered, row, target, HALO + step * ROWS, groups, by)
            return carry

        lax.fori_loop(0, depth // ROWS, body, 0)
        for side, plane in enumerate((0, HALO + depth)):
            for start in (0, ROWS, HALO - ROWS):
                row = 3 * depth + side * SLAB + index * HALO + start
                place(gathered, row, target, plane + start, groups, by)

    fine, coarse = Level(0), Level(1)
    down1, down2 = lanes_down(0), lanes_down(1)
    planes = depth + 2 * HALO
    fields1 = (rhs1, pin1, wx1, wy1, wz1)
    fields2 = (rhs2, pin2, wx2, wy2, wz2)
    set_level(fine, 1, planes - 1, sizes[0], fluid1, pin1, rhs1, wx1, wy1, wz1, gain1, other1)
    sweep(fine, 2, planes - 2, sizes[1], fields1, gain1, other1, corr1)
    sweep(fine, 3, planes - 3, sizes[1], fields1, gain1, corr1, other1)
    corr1[...] = other1[...]
    count2 = depth // 2 + 2 * NEAR
    begin = HALO - 2 * NEAR
    for source, target, share in ((fluid1, fluid2, 8.0), (pin1, pin2, 4.0)):
        whole = pair_sum(source[begin : begin + 2 * count2])
        target[...] = in_lanes(whole, down1) * (1.0 / share)
    inner = count2 - 2
    coarse_residual(fine, begin + 2, begin + 2 + 2 * inner, sizes[2], fields1, corr1, sums)
    rhs2[1 : 1 + inner] = in_lanes(sums[0:inner], down1)
    set_level(coarse, 1, 1 + inner, sizes[3], fluid2, pin2, rhs2, wx2, wy2, wz2, gain2, other2)
    sweep(coarse, 2, inner, sizes[4], fields2, gain2, other2, corr2)
    sweep(coarse, 3, inner - 1, sizes[4], fields2, gain2, corr2, other2)
    corr2[...] = other2[...]
    coarse_residual(coarse, NEAR, NEAR + depth // 2, sizes[5], fields2, corr2, sums)
    count3 = depth // 4
    rhs3 = in_lanes(sums[0:count3], down2)
    fluid3 = in_lanes(pair_sum(fluid2[NEAR : NEAR + 2 * count3]), down2) * 0.125
    pin3 = in_lanes(pair_sum(pin2[NEAR : NEAR + 2 * count3]), down2) * 0.25
    lane = iota((count3, LANES), 1) // ROWS
    first = jnp.zeros((count3, LANES), F32)
    second = jnp.zeros((count3, LANES), F32)
    for row in range(ROWS):
        first = jnp.where(lane == row, rhs3[:, row, :], first)
        first = jnp.where(lane == ROWS + row, fluid3[:, row, :], first)
        second = jnp.where(lane == row, pin3[:, row, :], second)
    packed[0:count3] = first
    packed[count3 : 2 * count3] = second


def columns(rhs, fluid, pin):
    shape = fluid.shape
    depth = shape[2]
    lane, y = iota(shape, 2), iota(shape, 1)
    edge = jnp.zeros((1,) + shape[1:], F32)
    wz = jnp.where(lane == depth - 1, 0.0, mean_of(fluid, pltpu.roll(fluid, depth - 1, 2), 4.0))
    wy = jnp.where(y == ROWS - 1, 0.0, mean_of(fluid, pltpu.roll(fluid, ROWS - 1, 1), 4.0))
    wx = jnp.concatenate([mean_of(fluid[:-1], fluid[1:], 4.0), edge], axis=0)
    back_x = jnp.concatenate([edge, wx[:-1]], axis=0)
    across = (wx + back_x) + (wy + pltpu.roll(wy, 1, 1)) + pin
    share = 1.0 / jnp.sum(across, axis=2, keepdims=True)

    above, below, own = pltpu.roll(wz, 1, 2), wz, across
    steps = []
    stride = 1
    while stride < depth:
        inverse = 1.0 / (above + below + own)
        up = above * pltpu.roll(inverse, stride, 2)
        down = below * pltpu.roll(inverse, depth - stride, 2)
        own = own + up * pltpu.roll(own, stride, 2) + down * pltpu.roll(own, depth - stride, 2)
        above = up * pltpu.roll(above, stride, 2)
        below = down * pltpu.roll(below, depth - stride, 2)
        steps.append((stride, up, down))
        stride *= 2
    inverse = 1.0 / (above + below + own)

    def solve(right):
        mean = jnp.sum(right, axis=2, keepdims=True) * share
        for stride, up, down in steps:
            right = (
                right
                + up * pltpu.roll(right, stride, 2)
                + down * pltpu.roll(right, depth - stride, 2)
            )
        return right * inverse + mean

    corr = solve(rhs)
    flow_x = wx[:-1] * (corr[1:] - corr[:-1])
    flow_x = jnp.concatenate([flow_x, edge], 0) - jnp.concatenate([edge, flow_x], 0)
    flow_y = wy * (pltpu.roll(corr, ROWS - 1, 1) - corr)
    flow_z = wz * (pltpu.roll(corr, depth - 1, 2) - corr)
    rest = (
        (rhs - pin * corr)
        + flow_x
        + (flow_y - pltpu.roll(flow_y, 1, 1))
        + (flow_z - pltpu.roll(flow_z, 1, 2))
    )
    return corr + solve(rest)


def up_kernel(
    groups, by, depth, sizes,
    packed,
    rhs1, pin1, wx1, wy1, wz1, gain1, corr1,
    rhs2, pin2, wx2, wy2, wz2, gain2, corr2,
    out_ref,
    one1, two1, one2, two2, lifted,
):
    count3 = depth // 4
    shares = packed.shape[0]
    first = jnp.concatenate([packed[i, 0:count3] for i in range(shares)], axis=0).T
    second = jnp.concatenate([packed[i, count3 : 2 * count3] for i in range(shares)], axis=0).T
    cells = ROWS * ROWS
    total3 = shares * count3
    shape3 = (ROWS, ROWS, total3)
    corr3 = columns(
        first[:cells].reshape(shape3), first[cells:].reshape(shape3), second[:cells].reshape(shape3)
    ).reshape(cells, total3)

    part = lax.axis_index("gz")
    mine = pltpu.roll(corr3, lax.rem(NEAR - part * count3 + total3, total3), 1)
    tall = jnp.concatenate([mine, mine], axis=0).T
    count = count3 + 2 * NEAR
    fine, coarse = Level(0), Level(1)
    cell = iota((LANES, ROWS * LANES), 0)
    lane = iota((LANES, ROWS * LANES), 1)
    same_y = cell % ROWS == (lane % coarse.ny) // 2
    spread = where01((cell // ROWS == lane // LANES) & same_y)
    wide = dot01(tall[0:count], spread)
    for row in range(ROWS):
        lifted[0:count, row, :] = wide[:, row * LANES : (row + 1) * LANES]

    fields1 = (rhs1, pin1, wx1, wy1, wz1)
    fields2 = (rhs2, pin2, wx2, wy2, wz2)
    low, high = NEAR - 6, NEAR + depth // 2 + 6
    parents = lifted[low // 2 + NEAR // 2 : high // 2 + NEAR // 2]
    twice = jnp.broadcast_to(parents[:, None], (parents.shape[0], 2, ROWS, LANES))
    one2[low:high] = corr2[low:high] + twice.reshape(high - low, ROWS, LANES)
    reach = depth // 2 + NEAR
    sweep(coarse, NEAR - 4, reach + 4, sizes[4], fields2, gain2, one2, two2)
    sweep(coarse, NEAR - 3, reach + 3, sizes[4], fields2, gain2, two2, one2)
    sweep(coarse, NEAR - 2, reach + 2, sizes[4], fields2, gain2, one2, two2)

    fine_lane, coarse_lane = iota((LANES, LANES), 1), iota((LANES, LANES), 0)
    x_of = (fine_lane // fine.ny) // 2
    y_of = (fine_lane % fine.ny) // 2
    up = where01(coarse_lane == x_of * coarse.ny + y_of)
    lifted[0 : depth // 2 + 4] = in_lanes(two2[NEAR - 2 : reach + 2], up)
    parents = lifted[0 : depth // 2 + 4]
    twice = jnp.broadcast_to(parents[:, None], (parents.shape[0], 2, ROWS, LANES))
    low, high = HALO - 4, HALO + depth + 4
    one1[low:high] = corr1[low:high] + twice.reshape(high - low, ROWS, LANES)
    reach = depth + HALO
    sweep(fine, HALO - 2, reach + 2, sizes[1], fields1, gain1, one1, two1)
    sweep(fine, HALO - 1, reach + 1, sizes[1], fields1, gain1, two1, one1)
    sweep(fine, HALO, reach, sizes[1], fields1, gain1, one1, two1)

    ix, iy = lax.axis_index("gx"), lax.axis_index("gy")
    cells = 4 * groups * by
    cell = iota((cells, LANES), 0)
    lane = iota((cells, LANES), 1)
    total = None
    for part in range(groups):
        scaled = two1[pl.ds(HALO, depth), ix * groups + part, :] * (
            OMEGA / gain1[pl.ds(HALO, depth), ix * groups + part, :]
        )
        x, y = cell // by, cell % by
        chosen = where01((x // 4 == part) & (lane == (x % 4) * fine.ny + iy * by + y))
        term = dot01(scaled, chosen, (((1,), (1,)), ((), ())))
        total = term if total is None else total + term
    out_ref[...] = total.T.reshape(out_ref.shape)


def whole_planes(residual_q2, viscosity, pinned):
    bx, by, depth = viscosity.shape
    groups = bx // 4
    sizes = (9, 16, 12, 13, 16, 16)
    planes = depth + 2 * HALO
    count2 = depth // 2 + 2 * NEAR
    limit = pltpu.CompilerParams(vmem_limit_bytes=32 * 2**20)

    def flat(rows):
        return jax.ShapeDtypeStruct((rows, LANES), F32)

    def field(count):
        return jax.ShapeDtypeStruct((count, ROWS, LANES), F32)

    def room(count):
        return pltpu.VMEM((count, ROWS, LANES), F32)

    own, top, bottom = pl.pallas_call(
        prepare_kernel,
        out_shape=(flat(3 * depth), flat(SLAB), flat(SLAB)),
        compiler_params=limit,
        name="prepare",
    )(residual_q2.reshape(4 * bx * by, 2 * depth), viscosity, pinned)
    length = lax.axis_size("gz")
    forward = [(i, i + 1) for i in range(length - 1)]
    low = lax.ppermute(top, "gz", forward)
    high = lax.ppermute(bottom, "gz", [(target, source) for source, target in forward])
    whole = lax.all_gather(jnp.concatenate([own, low, high], axis=0), ("gx", "gy"))
    saved = (field(planes),) * 7 + (field(count2),) * 7
    results = pl.pallas_call(
        functools.partial(down_kernel, groups, by, depth, sizes),
        out_shape=saved + (flat(depth // 2),),
        scratch_shapes=[room(planes), room(planes), room(count2), room(count2), room(count2)],
        compiler_params=limit,
        name="down",
    )(whole)
    packed = lax.all_gather(results[-1], "gz")
    return pl.pallas_call(
        functools.partial(up_kernel, groups, by, depth, sizes),
        out_shape=jax.ShapeDtypeStruct((bx, by, depth), F32),
        scratch_shapes=[room(planes), room(planes), room(count2), room(count2), room(count2)],
        compiler_params=limit,
        name="up",
    )(packed, *results[:-1])


def one_tile_planes(mesh, viscosity):
    split = (mesh.shape["gx"], mesh.shape["gy"])
    depth = viscosity.shape[2]
    fits = viscosity.shape[:2] == PLANE and split == SPLIT
    return fits and depth == 4 * LANES and depth // mesh.shape["gz"] == LANES


def solution(mesh):
    placed = (P("gx", "gy", "gz"), P("gx", "gy", "gz"), P("gx", "gy", "gz"))

    def cycle(residual_q2, viscosity, pinned):
        chosen = whole_planes if one_tile_planes(mesh, viscosity) else per_device
        return jax.shard_map(
            chosen, mesh=mesh, in_specs=placed, out_specs=P("gx", "gy", "gz"), check_vma=False
        )(residual_q2, viscosity, pinned)

    return cycle
```

```python
import functools

import jax
import jax.numpy as jnp
from jax import lax
from jax.experimental import pallas as pl
from jax.experimental.pallas import tpu as pltpu
from jax.sharding import PartitionSpec as P

NU = 3


OMEGA = 0.6


def with_halo(block, sides, width):
    for axis, dim in sides:
        count = lax.axis_size(axis)
        forward = [(i, i + 1) for i in range(count - 1)]
        backward = [(target, source) for source, target in forward]
        low = lax.ppermute(
            lax.slice_in_dim(block, block.shape[dim] - width, None, axis=dim), axis, forward
        )
        high = lax.ppermute(lax.slice_in_dim(block, 0, width, axis=dim), axis, backward)
        block = jnp.concatenate([low, block, high], axis=dim)
    return block


def coarsen(x):
    a, b, c = x.shape
    return x.reshape(a // 2, 2, b // 2, 2, c // 2, 2).sum(axis=(1, 3, 5))


def refine(x):
    return jnp.repeat(jnp.repeat(jnp.repeat(x, 2, 0), 2, 1), 2, 2)


def extended(field):
    return with_halo(field, (("gx", 0), ("gy", 1), ("gz", 2)), 1)


def shifted(padded):
    return [
        padded[2:, 1:-1, 1:-1],
        padded[:-2, 1:-1, 1:-1],
        padded[1:-1, 2:, 1:-1],
        padded[1:-1, :-2, 1:-1],
        padded[1:-1, 1:-1, 2:],
        padded[1:-1, 1:-1, :-2],
    ]


def neighbours(field):
    return shifted(extended(field))


def harmonic(fluid, near, factor):
    total = fluid + near
    return jnp.where(total > 0, factor * 2.0 * fluid * near / jnp.where(total > 0, total, 1.0), 0.0)


def couplings(fluid, factor):
    return [harmonic(fluid, near, factor) for near in neighbours(fluid)]


def apply_op(field, weights, diag):
    total = diag * field
    for weight, near in zip(weights, neighbours(field)):
        total = total - weight * near
    return total


def presmooth(rhs, weights, diag):
    corr = OMEGA * rhs / diag
    for sweep in range(NU - 1):
        corr = corr + OMEGA * (rhs - apply_op(corr, weights, diag)) / diag
    return corr


def postsmooth(corr, rhs, weights, diag):
    for sweep in range(NU):
        corr = corr + OMEGA * (rhs - apply_op(corr, weights, diag)) / diag
    return corr


def tridiag(coeffs, rhs):
    solved = lax.linalg.tridiagonal_solve(coeffs[0], coeffs[1], coeffs[2], rhs[..., None])[..., 0]
    last = rhs.ndim - 1
    shift_col = jnp.sum(rhs, axis=last, keepdims=True) / jnp.sum(
        coeffs[3], axis=last, keepdims=True
    )
    return solved + shift_col


def prepare_columns(weights, diag):
    lower = -weights[5]
    upper = -weights[4]
    across = diag + lower + upper
    return (
        lax.all_gather(lower, "gz", axis=2, tiled=True),
        lax.all_gather(diag, "gz", axis=2, tiled=True),
        lax.all_gather(upper, "gz", axis=2, tiled=True),
        lax.all_gather(across, "gz", axis=2, tiled=True),
    )


def column_solve(rhs, coeffs):
    depth = rhs.shape[2]
    whole = lax.all_gather(rhs, "gz", axis=2, tiled=True)
    solved = tridiag(coeffs, whole)
    return lax.dynamic_slice_in_dim(solved, lax.axis_index("gz") * depth, depth, 2)


def per_device(residual_q2, viscosity, pinned):
    fluid1 = 1.0 / viscosity
    pin1 = 4.0 * pinned.astype(jnp.float32) * fluid1
    rhs1 = coarsen(residual_q2.astype(jnp.float32))
    fluid2 = coarsen(fluid1) / 8.0
    pin2 = coarsen(pin1) / 4.0
    fluid3 = coarsen(fluid2) / 8.0
    pin3 = coarsen(pin2) / 4.0
    weights1 = couplings(fluid1, 1.0)
    weights2 = couplings(fluid2, 2.0)
    weights3 = couplings(fluid3, 4.0)
    diag1 = sum(weights1) + pin1
    diag2 = sum(weights2) + pin2
    diag3 = sum(weights3) + pin3
    coeffs = prepare_columns(weights3, diag3)
    corr1 = presmooth(rhs1, weights1, diag1)
    rhs2 = coarsen(rhs1 - apply_op(corr1, weights1, diag1))
    corr2 = presmooth(rhs2, weights2, diag2)
    rhs3 = coarsen(rhs2 - apply_op(corr2, weights2, diag2))
    corr3 = column_solve(rhs3, coeffs)
    corr3 = corr3 + column_solve(rhs3 - apply_op(corr3, weights3, diag3), coeffs)
    corr2 = postsmooth(corr2 + refine(corr3), rhs2, weights2, diag2)
    corr1 = postsmooth(corr1 + refine(corr2), rhs1, weights1, diag1)
    return diag1 * corr1


PLANE = (32, 32)
SPLIT = (2, 4)
ROWS = 8
LANES = 128
HALO = 18
SLAB = 56
NEAR = 8
F32 = jnp.float32


def iota(shape, dim):
    return lax.broadcasted_iota(jnp.int32, shape, dim)


def dot01(field, chosen, dims=(((1,), (0,)), ((), ()))):
    total = None
    rest = field
    for part in range(3):
        piece = rest.astype(jnp.bfloat16)
        term = lax.dot_general(piece, chosen, dims, preferred_element_type=F32)
        total = term if total is None else total + term
        if part < 2:
            rest = rest - piece.astype(F32)
    return total


def where01(condition):
    return jnp.where(condition, 1.0, 0.0).astype(jnp.bfloat16)


def loop(low, high, size, body):
    size = min(size, high - low)
    steps = -(-(high - low) // size)

    def step(index, carry):
        body(jnp.minimum(low + index * size, high - size), size)
        return carry

    if steps == 1:
        body(low, size)
    else:
        lax.fori_loop(0, steps, step, 0)


class Level:
    def __init__(self, level):
        self.ny = PLANE[1] >> level
        self.xs = 4 >> level
        self.factor = float(2**level)

    def masks(self, shape):
        lane = iota(shape, 2)
        row = iota(shape, 1)
        within = (lane // self.ny) % self.xs
        y = lane % self.ny
        last_x = (row == ROWS - 1) & (within == self.xs - 1)
        return within, y == self.ny - 1, last_x

    def next_x(self, field):
        within = (iota(field.shape, 2) // self.ny) % self.xs
        moved = pltpu.roll(field, LANES - self.ny, 2)
        return jnp.where(within == self.xs - 1, pltpu.roll(moved, ROWS - 1, 1), moved)

    def last_x(self, field):
        within = (iota(field.shape, 2) // self.ny) % self.xs
        moved = pltpu.roll(field, self.ny, 2)
        return jnp.where(within == 0, pltpu.roll(moved, 1, 1), moved)

    def next_y(self, field):
        return pltpu.roll(field, LANES - 1, 2)

    def last_y(self, field):
        return pltpu.roll(field, 1, 2)

    def balance(self, field, wx, wy, wz):
        mid = field[1:-1]
        flow_x = wx * (self.next_x(mid) - mid)
        flow_y = wy * (self.next_y(mid) - mid)
        flow_z = wz * (field[1:] - field[:-1])
        return (
            (flow_x - self.last_x(flow_x))
            + (flow_y - self.last_y(flow_y))
            + (flow_z[1:] - flow_z[:-1])
        )


def mean_of(fluid, near, factor):
    total = fluid + near
    safe = jnp.where(total > 0, total, 1.0)
    return jnp.where(total > 0, (factor * 2.0) * fluid * near / safe, 0.0)


def set_level(level, low, high, size, fluid, pin, rhs, wx, wy, wz, gain, corr):
    def body(plane, count):
        wide = fluid[pl.ds(plane - 1, count + 2)]
        mid = wide[1:-1]
        within, end_y, end_x = level.masks(mid.shape)
        to_x = jnp.where(end_x, 0.0, mean_of(mid, level.next_x(mid), level.factor))
        to_y = jnp.where(end_y, 0.0, mean_of(mid, level.next_y(mid), level.factor))
        to_z = mean_of(wide[:-1], wide[1:], level.factor)
        diag = (
            (to_x + level.last_x(to_x))
            + (to_y + level.last_y(to_y))
            + (to_z[1:] + to_z[:-1])
            + pin[pl.ds(plane, count)]
        )
        some = diag > 0
        scale = jnp.where(some, OMEGA / jnp.where(some, diag, 1.0), 0.0)
        wx[pl.ds(plane, count)] = to_x
        wy[pl.ds(plane, count)] = to_y
        wz[pl.ds(plane, count)] = to_z[1:]
        gain[pl.ds(plane, count)] = scale
        if corr is not None:
            corr[pl.ds(plane, count)] = scale * rhs[pl.ds(plane, count)]

    loop(low, high, size, body)


def residual_of(level, plane, count, fields, corr):
    rhs, pin, wx, wy, wz = fields
    field = corr[pl.ds(plane - 1, count + 2)]
    spread = level.balance(
        field, wx[pl.ds(plane, count)], wy[pl.ds(plane, count)], wz[pl.ds(plane - 1, count + 1)]
    )
    mid = field[1:-1]
    return mid, (rhs[pl.ds(plane, count)] - pin[pl.ds(plane, count)] * mid) + spread


def sweep(level, low, high, size, fields, gain, source, target):
    def body(plane, count):
        mid, rest = residual_of(level, plane, count, fields, source)
        target[pl.ds(plane, count)] = mid + gain[pl.ds(plane, count)] * rest

    loop(low, high, size, body)


def pair_sum(field):
    half = field.reshape((field.shape[0] // 2, 2) + field.shape[1:])
    return half[:, 0] + half[:, 1]


def coarse_residual(level, low, high, size, fields, corr, target):
    size = min(size, high - low)
    assert (high - low) % size == 0 and size % 2 == 0

    def body(plane, count):
        _, rest = residual_of(level, plane, count, fields, corr)
        target[pl.ds((plane - low) // 2, count // 2)] = pair_sum(rest)

    loop(low, high, size, body)


def lanes_down(level):
    fine = iota((LANES, LANES), 0)
    coarse = iota((LANES, LANES), 1)
    ny, xs = PLANE[1] >> level, 4 >> level
    half = xs // 2
    same_x = ((fine // ny) % xs) // 2 == (coarse // (ny // 2)) % half
    same_y = (fine % ny) // 2 == coarse % (ny // 2)
    return where01((fine < ny * xs) & same_x & same_y)


def in_lanes(field, chosen):
    flat = field.reshape(field.shape[0] * ROWS, LANES)
    return dot01(flat, chosen).reshape(field.shape)


def prepare_kernel(
    res_in, visc_in, pin_in, own_ref, top_ref, bottom_ref, res_ref, visc_ref, pin_ref, arrived
):
    copies = [
        pltpu.make_async_copy(source, target, arrived.at[index])
        for index, (source, target) in enumerate(
            ((visc_in, visc_ref), (pin_in, pin_ref), (res_in, res_ref))
        )
    ]
    for copy in copies:
        copy.start()
    for copy in copies:
        copy.wait()
    bx, by, depth = visc_ref.shape
    cells = bx * by
    groups = bx // 4
    pick = where01(iota((depth, 2 * depth), 1) // 2 == iota((depth, 2 * depth), 0))
    deep = lax.dot_general(
        pick, res_ref[...], (((1,), (1,)), ((), ())), preferred_element_type=F32
    )

    def lane_of(x, y):
        return (x % 4) * (groups * by) + (x // 4) * by + y

    fine = iota((4 * cells, cells), 0)
    lane = iota((4 * cells, cells), 1)
    chosen = where01(lane_of(fine // (4 * by), (fine % (2 * by)) // 2) == lane)
    rhs = dot01(deep, chosen)
    fluid = 1.0 / visc_ref[...].reshape(cells, depth)
    pin = 4.0 * pin_ref[...].reshape(cells, depth).astype(F32) * fluid
    cell = iota((cells, cells), 0)
    lane = iota((cells, cells), 1)
    chosen = where01(lane_of(cell // by, cell % by) == lane)
    fluid = dot01(fluid.T, chosen)
    pin = dot01(pin.T, chosen)
    for index, field in enumerate((fluid, rhs, pin)):
        own_ref[index * depth : (index + 1) * depth] = field
        top_ref[index * HALO : (index + 1) * HALO] = field[depth - HALO :]
        bottom_ref[index * HALO : (index + 1) * HALO] = field[:HALO]
    empty = jnp.zeros((SLAB - 3 * HALO, LANES), F32)
    top_ref[3 * HALO :] = empty
    bottom_ref[3 * HALO :] = empty


def pack_kernel(depth, span, own, low, high, out_ref):
    share = span - 2 * HALO
    for index in range(3):
        for peer in range(depth // share):
            begin, end = peer * share - HALO, peer * share + share + HALO
            row = index * span
            ahead, behind = max(0, -begin), max(0, end - depth)
            if ahead:
                first = (index + 1) * HALO
                out_ref[peer, row : row + ahead] = low[first - ahead : first]
            inner = own[index * depth + max(begin, 0) : index * depth + min(end, depth)]
            out_ref[peer, row + ahead : row + span - behind] = inner
            if behind:
                first = index * HALO
                out_ref[peer, row + span - behind : row + span] = high[first : first + behind]
    spare = out_ref.shape[1] - 3 * span
    out_ref[:, 3 * span :] = jnp.zeros((depth // share, spare, LANES), F32)


def place(gathered, row, target, plane, groups, by):
    group = (iota((ROWS, LANES), 1) // by) % groups
    nx, ny = SPLIT
    for ix in range(nx):
        found = [gathered[ix * ny + iy, pl.ds(row, ROWS), :] for iy in range(ny)]
        for part in range(groups):
            total = found[part]
            for iy in range(ny):
                if iy != part:
                    moved = pltpu.roll(found[iy], (by * (iy - part)) % LANES, 1)
                    total = jnp.where(group == iy, moved, total)
            target[pl.ds(plane, ROWS), ix * groups + part, :] = total


def down_kernel(
    groups, by, depth, sizes,
    gathered,
    rhs1, pin1, wx1, wy1, wz1, gain1, corr1,
    rhs2, pin2, wx2, wy2, wz2, gain2, corr2,
    packed,
    fluid1, other1, fluid2, other2, sums,
):
    planes = depth + 2 * HALO
    for index, target in enumerate((fluid1, rhs1, pin1)):
        for start in [*range(0, planes - ROWS, ROWS), planes - ROWS]:
            place(gathered, index * planes + start, target, start, groups, by)

    fine, coarse = Level(0), Level(1)
    down1, down2 = lanes_down(0), lanes_down(1)
    fields1 = (rhs1, pin1, wx1, wy1, wz1)
    fields2 = (rhs2, pin2, wx2, wy2, wz2)
    set_level(fine, 1, planes - 1, sizes[0], fluid1, pin1, rhs1, wx1, wy1, wz1, gain1, other1)
    sweep(fine, 2, planes - 2, sizes[1], fields1, gain1, other1, corr1)
    sweep(fine, 3, planes - 3, sizes[1], fields1, gain1, corr1, other1)
    corr1[...] = other1[...]
    count2 = depth // 2 + 2 * NEAR
    begin = HALO - 2 * NEAR
    for source, target, share in ((fluid1, fluid2, 8.0), (pin1, pin2, 4.0)):
        whole = pair_sum(source[begin : begin + 2 * count2])
        target[...] = in_lanes(whole, down1) * (1.0 / share)
    inner = count2 - 2
    coarse_residual(fine, begin + 2, begin + 2 + 2 * inner, sizes[2], fields1, corr1, sums)
    rhs2[1 : 1 + inner] = in_lanes(sums[0:inner], down1)
    set_level(coarse, 1, 1 + inner, sizes[3], fluid2, pin2, rhs2, wx2, wy2, wz2, gain2, other2)
    sweep(coarse, 2, inner, sizes[4], fields2, gain2, other2, corr2)
    sweep(coarse, 3, inner - 1, sizes[4], fields2, gain2, corr2, other2)
    corr2[...] = other2[...]
    coarse_residual(coarse, NEAR, NEAR + depth // 2, sizes[5], fields2, corr2, sums)
    count3 = depth // 4
    rhs3 = in_lanes(sums[0:count3], down2)
    fluid3 = in_lanes(pair_sum(fluid2[NEAR : NEAR + 2 * count3]), down2) * 0.125
    pin3 = in_lanes(pair_sum(pin2[NEAR : NEAR + 2 * count3]), down2) * 0.25
    lane = iota((count3, LANES), 1) // ROWS
    first = jnp.zeros((count3, LANES), F32)
    second = jnp.zeros((count3, LANES), F32)
    for row in range(ROWS):
        first = jnp.where(lane == row, rhs3[:, row, :], first)
        first = jnp.where(lane == ROWS + row, fluid3[:, row, :], first)
        second = jnp.where(lane == row, pin3[:, row, :], second)
    packed[0:count3] = first
    packed[count3 : 2 * count3] = second


def columns(rhs, fluid, pin):
    shape = fluid.shape
    depth = shape[2]
    lane, y = iota(shape, 2), iota(shape, 1)
    edge = jnp.zeros((1,) + shape[1:], F32)
    wz = jnp.where(lane == depth - 1, 0.0, mean_of(fluid, pltpu.roll(fluid, depth - 1, 2), 4.0))
    wy = jnp.where(y == ROWS - 1, 0.0, mean_of(fluid, pltpu.roll(fluid, ROWS - 1, 1), 4.0))
    wx = jnp.concatenate([mean_of(fluid[:-1], fluid[1:], 4.0), edge], axis=0)
    back_x = jnp.concatenate([edge, wx[:-1]], axis=0)
    across = (wx + back_x) + (wy + pltpu.roll(wy, 1, 1)) + pin
    share = 1.0 / jnp.sum(across, axis=2, keepdims=True)

    above, below, own = pltpu.roll(wz, 1, 2), wz, across
    steps = []
    stride = 1
    while stride < depth:
        inverse = 1.0 / (above + below + own)
        up = above * pltpu.roll(inverse, stride, 2)
        down = below * pltpu.roll(inverse, depth - stride, 2)
        own = own + up * pltpu.roll(own, stride, 2) + down * pltpu.roll(own, depth - stride, 2)
        above = up * pltpu.roll(above, stride, 2)
        below = down * pltpu.roll(below, depth - stride, 2)
        steps.append((stride, up, down))
        stride *= 2
    inverse = 1.0 / (above + below + own)

    def solve(right):
        mean = jnp.sum(right, axis=2, keepdims=True) * share
        for stride, up, down in steps:
            right = (
                right
                + up * pltpu.roll(right, stride, 2)
                + down * pltpu.roll(right, depth - stride, 2)
            )
        return right * inverse + mean

    corr = solve(rhs)
    flow_x = wx[:-1] * (corr[1:] - corr[:-1])
    flow_x = jnp.concatenate([flow_x, edge], 0) - jnp.concatenate([edge, flow_x], 0)
    flow_y = wy * (pltpu.roll(corr, ROWS - 1, 1) - corr)
    flow_z = wz * (pltpu.roll(corr, depth - 1, 2) - corr)
    rest = (
        (rhs - pin * corr)
        + flow_x
        + (flow_y - pltpu.roll(flow_y, 1, 1))
        + (flow_z - pltpu.roll(flow_z, 1, 2))
    )
    return corr + solve(rest)


def up_kernel(
    groups, by, depth, sizes,
    packed,
    rhs1, pin1, wx1, wy1, wz1, gain1, corr1,
    rhs2, pin2, wx2, wy2, wz2, gain2, corr2,
    out_ref,
    one1, two1, one2, two2, lifted,
):
    count3 = depth // 4
    shares = packed.shape[0]
    first = jnp.concatenate([packed[i, 0:count3] for i in range(shares)], axis=0).T
    second = jnp.concatenate([packed[i, count3 : 2 * count3] for i in range(shares)], axis=0).T
    cells = ROWS * ROWS
    total3 = shares * count3
    shape3 = (ROWS, ROWS, total3)
    corr3 = columns(
        first[:cells].reshape(shape3), first[cells:].reshape(shape3), second[:cells].reshape(shape3)
    ).reshape(cells, total3)

    nx, ny = SPLIT
    ix, iy = lax.axis_index("gx"), lax.axis_index("gy")
    part = (lax.axis_index("gz") * nx + ix) * ny + iy
    mine = pltpu.roll(corr3, lax.rem(NEAR - part * count3 + total3, total3), 1)
    tall = jnp.concatenate([mine, mine], axis=0).T
    count = count3 + 2 * NEAR
    fine, coarse = Level(0), Level(1)
    cell = iota((LANES, ROWS * LANES), 0)
    lane = iota((LANES, ROWS * LANES), 1)
    same_y = cell % ROWS == (lane % coarse.ny) // 2
    spread = where01((cell // ROWS == lane // LANES) & same_y)
    wide = dot01(tall[0:count], spread)
    for row in range(ROWS):
        lifted[0:count, row, :] = wide[:, row * LANES : (row + 1) * LANES]

    fields1 = (rhs1, pin1, wx1, wy1, wz1)
    fields2 = (rhs2, pin2, wx2, wy2, wz2)
    low, high = NEAR - 6, NEAR + depth // 2 + 6
    parents = lifted[low // 2 + NEAR // 2 : high // 2 + NEAR // 2]
    twice = jnp.broadcast_to(parents[:, None], (parents.shape[0], 2, ROWS, LANES))
    one2[low:high] = corr2[low:high] + twice.reshape(high - low, ROWS, LANES)
    reach = depth // 2 + NEAR
    sweep(coarse, NEAR - 4, reach + 4, sizes[4], fields2, gain2, one2, two2)
    sweep(coarse, NEAR - 3, reach + 3, sizes[4], fields2, gain2, two2, one2)
    sweep(coarse, NEAR - 2, reach + 2, sizes[4], fields2, gain2, one2, two2)

    fine_lane, coarse_lane = iota((LANES, LANES), 1), iota((LANES, LANES), 0)
    x_of = (fine_lane // fine.ny) // 2
    y_of = (fine_lane % fine.ny) // 2
    up = where01(coarse_lane == x_of * coarse.ny + y_of)
    lifted[0 : depth // 2 + 4] = in_lanes(two2[NEAR - 2 : reach + 2], up)
    parents = lifted[0 : depth // 2 + 4]
    twice = jnp.broadcast_to(parents[:, None], (parents.shape[0], 2, ROWS, LANES))
    low, high = HALO - 4, HALO + depth + 4
    one1[low:high] = corr1[low:high] + twice.reshape(high - low, ROWS, LANES)
    reach = depth + HALO
    sweep(fine, HALO - 2, reach + 2, sizes[1], fields1, gain1, one1, two1)
    sweep(fine, HALO - 1, reach + 1, sizes[1], fields1, gain1, two1, one1)
    sweep(fine, HALO, reach, sizes[1], fields1, gain1, one1, two1)

    group = (iota((depth, LANES), 1) // by) % groups
    for ix in range(nx):
        scaled = [
            two1[HALO:reach, ix * groups + part, :]
            * (OMEGA / gain1[HALO:reach, ix * groups + part, :])
            for part in range(groups)
        ]
        for iy in range(ny):
            total = scaled[iy]
            for part in range(groups):
                if part != iy:
                    moved = pltpu.roll(scaled[part], (by * (part - iy)) % LANES, 1)
                    total = jnp.where(group == part, moved, total)
            out_ref[ix * ny + iy] = total


def finish_kernel(blocks, out_ref):
    bx, by, depth = out_ref.shape
    cells = bx * by
    cell = iota((cells, cells), 0)
    lane = iota((cells, cells), 1)
    x, y = cell // by, cell % by
    chosen = where01((x % 4) * (bx // 4 * by) + (x // 4) * by + y == lane)
    turned = dot01(blocks[...].reshape(depth, cells), chosen, (((1,), (1,)), ((), ())))
    out_ref[...] = turned.T.reshape(out_ref.shape)


def whole_planes(residual_q2, viscosity, pinned):
    bx, by, depth = viscosity.shape
    groups = bx // 4
    peers = SPLIT[0] * SPLIT[1]
    share = depth // peers
    planes = share + 2 * HALO
    count2 = share // 2 + 2 * NEAR
    sizes = (10, 24, 22, 11, 24, 24)
    limit = pltpu.CompilerParams(vmem_limit_bytes=32 * 2**20)

    def flat(rows):
        return jax.ShapeDtypeStruct((rows, LANES), F32)

    def blocks(count, rows):
        return jax.ShapeDtypeStruct((count, rows, LANES), F32)

    def room(count):
        return pltpu.VMEM((count, ROWS, LANES), F32)

    residual = residual_q2.reshape(4 * bx * by, 2 * depth)
    own, top, bottom = pl.pallas_call(
        prepare_kernel,
        in_specs=[pl.BlockSpec(memory_space=pltpu.HBM)] * 3,
        out_shape=(flat(3 * depth), flat(SLAB), flat(SLAB)),
        scratch_shapes=[
            pltpu.VMEM(residual.shape, residual.dtype),
            pltpu.VMEM(viscosity.shape, viscosity.dtype),
            pltpu.VMEM(pinned.shape, pinned.dtype),
            pltpu.SemaphoreType.DMA((3,)),
        ],
        compiler_params=limit,
        name="prepare",
    )(residual, viscosity, pinned)
    length = lax.axis_size("gz")
    forward = [(i, i + 1) for i in range(length - 1)]
    low = lax.ppermute(top, "gz", forward)
    high = lax.ppermute(bottom, "gz", [(target, source) for source, target in forward])
    rows = -(-3 * planes // ROWS) * ROWS
    parcels = pl.pallas_call(
        functools.partial(pack_kernel, depth, planes),
        out_shape=blocks(peers, rows),
        compiler_params=limit,
        name="pack",
    )(own, low, high)
    gathered = lax.all_to_all(parcels, ("gx", "gy"), 0, 0, tiled=True)
    saved = (blocks(planes, ROWS),) * 7 + (blocks(count2, ROWS),) * 7
    results = pl.pallas_call(
        functools.partial(down_kernel, groups, by, share, sizes),
        out_shape=saved + (flat(share // 2),),
        scratch_shapes=[room(planes), room(planes), room(count2), room(count2), room(count2)],
        compiler_params=limit,
        name="down",
    )(gathered)
    copies = jnp.broadcast_to(results[-1], (length * peers, share // 2, LANES))
    packed = lax.all_to_all(copies, ("gz", "gx", "gy"), 0, 0, tiled=True)
    mine = pl.pallas_call(
        functools.partial(up_kernel, groups, by, share, sizes),
        out_shape=blocks(peers, share),
        scratch_shapes=[room(planes), room(planes), room(count2), room(count2), room(count2)],
        compiler_params=limit,
        name="up",
    )(packed, *results[:-1])
    return pl.pallas_call(
        finish_kernel,
        out_shape=jax.ShapeDtypeStruct((bx, by, depth), F32),
        compiler_params=limit,
        name="finish",
    )(lax.all_to_all(mine, ("gx", "gy"), 0, 0, tiled=True))


def one_tile_planes(mesh, viscosity):
    split = (mesh.shape["gx"], mesh.shape["gy"])
    depth = viscosity.shape[2]
    fits = viscosity.shape[:2] == PLANE and split == SPLIT
    return fits and depth == 4 * LANES and depth // mesh.shape["gz"] == LANES


def solution(mesh):
    placed = (P("gx", "gy", "gz"), P("gx", "gy", "gz"), P("gx", "gy", "gz"))

    def cycle(residual_q2, viscosity, pinned):
        chosen = whole_planes if one_tile_planes(mesh, viscosity) else per_device
        return jax.shard_map(
            chosen, mesh=mesh, in_specs=placed, out_specs=P("gx", "gy", "gz"), check_vma=False
        )(residual_q2, viscosity, pinned)

    return cycle
```

```python
import functools

import jax
import jax.numpy as jnp
from jax import lax
from jax.experimental import pallas as pl
from jax.experimental.pallas import tpu as pltpu
from jax.sharding import PartitionSpec as P

NU = 3


OMEGA = 0.6


def with_halo(block, sides, width):
    for axis, dim in sides:
        count = lax.axis_size(axis)
        forward = [(i, i + 1) for i in range(count - 1)]
        backward = [(target, source) for source, target in forward]
        low = lax.ppermute(
            lax.slice_in_dim(block, block.shape[dim] - width, None, axis=dim), axis, forward
        )
        high = lax.ppermute(lax.slice_in_dim(block, 0, width, axis=dim), axis, backward)
        block = jnp.concatenate([low, block, high], axis=dim)
    return block


def coarsen(x):
    a, b, c = x.shape
    return x.reshape(a // 2, 2, b // 2, 2, c // 2, 2).sum(axis=(1, 3, 5))


def refine(x):
    return jnp.repeat(jnp.repeat(jnp.repeat(x, 2, 0), 2, 1), 2, 2)


def extended(field):
    return with_halo(field, (("gx", 0), ("gy", 1), ("gz", 2)), 1)


def shifted(padded):
    return [
        padded[2:, 1:-1, 1:-1],
        padded[:-2, 1:-1, 1:-1],
        padded[1:-1, 2:, 1:-1],
        padded[1:-1, :-2, 1:-1],
        padded[1:-1, 1:-1, 2:],
        padded[1:-1, 1:-1, :-2],
    ]


def neighbours(field):
    return shifted(extended(field))


def harmonic(fluid, near, factor):
    total = fluid + near
    return jnp.where(total > 0, factor * 2.0 * fluid * near / jnp.where(total > 0, total, 1.0), 0.0)


def couplings(fluid, factor):
    return [harmonic(fluid, near, factor) for near in neighbours(fluid)]


def apply_op(field, weights, diag):
    total = diag * field
    for weight, near in zip(weights, neighbours(field)):
        total = total - weight * near
    return total


def presmooth(rhs, weights, diag):
    corr = OMEGA * rhs / diag
    for sweep in range(NU - 1):
        corr = corr + OMEGA * (rhs - apply_op(corr, weights, diag)) / diag
    return corr


def postsmooth(corr, rhs, weights, diag):
    for sweep in range(NU):
        corr = corr + OMEGA * (rhs - apply_op(corr, weights, diag)) / diag
    return corr


def tridiag(coeffs, rhs):
    solved = lax.linalg.tridiagonal_solve(coeffs[0], coeffs[1], coeffs[2], rhs[..., None])[..., 0]
    last = rhs.ndim - 1
    shift_col = jnp.sum(rhs, axis=last, keepdims=True) / jnp.sum(
        coeffs[3], axis=last, keepdims=True
    )
    return solved + shift_col


def prepare_columns(weights, diag):
    lower = -weights[5]
    upper = -weights[4]
    across = diag + lower + upper
    return (
        lax.all_gather(lower, "gz", axis=2, tiled=True),
        lax.all_gather(diag, "gz", axis=2, tiled=True),
        lax.all_gather(upper, "gz", axis=2, tiled=True),
        lax.all_gather(across, "gz", axis=2, tiled=True),
    )


def column_solve(rhs, coeffs):
    depth = rhs.shape[2]
    whole = lax.all_gather(rhs, "gz", axis=2, tiled=True)
    solved = tridiag(coeffs, whole)
    return lax.dynamic_slice_in_dim(solved, lax.axis_index("gz") * depth, depth, 2)


def per_device(residual_q2, viscosity, pinned):
    fluid1 = 1.0 / viscosity
    pin1 = 4.0 * pinned.astype(jnp.float32) * fluid1
    rhs1 = coarsen(residual_q2.astype(jnp.float32))
    fluid2 = coarsen(fluid1) / 8.0
    pin2 = coarsen(pin1) / 4.0
    fluid3 = coarsen(fluid2) / 8.0
    pin3 = coarsen(pin2) / 4.0
    weights1 = couplings(fluid1, 1.0)
    weights2 = couplings(fluid2, 2.0)
    weights3 = couplings(fluid3, 4.0)
    diag1 = sum(weights1) + pin1
    diag2 = sum(weights2) + pin2
    diag3 = sum(weights3) + pin3
    coeffs = prepare_columns(weights3, diag3)
    corr1 = presmooth(rhs1, weights1, diag1)
    rhs2 = coarsen(rhs1 - apply_op(corr1, weights1, diag1))
    corr2 = presmooth(rhs2, weights2, diag2)
    rhs3 = coarsen(rhs2 - apply_op(corr2, weights2, diag2))
    corr3 = column_solve(rhs3, coeffs)
    corr3 = corr3 + column_solve(rhs3 - apply_op(corr3, weights3, diag3), coeffs)
    corr2 = postsmooth(corr2 + refine(corr3), rhs2, weights2, diag2)
    corr1 = postsmooth(corr1 + refine(corr2), rhs1, weights1, diag1)
    return diag1 * corr1


PLANE = (32, 32)
SPLIT = (2, 4)
ROWS = 8
LANES = 128
HALO = 18
NEAR = 8
F32 = jnp.float32


def iota(shape, dim):
    return lax.broadcasted_iota(jnp.int32, shape, dim)


def dot01(field, chosen, dims=(((1,), (0,)), ((), ()))):
    total = None
    rest = field
    for part in range(3):
        piece = rest.astype(jnp.bfloat16)
        term = lax.dot_general(piece, chosen, dims, preferred_element_type=F32)
        total = term if total is None else total + term
        if part < 2:
            rest = rest - piece.astype(F32)
    return total


def where01(condition):
    return jnp.where(condition, 1.0, 0.0).astype(jnp.bfloat16)


def loop(low, high, size, body):
    size = min(size, high - low)
    steps = -(-(high - low) // size)

    def step(index, carry):
        body(jnp.minimum(low + index * size, high - size), size)
        return carry

    if steps == 1:
        body(low, size)
    else:
        lax.fori_loop(0, steps, step, 0)


class Level:
    def __init__(self, level):
        self.ny = PLANE[1] >> level
        self.xs = 4 >> level
        self.factor = float(2**level)

    def masks(self, shape):
        lane = iota(shape, 2)
        row = iota(shape, 1)
        within = (lane // self.ny) % self.xs
        y = lane % self.ny
        last_x = (row == ROWS - 1) & (within == self.xs - 1)
        return within, y == self.ny - 1, last_x

    def next_x(self, field):
        within = (iota(field.shape, 2) // self.ny) % self.xs
        moved = pltpu.roll(field, LANES - self.ny, 2)
        return jnp.where(within == self.xs - 1, pltpu.roll(moved, ROWS - 1, 1), moved)

    def last_x(self, field):
        within = (iota(field.shape, 2) // self.ny) % self.xs
        moved = pltpu.roll(field, self.ny, 2)
        return jnp.where(within == 0, pltpu.roll(moved, 1, 1), moved)

    def next_y(self, field):
        return pltpu.roll(field, LANES - 1, 2)

    def last_y(self, field):
        return pltpu.roll(field, 1, 2)

    def balance(self, field, wx, wy, wz):
        mid = field[1:-1]
        flow_x = wx * (self.next_x(mid) - mid)
        flow_y = wy * (self.next_y(mid) - mid)
        flow_z = wz * (field[1:] - field[:-1])
        return (
            (flow_x - self.last_x(flow_x))
            + (flow_y - self.last_y(flow_y))
            + (flow_z[1:] - flow_z[:-1])
        )


def mean_of(fluid, near, factor):
    total = fluid + near
    safe = jnp.where(total > 0, total, 1.0)
    return jnp.where(total > 0, (factor * 2.0) * fluid * near / safe, 0.0)


def set_level(level, low, high, size, fluid, pin, rhs, wx, wy, wz, gain, corr):
    def body(plane, count):
        wide = fluid[pl.ds(plane - 1, count + 2)]
        mid = wide[1:-1]
        within, end_y, end_x = level.masks(mid.shape)
        to_x = jnp.where(end_x, 0.0, mean_of(mid, level.next_x(mid), level.factor))
        to_y = jnp.where(end_y, 0.0, mean_of(mid, level.next_y(mid), level.factor))
        to_z = mean_of(wide[:-1], wide[1:], level.factor)
        diag = (
            (to_x + level.last_x(to_x))
            + (to_y + level.last_y(to_y))
            + (to_z[1:] + to_z[:-1])
            + pin[pl.ds(plane, count)]
        )
        some = diag > 0
        scale = jnp.where(some, OMEGA / jnp.where(some, diag, 1.0), 0.0)
        wx[pl.ds(plane, count)] = to_x
        wy[pl.ds(plane, count)] = to_y
        wz[pl.ds(plane, count)] = to_z[1:]
        gain[pl.ds(plane, count)] = scale
        if corr is not None:
            corr[pl.ds(plane, count)] = scale * rhs[pl.ds(plane, count)]

    loop(low, high, size, body)


def residual_of(level, plane, count, fields, corr):
    rhs, pin, wx, wy, wz = fields
    field = corr[pl.ds(plane - 1, count + 2)]
    spread = level.balance(
        field, wx[pl.ds(plane, count)], wy[pl.ds(plane, count)], wz[pl.ds(plane - 1, count + 1)]
    )
    mid = field[1:-1]
    return mid, (rhs[pl.ds(plane, count)] - pin[pl.ds(plane, count)] * mid) + spread


def sweep(level, low, high, size, fields, gain, source, target):
    def body(plane, count):
        mid, rest = residual_of(level, plane, count, fields, source)
        target[pl.ds(plane, count)] = mid + gain[pl.ds(plane, count)] * rest

    loop(low, high, size, body)


def pair_sum(field):
    half = field.reshape((field.shape[0] // 2, 2) + field.shape[1:])
    return half[:, 0] + half[:, 1]


def coarse_residual(level, low, high, size, fields, corr, target):
    size = min(size, high - low)
    assert (high - low) % size == 0 and size % 2 == 0

    def body(plane, count):
        _, rest = residual_of(level, plane, count, fields, corr)
        target[pl.ds((plane - low) // 2, count // 2)] = pair_sum(rest)

    loop(low, high, size, body)


def lanes_down(level):
    fine = iota((LANES, LANES), 0)
    coarse = iota((LANES, LANES), 1)
    ny, xs = PLANE[1] >> level, 4 >> level
    half = xs // 2
    same_x = ((fine // ny) % xs) // 2 == (coarse // (ny // 2)) % half
    same_y = (fine % ny) // 2 == coarse % (ny // 2)
    return where01((fine < ny * xs) & same_x & same_y)


def in_lanes(field, chosen):
    flat = field.reshape(field.shape[0] * ROWS, LANES)
    return dot01(flat, chosen).reshape(field.shape)


def rank_of(peer):
    ny = SPLIT[1]
    ix, iy = peer // ny, peer % ny
    return ix * ny + (ny - 1 - iy if ix % 2 else iy)


def prepare_kernel(share, res_ref, fluid_ref, pin_ref, out_ref):
    bx, by, depth = fluid_ref.shape
    cells = bx * by
    groups = bx // 4
    pick = where01(iota((depth, 2 * depth), 1) // 2 == iota((depth, 2 * depth), 0))
    deep = lax.dot_general(
        pick, res_ref[...], (((1,), (1,)), ((), ())), preferred_element_type=F32
    )

    def lane_of(x, y):
        return (x % 4) * (groups * by) + (x // 4) * by + y

    fine = iota((4 * cells, cells), 0)
    lane = iota((4 * cells, cells), 1)
    chosen = where01(lane_of(fine // (4 * by), (fine % (2 * by)) // 2) == lane)
    rhs = dot01(deep, chosen)
    cell = iota((cells, cells), 0)
    lane = iota((cells, cells), 1)
    chosen = where01(lane_of(cell // by, cell % by) == lane)
    fluid = dot01(fluid_ref[...].reshape(cells, depth).T, chosen)
    pin = dot01(pin_ref[...].reshape(cells, depth).T, chosen)
    for index, field in enumerate((fluid, rhs, pin)):
        for peer in range(depth // share):
            begin = rank_of(peer) * share
            out_ref[peer, index * share : (index + 1) * share] = field[begin : begin + share]


def spread_kernel(groups, by, edge, gathered, own, top, bottom):
    rows = own.shape[0]
    for start in range(0, rows, ROWS):
        place(gathered, start, own, start, groups, by)
    share = rows // 3
    for index in range(3):
        first, last = index * share, (index + 1) * share
        top[index * edge : (index + 1) * edge] = own[last - edge : last]
        bottom[index * edge : (index + 1) * edge] = own[first : first + edge]


def place(gathered, row, target, plane, groups, by):
    group = (iota((ROWS, LANES), 1) // by) % groups
    nx, ny = SPLIT
    for ix in range(nx):
        found = [gathered[ix * ny + iy, pl.ds(row, ROWS), :] for iy in range(ny)]
        for part in range(groups):
            total = found[part]
            for iy in range(ny):
                if iy != part:
                    moved = pltpu.roll(found[iy], (by * (iy - part)) % LANES, 1)
                    total = jnp.where(group == iy, moved, total)
            target[pl.ds(plane, ROWS), ix * groups + part, :] = total


def down_kernel(
    groups, by, depth, sizes,
    low2, low1, own, high1, high2,
    rhs1, pin1, wx1, wy1, wz1, gain1, corr1,
    rhs2, pin2, wx2, wy2, wz2, gain2, corr2,
    packed,
    fluid1, other1, fluid2, other2, sums,
):
    planes = depth + 2 * HALO
    for index, target in enumerate((fluid1, rhs1, pin1)):
        start = 0
        for piece in (low2, low1, own, high1, high2):
            count = piece.shape[0] // 3
            target[start : start + count] = piece[index * count : (index + 1) * count]
            start += count

    fine, coarse = Level(0), Level(1)
    down1, down2 = lanes_down(0), lanes_down(1)
    fields1 = (rhs1, pin1, wx1, wy1, wz1)
    fields2 = (rhs2, pin2, wx2, wy2, wz2)
    set_level(fine, 1, planes - 1, sizes[0], fluid1, pin1, rhs1, wx1, wy1, wz1, gain1, other1)
    sweep(fine, 2, planes - 2, sizes[1], fields1, gain1, other1, corr1)
    sweep(fine, 3, planes - 3, sizes[1], fields1, gain1, corr1, other1)
    corr1[...] = other1[...]
    count2 = depth // 2 + 2 * NEAR
    begin = HALO - 2 * NEAR
    for source, target, share in ((fluid1, fluid2, 8.0), (pin1, pin2, 4.0)):
        whole = pair_sum(source[begin : begin + 2 * count2])
        target[...] = in_lanes(whole, down1) * (1.0 / share)
    inner = count2 - 2
    coarse_residual(fine, begin + 2, begin + 2 + 2 * inner, sizes[2], fields1, corr1, sums)
    rhs2[1 : 1 + inner] = in_lanes(sums[0:inner], down1)
    set_level(coarse, 1, 1 + inner, sizes[3], fluid2, pin2, rhs2, wx2, wy2, wz2, gain2, other2)
    sweep(coarse, 2, inner, sizes[4], fields2, gain2, other2, corr2)
    sweep(coarse, 3, inner - 1, sizes[4], fields2, gain2, corr2, other2)
    corr2[...] = other2[...]
    coarse_residual(coarse, NEAR, NEAR + depth // 2, sizes[5], fields2, corr2, sums)
    count3 = depth // 4
    rhs3 = in_lanes(sums[0:count3], down2)
    fluid3 = in_lanes(pair_sum(fluid2[NEAR : NEAR + 2 * count3]), down2) * 0.125
    pin3 = in_lanes(pair_sum(pin2[NEAR : NEAR + 2 * count3]), down2) * 0.25
    lane = iota((count3, LANES), 1) // ROWS
    first = jnp.zeros((count3, LANES), F32)
    second = jnp.zeros((count3, LANES), F32)
    for row in range(ROWS):
        first = jnp.where(lane == row, rhs3[:, row, :], first)
        first = jnp.where(lane == ROWS + row, fluid3[:, row, :], first)
        second = jnp.where(lane == row, pin3[:, row, :], second)
    packed[0:count3] = first
    packed[count3 : 2 * count3] = second


def columns(rhs, fluid, pin):
    shape = fluid.shape
    depth = shape[2]
    lane, y = iota(shape, 2), iota(shape, 1)
    edge = jnp.zeros((1,) + shape[1:], F32)
    wz = jnp.where(lane == depth - 1, 0.0, mean_of(fluid, pltpu.roll(fluid, depth - 1, 2), 4.0))
    wy = jnp.where(y == ROWS - 1, 0.0, mean_of(fluid, pltpu.roll(fluid, ROWS - 1, 1), 4.0))
    wx = jnp.concatenate([mean_of(fluid[:-1], fluid[1:], 4.0), edge], axis=0)
    back_x = jnp.concatenate([edge, wx[:-1]], axis=0)
    across = (wx + back_x) + (wy + pltpu.roll(wy, 1, 1)) + pin
    share = 1.0 / jnp.sum(across, axis=2, keepdims=True)

    above, below, own = pltpu.roll(wz, 1, 2), wz, across
    steps = []
    stride = 1
    while stride < depth:
        inverse = 1.0 / (above + below + own)
        up = above * pltpu.roll(inverse, stride, 2)
        down = below * pltpu.roll(inverse, depth - stride, 2)
        own = own + up * pltpu.roll(own, stride, 2) + down * pltpu.roll(own, depth - stride, 2)
        above = up * pltpu.roll(above, stride, 2)
        below = down * pltpu.roll(below, depth - stride, 2)
        steps.append((stride, up, down))
        stride *= 2
    inverse = 1.0 / (above + below + own)

    def solve(right):
        mean = jnp.sum(right, axis=2, keepdims=True) * share
        for stride, up, down in steps:
            right = (
                right
                + up * pltpu.roll(right, stride, 2)
                + down * pltpu.roll(right, depth - stride, 2)
            )
        return right * inverse + mean

    corr = solve(rhs)
    flow_x = wx[:-1] * (corr[1:] - corr[:-1])
    flow_x = jnp.concatenate([flow_x, edge], 0) - jnp.concatenate([edge, flow_x], 0)
    flow_y = wy * (pltpu.roll(corr, ROWS - 1, 1) - corr)
    flow_z = wz * (pltpu.roll(corr, depth - 1, 2) - corr)
    rest = (
        (rhs - pin * corr)
        + flow_x
        + (flow_y - pltpu.roll(flow_y, 1, 1))
        + (flow_z - pltpu.roll(flow_z, 1, 2))
    )
    return corr + solve(rest)


def up_kernel(
    groups, by, depth, sizes,
    packed,
    rhs1, pin1, wx1, wy1, wz1, gain1, corr1,
    rhs2, pin2, wx2, wy2, wz2, gain2, corr2,
    out_ref,
    one1, two1, one2, two2, lifted,
):
    count3 = depth // 4
    shares = packed.shape[0]
    peers = SPLIT[0] * SPLIT[1]
    slabs = sorted(range(shares), key=lambda i: (i // peers, rank_of(i % peers)))
    first = jnp.concatenate([packed[i, 0:count3] for i in slabs], axis=0).T
    second = jnp.concatenate([packed[i, count3 : 2 * count3] for i in slabs], axis=0).T
    cells = ROWS * ROWS
    total3 = shares * count3
    shape3 = (ROWS, ROWS, total3)
    corr3 = columns(
        first[:cells].reshape(shape3), first[cells:].reshape(shape3), second[:cells].reshape(shape3)
    ).reshape(cells, total3)

    nx, ny = SPLIT
    ix, iy = lax.axis_index("gx"), lax.axis_index("gy")
    along = jnp.where(lax.rem(ix, 2) == 1, ny - 1 - iy, iy)
    part = (lax.axis_index("gz") * nx + ix) * ny + along
    mine = pltpu.roll(corr3, lax.rem(NEAR - part * count3 + total3, total3), 1)
    tall = jnp.concatenate([mine, mine], axis=0).T
    count = count3 + 2 * NEAR
    fine, coarse = Level(0), Level(1)
    cell = iota((LANES, ROWS * LANES), 0)
    lane = iota((LANES, ROWS * LANES), 1)
    same_y = cell % ROWS == (lane % coarse.ny) // 2
    spread = where01((cell // ROWS == lane // LANES) & same_y)
    wide = dot01(tall[0:count], spread)
    for row in range(ROWS):
        lifted[0:count, row, :] = wide[:, row * LANES : (row + 1) * LANES]

    fields1 = (rhs1, pin1, wx1, wy1, wz1)
    fields2 = (rhs2, pin2, wx2, wy2, wz2)
    low, high = NEAR - 6, NEAR + depth // 2 + 6
    parents = lifted[low // 2 + NEAR // 2 : high // 2 + NEAR // 2]
    twice = jnp.broadcast_to(parents[:, None], (parents.shape[0], 2, ROWS, LANES))
    one2[low:high] = corr2[low:high] + twice.reshape(high - low, ROWS, LANES)
    reach = depth // 2 + NEAR
    sweep(coarse, NEAR - 4, reach + 4, sizes[4], fields2, gain2, one2, two2)
    sweep(coarse, NEAR - 3, reach + 3, sizes[4], fields2, gain2, two2, one2)
    sweep(coarse, NEAR - 2, reach + 2, sizes[4], fields2, gain2, one2, two2)

    fine_lane, coarse_lane = iota((LANES, LANES), 1), iota((LANES, LANES), 0)
    x_of = (fine_lane // fine.ny) // 2
    y_of = (fine_lane % fine.ny) // 2
    up = where01(coarse_lane == x_of * coarse.ny + y_of)
    lifted[0 : depth // 2 + 4] = in_lanes(two2[NEAR - 2 : reach + 2], up)
    parents = lifted[0 : depth // 2 + 4]
    twice = jnp.broadcast_to(parents[:, None], (parents.shape[0], 2, ROWS, LANES))
    low, high = HALO - 4, HALO + depth + 4
    one1[low:high] = corr1[low:high] + twice.reshape(high - low, ROWS, LANES)
    reach = depth + HALO
    sweep(fine, HALO - 2, reach + 2, sizes[1], fields1, gain1, one1, two1)
    sweep(fine, HALO - 1, reach + 1, sizes[1], fields1, gain1, two1, one1)
    sweep(fine, HALO, reach, sizes[1], fields1, gain1, one1, two1)

    group = (iota((depth, LANES), 1) // by) % groups
    for ix in range(nx):
        scaled = [
            two1[HALO:reach, ix * groups + part, :]
            * (OMEGA / gain1[HALO:reach, ix * groups + part, :])
            for part in range(groups)
        ]
        for iy in range(ny):
            total = scaled[iy]
            for part in range(groups):
                if part != iy:
                    moved = pltpu.roll(scaled[part], (by * (part - iy)) % LANES, 1)
                    total = jnp.where(group == part, moved, total)
            out_ref[ix * ny + iy] = total


def finish_kernel(blocks, out_ref):
    bx, by, depth = out_ref.shape
    cells = bx * by
    cell = iota((cells, cells), 0)
    lane = iota((cells, cells), 1)
    x, y = cell // by, cell % by
    chosen = where01((x % 4) * (bx // 4 * by) + (x // 4) * by + y == lane)
    peers = blocks.shape[0]
    ordered = jnp.concatenate([blocks[i] for i in sorted(range(peers), key=rank_of)], axis=0)
    turned = dot01(ordered, chosen, (((1,), (1,)), ((), ())))
    out_ref[...] = turned.T.reshape(out_ref.shape)


def whole_planes(residual_q2, viscosity, pinned):
    bx, by, depth = viscosity.shape
    groups = bx // 4
    peers = SPLIT[0] * SPLIT[1]
    share = depth // peers
    planes = share + 2 * HALO
    count2 = share // 2 + 2 * NEAR
    sizes = (10, 24, 22, 11, 24, 24)
    limit = pltpu.CompilerParams(vmem_limit_bytes=32 * 2**20)

    def flat(rows):
        return jax.ShapeDtypeStruct((rows, LANES), F32)

    def blocks(count, rows):
        return jax.ShapeDtypeStruct((count, rows, LANES), F32)

    def room(count):
        return pltpu.VMEM((count, ROWS, LANES), F32)

    fluid = 1.0 / viscosity
    pin = 4.0 * pinned.astype(F32) * fluid
    parcels = pl.pallas_call(
        functools.partial(prepare_kernel, share),
        out_shape=blocks(peers, 3 * share),
        compiler_params=limit,
        name="prepare",
    )(residual_q2.reshape(4 * bx * by, 2 * depth), fluid, pin)
    edge = HALO - share
    own, top, bottom = pl.pallas_call(
        functools.partial(spread_kernel, groups, by, edge),
        out_shape=(blocks(3 * share, ROWS), blocks(3 * edge, ROWS), blocks(3 * edge, ROWS)),
        compiler_params=limit,
        name="spread",
    )(lax.all_to_all(parcels, ("gx", "gy"), 0, 0, tiled=True))
    length = lax.axis_size("gz")
    slabs = sorted(range(peers), key=rank_of)
    parts = length * peers

    def step(field, ahead):
        device = [slabs[i % peers] * length + i // peers for i in range(parts)]
        pairs = [(device[i], device[i + ahead]) for i in range(parts) if 0 <= i + ahead < parts]
        return lax.ppermute(field, ("gx", "gy", "gz"), pairs)

    low1, high1 = step(own, 1), step(own, -1)
    low2, high2 = step(top, 2), step(bottom, -2)
    saved = (blocks(planes, ROWS),) * 7 + (blocks(count2, ROWS),) * 7
    results = pl.pallas_call(
        functools.partial(down_kernel, groups, by, share, sizes),
        out_shape=saved + (flat(share // 2),),
        scratch_shapes=[room(planes), room(planes), room(count2), room(count2), room(count2)],
        compiler_params=limit,
        name="down",
    )(low2, low1, own, high1, high2)
    copies = jnp.broadcast_to(results[-1], (parts, share // 2, LANES))
    packed = lax.all_to_all(copies, ("gz", "gx", "gy"), 0, 0, tiled=True)
    mine = pl.pallas_call(
        functools.partial(up_kernel, groups, by, share, sizes),
        out_shape=blocks(peers, share),
        scratch_shapes=[room(planes), room(planes), room(count2), room(count2), room(count2)],
        compiler_params=limit,
        name="up",
    )(packed, *results[:-1])
    return pl.pallas_call(
        finish_kernel,
        out_shape=jax.ShapeDtypeStruct((bx, by, depth), F32),
        compiler_params=limit,
        name="finish",
    )(lax.all_to_all(mine, ("gx", "gy"), 0, 0, tiled=True))


def one_tile_planes(mesh, viscosity):
    split = (mesh.shape["gx"], mesh.shape["gy"])
    depth = viscosity.shape[2]
    fits = viscosity.shape[:2] == PLANE and split == SPLIT
    return fits and depth == 4 * LANES and depth // mesh.shape["gz"] == LANES


def solution(mesh):
    placed = (P("gx", "gy", "gz"), P("gx", "gy", "gz"), P("gx", "gy", "gz"))

    def cycle(residual_q2, viscosity, pinned):
        chosen = whole_planes if one_tile_planes(mesh, viscosity) else per_device
        return jax.shard_map(
            chosen, mesh=mesh, in_specs=placed, out_specs=P("gx", "gy", "gz"), check_vma=False
        )(residual_q2, viscosity, pinned)

    return cycle
```

```python
import functools

import jax
import jax.numpy as jnp
from jax import lax
from jax.experimental import pallas as pl
from jax.experimental.pallas import tpu as pltpu
from jax.sharding import PartitionSpec as P

NU = 3


OMEGA = 0.6


def with_halo(block, sides, width):
    for axis, dim in sides:
        count = lax.axis_size(axis)
        forward = [(i, i + 1) for i in range(count - 1)]
        backward = [(target, source) for source, target in forward]
        low = lax.ppermute(
            lax.slice_in_dim(block, block.shape[dim] - width, None, axis=dim), axis, forward
        )
        high = lax.ppermute(lax.slice_in_dim(block, 0, width, axis=dim), axis, backward)
        block = jnp.concatenate([low, block, high], axis=dim)
    return block


def coarsen(x):
    a, b, c = x.shape
    return x.reshape(a // 2, 2, b // 2, 2, c // 2, 2).sum(axis=(1, 3, 5))


def refine(x):
    return jnp.repeat(jnp.repeat(jnp.repeat(x, 2, 0), 2, 1), 2, 2)


def extended(field):
    return with_halo(field, (("gx", 0), ("gy", 1), ("gz", 2)), 1)


def shifted(padded):
    return [
        padded[2:, 1:-1, 1:-1],
        padded[:-2, 1:-1, 1:-1],
        padded[1:-1, 2:, 1:-1],
        padded[1:-1, :-2, 1:-1],
        padded[1:-1, 1:-1, 2:],
        padded[1:-1, 1:-1, :-2],
    ]


def neighbours(field):
    return shifted(extended(field))


def harmonic(fluid, near, factor):
    total = fluid + near
    return jnp.where(total > 0, factor * 2.0 * fluid * near / jnp.where(total > 0, total, 1.0), 0.0)


def couplings(fluid, factor):
    return [harmonic(fluid, near, factor) for near in neighbours(fluid)]


def apply_op(field, weights, diag):
    total = diag * field
    for weight, near in zip(weights, neighbours(field)):
        total = total - weight * near
    return total


def presmooth(rhs, weights, diag):
    corr = OMEGA * rhs / diag
    for sweep in range(NU - 1):
        corr = corr + OMEGA * (rhs - apply_op(corr, weights, diag)) / diag
    return corr


def postsmooth(corr, rhs, weights, diag):
    for sweep in range(NU):
        corr = corr + OMEGA * (rhs - apply_op(corr, weights, diag)) / diag
    return corr


def tridiag(coeffs, rhs):
    solved = lax.linalg.tridiagonal_solve(coeffs[0], coeffs[1], coeffs[2], rhs[..., None])[..., 0]
    last = rhs.ndim - 1
    shift_col = jnp.sum(rhs, axis=last, keepdims=True) / jnp.sum(
        coeffs[3], axis=last, keepdims=True
    )
    return solved + shift_col


def prepare_columns(weights, diag):
    lower = -weights[5]
    upper = -weights[4]
    across = diag + lower + upper
    return (
        lax.all_gather(lower, "gz", axis=2, tiled=True),
        lax.all_gather(diag, "gz", axis=2, tiled=True),
        lax.all_gather(upper, "gz", axis=2, tiled=True),
        lax.all_gather(across, "gz", axis=2, tiled=True),
    )


def column_solve(rhs, coeffs):
    depth = rhs.shape[2]
    whole = lax.all_gather(rhs, "gz", axis=2, tiled=True)
    solved = tridiag(coeffs, whole)
    return lax.dynamic_slice_in_dim(solved, lax.axis_index("gz") * depth, depth, 2)


def per_device(residual_q2, viscosity, pinned):
    fluid1 = 1.0 / viscosity
    pin1 = 4.0 * pinned.astype(jnp.float32) * fluid1
    rhs1 = coarsen(residual_q2.astype(jnp.float32))
    fluid2 = coarsen(fluid1) / 8.0
    pin2 = coarsen(pin1) / 4.0
    fluid3 = coarsen(fluid2) / 8.0
    pin3 = coarsen(pin2) / 4.0
    weights1 = couplings(fluid1, 1.0)
    weights2 = couplings(fluid2, 2.0)
    weights3 = couplings(fluid3, 4.0)
    diag1 = sum(weights1) + pin1
    diag2 = sum(weights2) + pin2
    diag3 = sum(weights3) + pin3
    coeffs = prepare_columns(weights3, diag3)
    corr1 = presmooth(rhs1, weights1, diag1)
    rhs2 = coarsen(rhs1 - apply_op(corr1, weights1, diag1))
    corr2 = presmooth(rhs2, weights2, diag2)
    rhs3 = coarsen(rhs2 - apply_op(corr2, weights2, diag2))
    corr3 = column_solve(rhs3, coeffs)
    corr3 = corr3 + column_solve(rhs3 - apply_op(corr3, weights3, diag3), coeffs)
    corr2 = postsmooth(corr2 + refine(corr3), rhs2, weights2, diag2)
    corr1 = postsmooth(corr1 + refine(corr2), rhs1, weights1, diag1)
    return diag1 * corr1


PLANE = (32, 32)
SPLIT = (2, 4)
ROWS = 8
LANES = 128
HALO = 16
NEAR = 8
F32 = jnp.float32


def iota(shape, dim):
    return lax.broadcasted_iota(jnp.int32, shape, dim)


def dot01(field, chosen, dims=(((1,), (0,)), ((), ()))):
    total = None
    rest = field
    for part in range(3):
        piece = rest.astype(jnp.bfloat16)
        term = lax.dot_general(piece, chosen, dims, preferred_element_type=F32)
        total = term if total is None else total + term
        if part < 2:
            rest = rest - piece.astype(F32)
    return total


def where01(condition):
    return jnp.where(condition, 1.0, 0.0).astype(jnp.bfloat16)


def loop(low, high, size, body):
    size = min(size, high - low)
    steps = -(-(high - low) // size)

    def step(index, carry):
        body(jnp.minimum(low + index * size, high - size), size)
        return carry

    if steps == 1:
        body(low, size)
    else:
        lax.fori_loop(0, steps, step, 0)


class Level:
    def __init__(self, level):
        self.ny = PLANE[1] >> level
        self.xs = 4 >> level
        self.factor = float(2**level)

    def masks(self, shape):
        lane = iota(shape, 2)
        row = iota(shape, 1)
        within = (lane // self.ny) % self.xs
        y = lane % self.ny
        last_x = (row == ROWS - 1) & (within == self.xs - 1)
        return within, y == self.ny - 1, last_x

    def next_x(self, field):
        within = (iota(field.shape, 2) // self.ny) % self.xs
        moved = pltpu.roll(field, LANES - self.ny, 2)
        return jnp.where(within == self.xs - 1, pltpu.roll(moved, ROWS - 1, 1), moved)

    def last_x(self, field):
        within = (iota(field.shape, 2) // self.ny) % self.xs
        moved = pltpu.roll(field, self.ny, 2)
        return jnp.where(within == 0, pltpu.roll(moved, 1, 1), moved)

    def next_y(self, field):
        return pltpu.roll(field, LANES - 1, 2)

    def last_y(self, field):
        return pltpu.roll(field, 1, 2)

    def balance(self, field, wx, wy, wz):
        mid = field[1:-1]
        flow_x = wx * (self.next_x(mid) - mid)
        flow_y = wy * (self.next_y(mid) - mid)
        flow_z = wz * (field[1:] - field[:-1])
        return (
            (flow_x - self.last_x(flow_x))
            + (flow_y - self.last_y(flow_y))
            + (flow_z[1:] - flow_z[:-1])
        )


def mean_of(fluid, near, factor):
    total = fluid + near
    safe = jnp.where(total > 0, total, 1.0)
    return jnp.where(total > 0, (factor * 2.0) * fluid * near / safe, 0.0)


def set_level(level, low, high, size, fluid, pin, rhs, wx, wy, wz, gain, corr):
    def body(plane, count):
        wide = fluid[pl.ds(plane - 1, count + 2)]
        mid = wide[1:-1]
        within, end_y, end_x = level.masks(mid.shape)
        to_x = jnp.where(end_x, 0.0, mean_of(mid, level.next_x(mid), level.factor))
        to_y = jnp.where(end_y, 0.0, mean_of(mid, level.next_y(mid), level.factor))
        to_z = mean_of(wide[:-1], wide[1:], level.factor)
        diag = (
            (to_x + level.last_x(to_x))
            + (to_y + level.last_y(to_y))
            + (to_z[1:] + to_z[:-1])
            + pin[pl.ds(plane, count)]
        )
        some = diag > 0
        scale = jnp.where(some, OMEGA / jnp.where(some, diag, 1.0), 0.0)
        wx[pl.ds(plane, count)] = to_x
        wy[pl.ds(plane, count)] = to_y
        wz[pl.ds(plane, count)] = to_z[1:]
        gain[pl.ds(plane, count)] = scale
        if corr is not None:
            corr[pl.ds(plane, count)] = scale * rhs[pl.ds(plane, count)]

    loop(low, high, size, body)


def residual_of(level, plane, count, fields, corr):
    rhs, pin, wx, wy, wz = fields
    field = corr[pl.ds(plane - 1, count + 2)]
    spread = level.balance(
        field, wx[pl.ds(plane, count)], wy[pl.ds(plane, count)], wz[pl.ds(plane - 1, count + 1)]
    )
    mid = field[1:-1]
    return mid, (rhs[pl.ds(plane, count)] - pin[pl.ds(plane, count)] * mid) + spread


def sweep(level, low, high, size, fields, gain, source, target):
    def body(plane, count):
        mid, rest = residual_of(level, plane, count, fields, source)
        target[pl.ds(plane, count)] = mid + gain[pl.ds(plane, count)] * rest

    loop(low, high, size, body)


def pair_sum(field):
    half = field.reshape((field.shape[0] // 2, 2) + field.shape[1:])
    return half[:, 0] + half[:, 1]


def coarse_residual(level, low, high, size, fields, corr, target):
    size = min(size, high - low)
    assert (high - low) % size == 0 and size % 2 == 0

    def body(plane, count):
        _, rest = residual_of(level, plane, count, fields, corr)
        target[pl.ds((plane - low) // 2, count // 2)] = pair_sum(rest)

    loop(low, high, size, body)


def lanes_down(level):
    fine = iota((LANES, LANES), 0)
    coarse = iota((LANES, LANES), 1)
    ny, xs = PLANE[1] >> level, 4 >> level
    half = xs // 2
    same_x = ((fine // ny) % xs) // 2 == (coarse // (ny // 2)) % half
    same_y = (fine % ny) // 2 == coarse % (ny // 2)
    return where01((fine < ny * xs) & same_x & same_y)


def in_lanes(field, chosen):
    flat = field.reshape(field.shape[0] * ROWS, LANES)
    return dot01(flat, chosen).reshape(field.shape)


def rank_of(peer):
    ny = SPLIT[1]
    ix, iy = peer // ny, peer % ny
    return ix * ny + (ny - 1 - iy if ix % 2 else iy)


def prepare_kernel(share, res_ref, fluid_ref, pin_ref, out_ref):
    bx, by, depth = fluid_ref.shape
    cells = bx * by
    groups = bx // 4
    pick = where01(iota((depth, 2 * depth), 1) // 2 == iota((depth, 2 * depth), 0))
    deep = lax.dot_general(
        pick, res_ref[...], (((1,), (1,)), ((), ())), preferred_element_type=F32
    )

    def lane_of(x, y):
        return (x % 4) * (groups * by) + (x // 4) * by + y

    fine = iota((4 * cells, cells), 0)
    lane = iota((4 * cells, cells), 1)
    chosen = where01(lane_of(fine // (4 * by), (fine % (2 * by)) // 2) == lane)
    rhs = dot01(deep, chosen)
    cell = iota((cells, cells), 0)
    lane = iota((cells, cells), 1)
    chosen = where01(lane_of(cell // by, cell % by) == lane)
    fluid = dot01(fluid_ref[...].reshape(cells, depth).T, chosen)
    pin = dot01(pin_ref[...].reshape(cells, depth).T, chosen)
    for index, field in enumerate((fluid, rhs, pin)):
        for peer in range(depth // share):
            begin = rank_of(peer) * share
            out_ref[peer, index * share : (index + 1) * share] = field[begin : begin + share]


def spread_kernel(groups, by, gathered, own):
    for start in range(0, own.shape[0], ROWS):
        place(gathered, start, own, start, groups, by)


def place(gathered, row, target, plane, groups, by):
    group = (iota((ROWS, LANES), 1) // by) % groups
    nx, ny = SPLIT
    for ix in range(nx):
        found = [gathered[ix * ny + iy, pl.ds(row, ROWS), :] for iy in range(ny)]
        for part in range(groups):
            total = found[part]
            for iy in range(ny):
                if iy != part:
                    moved = pltpu.roll(found[iy], (by * (iy - part)) % LANES, 1)
                    total = jnp.where(group == iy, moved, total)
            target[pl.ds(plane, ROWS), ix * groups + part, :] = total


def down_kernel(
    groups, by, depth, sizes,
    low, own, high,
    rhs1, pin1, wx1, wy1, wz1, gain1, corr1,
    rhs2, pin2, wx2, wy2, wz2, gain2, corr2,
    packed,
    fluid1, other1, fluid2, other2, sums,
):
    planes = depth + 2 * HALO
    for index, target in enumerate((fluid1, rhs1, pin1)):
        start = 0
        for piece in (low, own, high):
            count = piece.shape[0] // 3
            target[start : start + count] = piece[index * count : (index + 1) * count]
            start += count

    fine, coarse = Level(0), Level(1)
    down1, down2 = lanes_down(0), lanes_down(1)
    fields1 = (rhs1, pin1, wx1, wy1, wz1)
    fields2 = (rhs2, pin2, wx2, wy2, wz2)
    set_level(fine, 1, planes - 1, sizes[0], fluid1, pin1, rhs1, wx1, wy1, wz1, gain1, other1)
    sweep(fine, 2, planes - 2, sizes[1], fields1, gain1, other1, corr1)
    sweep(fine, 3, planes - 3, sizes[1], fields1, gain1, corr1, other1)
    corr1[...] = other1[...]
    count2 = depth // 2 + 2 * NEAR
    begin = HALO - 2 * NEAR
    for source, target, share in ((fluid1, fluid2, 8.0), (pin1, pin2, 4.0)):
        whole = pair_sum(source[begin : begin + 2 * count2])
        target[...] = in_lanes(whole, down1) * (1.0 / share)
    low2, high2 = (begin + 4) // 2, count2 - (begin + 4) // 2
    inner = high2 - low2
    coarse_residual(
        fine, begin + 2 * low2, begin + 2 * high2, sizes[2], fields1, corr1, sums
    )
    rhs2[low2:high2] = in_lanes(sums[0:inner], down1)
    set_level(coarse, low2, high2, sizes[3], fluid2, pin2, rhs2, wx2, wy2, wz2, gain2, other2)
    sweep(coarse, low2 + 1, high2 - 1, sizes[4], fields2, gain2, other2, corr2)
    sweep(coarse, low2 + 2, high2 - 2, sizes[4], fields2, gain2, corr2, other2)
    corr2[...] = other2[...]
    coarse_residual(coarse, NEAR, NEAR + depth // 2, sizes[5], fields2, corr2, sums)
    count3 = depth // 4
    rhs3 = in_lanes(sums[0:count3], down2)
    fluid3 = in_lanes(pair_sum(fluid2[NEAR : NEAR + 2 * count3]), down2) * 0.125
    pin3 = in_lanes(pair_sum(pin2[NEAR : NEAR + 2 * count3]), down2) * 0.25
    lane = iota((count3, LANES), 1) // ROWS
    first = jnp.zeros((count3, LANES), F32)
    second = jnp.zeros((count3, LANES), F32)
    for row in range(ROWS):
        first = jnp.where(lane == row, rhs3[:, row, :], first)
        first = jnp.where(lane == ROWS + row, fluid3[:, row, :], first)
        second = jnp.where(lane == row, pin3[:, row, :], second)
    packed[0:count3] = first
    packed[count3 : 2 * count3] = second
    lane = iota((ROWS, LANES), 1)
    packed[2 * count3 :] = jnp.where(
        lane < LANES // 2, corr2[NEAR + depth // 2 - 5], corr2[NEAR + 4]
    )


def columns(rhs, fluid, pin):
    shape = fluid.shape
    depth = shape[2]
    lane, y = iota(shape, 2), iota(shape, 1)
    edge = jnp.zeros((1,) + shape[1:], F32)
    wz = jnp.where(lane == depth - 1, 0.0, mean_of(fluid, pltpu.roll(fluid, depth - 1, 2), 4.0))
    wy = jnp.where(y == ROWS - 1, 0.0, mean_of(fluid, pltpu.roll(fluid, ROWS - 1, 1), 4.0))
    wx = jnp.concatenate([mean_of(fluid[:-1], fluid[1:], 4.0), edge], axis=0)
    back_x = jnp.concatenate([edge, wx[:-1]], axis=0)
    across = (wx + back_x) + (wy + pltpu.roll(wy, 1, 1)) + pin
    share = 1.0 / jnp.sum(across, axis=2, keepdims=True)

    above, below, own = pltpu.roll(wz, 1, 2), wz, across
    steps = []
    stride = 1
    while stride < depth:
        inverse = 1.0 / (above + below + own)
        up = above * pltpu.roll(inverse, stride, 2)
        down = below * pltpu.roll(inverse, depth - stride, 2)
        own = own + up * pltpu.roll(own, stride, 2) + down * pltpu.roll(own, depth - stride, 2)
        above = up * pltpu.roll(above, stride, 2)
        below = down * pltpu.roll(below, depth - stride, 2)
        steps.append((stride, up, down))
        stride *= 2
    inverse = 1.0 / (above + below + own)

    def solve(right):
        mean = jnp.sum(right, axis=2, keepdims=True) * share
        for stride, up, down in steps:
            right = (
                right
                + up * pltpu.roll(right, stride, 2)
                + down * pltpu.roll(right, depth - stride, 2)
            )
        return right * inverse + mean

    corr = solve(rhs)
    flow_x = wx[:-1] * (corr[1:] - corr[:-1])
    flow_x = jnp.concatenate([flow_x, edge], 0) - jnp.concatenate([edge, flow_x], 0)
    flow_y = wy * (pltpu.roll(corr, ROWS - 1, 1) - corr)
    flow_z = wz * (pltpu.roll(corr, depth - 1, 2) - corr)
    rest = (
        (rhs - pin * corr)
        + flow_x
        + (flow_y - pltpu.roll(flow_y, 1, 1))
        + (flow_z - pltpu.roll(flow_z, 1, 2))
    )
    return corr + solve(rest)


def up_kernel(
    groups, by, depth, sizes,
    packed,
    rhs1, pin1, wx1, wy1, wz1, gain1, corr1,
    rhs2, pin2, wx2, wy2, wz2, gain2, corr2,
    out_ref,
    one1, two1, one2, two2, lifted,
):
    count3 = depth // 4
    shares = packed.shape[0]
    peers = SPLIT[0] * SPLIT[1]
    slabs = sorted(range(shares), key=lambda i: (i // peers, rank_of(i % peers)))
    first = jnp.concatenate([packed[i, 0:count3] for i in slabs], axis=0).T
    second = jnp.concatenate([packed[i, count3 : 2 * count3] for i in slabs], axis=0).T
    cells = ROWS * ROWS
    total3 = shares * count3
    shape3 = (ROWS, ROWS, total3)
    corr3 = columns(
        first[:cells].reshape(shape3), first[cells:].reshape(shape3), second[:cells].reshape(shape3)
    ).reshape(cells, total3)

    def slab_of(index):
        index = jnp.clip(index, 0, shares - 1)
        row = lax.rem(index, peers) // ny
        column = lax.rem(index, ny)
        column = jnp.where(lax.rem(row, 2) == 1, ny - 1 - column, column)
        return (index // peers) * peers + row * ny + column

    nx, ny = SPLIT
    ix, iy = lax.axis_index("gx"), lax.axis_index("gy")
    along = jnp.where(lax.rem(ix, 2) == 1, ny - 1 - iy, iy)
    part = (lax.axis_index("gz") * nx + ix) * ny + along
    mine = pltpu.roll(corr3, lax.rem(NEAR - part * count3 + total3, total3), 1)
    tall = jnp.concatenate([mine, mine], axis=0).T
    count = count3 + 2 * NEAR
    fine, coarse = Level(0), Level(1)
    cell = iota((LANES, ROWS * LANES), 0)
    lane = iota((LANES, ROWS * LANES), 1)
    same_y = cell % ROWS == (lane % coarse.ny) // 2
    spread = where01((cell // ROWS == lane // LANES) & same_y)
    wide = dot01(tall[0:count], spread)
    for row in range(ROWS):
        lifted[0:count, row, :] = wide[:, row * LANES : (row + 1) * LANES]

    fields1 = (rhs1, pin1, wx1, wy1, wz1)
    fields2 = (rhs2, pin2, wx2, wy2, wz2)
    low, high = NEAR - 4, NEAR + depth // 2 + 4
    parents = lifted[low // 2 + NEAR // 2 : high // 2 + NEAR // 2]
    twice = jnp.broadcast_to(parents[:, None], (parents.shape[0], 2, ROWS, LANES))
    reach = depth // 2 + NEAR
    half = iota((ROWS, LANES), 1) < LANES // 2
    before = packed[slab_of(part - 1), 2 * count3 :]
    after = packed[slab_of(part + 1), 2 * count3 :]
    before = jnp.where(half, before, pltpu.roll(before, LANES // 2, 1))
    after = jnp.where(half, pltpu.roll(after, LANES // 2, 1), after)
    one2[low - 1] = before + lifted[(low - 1) // 2 + NEAR // 2]
    one2[low:high] = corr2[low:high] + twice.reshape(high - low, ROWS, LANES)
    one2[high] = after + lifted[high // 2 + NEAR // 2]
    sweep(coarse, NEAR - 4, reach + 4, sizes[4], fields2, gain2, one2, two2)
    sweep(coarse, NEAR - 3, reach + 3, sizes[4], fields2, gain2, two2, one2)
    sweep(coarse, NEAR - 2, reach + 2, sizes[4], fields2, gain2, one2, two2)

    fine_lane, coarse_lane = iota((LANES, LANES), 1), iota((LANES, LANES), 0)
    x_of = (fine_lane // fine.ny) // 2
    y_of = (fine_lane % fine.ny) // 2
    up = where01(coarse_lane == x_of * coarse.ny + y_of)
    lifted[0 : depth // 2 + 4] = in_lanes(two2[NEAR - 2 : reach + 2], up)
    parents = lifted[0 : depth // 2 + 4]
    twice = jnp.broadcast_to(parents[:, None], (parents.shape[0], 2, ROWS, LANES))
    low, high = HALO - 4, HALO + depth + 4
    one1[low:high] = corr1[low:high] + twice.reshape(high - low, ROWS, LANES)
    reach = depth + HALO
    sweep(fine, HALO - 2, reach + 2, sizes[1], fields1, gain1, one1, two1)
    sweep(fine, HALO - 1, reach + 1, sizes[1], fields1, gain1, two1, one1)
    sweep(fine, HALO, reach, sizes[1], fields1, gain1, one1, two1)

    group = (iota((depth, LANES), 1) // by) % groups
    for ix in range(nx):
        scaled = [
            two1[HALO:reach, ix * groups + part, :]
            * (OMEGA / gain1[HALO:reach, ix * groups + part, :])
            for part in range(groups)
        ]
        for iy in range(ny):
            total = scaled[iy]
            for part in range(groups):
                if part != iy:
                    moved = pltpu.roll(scaled[part], (by * (part - iy)) % LANES, 1)
                    total = jnp.where(group == part, moved, total)
            out_ref[ix * ny + iy] = total


def finish_kernel(blocks, out_ref):
    bx, by, depth = out_ref.shape
    cells = bx * by
    cell = iota((cells, cells), 0)
    lane = iota((cells, cells), 1)
    x, y = cell // by, cell % by
    chosen = where01((x % 4) * (bx // 4 * by) + (x // 4) * by + y == lane)
    peers = blocks.shape[0]
    ordered = jnp.concatenate([blocks[i] for i in sorted(range(peers), key=rank_of)], axis=0)
    turned = dot01(ordered, chosen, (((1,), (1,)), ((), ())))
    out_ref[...] = turned.T.reshape(out_ref.shape)


def whole_planes(residual_q2, viscosity, pinned):
    bx, by, depth = viscosity.shape
    groups = bx // 4
    peers = SPLIT[0] * SPLIT[1]
    share = depth // peers
    planes = share + 2 * HALO
    count2 = share // 2 + 2 * NEAR
    sizes = (23, 22, 20, 10, 24, 24)
    limit = pltpu.CompilerParams(vmem_limit_bytes=32 * 2**20)

    def flat(rows):
        return jax.ShapeDtypeStruct((rows, LANES), F32)

    def blocks(count, rows):
        return jax.ShapeDtypeStruct((count, rows, LANES), F32)

    def room(count):
        return pltpu.VMEM((count, ROWS, LANES), F32)

    fluid = 1.0 / viscosity
    pin = 4.0 * pinned.astype(F32) * fluid
    parcels = pl.pallas_call(
        functools.partial(prepare_kernel, share),
        out_shape=blocks(peers, 3 * share),
        compiler_params=limit,
        name="prepare",
    )(residual_q2.reshape(4 * bx * by, 2 * depth), fluid, pin)
    own = pl.pallas_call(
        functools.partial(spread_kernel, groups, by),
        out_shape=blocks(3 * share, ROWS),
        compiler_params=limit,
        name="spread",
    )(lax.all_to_all(parcels, ("gx", "gy"), 0, 0, tiled=True))
    length = lax.axis_size("gz")
    slabs = sorted(range(peers), key=rank_of)
    parts = length * peers

    def step(field, ahead):
        device = [slabs[i % peers] * length + i // peers for i in range(parts)]
        pairs = [(device[i], device[i + ahead]) for i in range(parts) if 0 <= i + ahead < parts]
        return lax.ppermute(field, ("gx", "gy", "gz"), pairs)

    low, high = step(own, 1), step(own, -1)
    saved = (blocks(planes, ROWS),) * 7 + (blocks(count2, ROWS),) * 7
    results = pl.pallas_call(
        functools.partial(down_kernel, groups, by, share, sizes),
        out_shape=saved + (flat(share // 2 + ROWS),),
        scratch_shapes=[room(planes), room(planes), room(count2), room(count2), room(count2)],
        compiler_params=limit,
        name="down",
    )(low, own, high)
    packed = lax.all_gather(results[-1], ("gz", "gx", "gy"))
    mine = pl.pallas_call(
        functools.partial(up_kernel, groups, by, share, sizes),
        out_shape=blocks(peers, share),
        scratch_shapes=[room(planes), room(planes), room(count2), room(count2), room(count2)],
        compiler_params=limit,
        name="up",
    )(packed, *results[:-1])
    return pl.pallas_call(
        finish_kernel,
        out_shape=jax.ShapeDtypeStruct((bx, by, depth), F32),
        compiler_params=limit,
        name="finish",
    )(lax.all_to_all(mine, ("gx", "gy"), 0, 0, tiled=True))


def one_tile_planes(mesh, viscosity):
    split = (mesh.shape["gx"], mesh.shape["gy"])
    depth = viscosity.shape[2]
    fits = viscosity.shape[:2] == PLANE and split == SPLIT
    return fits and depth == 4 * LANES and depth // mesh.shape["gz"] == LANES


def solution(mesh):
    placed = (P("gx", "gy", "gz"), P("gx", "gy", "gz"), P("gx", "gy", "gz"))

    def cycle(residual_q2, viscosity, pinned):
        chosen = whole_planes if one_tile_planes(mesh, viscosity) else per_device
        return jax.shard_map(
            chosen, mesh=mesh, in_specs=placed, out_specs=P("gx", "gy", "gz"), check_vma=False
        )(residual_q2, viscosity, pinned)

    return cycle
```

```python
import functools

import jax
import jax.numpy as jnp
from jax import lax
from jax.experimental import pallas as pl
from jax.experimental.pallas import tpu as pltpu
from jax.sharding import PartitionSpec as P

NU = 3


OMEGA = 0.6


def with_halo(block, sides, width):
    for axis, dim in sides:
        count = lax.axis_size(axis)
        forward = [(i, i + 1) for i in range(count - 1)]
        backward = [(target, source) for source, target in forward]
        low = lax.ppermute(
            lax.slice_in_dim(block, block.shape[dim] - width, None, axis=dim), axis, forward
        )
        high = lax.ppermute(lax.slice_in_dim(block, 0, width, axis=dim), axis, backward)
        block = jnp.concatenate([low, block, high], axis=dim)
    return block


def coarsen(x):
    a, b, c = x.shape
    return x.reshape(a // 2, 2, b // 2, 2, c // 2, 2).sum(axis=(1, 3, 5))


def refine(x):
    return jnp.repeat(jnp.repeat(jnp.repeat(x, 2, 0), 2, 1), 2, 2)


def extended(field):
    return with_halo(field, (("gx", 0), ("gy", 1), ("gz", 2)), 1)


def shifted(padded):
    return [
        padded[2:, 1:-1, 1:-1],
        padded[:-2, 1:-1, 1:-1],
        padded[1:-1, 2:, 1:-1],
        padded[1:-1, :-2, 1:-1],
        padded[1:-1, 1:-1, 2:],
        padded[1:-1, 1:-1, :-2],
    ]


def neighbours(field):
    return shifted(extended(field))


def harmonic(fluid, near, factor):
    total = fluid + near
    return jnp.where(total > 0, factor * 2.0 * fluid * near / jnp.where(total > 0, total, 1.0), 0.0)


def couplings(fluid, factor):
    return [harmonic(fluid, near, factor) for near in neighbours(fluid)]


def apply_op(field, weights, diag):
    total = diag * field
    for weight, near in zip(weights, neighbours(field)):
        total = total - weight * near
    return total


def presmooth(rhs, weights, diag):
    corr = OMEGA * rhs / diag
    for sweep in range(NU - 1):
        corr = corr + OMEGA * (rhs - apply_op(corr, weights, diag)) / diag
    return corr


def postsmooth(corr, rhs, weights, diag):
    for sweep in range(NU):
        corr = corr + OMEGA * (rhs - apply_op(corr, weights, diag)) / diag
    return corr


def tridiag(coeffs, rhs):
    solved = lax.linalg.tridiagonal_solve(coeffs[0], coeffs[1], coeffs[2], rhs[..., None])[..., 0]
    last = rhs.ndim - 1
    shift_col = jnp.sum(rhs, axis=last, keepdims=True) / jnp.sum(
        coeffs[3], axis=last, keepdims=True
    )
    return solved + shift_col


def prepare_columns(weights, diag):
    lower = -weights[5]
    upper = -weights[4]
    across = diag + lower + upper
    return (
        lax.all_gather(lower, "gz", axis=2, tiled=True),
        lax.all_gather(diag, "gz", axis=2, tiled=True),
        lax.all_gather(upper, "gz", axis=2, tiled=True),
        lax.all_gather(across, "gz", axis=2, tiled=True),
    )


def column_solve(rhs, coeffs):
    depth = rhs.shape[2]
    whole = lax.all_gather(rhs, "gz", axis=2, tiled=True)
    solved = tridiag(coeffs, whole)
    return lax.dynamic_slice_in_dim(solved, lax.axis_index("gz") * depth, depth, 2)


def per_device(residual_q2, viscosity, pinned):
    fluid1 = 1.0 / viscosity
    pin1 = 4.0 * pinned.astype(jnp.float32) * fluid1
    rhs1 = coarsen(residual_q2.astype(jnp.float32))
    fluid2 = coarsen(fluid1) / 8.0
    pin2 = coarsen(pin1) / 4.0
    fluid3 = coarsen(fluid2) / 8.0
    pin3 = coarsen(pin2) / 4.0
    weights1 = couplings(fluid1, 1.0)
    weights2 = couplings(fluid2, 2.0)
    weights3 = couplings(fluid3, 4.0)
    diag1 = sum(weights1) + pin1
    diag2 = sum(weights2) + pin2
    diag3 = sum(weights3) + pin3
    coeffs = prepare_columns(weights3, diag3)
    corr1 = presmooth(rhs1, weights1, diag1)
    rhs2 = coarsen(rhs1 - apply_op(corr1, weights1, diag1))
    corr2 = presmooth(rhs2, weights2, diag2)
    rhs3 = coarsen(rhs2 - apply_op(corr2, weights2, diag2))
    corr3 = column_solve(rhs3, coeffs)
    corr3 = corr3 + column_solve(rhs3 - apply_op(corr3, weights3, diag3), coeffs)
    corr2 = postsmooth(corr2 + refine(corr3), rhs2, weights2, diag2)
    corr1 = postsmooth(corr1 + refine(corr2), rhs1, weights1, diag1)
    return diag1 * corr1


PLANE = (32, 32)
SPLIT = (2, 4)
ROWS = 8
LANES = 128
HALO = 16
NEAR = 8
F32 = jnp.float32


def iota(shape, dim):
    return lax.broadcasted_iota(jnp.int32, shape, dim)


def dot01(field, chosen, dims=(((1,), (0,)), ((), ()))):
    total = None
    rest = field
    for part in range(3):
        piece = rest.astype(jnp.bfloat16)
        term = lax.dot_general(piece, chosen, dims, preferred_element_type=F32)
        total = term if total is None else total + term
        if part < 2:
            rest = rest - piece.astype(F32)
    return total


def where01(condition):
    return jnp.where(condition, 1.0, 0.0).astype(jnp.bfloat16)


def loop(low, high, size, body):
    size = min(size, high - low)
    steps = -(-(high - low) // size)

    def step(index, carry):
        body(jnp.minimum(low + index * size, high - size), size)
        return carry

    if steps == 1:
        body(low, size)
    else:
        lax.fori_loop(0, steps, step, 0)


class Level:
    def __init__(self, level):
        self.ny = PLANE[1] >> level
        self.xs = 4 >> level
        self.factor = float(2**level)

    def masks(self, shape):
        lane = iota(shape, 2)
        row = iota(shape, 1)
        within = (lane // self.ny) % self.xs
        y = lane % self.ny
        last_x = (row == ROWS - 1) & (within == self.xs - 1)
        return within, y == self.ny - 1, last_x

    def next_x(self, field):
        within = (iota(field.shape, 2) // self.ny) % self.xs
        moved = pltpu.roll(field, LANES - self.ny, 2)
        return jnp.where(within == self.xs - 1, pltpu.roll(moved, ROWS - 1, 1), moved)

    def last_x(self, field):
        within = (iota(field.shape, 2) // self.ny) % self.xs
        moved = pltpu.roll(field, self.ny, 2)
        return jnp.where(within == 0, pltpu.roll(moved, 1, 1), moved)

    def next_y(self, field):
        return pltpu.roll(field, LANES - 1, 2)

    def last_y(self, field):
        return pltpu.roll(field, 1, 2)

    def balance(self, field, wx, wy, wz):
        mid = field[1:-1]
        flow_x = wx * (self.next_x(mid) - mid)
        flow_y = wy * (self.next_y(mid) - mid)
        flow_z = wz * (field[1:] - field[:-1])
        return (
            (flow_x - self.last_x(flow_x))
            + (flow_y - self.last_y(flow_y))
            + (flow_z[1:] - flow_z[:-1])
        )


def mean_of(fluid, near, factor):
    total = fluid + near
    safe = jnp.where(total > 0, total, 1.0)
    return jnp.where(total > 0, (factor * 2.0) * fluid * near / safe, 0.0)


def set_level(level, low, high, size, fluid, pin, rhs, wx, wy, wz, gain, corr):
    def body(plane, count):
        wide = fluid[pl.ds(plane - 1, count + 2)]
        mid = wide[1:-1]
        within, end_y, end_x = level.masks(mid.shape)
        to_x = jnp.where(end_x, 0.0, mean_of(mid, level.next_x(mid), level.factor))
        to_y = jnp.where(end_y, 0.0, mean_of(mid, level.next_y(mid), level.factor))
        to_z = mean_of(wide[:-1], wide[1:], level.factor)
        diag = (
            (to_x + level.last_x(to_x))
            + (to_y + level.last_y(to_y))
            + (to_z[1:] + to_z[:-1])
            + pin[pl.ds(plane, count)]
        )
        some = diag > 0
        scale = jnp.where(some, OMEGA / jnp.where(some, diag, 1.0), 0.0)
        wx[pl.ds(plane, count)] = to_x
        wy[pl.ds(plane, count)] = to_y
        wz[pl.ds(plane, count)] = to_z[1:]
        gain[pl.ds(plane, count)] = scale
        if corr is not None:
            corr[pl.ds(plane, count)] = scale * rhs[pl.ds(plane, count)]

    loop(low, high, size, body)


def residual_of(level, plane, count, fields, corr):
    rhs, pin, wx, wy, wz = fields
    field = corr[pl.ds(plane - 1, count + 2)]
    spread = level.balance(
        field, wx[pl.ds(plane, count)], wy[pl.ds(plane, count)], wz[pl.ds(plane - 1, count + 1)]
    )
    mid = field[1:-1]
    return mid, (rhs[pl.ds(plane, count)] - pin[pl.ds(plane, count)] * mid) + spread


def sweep(level, low, high, size, fields, gain, source, target):
    def body(plane, count):
        mid, rest = residual_of(level, plane, count, fields, source)
        target[pl.ds(plane, count)] = mid + gain[pl.ds(plane, count)] * rest

    loop(low, high, size, body)


def pair_sum(field):
    half = field.reshape((field.shape[0] // 2, 2) + field.shape[1:])
    return half[:, 0] + half[:, 1]


def coarse_residual(level, low, high, size, fields, corr, target):
    size = min(size, high - low)
    assert (high - low) % size == 0 and size % 2 == 0

    def body(plane, count):
        _, rest = residual_of(level, plane, count, fields, corr)
        target[pl.ds((plane - low) // 2, count // 2)] = pair_sum(rest)

    loop(low, high, size, body)


def lanes_down(level):
    fine = iota((LANES, LANES), 0)
    coarse = iota((LANES, LANES), 1)
    ny, xs = PLANE[1] >> level, 4 >> level
    half = xs // 2
    same_x = ((fine // ny) % xs) // 2 == (coarse // (ny // 2)) % half
    same_y = (fine % ny) // 2 == coarse % (ny // 2)
    return where01((fine < ny * xs) & same_x & same_y)


def in_lanes(field, chosen):
    flat = field.reshape(field.shape[0] * ROWS, LANES)
    return dot01(flat, chosen).reshape(field.shape)


def rank_of(peer):
    ny = SPLIT[1]
    ix, iy = peer // ny, peer % ny
    return ix * ny + (ny - 1 - iy if ix % 2 else iy)


def prepare_kernel(share, res_ref, fluid_ref, pin_ref, out_ref):
    bx, by, depth = fluid_ref.shape
    cells = bx * by
    groups = bx // 4
    pick = where01(iota((depth, 2 * depth), 1) // 2 == iota((depth, 2 * depth), 0))
    deep = lax.dot_general(
        pick, res_ref[...], (((1,), (1,)), ((), ())), preferred_element_type=F32
    )

    def lane_of(x, y):
        return (x % 4) * (groups * by) + (x // 4) * by + y

    fine = iota((4 * cells, cells), 0)
    lane = iota((4 * cells, cells), 1)
    chosen = where01(lane_of(fine // (4 * by), (fine % (2 * by)) // 2) == lane)
    rhs = dot01(deep, chosen)
    cell = iota((cells, cells), 0)
    lane = iota((cells, cells), 1)
    chosen = where01(lane_of(cell // by, cell % by) == lane)
    fluid = dot01(fluid_ref[...].reshape(cells, depth).T, chosen)
    pin = dot01(pin_ref[...].reshape(cells, depth).T, chosen)
    for index, field in enumerate((fluid, rhs, pin)):
        for peer in range(depth // share):
            begin = rank_of(peer) * share
            out_ref[peer, index * share : (index + 1) * share] = field[begin : begin + share]


def spread_kernel(groups, by, gathered, own):
    for start in range(0, own.shape[0], ROWS):
        place(gathered, start, own, start, groups, by)


def place(gathered, row, target, plane, groups, by):
    group = (iota((ROWS, LANES), 1) // by) % groups
    nx, ny = SPLIT
    for ix in range(nx):
        found = [gathered[ix * ny + iy, pl.ds(row, ROWS), :] for iy in range(ny)]
        for part in range(groups):
            total = found[part]
            for iy in range(ny):
                if iy != part:
                    moved = pltpu.roll(found[iy], (by * (iy - part)) % LANES, 1)
                    total = jnp.where(group == iy, moved, total)
            target[pl.ds(plane, ROWS), ix * groups + part, :] = total


def down_kernel(
    groups, by, depth, sizes,
    low, own, high,
    rhs1, pin1, wx1, wy1, wz1, gain1, corr1,
    rhs2, pin2, wx2, wy2, wz2, gain2, corr2,
    packed,
    fluid1, other1, fluid2, other2, sums,
):
    planes = depth + 2 * HALO
    for index, target in enumerate((fluid1, rhs1, pin1)):
        start = 0
        for piece in (low, own, high):
            count = piece.shape[0] // 3
            target[start : start + count] = piece[index * count : (index + 1) * count]
            start += count

    fine, coarse = Level(0), Level(1)
    down1, down2 = lanes_down(0), lanes_down(1)
    fields1 = (rhs1, pin1, wx1, wy1, wz1)
    fields2 = (rhs2, pin2, wx2, wy2, wz2)
    set_level(fine, 1, planes - 1, sizes[0], fluid1, pin1, rhs1, wx1, wy1, wz1, gain1, other1)
    sweep(fine, 2, planes - 2, sizes[1], fields1, gain1, other1, corr1)
    sweep(fine, 3, planes - 3, sizes[1], fields1, gain1, corr1, other1)
    corr1[...] = other1[...]
    count2 = depth // 2 + 2 * NEAR
    begin = HALO - 2 * NEAR
    for source, target, share in ((fluid1, fluid2, 8.0), (pin1, pin2, 4.0)):
        whole = pair_sum(source[begin : begin + 2 * count2])
        target[...] = in_lanes(whole, down1) * (1.0 / share)
    low2, high2 = (begin + 4) // 2, count2 - (begin + 4) // 2
    inner = high2 - low2
    coarse_residual(
        fine, begin + 2 * low2, begin + 2 * high2, sizes[2], fields1, corr1, sums
    )
    rhs2[low2:high2] = in_lanes(sums[0:inner], down1)
    set_level(coarse, low2, high2, sizes[3], fluid2, pin2, rhs2, wx2, wy2, wz2, gain2, other2)
    sweep(coarse, low2 + 1, high2 - 1, sizes[4], fields2, gain2, other2, corr2)
    sweep(coarse, low2 + 2, high2 - 2, sizes[4], fields2, gain2, corr2, other2)
    corr2[...] = other2[...]
    coarse_residual(coarse, NEAR, NEAR + depth // 2, sizes[5], fields2, corr2, sums)
    count3 = depth // 4
    rhs3 = in_lanes(sums[0:count3], down2)
    fluid3 = in_lanes(pair_sum(fluid2[NEAR : NEAR + 2 * count3]), down2) * 0.125
    pin3 = in_lanes(pair_sum(pin2[NEAR : NEAR + 2 * count3]), down2) * 0.25
    lane = iota((count3, LANES), 1) // ROWS
    first = jnp.zeros((count3, LANES), F32)
    second = jnp.zeros((count3, LANES), F32)
    for row in range(ROWS):
        first = jnp.where(lane == row, rhs3[:, row, :], first)
        first = jnp.where(lane == ROWS + row, fluid3[:, row, :], first)
        second = jnp.where(lane == row, pin3[:, row, :], second)
    packed[0:count3] = first
    packed[count3 : 2 * count3] = second
    lane = iota((ROWS, LANES), 1)
    packed[2 * count3 :] = jnp.where(
        lane < LANES // 2, corr2[NEAR + depth // 2 - 5], corr2[NEAR + 4]
    )


def columns(rhs, fluid, pin):
    shape = fluid.shape
    depth = shape[2]
    lane, y = iota(shape, 2), iota(shape, 1)
    edge = jnp.zeros((1,) + shape[1:], F32)
    wz = jnp.where(lane == depth - 1, 0.0, mean_of(fluid, pltpu.roll(fluid, depth - 1, 2), 4.0))
    wy = jnp.where(y == ROWS - 1, 0.0, mean_of(fluid, pltpu.roll(fluid, ROWS - 1, 1), 4.0))
    wx = jnp.concatenate([mean_of(fluid[:-1], fluid[1:], 4.0), edge], axis=0)
    back_x = jnp.concatenate([edge, wx[:-1]], axis=0)
    across = (wx + back_x) + (wy + pltpu.roll(wy, 1, 1)) + pin
    share = 1.0 / jnp.sum(across, axis=2, keepdims=True)

    above, below, own = pltpu.roll(wz, 1, 2), wz, across
    steps = []
    stride = 1
    while stride < depth:
        inverse = 1.0 / (above + below + own)
        up = above * pltpu.roll(inverse, stride, 2)
        down = below * pltpu.roll(inverse, depth - stride, 2)
        own = own + up * pltpu.roll(own, stride, 2) + down * pltpu.roll(own, depth - stride, 2)
        above = up * pltpu.roll(above, stride, 2)
        below = down * pltpu.roll(below, depth - stride, 2)
        steps.append((stride, up, down))
        stride *= 2
    inverse = 1.0 / (above + below + own)

    def solve(right):
        mean = jnp.sum(right, axis=2, keepdims=True) * share
        for stride, up, down in steps:
            right = (
                right
                + up * pltpu.roll(right, stride, 2)
                + down * pltpu.roll(right, depth - stride, 2)
            )
        return right * inverse + mean

    corr = solve(rhs)
    flow_x = wx[:-1] * (corr[1:] - corr[:-1])
    flow_x = jnp.concatenate([flow_x, edge], 0) - jnp.concatenate([edge, flow_x], 0)
    flow_y = wy * (pltpu.roll(corr, ROWS - 1, 1) - corr)
    flow_z = wz * (pltpu.roll(corr, depth - 1, 2) - corr)
    rest = (
        (rhs - pin * corr)
        + flow_x
        + (flow_y - pltpu.roll(flow_y, 1, 1))
        + (flow_z - pltpu.roll(flow_z, 1, 2))
    )
    return corr + solve(rest)


def up_kernel(
    groups, by, depth, sizes,
    packed,
    rhs1, pin1, wx1, wy1, wz1, gain1, corr1,
    rhs2, pin2, wx2, wy2, wz2, gain2, corr2,
    out_ref,
    one1, two1, one2, two2, lifted,
):
    count3 = depth // 4
    shares = packed.shape[0]
    peers = SPLIT[0] * SPLIT[1]
    slabs = sorted(range(shares), key=lambda i: (i // peers, rank_of(i % peers)))
    first = jnp.concatenate([packed[i, 0:count3] for i in slabs], axis=0).T
    second = jnp.concatenate([packed[i, count3 : 2 * count3] for i in slabs], axis=0).T
    cells = ROWS * ROWS
    total3 = shares * count3
    shape3 = (ROWS, ROWS, total3)
    corr3 = columns(
        first[:cells].reshape(shape3), first[cells:].reshape(shape3), second[:cells].reshape(shape3)
    ).reshape(cells, total3)

    def slab_of(index):
        index = jnp.clip(index, 0, shares - 1)
        row = lax.rem(index, peers) // ny
        column = lax.rem(index, ny)
        column = jnp.where(lax.rem(row, 2) == 1, ny - 1 - column, column)
        return (index // peers) * peers + row * ny + column

    nx, ny = SPLIT
    ix, iy = lax.axis_index("gx"), lax.axis_index("gy")
    along = jnp.where(lax.rem(ix, 2) == 1, ny - 1 - iy, iy)
    part = (lax.axis_index("gz") * nx + ix) * ny + along
    mine = pltpu.roll(corr3, lax.rem(NEAR - part * count3 + total3, total3), 1)
    tall = jnp.concatenate([mine, mine], axis=0).T
    count = count3 + 2 * NEAR
    fine, coarse = Level(0), Level(1)
    cell = iota((LANES, ROWS * LANES), 0)
    lane = iota((LANES, ROWS * LANES), 1)
    same_y = cell % ROWS == (lane % coarse.ny) // 2
    spread = where01((cell // ROWS == lane // LANES) & same_y)
    wide = dot01(tall[0:count], spread)
    for row in range(ROWS):
        lifted[0:count, row, :] = wide[:, row * LANES : (row + 1) * LANES]

    fields1 = (rhs1, pin1, wx1, wy1, wz1)
    fields2 = (rhs2, pin2, wx2, wy2, wz2)
    low, high = NEAR - 4, NEAR + depth // 2 + 4
    parents = lifted[low // 2 + NEAR // 2 : high // 2 + NEAR // 2]
    twice = jnp.broadcast_to(parents[:, None], (parents.shape[0], 2, ROWS, LANES))
    reach = depth // 2 + NEAR
    half = iota((ROWS, LANES), 1) < LANES // 2
    before = packed[slab_of(part - 1), 2 * count3 :]
    after = packed[slab_of(part + 1), 2 * count3 :]
    before = jnp.where(half, before, pltpu.roll(before, LANES // 2, 1))
    after = jnp.where(half, pltpu.roll(after, LANES // 2, 1), after)
    one2[low - 1] = before + lifted[(low - 1) // 2 + NEAR // 2]
    one2[low:high] = corr2[low:high] + twice.reshape(high - low, ROWS, LANES)
    one2[high] = after + lifted[high // 2 + NEAR // 2]
    sweep(coarse, NEAR - 4, reach + 4, sizes[4], fields2, gain2, one2, two2)
    sweep(coarse, NEAR - 3, reach + 3, sizes[4], fields2, gain2, two2, one2)
    sweep(coarse, NEAR - 2, reach + 2, sizes[4], fields2, gain2, one2, two2)

    fine_lane, coarse_lane = iota((LANES, LANES), 1), iota((LANES, LANES), 0)
    x_of = (fine_lane // fine.ny) // 2
    y_of = (fine_lane % fine.ny) // 2
    up = where01(coarse_lane == x_of * coarse.ny + y_of)
    lifted[0 : depth // 2 + 4] = in_lanes(two2[NEAR - 2 : reach + 2], up)
    parents = lifted[0 : depth // 2 + 4]
    twice = jnp.broadcast_to(parents[:, None], (parents.shape[0], 2, ROWS, LANES))
    low, high = HALO - 4, HALO + depth + 4
    one1[low:high] = corr1[low:high] + twice.reshape(high - low, ROWS, LANES)
    reach = depth + HALO
    sweep(fine, HALO - 2, reach + 2, sizes[1], fields1, gain1, one1, two1)
    sweep(fine, HALO - 1, reach + 1, sizes[1], fields1, gain1, two1, one1)
    sweep(fine, HALO, reach, sizes[1], fields1, gain1, one1, two1)

    group = (iota((depth, LANES), 1) // by) % groups
    for ix in range(nx):
        scaled = [
            two1[HALO:reach, ix * groups + part, :]
            * (OMEGA / gain1[HALO:reach, ix * groups + part, :])
            for part in range(groups)
        ]
        for iy in range(ny):
            total = scaled[iy]
            for part in range(groups):
                if part != iy:
                    moved = pltpu.roll(scaled[part], (by * (part - iy)) % LANES, 1)
                    total = jnp.where(group == part, moved, total)
            out_ref[ix * ny + iy] = total


def finish_kernel(blocks, out_ref):
    bx, by, depth = out_ref.shape
    cells = bx * by
    cell = iota((cells, cells), 0)
    lane = iota((cells, cells), 1)
    x, y = cell // by, cell % by
    chosen = where01((x % 4) * (bx // 4 * by) + (x // 4) * by + y == lane)
    peers = blocks.shape[0]
    ordered = jnp.concatenate([blocks[i] for i in sorted(range(peers), key=rank_of)], axis=0)
    turned = dot01(ordered, chosen, (((1,), (1,)), ((), ())))
    out_ref[...] = turned.T.reshape(out_ref.shape)


def whole_planes(residual_q2, viscosity, pinned):
    bx, by, depth = viscosity.shape
    groups = bx // 4
    peers = SPLIT[0] * SPLIT[1]
    share = depth // peers
    planes = share + 2 * HALO
    count2 = share // 2 + 2 * NEAR
    sizes = (23, 22, 20, 10, 24, 24)
    limit = pltpu.CompilerParams(vmem_limit_bytes=32 * 2**20)

    def flat(rows):
        return jax.ShapeDtypeStruct((rows, LANES), F32)

    def blocks(count, rows):
        return jax.ShapeDtypeStruct((count, rows, LANES), F32)

    def room(count):
        return pltpu.VMEM((count, ROWS, LANES), F32)

    fluid = 1.0 / viscosity
    pin = 4.0 * pinned.astype(F32) * fluid
    parcels = pl.pallas_call(
        functools.partial(prepare_kernel, share),
        out_shape=blocks(peers, 3 * share),
        compiler_params=limit,
        name="prepare",
    )(residual_q2.reshape(4 * bx * by, 2 * depth), fluid, pin)
    own = pl.pallas_call(
        functools.partial(spread_kernel, groups, by),
        out_shape=blocks(3 * share, ROWS),
        compiler_params=limit,
        name="spread",
    )(lax.all_to_all(parcels, ("gx", "gy"), 0, 0, tiled=True))
    length = lax.axis_size("gz")
    slabs = sorted(range(peers), key=rank_of)
    parts = length * peers

    def step(field, ahead):
        device = [slabs[i % peers] * length + i // peers for i in range(parts)]
        pairs = [(device[i], device[i + ahead]) for i in range(parts) if 0 <= i + ahead < parts]
        return lax.ppermute(field, ("gx", "gy", "gz"), pairs)

    low, high = step(own, 1), step(own, -1)
    saved = (blocks(planes, ROWS),) * 7 + (blocks(count2, ROWS),) * 7
    results = pl.pallas_call(
        functools.partial(down_kernel, groups, by, share, sizes),
        out_shape=saved + (flat(share // 2 + ROWS),),
        scratch_shapes=[room(planes), room(planes), room(count2), room(count2), room(count2)],
        compiler_params=limit,
        name="down",
    )(low, own, high)
    copies = jnp.broadcast_to(results[-1], (parts,) + results[-1].shape)
    packed = lax.all_to_all(copies, ("gz", "gx", "gy"), 0, 0, tiled=True)
    mine = pl.pallas_call(
        functools.partial(up_kernel, groups, by, share, sizes),
        out_shape=blocks(peers, share),
        scratch_shapes=[room(planes), room(planes), room(count2), room(count2), room(count2)],
        compiler_params=limit,
        name="up",
    )(packed, *results[:-1])
    return pl.pallas_call(
        finish_kernel,
        out_shape=jax.ShapeDtypeStruct((bx, by, depth), F32),
        compiler_params=limit,
        name="finish",
    )(lax.all_to_all(mine, ("gx", "gy"), 0, 0, tiled=True))


def one_tile_planes(mesh, viscosity):
    split = (mesh.shape["gx"], mesh.shape["gy"])
    depth = viscosity.shape[2]
    fits = viscosity.shape[:2] == PLANE and split == SPLIT
    return fits and depth == 4 * LANES and depth // mesh.shape["gz"] == LANES


def solution(mesh):
    placed = (P("gx", "gy", "gz"), P("gx", "gy", "gz"), P("gx", "gy", "gz"))

    def cycle(residual_q2, viscosity, pinned):
        chosen = whole_planes if one_tile_planes(mesh, viscosity) else per_device
        return jax.shard_map(
            chosen, mesh=mesh, in_specs=placed, out_specs=P("gx", "gy", "gz"), check_vma=False
        )(residual_q2, viscosity, pinned)

    return cycle
```

```python
import functools

import jax
import jax.numpy as jnp
from jax import lax
from jax.experimental import pallas as pl
from jax.experimental.pallas import tpu as pltpu
from jax.sharding import PartitionSpec as P

NU = 3


OMEGA = 0.6


def with_halo(block, sides, width):
    for axis, dim in sides:
        count = lax.axis_size(axis)
        forward = [(i, i + 1) for i in range(count - 1)]
        backward = [(target, source) for source, target in forward]
        low = lax.ppermute(
            lax.slice_in_dim(block, block.shape[dim] - width, None, axis=dim), axis, forward
        )
        high = lax.ppermute(lax.slice_in_dim(block, 0, width, axis=dim), axis, backward)
        block = jnp.concatenate([low, block, high], axis=dim)
    return block


def coarsen(x):
    a, b, c = x.shape
    return x.reshape(a // 2, 2, b // 2, 2, c // 2, 2).sum(axis=(1, 3, 5))


def refine(x):
    return jnp.repeat(jnp.repeat(jnp.repeat(x, 2, 0), 2, 1), 2, 2)


def extended(field):
    return with_halo(field, (("gx", 0), ("gy", 1), ("gz", 2)), 1)


def shifted(padded):
    return [
        padded[2:, 1:-1, 1:-1],
        padded[:-2, 1:-1, 1:-1],
        padded[1:-1, 2:, 1:-1],
        padded[1:-1, :-2, 1:-1],
        padded[1:-1, 1:-1, 2:],
        padded[1:-1, 1:-1, :-2],
    ]


def neighbours(field):
    return shifted(extended(field))


def harmonic(fluid, near, factor):
    total = fluid + near
    return jnp.where(total > 0, factor * 2.0 * fluid * near / jnp.where(total > 0, total, 1.0), 0.0)


def couplings(fluid, factor):
    return [harmonic(fluid, near, factor) for near in neighbours(fluid)]


def apply_op(field, weights, diag):
    total = diag * field
    for weight, near in zip(weights, neighbours(field)):
        total = total - weight * near
    return total


def presmooth(rhs, weights, diag):
    corr = OMEGA * rhs / diag
    for sweep in range(NU - 1):
        corr = corr + OMEGA * (rhs - apply_op(corr, weights, diag)) / diag
    return corr


def postsmooth(corr, rhs, weights, diag):
    for sweep in range(NU):
        corr = corr + OMEGA * (rhs - apply_op(corr, weights, diag)) / diag
    return corr


def tridiag(coeffs, rhs):
    solved = lax.linalg.tridiagonal_solve(coeffs[0], coeffs[1], coeffs[2], rhs[..., None])[..., 0]
    last = rhs.ndim - 1
    shift_col = jnp.sum(rhs, axis=last, keepdims=True) / jnp.sum(
        coeffs[3], axis=last, keepdims=True
    )
    return solved + shift_col


def prepare_columns(weights, diag):
    lower = -weights[5]
    upper = -weights[4]
    across = diag + lower + upper
    return (
        lax.all_gather(lower, "gz", axis=2, tiled=True),
        lax.all_gather(diag, "gz", axis=2, tiled=True),
        lax.all_gather(upper, "gz", axis=2, tiled=True),
        lax.all_gather(across, "gz", axis=2, tiled=True),
    )


def column_solve(rhs, coeffs):
    depth = rhs.shape[2]
    whole = lax.all_gather(rhs, "gz", axis=2, tiled=True)
    solved = tridiag(coeffs, whole)
    return lax.dynamic_slice_in_dim(solved, lax.axis_index("gz") * depth, depth, 2)


def per_device(residual_q2, viscosity, pinned):
    fluid1 = 1.0 / viscosity
    pin1 = 4.0 * pinned.astype(jnp.float32) * fluid1
    rhs1 = coarsen(residual_q2.astype(jnp.float32))
    fluid2 = coarsen(fluid1) / 8.0
    pin2 = coarsen(pin1) / 4.0
    fluid3 = coarsen(fluid2) / 8.0
    pin3 = coarsen(pin2) / 4.0
    weights1 = couplings(fluid1, 1.0)
    weights2 = couplings(fluid2, 2.0)
    weights3 = couplings(fluid3, 4.0)
    diag1 = sum(weights1) + pin1
    diag2 = sum(weights2) + pin2
    diag3 = sum(weights3) + pin3
    coeffs = prepare_columns(weights3, diag3)
    corr1 = presmooth(rhs1, weights1, diag1)
    rhs2 = coarsen(rhs1 - apply_op(corr1, weights1, diag1))
    corr2 = presmooth(rhs2, weights2, diag2)
    rhs3 = coarsen(rhs2 - apply_op(corr2, weights2, diag2))
    corr3 = column_solve(rhs3, coeffs)
    corr3 = corr3 + column_solve(rhs3 - apply_op(corr3, weights3, diag3), coeffs)
    corr2 = postsmooth(corr2 + refine(corr3), rhs2, weights2, diag2)
    corr1 = postsmooth(corr1 + refine(corr2), rhs1, weights1, diag1)
    return diag1 * corr1


PLANE = (32, 32)
SPLIT = (2, 4)
ROWS = 8
LANES = 128
HALO = 16
NEAR = 8
F32 = jnp.float32


def iota(shape, dim):
    return lax.broadcasted_iota(jnp.int32, shape, dim)


def dot01(field, chosen, dims=(((1,), (0,)), ((), ()))):
    total = None
    rest = field
    for part in range(3):
        piece = rest.astype(jnp.bfloat16)
        term = lax.dot_general(piece, chosen, dims, preferred_element_type=F32)
        total = term if total is None else total + term
        if part < 2:
            rest = rest - piece.astype(F32)
    return total


def where01(condition):
    return jnp.where(condition, 1.0, 0.0).astype(jnp.bfloat16)


def loop(low, high, size, body):
    size = min(size, high - low)
    steps = -(-(high - low) // size)

    def step(index, carry):
        body(jnp.minimum(low + index * size, high - size), size)
        return carry

    if steps == 1:
        body(low, size)
    else:
        lax.fori_loop(0, steps, step, 0)


class Level:
    def __init__(self, level):
        self.ny = PLANE[1] >> level
        self.xs = 4 >> level
        self.factor = float(2**level)

    def masks(self, shape):
        lane = iota(shape, 2)
        row = iota(shape, 1)
        within = (lane // self.ny) % self.xs
        y = lane % self.ny
        last_x = (row == ROWS - 1) & (within == self.xs - 1)
        return within, y == self.ny - 1, last_x

    def next_x(self, field):
        within = (iota(field.shape, 2) // self.ny) % self.xs
        moved = pltpu.roll(field, LANES - self.ny, 2)
        return jnp.where(within == self.xs - 1, pltpu.roll(moved, ROWS - 1, 1), moved)

    def last_x(self, field):
        within = (iota(field.shape, 2) // self.ny) % self.xs
        moved = pltpu.roll(field, self.ny, 2)
        return jnp.where(within == 0, pltpu.roll(moved, 1, 1), moved)

    def next_y(self, field):
        return pltpu.roll(field, LANES - 1, 2)

    def last_y(self, field):
        return pltpu.roll(field, 1, 2)

    def balance(self, field, wx, wy, wz):
        mid = field[1:-1]
        flow_x = wx * (self.next_x(mid) - mid)
        flow_y = wy * (self.next_y(mid) - mid)
        flow_z = wz * (field[1:] - field[:-1])
        return (
            (flow_x - self.last_x(flow_x))
            + (flow_y - self.last_y(flow_y))
            + (flow_z[1:] - flow_z[:-1])
        )


def mean_of(fluid, near, factor):
    total = fluid + near
    safe = jnp.where(total > 0, total, 1.0)
    return jnp.where(total > 0, (factor * 2.0) * fluid * near / safe, 0.0)


def set_level(level, low, high, size, fluid, pin, rhs, wx, wy, wz, gain, corr):
    def body(plane, count):
        wide = fluid[pl.ds(plane - 1, count + 2)]
        mid = wide[1:-1]
        within, end_y, end_x = level.masks(mid.shape)
        to_x = jnp.where(end_x, 0.0, mean_of(mid, level.next_x(mid), level.factor))
        to_y = jnp.where(end_y, 0.0, mean_of(mid, level.next_y(mid), level.factor))
        to_z = mean_of(wide[:-1], wide[1:], level.factor)
        diag = (
            (to_x + level.last_x(to_x))
            + (to_y + level.last_y(to_y))
            + (to_z[1:] + to_z[:-1])
            + pin[pl.ds(plane, count)]
        )
        some = diag > 0
        scale = jnp.where(some, OMEGA / jnp.where(some, diag, 1.0), 0.0)
        wx[pl.ds(plane, count)] = to_x
        wy[pl.ds(plane, count)] = to_y
        wz[pl.ds(plane, count)] = to_z[1:]
        gain[pl.ds(plane, count)] = scale
        if corr is not None:
            corr[pl.ds(plane, count)] = scale * rhs[pl.ds(plane, count)]

    loop(low, high, size, body)


def residual_of(level, plane, count, fields, corr):
    rhs, pin, wx, wy, wz = fields
    field = corr[pl.ds(plane - 1, count + 2)]
    spread = level.balance(
        field, wx[pl.ds(plane, count)], wy[pl.ds(plane, count)], wz[pl.ds(plane - 1, count + 1)]
    )
    mid = field[1:-1]
    return mid, (rhs[pl.ds(plane, count)] - pin[pl.ds(plane, count)] * mid) + spread


def sweep(level, low, high, size, fields, gain, source, target):
    def body(plane, count):
        mid, rest = residual_of(level, plane, count, fields, source)
        target[pl.ds(plane, count)] = mid + gain[pl.ds(plane, count)] * rest

    loop(low, high, size, body)


def pair_sum(field):
    half = field.reshape((field.shape[0] // 2, 2) + field.shape[1:])
    return half[:, 0] + half[:, 1]


def coarse_residual(level, low, high, size, fields, corr, target):
    size = min(size, high - low)
    assert (high - low) % size == 0 and size % 2 == 0

    def body(plane, count):
        _, rest = residual_of(level, plane, count, fields, corr)
        target[pl.ds((plane - low) // 2, count // 2)] = pair_sum(rest)

    loop(low, high, size, body)


def lanes_down(level):
    fine = iota((LANES, LANES), 0)
    coarse = iota((LANES, LANES), 1)
    ny, xs = PLANE[1] >> level, 4 >> level
    half = xs // 2
    same_x = ((fine // ny) % xs) // 2 == (coarse // (ny // 2)) % half
    same_y = (fine % ny) // 2 == coarse % (ny // 2)
    return where01((fine < ny * xs) & same_x & same_y)


def in_lanes(field, chosen):
    flat = field.reshape(field.shape[0] * ROWS, LANES)
    return dot01(flat, chosen).reshape(field.shape)


def rank_of(peer):
    ny = SPLIT[1]
    ix, iy = peer // ny, peer % ny
    return ix * ny + (ny - 1 - iy if ix % 2 else iy)


def prepare_kernel(share, res_ref, fluid_ref, pin_ref, out_ref):
    bx, by, depth = fluid_ref.shape
    cells = bx * by
    groups = bx // 4
    pick = where01(iota((depth, 2 * depth), 1) // 2 == iota((depth, 2 * depth), 0))
    deep = lax.dot_general(
        pick, res_ref[...], (((1,), (1,)), ((), ())), preferred_element_type=F32
    )

    def lane_of(x, y):
        return (x % 4) * (groups * by) + (x // 4) * by + y

    fine = iota((4 * cells, cells), 0)
    lane = iota((4 * cells, cells), 1)
    chosen = where01(lane_of(fine // (4 * by), (fine % (2 * by)) // 2) == lane)
    rhs = dot01(deep, chosen)
    cell = iota((cells, cells), 0)
    lane = iota((cells, cells), 1)
    chosen = where01(lane_of(cell // by, cell % by) == lane)
    fluid = dot01(fluid_ref[...].reshape(cells, depth).T, chosen)
    pin = dot01(pin_ref[...].reshape(cells, depth).T, chosen)
    for index, field in enumerate((fluid, rhs, pin)):
        for peer in range(depth // share):
            begin = rank_of(peer) * share
            out_ref[peer, index * share : (index + 1) * share] = field[begin : begin + share]


def spread_kernel(groups, by, gathered, own):
    for start in range(0, own.shape[0], ROWS):
        place(gathered, start, own, start, groups, by)


def place(gathered, row, target, plane, groups, by):
    group = (iota((ROWS, LANES), 1) // by) % groups
    nx, ny = SPLIT
    for ix in range(nx):
        found = [gathered[ix * ny + iy, pl.ds(row, ROWS), :] for iy in range(ny)]
        for part in range(groups):
            total = found[part]
            for iy in range(ny):
                if iy != part:
                    moved = pltpu.roll(found[iy], (by * (iy - part)) % LANES, 1)
                    total = jnp.where(group == iy, moved, total)
            target[pl.ds(plane, ROWS), ix * groups + part, :] = total


def down_kernel(
    groups, by, depth, sizes,
    low, own, high,
    rhs1, pin1, wx1, wy1, wz1, gain1, corr1,
    rhs2, pin2, wx2, wy2, wz2, gain2, corr2,
    packed,
    fluid1, other1, fluid2, other2, sums,
):
    planes = depth + 2 * HALO
    for index, target in enumerate((fluid1, rhs1, pin1)):
        start = 0
        for piece in (low, own, high):
            count = piece.shape[0] // 3
            target[start : start + count] = piece[index * count : (index + 1) * count]
            start += count

    fine, coarse = Level(0), Level(1)
    down1, down2 = lanes_down(0), lanes_down(1)
    fields1 = (rhs1, pin1, wx1, wy1, wz1)
    fields2 = (rhs2, pin2, wx2, wy2, wz2)
    set_level(fine, 1, planes - 1, sizes[0], fluid1, pin1, rhs1, wx1, wy1, wz1, gain1, corr1)
    sweep(fine, 2, planes - 2, sizes[1], fields1, gain1, corr1, other1)
    sweep(fine, 3, planes - 3, sizes[1], fields1, gain1, other1, corr1)
    count2 = depth // 2 + 2 * NEAR
    begin = HALO - 2 * NEAR
    for source, target, share in ((fluid1, fluid2, 8.0), (pin1, pin2, 4.0)):
        whole = pair_sum(source[begin : begin + 2 * count2])
        target[...] = in_lanes(whole, down1) * (1.0 / share)
    low2, high2 = (begin + 4) // 2, count2 - (begin + 4) // 2
    inner = high2 - low2
    coarse_residual(
        fine, begin + 2 * low2, begin + 2 * high2, sizes[2], fields1, corr1, sums
    )
    rhs2[low2:high2] = in_lanes(sums[0:inner], down1)
    set_level(coarse, low2, high2, sizes[3], fluid2, pin2, rhs2, wx2, wy2, wz2, gain2, corr2)
    sweep(coarse, low2 + 1, high2 - 1, sizes[4], fields2, gain2, corr2, other2)
    sweep(coarse, low2 + 2, high2 - 2, sizes[4], fields2, gain2, other2, corr2)
    coarse_residual(coarse, NEAR, NEAR + depth // 2, sizes[5], fields2, corr2, sums)
    count3 = depth // 4
    rhs3 = in_lanes(sums[0:count3], down2)
    fluid3 = in_lanes(pair_sum(fluid2[NEAR : NEAR + 2 * count3]), down2) * 0.125
    pin3 = in_lanes(pair_sum(pin2[NEAR : NEAR + 2 * count3]), down2) * 0.25
    lane = iota((count3, LANES), 1) // ROWS
    first = jnp.zeros((count3, LANES), F32)
    second = jnp.zeros((count3, LANES), F32)
    for row in range(ROWS):
        first = jnp.where(lane == row, rhs3[:, row, :], first)
        first = jnp.where(lane == ROWS + row, fluid3[:, row, :], first)
        second = jnp.where(lane % ROWS == row, pin3[:, row, :], second)
    packed[0] = first[0:2]
    packed[1] = first[2:4]
    packed[2] = jnp.where(lane[0:2] < ROWS, second[0:2], second[2:4])
    lane = iota((1, LANES), 1) // (LANES // 4)
    for index, plane in enumerate((NEAR + depth // 2 - 5, NEAR + 4)):
        for half in range(2):
            row = jnp.zeros((1, LANES), F32)
            for quarter in range(4):
                at = half * 4 + quarter
                row = jnp.where(lane == quarter, corr2[plane, at : at + 1, :], row)
            packed[3 + index, half : half + 1, :] = row


def rolled(field, shift):
    count = field.shape[0]
    shift %= count
    if shift % ROWS:
        return pltpu.roll(field, shift, 0)
    return jnp.concatenate([field[count - shift :], field[: count - shift]], axis=0)


def columns(rhs, fluid, pin):
    depth = fluid.shape[0]
    z, lane = iota(fluid.shape, 0), iota(fluid.shape, 1)
    y, x = lane % ROWS, (lane // ROWS) % ROWS

    def next_x(field):
        return pltpu.roll(field, LANES - ROWS, 1)

    def next_y(field):
        return pltpu.roll(field, LANES - 1, 1)

    wz = jnp.where(z == depth - 1, 0.0, mean_of(fluid, rolled(fluid, -1), 4.0))
    wy = jnp.where(y == ROWS - 1, 0.0, mean_of(fluid, next_y(fluid), 4.0))
    wx = jnp.where(x == ROWS - 1, 0.0, mean_of(fluid, next_x(fluid), 4.0))
    across = (wx + pltpu.roll(wx, ROWS, 1)) + (wy + pltpu.roll(wy, 1, 1)) + pin
    share = 1.0 / jnp.sum(across, axis=0, keepdims=True)

    above, below, own = rolled(wz, 1), wz, across
    steps = []
    stride = 1
    while stride < depth:
        inverse = 1.0 / (above + below + own)
        up = above * rolled(inverse, stride)
        down = below * rolled(inverse, -stride)
        own = own + up * rolled(own, stride) + down * rolled(own, -stride)
        above = up * rolled(above, stride)
        below = down * rolled(below, -stride)
        steps.append((stride, up, down))
        stride *= 2
    inverse = 1.0 / (above + below + own)

    def solve(right):
        mean = jnp.sum(right, axis=0, keepdims=True) * share
        for stride, up, down in steps:
            right = right + up * rolled(right, stride) + down * rolled(right, -stride)
        return right * inverse + mean

    corr = solve(rhs)
    flow_x = wx * (next_x(corr) - corr)
    flow_y = wy * (next_y(corr) - corr)
    flow_z = wz * (rolled(corr, -1) - corr)
    rest = (
        (rhs - pin * corr)
        + (flow_x - pltpu.roll(flow_x, ROWS, 1))
        + (flow_y - pltpu.roll(flow_y, 1, 1))
        + (flow_z - rolled(flow_z, 1))
    )
    return corr + solve(rest)


def up_kernel(
    groups, by, depth, sizes,
    packed,
    rhs1, pin1, wx1, wy1, wz1, gain1, corr1,
    rhs2, pin2, wx2, wy2, wz2, gain2, corr2,
    out_ref,
    one1, two1, one2, two2, lifted, first, second, solved,
):
    count3 = depth // 4
    shares = packed.shape[0]
    peers = SPLIT[0] * SPLIT[1]
    slabs = sorted(range(shares), key=lambda i: (i // peers, rank_of(i % peers)))
    for slab, index in enumerate(slabs):
        row = slab * count3
        first[row : row + 2] = packed[index, 0]
        first[row + 2 : row + 4] = packed[index, 1]
        both = packed[index, 2]
        second[row : row + 2] = both
        second[row + 2 : row + 4] = pltpu.roll(both, LANES // 2, 1)
    half = iota((shares * count3, LANES), 1) < LANES // 2

    def low_half(field):
        return jnp.where(half, field, pltpu.roll(field, LANES // 2, 1))

    def high_half(field):
        return jnp.where(half, pltpu.roll(field, LANES // 2, 1), field)

    solved[NEAR : NEAR + shares * count3] = columns(
        low_half(first[...]), high_half(first[...]), low_half(second[...])
    )
    solved[0:NEAR] = jnp.zeros((NEAR, LANES), F32)
    solved[NEAR + shares * count3 :] = jnp.zeros((2 * NEAR, LANES), F32)

    def slab_of(index):
        index = jnp.clip(index, 0, shares - 1)
        row = lax.rem(index, peers) // ny
        column = lax.rem(index, ny)
        column = jnp.where(lax.rem(row, 2) == 1, ny - 1 - column, column)
        return (index // peers) * peers + row * ny + column

    nx, ny = SPLIT
    ix, iy = lax.axis_index("gx"), lax.axis_index("gy")
    along = jnp.where(lax.rem(ix, 2) == 1, ny - 1 - iy, iy)
    part = (lax.axis_index("gz") * nx + ix) * ny + along
    count = count3 + 2 * NEAR
    tall = solved[pl.ds(part * count3, count + count3), :]
    fine, coarse = Level(0), Level(1)
    cell = iota((LANES, ROWS * LANES), 0)
    lane = iota((LANES, ROWS * LANES), 1)
    same_y = cell % ROWS == (lane % coarse.ny) // 2
    spread = where01((cell // ROWS == lane // LANES) & same_y)
    wide = dot01(tall, spread)
    for row in range(ROWS):
        lifted[0:count, row, :] = wide[:count, row * LANES : (row + 1) * LANES]

    fields1 = (rhs1, pin1, wx1, wy1, wz1)
    fields2 = (rhs2, pin2, wx2, wy2, wz2)
    low, high = NEAR - 4, NEAR + depth // 2 + 4
    parents = lifted[low // 2 + NEAR // 2 : high // 2 + NEAR // 2]
    twice = jnp.broadcast_to(parents[:, None], (parents.shape[0], 2, ROWS, LANES))
    reach = depth // 2 + NEAR
    quarter = iota((ROWS, LANES), 1) // (LANES // 4)
    row = iota((ROWS, LANES), 0)

    def unpacked(index, which):
        pair = packed[slab_of(index), which]
        total = None
        for shift in range(4):
            moved = pltpu.roll(pair, shift * (LANES // 4), 1)
            wide = jnp.where(row < 4, moved[0:1, :], moved[1:2, :])
            kept = jnp.where((quarter - shift) % 4 == row % 4, wide, 0.0)
            total = kept if total is None else total + kept
        return total

    before, after = unpacked(part - 1, 3), unpacked(part + 1, 4)
    one2[low - 1] = before + lifted[(low - 1) // 2 + NEAR // 2]
    one2[low:high] = corr2[low:high] + twice.reshape(high - low, ROWS, LANES)
    one2[high] = after + lifted[high // 2 + NEAR // 2]
    sweep(coarse, NEAR - 4, reach + 4, sizes[4], fields2, gain2, one2, two2)
    sweep(coarse, NEAR - 3, reach + 3, sizes[4], fields2, gain2, two2, one2)
    sweep(coarse, NEAR - 2, reach + 2, sizes[4], fields2, gain2, one2, two2)

    fine_lane, coarse_lane = iota((LANES, LANES), 1), iota((LANES, LANES), 0)
    x_of = (fine_lane // fine.ny) // 2
    y_of = (fine_lane % fine.ny) // 2
    up = where01(coarse_lane == x_of * coarse.ny + y_of)
    lifted[0 : depth // 2 + 4] = in_lanes(two2[NEAR - 2 : reach + 2], up)
    parents = lifted[0 : depth // 2 + 4]
    twice = jnp.broadcast_to(parents[:, None], (parents.shape[0], 2, ROWS, LANES))
    low, high = HALO - 4, HALO + depth + 4
    one1[low:high] = corr1[low:high] + twice.reshape(high - low, ROWS, LANES)
    reach = depth + HALO
    sweep(fine, HALO - 2, reach + 2, sizes[1], fields1, gain1, one1, two1)
    sweep(fine, HALO - 1, reach + 1, sizes[1], fields1, gain1, two1, one1)
    sweep(fine, HALO, reach, sizes[1], fields1, gain1, one1, two1)

    group = (iota((depth, LANES), 1) // by) % groups
    for ix in range(nx):
        scaled = [
            two1[HALO:reach, ix * groups + part, :]
            * (OMEGA / gain1[HALO:reach, ix * groups + part, :])
            for part in range(groups)
        ]
        for iy in range(ny):
            total = scaled[iy]
            for part in range(groups):
                if part != iy:
                    moved = pltpu.roll(scaled[part], (by * (part - iy)) % LANES, 1)
                    total = jnp.where(group == part, moved, total)
            out_ref[ix * ny + iy] = total


def finish_kernel(blocks, out_ref):
    bx, by, depth = out_ref.shape
    cells = bx * by
    cell = iota((cells, cells), 0)
    lane = iota((cells, cells), 1)
    x, y = cell // by, cell % by
    chosen = where01((x % 4) * (bx // 4 * by) + (x // 4) * by + y == lane)
    peers = blocks.shape[0]
    ordered = jnp.concatenate([blocks[i] for i in sorted(range(peers), key=rank_of)], axis=0)
    turned = dot01(ordered, chosen, (((1,), (1,)), ((), ())))
    out_ref[...] = turned.T.reshape(out_ref.shape)


def whole_planes(residual_q2, viscosity, pinned):
    bx, by, depth = viscosity.shape
    groups = bx // 4
    peers = SPLIT[0] * SPLIT[1]
    share = depth // peers
    planes = share + 2 * HALO
    count2 = share // 2 + 2 * NEAR
    sizes = (23, 22, 20, 10, 24, 24)
    limit = pltpu.CompilerParams(vmem_limit_bytes=32 * 2**20)

    def flat(rows):
        return jax.ShapeDtypeStruct((rows, LANES), F32)

    def blocks(count, rows):
        return jax.ShapeDtypeStruct((count, rows, LANES), F32)

    def room(count):
        return pltpu.VMEM((count, ROWS, LANES), F32)

    fluid = 1.0 / viscosity
    pin = 4.0 * pinned.astype(F32) * fluid
    parcels = pl.pallas_call(
        functools.partial(prepare_kernel, share),
        out_shape=blocks(peers, 3 * share),
        compiler_params=limit,
        name="prepare",
    )(residual_q2.reshape(4 * bx * by, 2 * depth), fluid, pin)
    own = pl.pallas_call(
        functools.partial(spread_kernel, groups, by),
        out_shape=blocks(3 * share, ROWS),
        compiler_params=limit,
        name="spread",
    )(lax.all_to_all(parcels, ("gx", "gy"), 0, 0, tiled=True))
    length = lax.axis_size("gz")
    slabs = sorted(range(peers), key=rank_of)
    parts = length * peers

    def step(field, ahead):
        device = [slabs[i % peers] * length + i // peers for i in range(parts)]
        pairs = [(device[i], device[i + ahead]) for i in range(parts) if 0 <= i + ahead < parts]
        return lax.ppermute(field, ("gx", "gy", "gz"), pairs)

    low, high = step(own, 1), step(own, -1)
    saved = (blocks(planes, ROWS),) * 7 + (blocks(count2, ROWS),) * 7
    results = pl.pallas_call(
        functools.partial(down_kernel, groups, by, share, sizes),
        out_shape=saved + (blocks(5, 2),),
        scratch_shapes=[room(planes), room(planes), room(count2), room(count2), room(count2)],
        compiler_params=limit,
        name="down",
    )(low, own, high)
    copies = jnp.broadcast_to(results[-1], (parts,) + results[-1].shape)
    packed = lax.all_to_all(copies, ("gz", "gx", "gy"), 0, 0, tiled=True)
    depth3 = parts * share // 4
    mine = pl.pallas_call(
        functools.partial(up_kernel, groups, by, share, sizes),
        out_shape=blocks(peers, share),
        scratch_shapes=[room(planes), room(planes), room(count2), room(count2), room(count2)]
        + [pltpu.VMEM((rows, LANES), F32) for rows in (depth3, depth3, depth3 + 3 * NEAR)],
        compiler_params=limit,
        name="up",
    )(packed, *results[:-1])
    return pl.pallas_call(
        finish_kernel,
        out_shape=jax.ShapeDtypeStruct((bx, by, depth), F32),
        compiler_params=limit,
        name="finish",
    )(lax.all_to_all(mine, ("gx", "gy"), 0, 0, tiled=True))


def one_tile_planes(mesh, viscosity):
    split = (mesh.shape["gx"], mesh.shape["gy"])
    depth = viscosity.shape[2]
    fits = viscosity.shape[:2] == PLANE and split == SPLIT
    return fits and depth == 4 * LANES and depth // mesh.shape["gz"] == LANES


def solution(mesh):
    placed = (P("gx", "gy", "gz"), P("gx", "gy", "gz"), P("gx", "gy", "gz"))

    def cycle(residual_q2, viscosity, pinned):
        chosen = whole_planes if one_tile_planes(mesh, viscosity) else per_device
        return jax.shard_map(
            chosen, mesh=mesh, in_specs=placed, out_specs=P("gx", "gy", "gz"), check_vma=False
        )(residual_q2, viscosity, pinned)

    return cycle
```

```python
import functools

import jax
import jax.numpy as jnp
from jax import lax
from jax.experimental import pallas as pl
from jax.experimental.pallas import tpu as pltpu
from jax.sharding import PartitionSpec as P

NU = 3


OMEGA = 0.6


def with_halo(block, sides, width):
    for axis, dim in sides:
        count = lax.axis_size(axis)
        forward = [(i, i + 1) for i in range(count - 1)]
        backward = [(target, source) for source, target in forward]
        low = lax.ppermute(
            lax.slice_in_dim(block, block.shape[dim] - width, None, axis=dim), axis, forward
        )
        high = lax.ppermute(lax.slice_in_dim(block, 0, width, axis=dim), axis, backward)
        block = jnp.concatenate([low, block, high], axis=dim)
    return block


def coarsen(x):
    a, b, c = x.shape
    return x.reshape(a // 2, 2, b // 2, 2, c // 2, 2).sum(axis=(1, 3, 5))


def refine(x):
    return jnp.repeat(jnp.repeat(jnp.repeat(x, 2, 0), 2, 1), 2, 2)


def extended(field):
    return with_halo(field, (("gx", 0), ("gy", 1), ("gz", 2)), 1)


def shifted(padded):
    return [
        padded[2:, 1:-1, 1:-1],
        padded[:-2, 1:-1, 1:-1],
        padded[1:-1, 2:, 1:-1],
        padded[1:-1, :-2, 1:-1],
        padded[1:-1, 1:-1, 2:],
        padded[1:-1, 1:-1, :-2],
    ]


def neighbours(field):
    return shifted(extended(field))


def harmonic(fluid, near, factor):
    total = fluid + near
    return jnp.where(total > 0, factor * 2.0 * fluid * near / jnp.where(total > 0, total, 1.0), 0.0)


def couplings(fluid, factor):
    return [harmonic(fluid, near, factor) for near in neighbours(fluid)]


def apply_op(field, weights, diag):
    total = diag * field
    for weight, near in zip(weights, neighbours(field)):
        total = total - weight * near
    return total


def presmooth(rhs, weights, diag):
    corr = OMEGA * rhs / diag
    for sweep in range(NU - 1):
        corr = corr + OMEGA * (rhs - apply_op(corr, weights, diag)) / diag
    return corr


def postsmooth(corr, rhs, weights, diag):
    for sweep in range(NU):
        corr = corr + OMEGA * (rhs - apply_op(corr, weights, diag)) / diag
    return corr


def tridiag(coeffs, rhs):
    solved = lax.linalg.tridiagonal_solve(coeffs[0], coeffs[1], coeffs[2], rhs[..., None])[..., 0]
    last = rhs.ndim - 1
    shift_col = jnp.sum(rhs, axis=last, keepdims=True) / jnp.sum(
        coeffs[3], axis=last, keepdims=True
    )
    return solved + shift_col


def prepare_columns(weights, diag):
    lower = -weights[5]
    upper = -weights[4]
    across = diag + lower + upper
    return (
        lax.all_gather(lower, "gz", axis=2, tiled=True),
        lax.all_gather(diag, "gz", axis=2, tiled=True),
        lax.all_gather(upper, "gz", axis=2, tiled=True),
        lax.all_gather(across, "gz", axis=2, tiled=True),
    )


def column_solve(rhs, coeffs):
    depth = rhs.shape[2]
    whole = lax.all_gather(rhs, "gz", axis=2, tiled=True)
    solved = tridiag(coeffs, whole)
    return lax.dynamic_slice_in_dim(solved, lax.axis_index("gz") * depth, depth, 2)


def per_device(residual_q2, viscosity, pinned):
    fluid1 = 1.0 / viscosity
    pin1 = 4.0 * pinned.astype(jnp.float32) * fluid1
    rhs1 = coarsen(residual_q2.astype(jnp.float32))
    fluid2 = coarsen(fluid1) / 8.0
    pin2 = coarsen(pin1) / 4.0
    fluid3 = coarsen(fluid2) / 8.0
    pin3 = coarsen(pin2) / 4.0
    weights1 = couplings(fluid1, 1.0)
    weights2 = couplings(fluid2, 2.0)
    weights3 = couplings(fluid3, 4.0)
    diag1 = sum(weights1) + pin1
    diag2 = sum(weights2) + pin2
    diag3 = sum(weights3) + pin3
    coeffs = prepare_columns(weights3, diag3)
    corr1 = presmooth(rhs1, weights1, diag1)
    rhs2 = coarsen(rhs1 - apply_op(corr1, weights1, diag1))
    corr2 = presmooth(rhs2, weights2, diag2)
    rhs3 = coarsen(rhs2 - apply_op(corr2, weights2, diag2))
    corr3 = column_solve(rhs3, coeffs)
    corr3 = corr3 + column_solve(rhs3 - apply_op(corr3, weights3, diag3), coeffs)
    corr2 = postsmooth(corr2 + refine(corr3), rhs2, weights2, diag2)
    corr1 = postsmooth(corr1 + refine(corr2), rhs1, weights1, diag1)
    return diag1 * corr1


PLANE = (32, 32)
SPLIT = (2, 4)
ROWS = 8
LANES = 128
HALO = 16
NEAR = 8
PIECE = 8
TINY = 1e-30
F32 = jnp.float32


def iota(shape, dim):
    return lax.broadcasted_iota(jnp.int32, shape, dim)


def dot01(field, chosen, dims=(((1,), (0,)), ((), ()))):
    total = None
    rest = field
    for part in range(3):
        piece = rest.astype(jnp.bfloat16)
        term = lax.dot_general(piece, chosen, dims, preferred_element_type=F32)
        total = term if total is None else total + term
        if part < 2:
            rest = rest - piece.astype(F32)
    return total


def dot10(chosen, field):
    total = None
    rest = field
    for part in range(3):
        piece = rest.astype(jnp.bfloat16)
        term = lax.dot_general(
            chosen, piece, (((1,), (1,)), ((), ())), preferred_element_type=F32
        )
        total = term if total is None else total + term
        if part < 2:
            rest = rest - piece.astype(F32)
    return total


def where01(condition):
    return jnp.where(condition, 1.0, 0.0).astype(jnp.bfloat16)


def loop(low, high, size, body):
    for plane in range(low, high, size):
        body(plane, min(size, high - plane))


def inverse_of(field):
    first = pl.reciprocal(field, approx=True)
    return first * (2.0 - field * first)


class Level:
    def __init__(self, level):
        self.ny = PLANE[1] >> level
        self.xs = 4 >> level
        self.factor = float(2**level)

    def masks(self, shape):
        lane = iota(shape, 2)
        row = iota(shape, 1)
        within = (lane // self.ny) % self.xs
        y = lane % self.ny
        last_x = (row == ROWS - 1) & (within == self.xs - 1)
        return within, y == self.ny - 1, last_x

    def next_x(self, field):
        within = (iota(field.shape, 2) // self.ny) % self.xs
        moved = pltpu.roll(field, LANES - self.ny, 2)
        return jnp.where(within == self.xs - 1, pltpu.roll(moved, ROWS - 1, 1), moved)

    def last_x(self, field):
        within = (iota(field.shape, 2) // self.ny) % self.xs
        moved = pltpu.roll(field, self.ny, 2)
        return jnp.where(within == 0, pltpu.roll(moved, 1, 1), moved)

    def next_y(self, field):
        return pltpu.roll(field, LANES - 1, 2)

    def last_y(self, field):
        return pltpu.roll(field, 1, 2)

    def spread(self, field, scaled, plane, count):
        mid = field[1:-1]
        near = (
            self.next_x(mid), self.last_x(mid), self.next_y(mid), self.last_y(mid),
            field[2:], field[:-2],
        )
        terms = [weight[pl.ds(plane, count)] * value for weight, value in zip(scaled, near)]
        return mid, ((terms[0] + terms[1]) + (terms[2] + terms[3])) + (terms[4] + terms[5])


def mean_of(fluid, near, factor):
    return ((factor * 2.0) * fluid * near) * inverse_of(jnp.maximum(fluid + near, TINY))


def set_level(level, low, high, fluid, pin, rhs, fields):
    scaled, start, diag = fields

    def body(plane, count):
        wide = fluid[pl.ds(plane - 1, count + 2)]
        mid = wide[1:-1]
        within, end_y, end_x = level.masks(mid.shape)
        to_x = jnp.where(end_x, 0.0, mean_of(mid, level.next_x(mid), level.factor))
        to_y = jnp.where(end_y, 0.0, mean_of(mid, level.next_y(mid), level.factor))
        to_z = mean_of(wide[:-1], wide[1:], level.factor)
        weights = (to_x, level.last_x(to_x), to_y, level.last_y(to_y), to_z[1:], to_z[:-1])
        total = (
            (weights[0] + weights[1])
            + (weights[2] + weights[3])
            + (weights[4] + weights[5])
            + pin[pl.ds(plane, count)]
        )
        gain = OMEGA * inverse_of(jnp.maximum(total, TINY))
        for target, weight in zip(scaled, weights):
            target[pl.ds(plane, count)] = gain * weight
        start[pl.ds(plane, count)] = gain * rhs[pl.ds(plane, count)]
        diag[pl.ds(plane, count)] = total

    loop(low, high, PIECE, body)


def sweep(level, low, high, fields, source, target):
    scaled, start, _ = fields

    def body(plane, count):
        mid, total = level.spread(source[pl.ds(plane - 1, count + 2)], scaled, plane, count)
        target[pl.ds(plane, count)] = (1.0 - OMEGA) * mid + (start[pl.ds(plane, count)] + total)

    loop(low, high, PIECE, body)


def pair_sum(field):
    half = field.reshape((field.shape[0] // 2, 2) + field.shape[1:])
    return half[:, 0] + half[:, 1]


def coarse_residual(level, low, high, fields, corr, target):
    scaled, start, diag = fields

    def body(plane, count):
        mid, total = level.spread(corr[pl.ds(plane - 1, count + 2)], scaled, plane, count)
        rest = (start[pl.ds(plane, count)] + total) - OMEGA * mid
        rest = rest * (diag[pl.ds(plane, count)] * (1.0 / OMEGA))
        target[pl.ds((plane - low) // 2, count // 2)] = pair_sum(rest)

    loop(low, high, PIECE, body)


def lanes_down(level):
    fine = iota((LANES, LANES), 0)
    coarse = iota((LANES, LANES), 1)
    ny, xs = PLANE[1] >> level, 4 >> level
    half = xs // 2
    same_x = ((fine // ny) % xs) // 2 == (coarse // (ny // 2)) % half
    same_y = (fine % ny) // 2 == coarse % (ny // 2)
    return where01((fine < ny * xs) & same_x & same_y)


def in_lanes(field, chosen):
    flat = field.reshape(field.shape[0] * ROWS, LANES)
    return dot01(flat, chosen).reshape(field.shape)


def rank_of(peer):
    ny = SPLIT[1]
    ix, iy = peer // ny, peer % ny
    return ix * ny + (ny - 1 - iy if ix % 2 else iy)


def prepare_kernel(share, res_ref, fluid_ref, pin_ref, out_ref):
    bx, by, depth = fluid_ref.shape
    cells = bx * by
    groups = bx // 4
    pick = where01(iota((depth, 2 * depth), 1) // 2 == iota((depth, 2 * depth), 0))
    deep = lax.dot_general(
        pick, res_ref[...], (((1,), (1,)), ((), ())), preferred_element_type=F32
    )

    def lane_of(x, y):
        return (x % 4) * (groups * by) + (x // 4) * by + y

    fine = iota((4 * cells, cells), 0)
    lane = iota((4 * cells, cells), 1)
    chosen = where01(lane_of(fine // (4 * by), (fine % (2 * by)) // 2) == lane)
    rhs = dot01(deep, chosen)
    cell = iota((cells, cells), 0)
    lane = iota((cells, cells), 1)
    chosen = where01(lane_of(cell // by, cell % by) == lane)
    fluid = dot01(fluid_ref[...].reshape(cells, depth).T, chosen)
    pin = dot01(pin_ref[...].reshape(cells, depth).T, chosen)
    for index, field in enumerate((fluid, rhs, pin)):
        for peer in range(depth // share):
            begin = rank_of(peer) * share
            out_ref[peer, index * share : (index + 1) * share] = field[begin : begin + share]


def spread_kernel(groups, by, gathered, own):
    for start in range(0, own.shape[0], ROWS):
        place(gathered, start, own, start, groups, by)


def place(gathered, row, target, plane, groups, by):
    group = (iota((ROWS, LANES), 1) // by) % groups
    nx, ny = SPLIT
    for ix in range(nx):
        found = [gathered[ix * ny + iy, pl.ds(row, ROWS), :] for iy in range(ny)]
        for part in range(groups):
            total = found[part]
            for iy in range(ny):
                if iy != part:
                    moved = pltpu.roll(found[iy], (by * (iy - part)) % LANES, 1)
                    total = jnp.where(group == iy, moved, total)
            target[pl.ds(plane, ROWS), ix * groups + part, :] = total


def down_kernel(
    groups, by, depth,
    low, own, high,
    xn1, xl1, yn1, yl1, zn1, zl1, start1, diag1, corr1,
    xn2, xl2, yn2, yl2, zn2, zl2, start2, diag2, corr2,
    packed,
    fluid1, rhs1, pin1, other1, fluid2, rhs2, pin2, other2, sums,
):
    planes = depth + 2 * HALO
    for index, target in enumerate((fluid1, rhs1, pin1)):
        start = 0
        for piece in (low, own, high):
            count = piece.shape[0] // 3
            target[start : start + count] = piece[index * count : (index + 1) * count]
            start += count

    fine, coarse = Level(0), Level(1)
    down1, down2 = lanes_down(0), lanes_down(1)
    fields1 = ((xn1, xl1, yn1, yl1, zn1, zl1), start1, diag1)
    fields2 = ((xn2, xl2, yn2, yl2, zn2, zl2), start2, diag2)
    set_level(fine, 1, planes - 1, fluid1, pin1, rhs1, fields1)
    sweep(fine, 2, planes - 2, fields1, start1, other1)
    sweep(fine, 3, planes - 3, fields1, other1, corr1)
    count2 = depth // 2 + 2 * NEAR
    begin = HALO - 2 * NEAR
    for source, target, share in ((fluid1, fluid2, 8.0), (pin1, pin2, 4.0)):
        whole = pair_sum(source[begin : begin + 2 * count2])
        target[...] = in_lanes(whole, down1) * (1.0 / share)
    low2, high2 = (begin + 4) // 2, count2 - (begin + 4) // 2
    inner = high2 - low2
    coarse_residual(fine, begin + 2 * low2, begin + 2 * high2, fields1, corr1, sums)
    rhs2[low2:high2] = in_lanes(sums[0:inner], down1)
    set_level(coarse, low2, high2, fluid2, pin2, rhs2, fields2)
    sweep(coarse, low2 + 1, high2 - 1, fields2, start2, other2)
    sweep(coarse, low2 + 2, high2 - 2, fields2, other2, corr2)
    coarse_residual(coarse, NEAR, NEAR + depth // 2, fields2, corr2, sums)
    count3 = depth // 4
    rhs3 = in_lanes(sums[0:count3], down2)
    fluid3 = in_lanes(pair_sum(fluid2[NEAR : NEAR + 2 * count3]), down2) * 0.125
    pin3 = in_lanes(pair_sum(pin2[NEAR : NEAR + 2 * count3]), down2) * 0.25
    lane = iota((count3, LANES), 1) // ROWS
    first = jnp.zeros((count3, LANES), F32)
    second = jnp.zeros((count3, LANES), F32)
    for row in range(ROWS):
        first = jnp.where(lane == row, rhs3[:, row, :], first)
        first = jnp.where(lane == ROWS + row, fluid3[:, row, :], first)
        second = jnp.where(lane % ROWS == row, pin3[:, row, :], second)
    packed[0] = first[0:2]
    packed[1] = first[2:4]
    packed[2] = jnp.where(lane[0:2] < ROWS, second[0:2], second[2:4])
    lane = iota((1, LANES), 1) // (LANES // 4)
    for index, plane in enumerate((NEAR + depth // 2 - 5, NEAR + 4)):
        for half in range(2):
            row = jnp.zeros((1, LANES), F32)
            for quarter in range(4):
                at = half * 4 + quarter
                row = jnp.where(lane == quarter, corr2[plane, at : at + 1, :], row)
            packed[3 + index, half : half + 1, :] = row


def rolled(field, shift):
    count = field.shape[0]
    shift %= count
    if shift % ROWS:
        return pltpu.roll(field, shift, 0)
    return jnp.concatenate([field[count - shift :], field[: count - shift]], axis=0)


def columns(rhs, fluid, pin):
    depth = fluid.shape[0]
    z, lane = iota(fluid.shape, 0), iota(fluid.shape, 1)
    y, x = lane % ROWS, (lane // ROWS) % ROWS

    def next_x(field):
        return pltpu.roll(field, LANES - ROWS, 1)

    def next_y(field):
        return pltpu.roll(field, LANES - 1, 1)

    wz = jnp.where(z == depth - 1, 0.0, mean_of(fluid, rolled(fluid, -1), 4.0))
    wy = jnp.where(y == ROWS - 1, 0.0, mean_of(fluid, next_y(fluid), 4.0))
    wx = jnp.where(x == ROWS - 1, 0.0, mean_of(fluid, next_x(fluid), 4.0))
    across = (wx + pltpu.roll(wx, ROWS, 1)) + (wy + pltpu.roll(wy, 1, 1)) + pin
    share = 1.0 / jnp.sum(across, axis=0, keepdims=True)

    above, below, own = rolled(wz, 1), wz, across
    steps = []
    stride = 1
    while stride < depth:
        inverse = inverse_of(above + below + own)
        up = above * rolled(inverse, stride)
        down = below * rolled(inverse, -stride)
        own = own + up * rolled(own, stride) + down * rolled(own, -stride)
        above = up * rolled(above, stride)
        below = down * rolled(below, -stride)
        steps.append((stride, up, down))
        stride *= 2
    inverse = inverse_of(above + below + own)

    def solve(right):
        mean = jnp.sum(right, axis=0, keepdims=True) * share
        for stride, up, down in steps:
            right = right + up * rolled(right, stride) + down * rolled(right, -stride)
        return right * inverse + mean

    corr = solve(rhs)
    flow_x = wx * (next_x(corr) - corr)
    flow_y = wy * (next_y(corr) - corr)
    flow_z = wz * (rolled(corr, -1) - corr)
    rest = (
        (rhs - pin * corr)
        + (flow_x - pltpu.roll(flow_x, ROWS, 1))
        + (flow_y - pltpu.roll(flow_y, 1, 1))
        + (flow_z - rolled(flow_z, 1))
    )
    return corr + solve(rest)


def up_kernel(
    groups, by, depth,
    packed,
    xn1, xl1, yn1, yl1, zn1, zl1, start1, diag1, corr1,
    xn2, xl2, yn2, yl2, zn2, zl2, start2, diag2, corr2,
    out_ref,
    one1, two1, one2, two2, lifted, first, second, solved,
):
    count3 = depth // 4
    shares = packed.shape[0]
    peers = SPLIT[0] * SPLIT[1]
    slabs = sorted(range(shares), key=lambda i: (i // peers, rank_of(i % peers)))
    for slab, index in enumerate(slabs):
        row = slab * count3
        first[row : row + 2] = packed[index, 0]
        first[row + 2 : row + 4] = packed[index, 1]
        both = packed[index, 2]
        second[row : row + 2] = both
        second[row + 2 : row + 4] = pltpu.roll(both, LANES // 2, 1)
    half = iota((shares * count3, LANES), 1) < LANES // 2

    def low_half(field):
        return jnp.where(half, field, pltpu.roll(field, LANES // 2, 1))

    def high_half(field):
        return jnp.where(half, pltpu.roll(field, LANES // 2, 1), field)

    solved[NEAR : NEAR + shares * count3] = columns(
        low_half(first[...]), high_half(first[...]), low_half(second[...])
    )
    solved[0:NEAR] = jnp.zeros((NEAR, LANES), F32)
    solved[NEAR + shares * count3 :] = jnp.zeros((2 * NEAR, LANES), F32)

    def slab_of(index):
        index = jnp.clip(index, 0, shares - 1)
        row = lax.rem(index, peers) // ny
        column = lax.rem(index, ny)
        column = jnp.where(lax.rem(row, 2) == 1, ny - 1 - column, column)
        return (index // peers) * peers + row * ny + column

    nx, ny = SPLIT
    ix, iy = lax.axis_index("gx"), lax.axis_index("gy")
    along = jnp.where(lax.rem(ix, 2) == 1, ny - 1 - iy, iy)
    part = (lax.axis_index("gz") * nx + ix) * ny + along
    count = count3 + 2 * NEAR
    tall = solved[pl.ds(part * count3, count + count3), :]
    fine, coarse = Level(0), Level(1)
    cell = iota((LANES, ROWS * LANES), 0)
    lane = iota((LANES, ROWS * LANES), 1)
    same_y = cell % ROWS == (lane % coarse.ny) // 2
    spread = where01((cell // ROWS == lane // LANES) & same_y)
    wide = dot01(tall, spread)
    for row in range(ROWS):
        lifted[0:count, row, :] = wide[:count, row * LANES : (row + 1) * LANES]

    fields1 = ((xn1, xl1, yn1, yl1, zn1, zl1), start1, diag1)
    fields2 = ((xn2, xl2, yn2, yl2, zn2, zl2), start2, diag2)
    low, high = NEAR - 4, NEAR + depth // 2 + 4
    parents = lifted[low // 2 + NEAR // 2 : high // 2 + NEAR // 2]
    twice = jnp.broadcast_to(parents[:, None], (parents.shape[0], 2, ROWS, LANES))
    reach = depth // 2 + NEAR
    quarter = iota((ROWS, LANES), 1) // (LANES // 4)
    row = iota((ROWS, LANES), 0)

    def unpacked(index, which):
        pair = packed[slab_of(index), which]
        total = None
        for shift in range(4):
            moved = pltpu.roll(pair, shift * (LANES // 4), 1)
            wide = jnp.where(row < 4, moved[0:1, :], moved[1:2, :])
            kept = jnp.where((quarter - shift) % 4 == row % 4, wide, 0.0)
            total = kept if total is None else total + kept
        return total

    before, after = unpacked(part - 1, 3), unpacked(part + 1, 4)
    one2[low - 1] = before + lifted[(low - 1) // 2 + NEAR // 2]
    one2[low:high] = corr2[low:high] + twice.reshape(high - low, ROWS, LANES)
    one2[high] = after + lifted[high // 2 + NEAR // 2]
    sweep(coarse, NEAR - 4, reach + 4, fields2, one2, two2)
    sweep(coarse, NEAR - 3, reach + 3, fields2, two2, one2)
    sweep(coarse, NEAR - 2, reach + 2, fields2, one2, two2)

    fine_lane, coarse_lane = iota((LANES, LANES), 1), iota((LANES, LANES), 0)
    x_of = (fine_lane // fine.ny) // 2
    y_of = (fine_lane % fine.ny) // 2
    up = where01(coarse_lane == x_of * coarse.ny + y_of)
    lifted[0 : depth // 2 + 4] = in_lanes(two2[NEAR - 2 : reach + 2], up)
    parents = lifted[0 : depth // 2 + 4]
    twice = jnp.broadcast_to(parents[:, None], (parents.shape[0], 2, ROWS, LANES))
    low, high = HALO - 4, HALO + depth + 4
    one1[low:high] = corr1[low:high] + twice.reshape(high - low, ROWS, LANES)
    reach = depth + HALO
    sweep(fine, HALO - 2, reach + 2, fields1, one1, two1)
    sweep(fine, HALO - 1, reach + 1, fields1, two1, one1)
    sweep(fine, HALO, reach, fields1, one1, two1)

    group = (iota((depth, LANES), 1) // by) % groups
    for ix in range(nx):
        scaled = [
            two1[HALO:reach, ix * groups + part, :] * diag1[HALO:reach, ix * groups + part, :]
            for part in range(groups)
        ]
        for iy in range(ny):
            total = scaled[iy]
            for part in range(groups):
                if part != iy:
                    moved = pltpu.roll(scaled[part], (by * (part - iy)) % LANES, 1)
                    total = jnp.where(group == part, moved, total)
            out_ref[ix * ny + iy] = total


def finish_kernel(blocks, out_ref):
    bx, by, depth = out_ref.shape
    cells = bx * by
    cell = iota((cells, cells), 0)
    lane = iota((cells, cells), 1)
    x, y = cell // by, cell % by
    chosen = where01((x % 4) * (bx // 4 * by) + (x // 4) * by + y == lane)
    peers = blocks.shape[0]
    ordered = jnp.concatenate([blocks[i] for i in sorted(range(peers), key=rank_of)], axis=0)
    out_ref[...] = dot10(chosen, ordered).reshape(out_ref.shape)


def whole_planes(residual_q2, viscosity, pinned):
    bx, by, depth = viscosity.shape
    groups = bx // 4
    peers = SPLIT[0] * SPLIT[1]
    share = depth // peers
    planes = share + 2 * HALO
    count2 = share // 2 + 2 * NEAR
    limit = pltpu.CompilerParams(vmem_limit_bytes=32 * 2**20)

    def flat(rows):
        return jax.ShapeDtypeStruct((rows, LANES), F32)

    def blocks(count, rows):
        return jax.ShapeDtypeStruct((count, rows, LANES), F32)

    def room(count):
        return pltpu.VMEM((count, ROWS, LANES), F32)

    fluid = 1.0 / viscosity
    pin = 4.0 * pinned.astype(F32) * fluid
    parcels = pl.pallas_call(
        functools.partial(prepare_kernel, share),
        out_shape=blocks(peers, 3 * share),
        compiler_params=limit,
        name="prepare",
    )(residual_q2.reshape(4 * bx * by, 2 * depth), fluid, pin)
    own = pl.pallas_call(
        functools.partial(spread_kernel, groups, by),
        out_shape=blocks(3 * share, ROWS),
        compiler_params=limit,
        name="spread",
    )(lax.all_to_all(parcels, ("gx", "gy"), 0, 0, tiled=True))
    length = lax.axis_size("gz")
    slabs = sorted(range(peers), key=rank_of)
    parts = length * peers

    def step(field, ahead):
        device = [slabs[i % peers] * length + i // peers for i in range(parts)]
        pairs = [(device[i], device[i + ahead]) for i in range(parts) if 0 <= i + ahead < parts]
        return lax.ppermute(field, ("gx", "gy", "gz"), pairs)

    low, high = step(own, 1), step(own, -1)
    saved = (blocks(planes, ROWS),) * 9 + (blocks(count2, ROWS),) * 9
    results = pl.pallas_call(
        functools.partial(down_kernel, groups, by, share),
        out_shape=saved + (blocks(5, 2),),
        scratch_shapes=[room(planes)] * 4 + [room(count2)] * 5,
        compiler_params=limit,
        name="down",
    )(low, own, high)
    copies = jnp.broadcast_to(results[-1], (parts,) + results[-1].shape)
    packed = lax.all_to_all(copies, ("gz", "gx", "gy"), 0, 0, tiled=True)
    depth3 = parts * share // 4
    mine = pl.pallas_call(
        functools.partial(up_kernel, groups, by, share),
        out_shape=blocks(peers, share),
        scratch_shapes=[room(planes), room(planes), room(count2), room(count2), room(count2)]
        + [pltpu.VMEM((rows, LANES), F32) for rows in (depth3, depth3, depth3 + 3 * NEAR)],
        compiler_params=limit,
        name="up",
    )(packed, *results[:-1])
    return pl.pallas_call(
        finish_kernel,
        out_shape=jax.ShapeDtypeStruct((bx, by, depth), F32),
        compiler_params=limit,
        name="finish",
    )(lax.all_to_all(mine, ("gx", "gy"), 0, 0, tiled=True))


def one_tile_planes(mesh, viscosity):
    split = (mesh.shape["gx"], mesh.shape["gy"])
    depth = viscosity.shape[2]
    fits = viscosity.shape[:2] == PLANE and split == SPLIT
    return fits and depth == 4 * LANES and depth // mesh.shape["gz"] == LANES


def solution(mesh):
    placed = (P("gx", "gy", "gz"), P("gx", "gy", "gz"), P("gx", "gy", "gz"))

    def cycle(residual_q2, viscosity, pinned):
        chosen = whole_planes if one_tile_planes(mesh, viscosity) else per_device
        return jax.shard_map(
            chosen, mesh=mesh, in_specs=placed, out_specs=P("gx", "gy", "gz"), check_vma=False
        )(residual_q2, viscosity, pinned)

    return cycle
```

```python
import functools

import jax
import jax.numpy as jnp
from jax import lax
from jax.experimental import pallas as pl
from jax.experimental.pallas import tpu as pltpu
from jax.sharding import PartitionSpec as P

NU = 3


OMEGA = 0.6


def with_halo(block, sides, width):
    for axis, dim in sides:
        count = lax.axis_size(axis)
        forward = [(i, i + 1) for i in range(count - 1)]
        backward = [(target, source) for source, target in forward]
        low = lax.ppermute(
            lax.slice_in_dim(block, block.shape[dim] - width, None, axis=dim), axis, forward
        )
        high = lax.ppermute(lax.slice_in_dim(block, 0, width, axis=dim), axis, backward)
        block = jnp.concatenate([low, block, high], axis=dim)
    return block


def coarsen(x):
    a, b, c = x.shape
    return x.reshape(a // 2, 2, b // 2, 2, c // 2, 2).sum(axis=(1, 3, 5))


def refine(x):
    return jnp.repeat(jnp.repeat(jnp.repeat(x, 2, 0), 2, 1), 2, 2)


def extended(field):
    return with_halo(field, (("gx", 0), ("gy", 1), ("gz", 2)), 1)


def shifted(padded):
    return [
        padded[2:, 1:-1, 1:-1],
        padded[:-2, 1:-1, 1:-1],
        padded[1:-1, 2:, 1:-1],
        padded[1:-1, :-2, 1:-1],
        padded[1:-1, 1:-1, 2:],
        padded[1:-1, 1:-1, :-2],
    ]


def neighbours(field):
    return shifted(extended(field))


def harmonic(fluid, near, factor):
    total = fluid + near
    return jnp.where(total > 0, factor * 2.0 * fluid * near / jnp.where(total > 0, total, 1.0), 0.0)


def couplings(fluid, factor):
    return [harmonic(fluid, near, factor) for near in neighbours(fluid)]


def apply_op(field, weights, diag):
    total = diag * field
    for weight, near in zip(weights, neighbours(field)):
        total = total - weight * near
    return total


def presmooth(rhs, weights, diag):
    corr = OMEGA * rhs / diag
    for sweep in range(NU - 1):
        corr = corr + OMEGA * (rhs - apply_op(corr, weights, diag)) / diag
    return corr


def postsmooth(corr, rhs, weights, diag):
    for sweep in range(NU):
        corr = corr + OMEGA * (rhs - apply_op(corr, weights, diag)) / diag
    return corr


def tridiag(coeffs, rhs):
    solved = lax.linalg.tridiagonal_solve(coeffs[0], coeffs[1], coeffs[2], rhs[..., None])[..., 0]
    last = rhs.ndim - 1
    shift_col = jnp.sum(rhs, axis=last, keepdims=True) / jnp.sum(
        coeffs[3], axis=last, keepdims=True
    )
    return solved + shift_col


def prepare_columns(weights, diag):
    lower = -weights[5]
    upper = -weights[4]
    across = diag + lower + upper
    return (
        lax.all_gather(lower, "gz", axis=2, tiled=True),
        lax.all_gather(diag, "gz", axis=2, tiled=True),
        lax.all_gather(upper, "gz", axis=2, tiled=True),
        lax.all_gather(across, "gz", axis=2, tiled=True),
    )


def column_solve(rhs, coeffs):
    depth = rhs.shape[2]
    whole = lax.all_gather(rhs, "gz", axis=2, tiled=True)
    solved = tridiag(coeffs, whole)
    return lax.dynamic_slice_in_dim(solved, lax.axis_index("gz") * depth, depth, 2)


def per_device(residual_q2, viscosity, pinned):
    fluid1 = 1.0 / viscosity
    pin1 = 4.0 * pinned.astype(jnp.float32) * fluid1
    rhs1 = coarsen(residual_q2.astype(jnp.float32))
    fluid2 = coarsen(fluid1) / 8.0
    pin2 = coarsen(pin1) / 4.0
    fluid3 = coarsen(fluid2) / 8.0
    pin3 = coarsen(pin2) / 4.0
    weights1 = couplings(fluid1, 1.0)
    weights2 = couplings(fluid2, 2.0)
    weights3 = couplings(fluid3, 4.0)
    diag1 = sum(weights1) + pin1
    diag2 = sum(weights2) + pin2
    diag3 = sum(weights3) + pin3
    coeffs = prepare_columns(weights3, diag3)
    corr1 = presmooth(rhs1, weights1, diag1)
    rhs2 = coarsen(rhs1 - apply_op(corr1, weights1, diag1))
    corr2 = presmooth(rhs2, weights2, diag2)
    rhs3 = coarsen(rhs2 - apply_op(corr2, weights2, diag2))
    corr3 = column_solve(rhs3, coeffs)
    corr3 = corr3 + column_solve(rhs3 - apply_op(corr3, weights3, diag3), coeffs)
    corr2 = postsmooth(corr2 + refine(corr3), rhs2, weights2, diag2)
    corr1 = postsmooth(corr1 + refine(corr2), rhs1, weights1, diag1)
    return diag1 * corr1


PLANE = (32, 32)
SPLIT = (2, 4)
ROWS = 8
LANES = 128
HALO = 16
NEAR = 8
PIECE = 8
TINY = 1e-30
F32 = jnp.float32


def iota(shape, dim):
    return lax.broadcasted_iota(jnp.int32, shape, dim)


def dot01(field, chosen, dims=(((1,), (0,)), ((), ()))):
    total = None
    rest = field
    for part in range(3):
        piece = rest.astype(jnp.bfloat16)
        term = lax.dot_general(piece, chosen, dims, preferred_element_type=F32)
        total = term if total is None else total + term
        if part < 2:
            rest = rest - piece.astype(F32)
    return total


def dot10(chosen, field):
    total = None
    rest = field
    for part in range(3):
        piece = rest.astype(jnp.bfloat16)
        term = lax.dot_general(
            chosen, piece, (((1,), (1,)), ((), ())), preferred_element_type=F32
        )
        total = term if total is None else total + term
        if part < 2:
            rest = rest - piece.astype(F32)
    return total


def where01(condition):
    return jnp.where(condition, 1.0, 0.0).astype(jnp.bfloat16)


def loop(low, high, size, body):
    for plane in range(low, high, size):
        body(plane, min(size, high - plane))


def inverse_of(field):
    first = pl.reciprocal(field, approx=True)
    return first * (2.0 - field * first)


class Level:
    def __init__(self, level):
        self.ny = PLANE[1] >> level
        self.xs = 4 >> level
        self.factor = float(2**level)

    def masks(self, shape):
        lane = iota(shape, 2)
        row = iota(shape, 1)
        within = (lane // self.ny) % self.xs
        y = lane % self.ny
        last_x = (row == ROWS - 1) & (within == self.xs - 1)
        return within, y == self.ny - 1, last_x

    def next_x(self, field):
        within = (iota(field.shape, 2) // self.ny) % self.xs
        moved = pltpu.roll(field, LANES - self.ny, 2)
        return jnp.where(within == self.xs - 1, pltpu.roll(moved, ROWS - 1, 1), moved)

    def last_x(self, field):
        within = (iota(field.shape, 2) // self.ny) % self.xs
        moved = pltpu.roll(field, self.ny, 2)
        return jnp.where(within == 0, pltpu.roll(moved, 1, 1), moved)

    def next_y(self, field):
        return pltpu.roll(field, LANES - 1, 2)

    def last_y(self, field):
        return pltpu.roll(field, 1, 2)

    def spread(self, field, scaled, plane, count):
        mid = field[1:-1]
        near = (
            self.next_x(mid), self.last_x(mid), self.next_y(mid), self.last_y(mid),
            field[2:], field[:-2],
        )
        terms = [weight[pl.ds(plane, count)] * value for weight, value in zip(scaled, near)]
        return mid, ((terms[0] + terms[1]) + (terms[2] + terms[3])) + (terms[4] + terms[5])


def mean_of(fluid, near, factor):
    return ((factor * 2.0) * fluid * near) * inverse_of(jnp.maximum(fluid + near, TINY))


def set_level(level, low, high, fluid, pin, rhs, fields):
    scaled, start, diag = fields

    def body(plane, count):
        wide = fluid[pl.ds(plane - 1, count + 2)]
        mid = wide[1:-1]
        within, end_y, end_x = level.masks(mid.shape)
        to_x = jnp.where(end_x, 0.0, mean_of(mid, level.next_x(mid), level.factor))
        to_y = jnp.where(end_y, 0.0, mean_of(mid, level.next_y(mid), level.factor))
        to_z = mean_of(wide[:-1], wide[1:], level.factor)
        weights = (to_x, level.last_x(to_x), to_y, level.last_y(to_y), to_z[1:], to_z[:-1])
        total = (
            (weights[0] + weights[1])
            + (weights[2] + weights[3])
            + (weights[4] + weights[5])
            + pin[pl.ds(plane, count)]
        )
        gain = OMEGA * inverse_of(jnp.maximum(total, TINY))
        for target, weight in zip(scaled, weights):
            target[pl.ds(plane, count)] = gain * weight
        start[pl.ds(plane, count)] = gain * rhs[pl.ds(plane, count)]
        diag[pl.ds(plane, count)] = total

    loop(low, high, PIECE, body)


def sweep(level, low, high, fields, source, target):
    scaled, start, _ = fields

    def body(plane, count):
        mid, total = level.spread(source[pl.ds(plane - 1, count + 2)], scaled, plane, count)
        target[pl.ds(plane, count)] = (1.0 - OMEGA) * mid + (start[pl.ds(plane, count)] + total)

    loop(low, high, PIECE, body)


def pair_sum(field):
    half = field.reshape((field.shape[0] // 2, 2) + field.shape[1:])
    return half[:, 0] + half[:, 1]


def coarse_residual(level, low, high, fields, corr, target):
    scaled, start, diag = fields

    def body(plane, count):
        mid, total = level.spread(corr[pl.ds(plane - 1, count + 2)], scaled, plane, count)
        rest = (start[pl.ds(plane, count)] + total) - OMEGA * mid
        rest = rest * (diag[pl.ds(plane, count)] * (1.0 / OMEGA))
        target[pl.ds((plane - low) // 2, count // 2)] = pair_sum(rest)

    loop(low, high, PIECE, body)


def lanes_down(level):
    fine = iota((LANES, LANES), 0)
    coarse = iota((LANES, LANES), 1)
    ny, xs = PLANE[1] >> level, 4 >> level
    half = xs // 2
    same_x = ((fine // ny) % xs) // 2 == (coarse // (ny // 2)) % half
    same_y = (fine % ny) // 2 == coarse % (ny // 2)
    return where01((fine < ny * xs) & same_x & same_y)


def in_lanes(field, chosen):
    flat = field.reshape(field.shape[0] * ROWS, LANES)
    return dot01(flat, chosen).reshape(field.shape)


def peer_at(rank):
    ny = SPLIT[1]
    ix, place_on_row = rank // ny, rank % ny
    return ix * ny + (ny - 1 - place_on_row if ix % 2 else place_on_row)


def peer_of(group, rank):
    return peer_at(SPLIT[0] * SPLIT[1] - 1 - rank if group % 2 else rank)


def own_peer_of(rank):
    return jnp.where(lax.axis_index("gz") % 2 == 1, peer_of(1, rank), peer_of(0, rank))


def slab_of(ix, iy, group):
    nx, ny = SPLIT
    rank = ix * ny + jnp.where(ix % 2 == 1, ny - 1 - iy, iy)
    return group * nx * ny + jnp.where(group % 2 == 1, nx * ny - 1 - rank, rank)


def device_of(slab):
    nx, ny = SPLIT
    group, rank = slab // (nx * ny), slab % (nx * ny)
    rank = jnp.where(group % 2 == 1, nx * ny - 1 - rank, rank)
    row, column = rank // ny, rank % ny
    return group * nx * ny + row * ny + jnp.where(row % 2 == 1, ny - 1 - column, column)


def prepare_kernel(share, res_ref, fluid_ref, pin_ref, out_ref):
    bx, by, depth = fluid_ref.shape
    cells = bx * by
    groups = bx // 4
    pick = where01(iota((depth, 2 * depth), 1) // 2 == iota((depth, 2 * depth), 0))
    deep = lax.dot_general(
        pick, res_ref[...], (((1,), (1,)), ((), ())), preferred_element_type=F32
    )

    def lane_of(x, y):
        return (x % 4) * (groups * by) + (x // 4) * by + y

    fine = iota((4 * cells, cells), 0)
    lane = iota((4 * cells, cells), 1)
    chosen = where01(lane_of(fine // (4 * by), (fine % (2 * by)) // 2) == lane)
    rhs = dot01(deep, chosen)
    cell = iota((cells, cells), 0)
    lane = iota((cells, cells), 1)
    chosen = where01(lane_of(cell // by, cell % by) == lane)
    fluid = dot01(fluid_ref[...].reshape(cells, depth).T, chosen)
    pin = dot01(pin_ref[...].reshape(cells, depth).T, chosen)
    for rank in range(depth // share):
        peer, begin = own_peer_of(rank), rank * share
        for index, field in enumerate((fluid, rhs, pin)):
            out_ref[peer, index * share : (index + 1) * share] = field[begin : begin + share]


def spread_kernel(groups, by, gathered, own):
    for start in range(0, own.shape[0], ROWS):
        place(gathered, start, own, start, groups, by)


def place(gathered, row, target, plane, groups, by):
    group = (iota((ROWS, LANES), 1) // by) % groups
    nx, ny = SPLIT
    for ix in range(nx):
        found = [gathered[ix * ny + iy, pl.ds(row, ROWS), :] for iy in range(ny)]
        for part in range(groups):
            total = found[part]
            for iy in range(ny):
                if iy != part:
                    moved = pltpu.roll(found[iy], (by * (iy - part)) % LANES, 1)
                    total = jnp.where(group == iy, moved, total)
            target[pl.ds(plane, ROWS), ix * groups + part, :] = total


def down_kernel(
    groups, by, depth,
    low, own, high,
    xn1, xl1, yn1, yl1, zn1, zl1, start1, diag1, corr1,
    xn2, xl2, yn2, yl2, zn2, zl2, start2, diag2, corr2,
    packed,
    fluid1, rhs1, pin1, other1, fluid2, rhs2, pin2, other2, sums,
):
    planes = depth + 2 * HALO
    for index, target in enumerate((fluid1, rhs1, pin1)):
        start = 0
        for piece in (low, own, high):
            count = piece.shape[0] // 3
            target[start : start + count] = piece[index * count : (index + 1) * count]
            start += count

    fine, coarse = Level(0), Level(1)
    down1, down2 = lanes_down(0), lanes_down(1)
    fields1 = ((xn1, xl1, yn1, yl1, zn1, zl1), start1, diag1)
    fields2 = ((xn2, xl2, yn2, yl2, zn2, zl2), start2, diag2)
    set_level(fine, 1, planes - 1, fluid1, pin1, rhs1, fields1)
    sweep(fine, 2, planes - 2, fields1, start1, other1)
    sweep(fine, 3, planes - 3, fields1, other1, corr1)
    count2 = depth // 2 + 2 * NEAR
    begin = HALO - 2 * NEAR
    for source, target, share in ((fluid1, fluid2, 8.0), (pin1, pin2, 4.0)):
        whole = pair_sum(source[begin : begin + 2 * count2])
        target[...] = in_lanes(whole, down1) * (1.0 / share)
    low2, high2 = (begin + 4) // 2, count2 - (begin + 4) // 2
    inner = high2 - low2
    coarse_residual(fine, begin + 2 * low2, begin + 2 * high2, fields1, corr1, sums)
    rhs2[low2:high2] = in_lanes(sums[0:inner], down1)
    set_level(coarse, low2, high2, fluid2, pin2, rhs2, fields2)
    sweep(coarse, low2 + 1, high2 - 1, fields2, start2, other2)
    sweep(coarse, low2 + 2, high2 - 2, fields2, other2, corr2)
    coarse_residual(coarse, NEAR, NEAR + depth // 2, fields2, corr2, sums)
    count3 = depth // 4
    rhs3 = in_lanes(sums[0:count3], down2)
    fluid3 = in_lanes(pair_sum(fluid2[NEAR : NEAR + 2 * count3]), down2) * 0.125
    pin3 = in_lanes(pair_sum(pin2[NEAR : NEAR + 2 * count3]), down2) * 0.25
    lane = iota((count3, LANES), 1) // ROWS
    first = jnp.zeros((count3, LANES), F32)
    second = jnp.zeros((count3, LANES), F32)
    for row in range(ROWS):
        first = jnp.where(lane == row, rhs3[:, row, :], first)
        first = jnp.where(lane == ROWS + row, fluid3[:, row, :], first)
        second = jnp.where(lane % ROWS == row, pin3[:, row, :], second)
    packed[0] = first[0:2]
    packed[1] = first[2:4]
    packed[2] = jnp.where(lane[0:2] < ROWS, second[0:2], second[2:4])
    lane = iota((1, LANES), 1) // (LANES // 4)
    for index, plane in enumerate((NEAR + depth // 2 - 5, NEAR + 4)):
        for half in range(2):
            row = jnp.zeros((1, LANES), F32)
            for quarter in range(4):
                at = half * 4 + quarter
                row = jnp.where(lane == quarter, corr2[plane, at : at + 1, :], row)
            packed[3 + index, half : half + 1, :] = row


def rolled(field, shift):
    count = field.shape[0]
    shift %= count
    if shift % ROWS:
        return pltpu.roll(field, shift, 0)
    return jnp.concatenate([field[count - shift :], field[: count - shift]], axis=0)


def columns(rhs, fluid, pin):
    depth = fluid.shape[0]
    z, lane = iota(fluid.shape, 0), iota(fluid.shape, 1)
    y, x = lane % ROWS, (lane // ROWS) % ROWS

    def next_x(field):
        return pltpu.roll(field, LANES - ROWS, 1)

    def next_y(field):
        return pltpu.roll(field, LANES - 1, 1)

    wz = jnp.where(z == depth - 1, 0.0, mean_of(fluid, rolled(fluid, -1), 4.0))
    wy = jnp.where(y == ROWS - 1, 0.0, mean_of(fluid, next_y(fluid), 4.0))
    wx = jnp.where(x == ROWS - 1, 0.0, mean_of(fluid, next_x(fluid), 4.0))
    across = (wx + pltpu.roll(wx, ROWS, 1)) + (wy + pltpu.roll(wy, 1, 1)) + pin
    share = 1.0 / jnp.sum(across, axis=0, keepdims=True)

    above, below, own = rolled(wz, 1), wz, across
    steps = []
    stride = 1
    while stride < depth:
        inverse = inverse_of(above + below + own)
        up = above * rolled(inverse, stride)
        down = below * rolled(inverse, -stride)
        own = own + up * rolled(own, stride) + down * rolled(own, -stride)
        above = up * rolled(above, stride)
        below = down * rolled(below, -stride)
        steps.append((stride, up, down))
        stride *= 2
    inverse = inverse_of(above + below + own)

    def solve(right):
        mean = jnp.sum(right, axis=0, keepdims=True) * share
        for stride, up, down in steps:
            right = right + up * rolled(right, stride) + down * rolled(right, -stride)
        return right * inverse + mean

    corr = solve(rhs)
    flow_x = wx * (next_x(corr) - corr)
    flow_y = wy * (next_y(corr) - corr)
    flow_z = wz * (rolled(corr, -1) - corr)
    rest = (
        (rhs - pin * corr)
        + (flow_x - pltpu.roll(flow_x, ROWS, 1))
        + (flow_y - pltpu.roll(flow_y, 1, 1))
        + (flow_z - rolled(flow_z, 1))
    )
    return corr + solve(rest)


def up_kernel(
    groups, by, depth,
    packed,
    xn1, xl1, yn1, yl1, zn1, zl1, start1, diag1, corr1,
    xn2, xl2, yn2, yl2, zn2, zl2, start2, diag2, corr2,
    out_ref,
    one1, two1, one2, two2, lifted, first, second, solved,
):
    count3 = depth // 4
    shares = packed.shape[0]
    peers = SPLIT[0] * SPLIT[1]
    for slab in range(shares):
        index = slab // peers * peers + peer_of(slab // peers, slab % peers)
        row = slab * count3
        first[row : row + 2] = packed[index, 0]
        first[row + 2 : row + 4] = packed[index, 1]
        both = packed[index, 2]
        second[row : row + 2] = both
        second[row + 2 : row + 4] = pltpu.roll(both, LANES // 2, 1)
    half = iota((shares * count3, LANES), 1) < LANES // 2

    def low_half(field):
        return jnp.where(half, field, pltpu.roll(field, LANES // 2, 1))

    def high_half(field):
        return jnp.where(half, pltpu.roll(field, LANES // 2, 1), field)

    solved[NEAR : NEAR + shares * count3] = columns(
        low_half(first[...]), high_half(first[...]), low_half(second[...])
    )
    solved[0:NEAR] = jnp.zeros((NEAR, LANES), F32)
    solved[NEAR + shares * count3 :] = jnp.zeros((2 * NEAR, LANES), F32)

    nx, ny = SPLIT
    part = slab_of(lax.axis_index("gx"), lax.axis_index("gy"), lax.axis_index("gz"))
    count = count3 + 2 * NEAR
    tall = solved[pl.ds(part * count3, count + count3), :]
    fine, coarse = Level(0), Level(1)
    cell = iota((LANES, ROWS * LANES), 0)
    lane = iota((LANES, ROWS * LANES), 1)
    same_y = cell % ROWS == (lane % coarse.ny) // 2
    spread = where01((cell // ROWS == lane // LANES) & same_y)
    wide = dot01(tall, spread)
    for row in range(ROWS):
        lifted[0:count, row, :] = wide[:count, row * LANES : (row + 1) * LANES]

    fields1 = ((xn1, xl1, yn1, yl1, zn1, zl1), start1, diag1)
    fields2 = ((xn2, xl2, yn2, yl2, zn2, zl2), start2, diag2)
    low, high = NEAR - 4, NEAR + depth // 2 + 4
    parents = lifted[low // 2 + NEAR // 2 : high // 2 + NEAR // 2]
    twice = jnp.broadcast_to(parents[:, None], (parents.shape[0], 2, ROWS, LANES))
    reach = depth // 2 + NEAR
    quarter = iota((ROWS, LANES), 1) // (LANES // 4)
    row = iota((ROWS, LANES), 0)

    def unpacked(index, which):
        pair = packed[device_of(jnp.clip(index, 0, shares - 1)), which]
        total = None
        for shift in range(4):
            moved = pltpu.roll(pair, shift * (LANES // 4), 1)
            wide = jnp.where(row < 4, moved[0:1, :], moved[1:2, :])
            kept = jnp.where((quarter - shift) % 4 == row % 4, wide, 0.0)
            total = kept if total is None else total + kept
        return total

    before, after = unpacked(part - 1, 3), unpacked(part + 1, 4)
    one2[low - 1] = before + lifted[(low - 1) // 2 + NEAR // 2]
    one2[low:high] = corr2[low:high] + twice.reshape(high - low, ROWS, LANES)
    one2[high] = after + lifted[high // 2 + NEAR // 2]
    sweep(coarse, NEAR - 4, reach + 4, fields2, one2, two2)
    sweep(coarse, NEAR - 3, reach + 3, fields2, two2, one2)
    sweep(coarse, NEAR - 2, reach + 2, fields2, one2, two2)

    fine_lane, coarse_lane = iota((LANES, LANES), 1), iota((LANES, LANES), 0)
    x_of = (fine_lane // fine.ny) // 2
    y_of = (fine_lane % fine.ny) // 2
    up = where01(coarse_lane == x_of * coarse.ny + y_of)
    lifted[0 : depth // 2 + 4] = in_lanes(two2[NEAR - 2 : reach + 2], up)
    parents = lifted[0 : depth // 2 + 4]
    twice = jnp.broadcast_to(parents[:, None], (parents.shape[0], 2, ROWS, LANES))
    low, high = HALO - 4, HALO + depth + 4
    one1[low:high] = corr1[low:high] + twice.reshape(high - low, ROWS, LANES)
    reach = depth + HALO
    sweep(fine, HALO - 2, reach + 2, fields1, one1, two1)
    sweep(fine, HALO - 1, reach + 1, fields1, two1, one1)
    sweep(fine, HALO, reach, fields1, one1, two1)

    group = (iota((depth, LANES), 1) // by) % groups
    for ix in range(nx):
        scaled = [
            two1[HALO:reach, ix * groups + part, :] * diag1[HALO:reach, ix * groups + part, :]
            for part in range(groups)
        ]
        for iy in range(ny):
            total = scaled[iy]
            for part in range(groups):
                if part != iy:
                    moved = pltpu.roll(scaled[part], (by * (part - iy)) % LANES, 1)
                    total = jnp.where(group == part, moved, total)
            out_ref[ix * ny + iy] = total


def finish_kernel(blocks, out_ref):
    bx, by, depth = out_ref.shape
    cells = bx * by
    cell = iota((cells, cells), 0)
    lane = iota((cells, cells), 1)
    x, y = cell // by, cell % by
    chosen = where01((x % 4) * (bx // 4 * by) + (x // 4) * by + y == lane)
    peers = blocks.shape[0]
    ordered = jnp.concatenate([blocks[own_peer_of(rank)] for rank in range(peers)], axis=0)
    out_ref[...] = dot10(chosen, ordered).reshape(out_ref.shape)


def whole_planes(residual_q2, viscosity, pinned):
    bx, by, depth = viscosity.shape
    groups = bx // 4
    peers = SPLIT[0] * SPLIT[1]
    share = depth // peers
    planes = share + 2 * HALO
    count2 = share // 2 + 2 * NEAR
    limit = pltpu.CompilerParams(vmem_limit_bytes=32 * 2**20)

    def flat(rows):
        return jax.ShapeDtypeStruct((rows, LANES), F32)

    def blocks(count, rows):
        return jax.ShapeDtypeStruct((count, rows, LANES), F32)

    def room(count):
        return pltpu.VMEM((count, ROWS, LANES), F32)

    fluid = 1.0 / viscosity
    pin = 4.0 * pinned.astype(F32) * fluid
    parcels = pl.pallas_call(
        functools.partial(prepare_kernel, share),
        out_shape=blocks(peers, 3 * share),
        compiler_params=limit,
        name="prepare",
    )(residual_q2.reshape(4 * bx * by, 2 * depth), fluid, pin)
    own = pl.pallas_call(
        functools.partial(spread_kernel, groups, by),
        out_shape=blocks(3 * share, ROWS),
        compiler_params=limit,
        name="spread",
    )(lax.all_to_all(parcels, ("gx", "gy"), 0, 0, tiled=True))
    length = lax.axis_size("gz")
    parts = length * peers

    def step(field, ahead):
        device = [peer_of(i // peers, i % peers) * length + i // peers for i in range(parts)]
        pairs = [(device[i], device[i + ahead]) for i in range(parts) if 0 <= i + ahead < parts]
        return lax.ppermute(field, ("gx", "gy", "gz"), pairs)

    low, high = step(own, 1), step(own, -1)
    saved = (blocks(planes, ROWS),) * 9 + (blocks(count2, ROWS),) * 9
    results = pl.pallas_call(
        functools.partial(down_kernel, groups, by, share),
        out_shape=saved + (blocks(5, 2),),
        scratch_shapes=[room(planes)] * 4 + [room(count2)] * 5,
        compiler_params=limit,
        name="down",
    )(low, own, high)
    copies = jnp.broadcast_to(results[-1], (parts,) + results[-1].shape)
    packed = lax.all_to_all(copies, ("gz", "gx", "gy"), 0, 0, tiled=True)
    depth3 = parts * share // 4
    mine = pl.pallas_call(
        functools.partial(up_kernel, groups, by, share),
        out_shape=blocks(peers, share),
        scratch_shapes=[room(planes), room(planes), room(count2), room(count2), room(count2)]
        + [pltpu.VMEM((rows, LANES), F32) for rows in (depth3, depth3, depth3 + 3 * NEAR)],
        compiler_params=limit,
        name="up",
    )(packed, *results[:-1])
    return pl.pallas_call(
        finish_kernel,
        out_shape=jax.ShapeDtypeStruct((bx, by, depth), F32),
        compiler_params=limit,
        name="finish",
    )(lax.all_to_all(mine, ("gx", "gy"), 0, 0, tiled=True))


def one_tile_planes(mesh, viscosity):
    split = (mesh.shape["gx"], mesh.shape["gy"])
    depth = viscosity.shape[2]
    fits = viscosity.shape[:2] == PLANE and split == SPLIT
    return fits and depth == 4 * LANES and depth // mesh.shape["gz"] == LANES


def solution(mesh):
    placed = (P("gx", "gy", "gz"), P("gx", "gy", "gz"), P("gx", "gy", "gz"))

    def cycle(residual_q2, viscosity, pinned):
        chosen = whole_planes if one_tile_planes(mesh, viscosity) else per_device
        return jax.shard_map(
            chosen, mesh=mesh, in_specs=placed, out_specs=P("gx", "gy", "gz"), check_vma=False
        )(residual_q2, viscosity, pinned)

    return cycle
```

```python
import functools

import jax
import jax.numpy as jnp
from jax import lax
from jax.experimental import pallas as pl
from jax.experimental.pallas import tpu as pltpu
from jax.sharding import PartitionSpec as P

NU = 3


OMEGA = 0.6


def with_halo(block, sides, width):
    for axis, dim in sides:
        count = lax.axis_size(axis)
        forward = [(i, i + 1) for i in range(count - 1)]
        backward = [(target, source) for source, target in forward]
        low = lax.ppermute(
            lax.slice_in_dim(block, block.shape[dim] - width, None, axis=dim), axis, forward
        )
        high = lax.ppermute(lax.slice_in_dim(block, 0, width, axis=dim), axis, backward)
        block = jnp.concatenate([low, block, high], axis=dim)
    return block


def coarsen(x):
    a, b, c = x.shape
    return x.reshape(a // 2, 2, b // 2, 2, c // 2, 2).sum(axis=(1, 3, 5))


def refine(x):
    return jnp.repeat(jnp.repeat(jnp.repeat(x, 2, 0), 2, 1), 2, 2)


def extended(field):
    return with_halo(field, (("gx", 0), ("gy", 1), ("gz", 2)), 1)


def shifted(padded):
    return [
        padded[2:, 1:-1, 1:-1],
        padded[:-2, 1:-1, 1:-1],
        padded[1:-1, 2:, 1:-1],
        padded[1:-1, :-2, 1:-1],
        padded[1:-1, 1:-1, 2:],
        padded[1:-1, 1:-1, :-2],
    ]


def neighbours(field):
    return shifted(extended(field))


def harmonic(fluid, near, factor):
    total = fluid + near
    return jnp.where(total > 0, factor * 2.0 * fluid * near / jnp.where(total > 0, total, 1.0), 0.0)


def couplings(fluid, factor):
    return [harmonic(fluid, near, factor) for near in neighbours(fluid)]


def apply_op(field, weights, diag):
    total = diag * field
    for weight, near in zip(weights, neighbours(field)):
        total = total - weight * near
    return total


def presmooth(rhs, weights, diag):
    corr = OMEGA * rhs / diag
    for sweep in range(NU - 1):
        corr = corr + OMEGA * (rhs - apply_op(corr, weights, diag)) / diag
    return corr


def postsmooth(corr, rhs, weights, diag):
    for sweep in range(NU):
        corr = corr + OMEGA * (rhs - apply_op(corr, weights, diag)) / diag
    return corr


def tridiag(coeffs, rhs):
    solved = lax.linalg.tridiagonal_solve(coeffs[0], coeffs[1], coeffs[2], rhs[..., None])[..., 0]
    last = rhs.ndim - 1
    shift_col = jnp.sum(rhs, axis=last, keepdims=True) / jnp.sum(
        coeffs[3], axis=last, keepdims=True
    )
    return solved + shift_col


def prepare_columns(weights, diag):
    lower = -weights[5]
    upper = -weights[4]
    across = diag + lower + upper
    return (
        lax.all_gather(lower, "gz", axis=2, tiled=True),
        lax.all_gather(diag, "gz", axis=2, tiled=True),
        lax.all_gather(upper, "gz", axis=2, tiled=True),
        lax.all_gather(across, "gz", axis=2, tiled=True),
    )


def column_solve(rhs, coeffs):
    depth = rhs.shape[2]
    whole = lax.all_gather(rhs, "gz", axis=2, tiled=True)
    solved = tridiag(coeffs, whole)
    return lax.dynamic_slice_in_dim(solved, lax.axis_index("gz") * depth, depth, 2)


def per_device(residual_q2, viscosity, pinned):
    fluid1 = 1.0 / viscosity
    pin1 = 4.0 * pinned.astype(jnp.float32) * fluid1
    rhs1 = coarsen(residual_q2.astype(jnp.float32))
    fluid2 = coarsen(fluid1) / 8.0
    pin2 = coarsen(pin1) / 4.0
    fluid3 = coarsen(fluid2) / 8.0
    pin3 = coarsen(pin2) / 4.0
    weights1 = couplings(fluid1, 1.0)
    weights2 = couplings(fluid2, 2.0)
    weights3 = couplings(fluid3, 4.0)
    diag1 = sum(weights1) + pin1
    diag2 = sum(weights2) + pin2
    diag3 = sum(weights3) + pin3
    coeffs = prepare_columns(weights3, diag3)
    corr1 = presmooth(rhs1, weights1, diag1)
    rhs2 = coarsen(rhs1 - apply_op(corr1, weights1, diag1))
    corr2 = presmooth(rhs2, weights2, diag2)
    rhs3 = coarsen(rhs2 - apply_op(corr2, weights2, diag2))
    corr3 = column_solve(rhs3, coeffs)
    corr3 = corr3 + column_solve(rhs3 - apply_op(corr3, weights3, diag3), coeffs)
    corr2 = postsmooth(corr2 + refine(corr3), rhs2, weights2, diag2)
    corr1 = postsmooth(corr1 + refine(corr2), rhs1, weights1, diag1)
    return diag1 * corr1


PLANE = (32, 32)
SPLIT = (2, 4)
ROWS = 8
LANES = 128
HALO = 16
NEAR = 8
PIECE = 8
TINY = 1e-30
F32 = jnp.float32


def iota(shape, dim):
    return lax.broadcasted_iota(jnp.int32, shape, dim)


def dot01(field, chosen, dims=(((1,), (0,)), ((), ()))):
    total = None
    rest = field
    for part in range(3):
        piece = rest.astype(jnp.bfloat16)
        term = lax.dot_general(piece, chosen, dims, preferred_element_type=F32)
        total = term if total is None else total + term
        if part < 2:
            rest = rest - piece.astype(F32)
    return total


def dot10(chosen, field):
    total = None
    rest = field
    for part in range(3):
        piece = rest.astype(jnp.bfloat16)
        term = lax.dot_general(
            chosen, piece, (((1,), (1,)), ((), ())), preferred_element_type=F32
        )
        total = term if total is None else total + term
        if part < 2:
            rest = rest - piece.astype(F32)
    return total


def where01(condition):
    return jnp.where(condition, 1.0, 0.0).astype(jnp.bfloat16)


def loop(low, high, size, body):
    for plane in range(low, high, size):
        body(plane, min(size, high - plane))


def inverse_of(field):
    first = pl.reciprocal(field, approx=True)
    return first * (2.0 - field * first)


class Level:
    def __init__(self, level):
        self.ny = PLANE[1] >> level
        self.xs = 4 >> level
        self.factor = float(2**level)

    def masks(self, shape):
        lane = iota(shape, 2)
        row = iota(shape, 1)
        within = (lane // self.ny) % self.xs
        y = lane % self.ny
        last_x = (row == ROWS - 1) & (within == self.xs - 1)
        return within, y == self.ny - 1, last_x

    def next_x(self, field):
        within = (iota(field.shape, 2) // self.ny) % self.xs
        moved = pltpu.roll(field, LANES - self.ny, 2)
        return jnp.where(within == self.xs - 1, pltpu.roll(moved, ROWS - 1, 1), moved)

    def last_x(self, field):
        within = (iota(field.shape, 2) // self.ny) % self.xs
        moved = pltpu.roll(field, self.ny, 2)
        return jnp.where(within == 0, pltpu.roll(moved, 1, 1), moved)

    def next_y(self, field):
        return pltpu.roll(field, LANES - 1, 2)

    def last_y(self, field):
        return pltpu.roll(field, 1, 2)

    def spread(self, field, scaled, plane, count):
        mid = field[1:-1]
        near = (
            self.next_x(mid), self.last_x(mid), self.next_y(mid), self.last_y(mid),
            field[2:], field[:-2],
        )
        terms = [weight[pl.ds(plane, count)] * value for weight, value in zip(scaled, near)]
        return mid, ((terms[0] + terms[1]) + (terms[2] + terms[3])) + (terms[4] + terms[5])


def mean_of(fluid, near, factor):
    return ((factor * 2.0) * fluid * near) * inverse_of(jnp.maximum(fluid + near, TINY))


def set_level(level, low, high, fluid, pin, rhs, fields):
    scaled, start, diag = fields

    def body(plane, count):
        wide = fluid[pl.ds(plane - 1, count + 2)]
        mid = wide[1:-1]
        within, end_y, end_x = level.masks(mid.shape)
        to_x = jnp.where(end_x, 0.0, mean_of(mid, level.next_x(mid), level.factor))
        to_y = jnp.where(end_y, 0.0, mean_of(mid, level.next_y(mid), level.factor))
        to_z = mean_of(wide[:-1], wide[1:], level.factor)
        weights = (to_x, level.last_x(to_x), to_y, level.last_y(to_y), to_z[1:], to_z[:-1])
        total = (
            (weights[0] + weights[1])
            + (weights[2] + weights[3])
            + (weights[4] + weights[5])
            + pin[pl.ds(plane, count)]
        )
        gain = OMEGA * inverse_of(jnp.maximum(total, TINY))
        for target, weight in zip(scaled, weights):
            target[pl.ds(plane, count)] = gain * weight
        start[pl.ds(plane, count)] = gain * rhs[pl.ds(plane, count)]
        diag[pl.ds(plane, count)] = total

    loop(low, high, PIECE, body)


def sweep(level, low, high, fields, source, target):
    scaled, start, _ = fields

    def body(plane, count):
        mid, total = level.spread(source[pl.ds(plane - 1, count + 2)], scaled, plane, count)
        target[pl.ds(plane, count)] = (1.0 - OMEGA) * mid + (start[pl.ds(plane, count)] + total)

    loop(low, high, PIECE, body)


def pair_sum(field):
    half = field.reshape((field.shape[0] // 2, 2) + field.shape[1:])
    return half[:, 0] + half[:, 1]


def coarse_residual(level, low, high, fields, corr, target):
    scaled, start, diag = fields

    def body(plane, count):
        mid, total = level.spread(corr[pl.ds(plane - 1, count + 2)], scaled, plane, count)
        rest = (start[pl.ds(plane, count)] + total) - OMEGA * mid
        rest = rest * (diag[pl.ds(plane, count)] * (1.0 / OMEGA))
        target[pl.ds((plane - low) // 2, count // 2)] = pair_sum(rest)

    loop(low, high, PIECE, body)


def lanes_down(level):
    fine = iota((LANES, LANES), 0)
    coarse = iota((LANES, LANES), 1)
    ny, xs = PLANE[1] >> level, 4 >> level
    half = xs // 2
    same_x = ((fine // ny) % xs) // 2 == (coarse // (ny // 2)) % half
    same_y = (fine % ny) // 2 == coarse % (ny // 2)
    return where01((fine < ny * xs) & same_x & same_y)


def in_lanes(field, chosen):
    flat = field.reshape(field.shape[0] * ROWS, LANES)
    return dot01(flat, chosen).reshape(field.shape)


def peer_at(rank):
    ny = SPLIT[1]
    ix, place_on_row = rank // ny, rank % ny
    return ix * ny + (ny - 1 - place_on_row if ix % 2 else place_on_row)


def peer_of(group, rank):
    return peer_at(SPLIT[0] * SPLIT[1] - 1 - rank if group % 2 else rank)


def own_peer_of(rank):
    return jnp.where(lax.axis_index("gz") % 2 == 1, peer_of(1, rank), peer_of(0, rank))


def slab_of(ix, iy, group):
    nx, ny = SPLIT
    rank = ix * ny + jnp.where(ix % 2 == 1, ny - 1 - iy, iy)
    return group * nx * ny + jnp.where(group % 2 == 1, nx * ny - 1 - rank, rank)


def device_of(slab):
    nx, ny = SPLIT
    group, rank = slab // (nx * ny), slab % (nx * ny)
    rank = jnp.where(group % 2 == 1, nx * ny - 1 - rank, rank)
    row, column = rank // ny, rank % ny
    return group * nx * ny + row * ny + jnp.where(row % 2 == 1, ny - 1 - column, column)


def prepare_kernel(share, res_ref, fluid_ref, pin_ref, out_ref):
    bx, by, depth = fluid_ref.shape
    cells = bx * by
    groups = bx // 4
    pick = where01(iota((depth, 2 * depth), 1) // 2 == iota((depth, 2 * depth), 0))
    deep = lax.dot_general(
        pick, res_ref[...], (((1,), (1,)), ((), ())), preferred_element_type=F32
    )

    def lane_of(x, y):
        return (x % 4) * (groups * by) + (x // 4) * by + y

    fine = iota((4 * cells, cells), 0)
    lane = iota((4 * cells, cells), 1)
    chosen = where01(lane_of(fine // (4 * by), (fine % (2 * by)) // 2) == lane)
    rhs = dot01(deep, chosen)
    cell = iota((cells, cells), 0)
    lane = iota((cells, cells), 1)
    chosen = where01(lane_of(cell // by, cell % by) == lane)
    fluid = dot01(fluid_ref[...].reshape(cells, depth).T, chosen)
    pin = dot01(pin_ref[...].reshape(cells, depth).T, chosen)
    for rank in range(depth // share):
        peer, begin = own_peer_of(rank), rank * share
        for index, field in enumerate((fluid, rhs, pin)):
            out_ref[peer, index * share : (index + 1) * share] = field[begin : begin + share]


def spread_kernel(groups, by, gathered, own):
    for start in range(0, own.shape[0], ROWS):
        place(gathered, start, own, start, groups, by)


def place(gathered, row, target, plane, groups, by):
    group = (iota((ROWS, LANES), 1) // by) % groups
    nx, ny = SPLIT
    for ix in range(nx):
        found = [gathered[ix * ny + iy, pl.ds(row, ROWS), :] for iy in range(ny)]
        for part in range(groups):
            total = found[part]
            for iy in range(ny):
                if iy != part:
                    moved = pltpu.roll(found[iy], (by * (iy - part)) % LANES, 1)
                    total = jnp.where(group == iy, moved, total)
            target[pl.ds(plane, ROWS), ix * groups + part, :] = total


def down_kernel(
    groups, by, depth,
    own, inner, outer,
    xn1, xl1, yn1, yl1, zn1, zl1, start1, diag1, corr1,
    xn2, xl2, yn2, yl2, zn2, zl2, start2, diag2, corr2,
    packed,
    fluid1, rhs1, pin1, other1, fluid2, rhs2, pin2, other2, sums,
):
    planes = depth + 2 * HALO
    part = slab_of(lax.axis_index("gx"), lax.axis_index("gy"), lax.axis_index("gz"))
    odd = part % 2 == 1
    for index, target in enumerate((fluid1, rhs1, pin1)):
        rows = slice(index * depth, (index + 1) * depth)
        target[0:HALO] = jnp.where(odd, inner[rows], outer[rows])
        target[HALO : HALO + depth] = own[rows]
        target[HALO + depth :] = jnp.where(odd, outer[rows], inner[rows])

    fine, coarse = Level(0), Level(1)
    down1, down2 = lanes_down(0), lanes_down(1)
    fields1 = ((xn1, xl1, yn1, yl1, zn1, zl1), start1, diag1)
    fields2 = ((xn2, xl2, yn2, yl2, zn2, zl2), start2, diag2)
    set_level(fine, 1, planes - 1, fluid1, pin1, rhs1, fields1)
    sweep(fine, 2, planes - 2, fields1, start1, other1)
    sweep(fine, 3, planes - 3, fields1, other1, corr1)
    count2 = depth // 2 + 2 * NEAR
    begin = HALO - 2 * NEAR
    for source, target, share in ((fluid1, fluid2, 8.0), (pin1, pin2, 4.0)):
        whole = pair_sum(source[begin : begin + 2 * count2])
        target[...] = in_lanes(whole, down1) * (1.0 / share)
    low2, high2 = (begin + 4) // 2, count2 - (begin + 4) // 2
    inner = high2 - low2
    coarse_residual(fine, begin + 2 * low2, begin + 2 * high2, fields1, corr1, sums)
    rhs2[low2:high2] = in_lanes(sums[0:inner], down1)
    set_level(coarse, low2, high2, fluid2, pin2, rhs2, fields2)
    sweep(coarse, low2 + 1, high2 - 1, fields2, start2, other2)
    sweep(coarse, low2 + 2, high2 - 2, fields2, other2, corr2)
    coarse_residual(coarse, NEAR, NEAR + depth // 2, fields2, corr2, sums)
    count3 = depth // 4
    rhs3 = in_lanes(sums[0:count3], down2)
    fluid3 = in_lanes(pair_sum(fluid2[NEAR : NEAR + 2 * count3]), down2) * 0.125
    pin3 = in_lanes(pair_sum(pin2[NEAR : NEAR + 2 * count3]), down2) * 0.25
    lane = iota((count3, LANES), 1) // ROWS
    first = jnp.zeros((count3, LANES), F32)
    second = jnp.zeros((count3, LANES), F32)
    for row in range(ROWS):
        first = jnp.where(lane == row, rhs3[:, row, :], first)
        first = jnp.where(lane == ROWS + row, fluid3[:, row, :], first)
        second = jnp.where(lane % ROWS == row, pin3[:, row, :], second)
    packed[0] = first[0:2]
    packed[1] = first[2:4]
    packed[2] = jnp.where(lane[0:2] < ROWS, second[0:2], second[2:4])
    lane = iota((1, LANES), 1) // (LANES // 4)
    for index, plane in enumerate((NEAR + depth // 2 - 5, NEAR + 4)):
        for half in range(2):
            row = jnp.zeros((1, LANES), F32)
            for quarter in range(4):
                at = half * 4 + quarter
                row = jnp.where(lane == quarter, corr2[plane, at : at + 1, :], row)
            packed[3 + index, half : half + 1, :] = row


def rolled(field, shift):
    count = field.shape[0]
    shift %= count
    if shift % ROWS:
        return pltpu.roll(field, shift, 0)
    return jnp.concatenate([field[count - shift :], field[: count - shift]], axis=0)


def columns(rhs, fluid, pin):
    depth = fluid.shape[0]
    z, lane = iota(fluid.shape, 0), iota(fluid.shape, 1)
    y, x = lane % ROWS, (lane // ROWS) % ROWS

    def next_x(field):
        return pltpu.roll(field, LANES - ROWS, 1)

    def next_y(field):
        return pltpu.roll(field, LANES - 1, 1)

    wz = jnp.where(z == depth - 1, 0.0, mean_of(fluid, rolled(fluid, -1), 4.0))
    wy = jnp.where(y == ROWS - 1, 0.0, mean_of(fluid, next_y(fluid), 4.0))
    wx = jnp.where(x == ROWS - 1, 0.0, mean_of(fluid, next_x(fluid), 4.0))
    across = (wx + pltpu.roll(wx, ROWS, 1)) + (wy + pltpu.roll(wy, 1, 1)) + pin
    share = 1.0 / jnp.sum(across, axis=0, keepdims=True)

    above, below, own = rolled(wz, 1), wz, across
    steps = []
    stride = 1
    while stride < depth:
        inverse = inverse_of(above + below + own)
        up = above * rolled(inverse, stride)
        down = below * rolled(inverse, -stride)
        own = own + up * rolled(own, stride) + down * rolled(own, -stride)
        above = up * rolled(above, stride)
        below = down * rolled(below, -stride)
        steps.append((stride, up, down))
        stride *= 2
    inverse = inverse_of(above + below + own)

    def solve(right):
        mean = jnp.sum(right, axis=0, keepdims=True) * share
        for stride, up, down in steps:
            right = right + up * rolled(right, stride) + down * rolled(right, -stride)
        return right * inverse + mean

    corr = solve(rhs)
    flow_x = wx * (next_x(corr) - corr)
    flow_y = wy * (next_y(corr) - corr)
    flow_z = wz * (rolled(corr, -1) - corr)
    rest = (
        (rhs - pin * corr)
        + (flow_x - pltpu.roll(flow_x, ROWS, 1))
        + (flow_y - pltpu.roll(flow_y, 1, 1))
        + (flow_z - rolled(flow_z, 1))
    )
    return corr + solve(rest)


def up_kernel(
    groups, by, depth,
    packed,
    xn1, xl1, yn1, yl1, zn1, zl1, start1, diag1, corr1,
    xn2, xl2, yn2, yl2, zn2, zl2, start2, diag2, corr2,
    out_ref,
    one1, two1, one2, two2, lifted, first, second, solved,
):
    count3 = depth // 4
    shares = packed.shape[0]
    peers = SPLIT[0] * SPLIT[1]
    for slab in range(shares):
        index = slab // peers * peers + peer_of(slab // peers, slab % peers)
        row = slab * count3
        first[row : row + 2] = packed[index, 0]
        first[row + 2 : row + 4] = packed[index, 1]
        both = packed[index, 2]
        second[row : row + 2] = both
        second[row + 2 : row + 4] = pltpu.roll(both, LANES // 2, 1)
    half = iota((shares * count3, LANES), 1) < LANES // 2

    def low_half(field):
        return jnp.where(half, field, pltpu.roll(field, LANES // 2, 1))

    def high_half(field):
        return jnp.where(half, pltpu.roll(field, LANES // 2, 1), field)

    solved[NEAR : NEAR + shares * count3] = columns(
        low_half(first[...]), high_half(first[...]), low_half(second[...])
    )
    solved[0:NEAR] = jnp.zeros((NEAR, LANES), F32)
    solved[NEAR + shares * count3 :] = jnp.zeros((2 * NEAR, LANES), F32)

    nx, ny = SPLIT
    part = slab_of(lax.axis_index("gx"), lax.axis_index("gy"), lax.axis_index("gz"))
    count = count3 + 2 * NEAR
    tall = solved[pl.ds(part * count3, count + count3), :]
    fine, coarse = Level(0), Level(1)
    cell = iota((LANES, ROWS * LANES), 0)
    lane = iota((LANES, ROWS * LANES), 1)
    same_y = cell % ROWS == (lane % coarse.ny) // 2
    spread = where01((cell // ROWS == lane // LANES) & same_y)
    wide = dot01(tall, spread)
    for row in range(ROWS):
        lifted[0:count, row, :] = wide[:count, row * LANES : (row + 1) * LANES]

    fields1 = ((xn1, xl1, yn1, yl1, zn1, zl1), start1, diag1)
    fields2 = ((xn2, xl2, yn2, yl2, zn2, zl2), start2, diag2)
    low, high = NEAR - 4, NEAR + depth // 2 + 4
    parents = lifted[low // 2 + NEAR // 2 : high // 2 + NEAR // 2]
    twice = jnp.broadcast_to(parents[:, None], (parents.shape[0], 2, ROWS, LANES))
    reach = depth // 2 + NEAR
    quarter = iota((ROWS, LANES), 1) // (LANES // 4)
    row = iota((ROWS, LANES), 0)

    def unpacked(index, which):
        pair = packed[device_of(jnp.clip(index, 0, shares - 1)), which]
        total = None
        for shift in range(4):
            moved = pltpu.roll(pair, shift * (LANES // 4), 1)
            wide = jnp.where(row < 4, moved[0:1, :], moved[1:2, :])
            kept = jnp.where((quarter - shift) % 4 == row % 4, wide, 0.0)
            total = kept if total is None else total + kept
        return total

    before, after = unpacked(part - 1, 3), unpacked(part + 1, 4)
    one2[low - 1] = before + lifted[(low - 1) // 2 + NEAR // 2]
    one2[low:high] = corr2[low:high] + twice.reshape(high - low, ROWS, LANES)
    one2[high] = after + lifted[high // 2 + NEAR // 2]
    sweep(coarse, NEAR - 4, reach + 4, fields2, one2, two2)
    sweep(coarse, NEAR - 3, reach + 3, fields2, two2, one2)
    sweep(coarse, NEAR - 2, reach + 2, fields2, one2, two2)

    fine_lane, coarse_lane = iota((LANES, LANES), 1), iota((LANES, LANES), 0)
    x_of = (fine_lane // fine.ny) // 2
    y_of = (fine_lane % fine.ny) // 2
    up = where01(coarse_lane == x_of * coarse.ny + y_of)
    lifted[0 : depth // 2 + 4] = in_lanes(two2[NEAR - 2 : reach + 2], up)
    parents = lifted[0 : depth // 2 + 4]
    twice = jnp.broadcast_to(parents[:, None], (parents.shape[0], 2, ROWS, LANES))
    low, high = HALO - 4, HALO + depth + 4
    one1[low:high] = corr1[low:high] + twice.reshape(high - low, ROWS, LANES)
    reach = depth + HALO
    sweep(fine, HALO - 2, reach + 2, fields1, one1, two1)
    sweep(fine, HALO - 1, reach + 1, fields1, two1, one1)
    sweep(fine, HALO, reach, fields1, one1, two1)

    group = (iota((depth, LANES), 1) // by) % groups
    for ix in range(nx):
        scaled = [
            two1[HALO:reach, ix * groups + part, :] * diag1[HALO:reach, ix * groups + part, :]
            for part in range(groups)
        ]
        for iy in range(ny):
            total = scaled[iy]
            for part in range(groups):
                if part != iy:
                    moved = pltpu.roll(scaled[part], (by * (part - iy)) % LANES, 1)
                    total = jnp.where(group == part, moved, total)
            out_ref[ix * ny + iy] = total


def finish_kernel(blocks, out_ref):
    bx, by, depth = out_ref.shape
    cells = bx * by
    cell = iota((cells, cells), 0)
    lane = iota((cells, cells), 1)
    x, y = cell // by, cell % by
    chosen = where01((x % 4) * (bx // 4 * by) + (x // 4) * by + y == lane)
    peers = blocks.shape[0]
    ordered = jnp.concatenate([blocks[own_peer_of(rank)] for rank in range(peers)], axis=0)
    out_ref[...] = dot10(chosen, ordered).reshape(out_ref.shape)


def whole_planes(residual_q2, viscosity, pinned):
    bx, by, depth = viscosity.shape
    groups = bx // 4
    peers = SPLIT[0] * SPLIT[1]
    share = depth // peers
    planes = share + 2 * HALO
    count2 = share // 2 + 2 * NEAR
    limit = pltpu.CompilerParams(vmem_limit_bytes=32 * 2**20)

    def flat(rows):
        return jax.ShapeDtypeStruct((rows, LANES), F32)

    def blocks(count, rows):
        return jax.ShapeDtypeStruct((count, rows, LANES), F32)

    def room(count):
        return pltpu.VMEM((count, ROWS, LANES), F32)

    fluid = 1.0 / viscosity
    pin = 4.0 * pinned.astype(F32) * fluid
    parcels = pl.pallas_call(
        functools.partial(prepare_kernel, share),
        out_shape=blocks(peers, 3 * share),
        compiler_params=limit,
        name="prepare",
    )(residual_q2.reshape(4 * bx * by, 2 * depth), fluid, pin)
    own = pl.pallas_call(
        functools.partial(spread_kernel, groups, by),
        out_shape=blocks(3 * share, ROWS),
        compiler_params=limit,
        name="spread",
    )(lax.all_to_all(parcels, ("gx", "gy"), 0, 0, tiled=True))
    length = lax.axis_size("gz")
    parts = length * peers

    device = [peer_of(i // peers, i % peers) * length + i // peers for i in range(parts)]

    def swap(field, first):
        pairs = [(device[i], device[i + 1]) for i in range(first, parts - 1, 2)]
        return lax.ppermute(field, ("gx", "gy", "gz"), pairs + [pair[::-1] for pair in pairs])

    inner, outer = swap(own, 0), swap(own, 1)
    saved = (blocks(planes, ROWS),) * 9 + (blocks(count2, ROWS),) * 9
    results = pl.pallas_call(
        functools.partial(down_kernel, groups, by, share),
        out_shape=saved + (blocks(5, 2),),
        scratch_shapes=[room(planes)] * 4 + [room(count2)] * 5,
        compiler_params=limit,
        name="down",
    )(own, inner, outer)
    copies = jnp.broadcast_to(results[-1], (parts,) + results[-1].shape)
    packed = lax.all_to_all(copies, ("gz", "gx", "gy"), 0, 0, tiled=True)
    depth3 = parts * share // 4
    mine = pl.pallas_call(
        functools.partial(up_kernel, groups, by, share),
        out_shape=blocks(peers, share),
        scratch_shapes=[room(planes), room(planes), room(count2), room(count2), room(count2)]
        + [pltpu.VMEM((rows, LANES), F32) for rows in (depth3, depth3, depth3 + 3 * NEAR)],
        compiler_params=limit,
        name="up",
    )(packed, *results[:-1])
    return pl.pallas_call(
        finish_kernel,
        out_shape=jax.ShapeDtypeStruct((bx, by, depth), F32),
        compiler_params=limit,
        name="finish",
    )(lax.all_to_all(mine, ("gx", "gy"), 0, 0, tiled=True))


def one_tile_planes(mesh, viscosity):
    split = (mesh.shape["gx"], mesh.shape["gy"])
    depth = viscosity.shape[2]
    fits = viscosity.shape[:2] == PLANE and split == SPLIT
    return fits and depth == 4 * LANES and depth // mesh.shape["gz"] == LANES


def solution(mesh):
    placed = (P("gx", "gy", "gz"), P("gx", "gy", "gz"), P("gx", "gy", "gz"))

    def cycle(residual_q2, viscosity, pinned):
        chosen = whole_planes if one_tile_planes(mesh, viscosity) else per_device
        return jax.shard_map(
            chosen, mesh=mesh, in_specs=placed, out_specs=P("gx", "gy", "gz"), check_vma=False
        )(residual_q2, viscosity, pinned)

    return cycle
```

```python
import functools

import jax
import jax.numpy as jnp
from jax import lax
from jax.experimental import pallas as pl
from jax.experimental.pallas import tpu as pltpu
from jax.sharding import PartitionSpec as P

NU = 3


OMEGA = 0.6


def with_halo(block, sides, width):
    for axis, dim in sides:
        count = lax.axis_size(axis)
        forward = [(i, i + 1) for i in range(count - 1)]
        backward = [(target, source) for source, target in forward]
        low = lax.ppermute(
            lax.slice_in_dim(block, block.shape[dim] - width, None, axis=dim), axis, forward
        )
        high = lax.ppermute(lax.slice_in_dim(block, 0, width, axis=dim), axis, backward)
        block = jnp.concatenate([low, block, high], axis=dim)
    return block


def coarsen(x):
    a, b, c = x.shape
    return x.reshape(a // 2, 2, b // 2, 2, c // 2, 2).sum(axis=(1, 3, 5))


def refine(x):
    return jnp.repeat(jnp.repeat(jnp.repeat(x, 2, 0), 2, 1), 2, 2)


def extended(field):
    return with_halo(field, (("gx", 0), ("gy", 1), ("gz", 2)), 1)


def shifted(padded):
    return [
        padded[2:, 1:-1, 1:-1],
        padded[:-2, 1:-1, 1:-1],
        padded[1:-1, 2:, 1:-1],
        padded[1:-1, :-2, 1:-1],
        padded[1:-1, 1:-1, 2:],
        padded[1:-1, 1:-1, :-2],
    ]


def neighbours(field):
    return shifted(extended(field))


def harmonic(fluid, near, factor):
    total = fluid + near
    return jnp.where(total > 0, factor * 2.0 * fluid * near / jnp.where(total > 0, total, 1.0), 0.0)


def couplings(fluid, factor):
    return [harmonic(fluid, near, factor) for near in neighbours(fluid)]


def apply_op(field, weights, diag):
    total = diag * field
    for weight, near in zip(weights, neighbours(field)):
        total = total - weight * near
    return total


def presmooth(rhs, weights, diag):
    corr = OMEGA * rhs / diag
    for sweep in range(NU - 1):
        corr = corr + OMEGA * (rhs - apply_op(corr, weights, diag)) / diag
    return corr


def postsmooth(corr, rhs, weights, diag):
    for sweep in range(NU):
        corr = corr + OMEGA * (rhs - apply_op(corr, weights, diag)) / diag
    return corr


def tridiag(coeffs, rhs):
    solved = lax.linalg.tridiagonal_solve(coeffs[0], coeffs[1], coeffs[2], rhs[..., None])[..., 0]
    last = rhs.ndim - 1
    shift_col = jnp.sum(rhs, axis=last, keepdims=True) / jnp.sum(
        coeffs[3], axis=last, keepdims=True
    )
    return solved + shift_col


def prepare_columns(weights, diag):
    lower = -weights[5]
    upper = -weights[4]
    across = diag + lower + upper
    return (
        lax.all_gather(lower, "gz", axis=2, tiled=True),
        lax.all_gather(diag, "gz", axis=2, tiled=True),
        lax.all_gather(upper, "gz", axis=2, tiled=True),
        lax.all_gather(across, "gz", axis=2, tiled=True),
    )


def column_solve(rhs, coeffs):
    depth = rhs.shape[2]
    whole = lax.all_gather(rhs, "gz", axis=2, tiled=True)
    solved = tridiag(coeffs, whole)
    return lax.dynamic_slice_in_dim(solved, lax.axis_index("gz") * depth, depth, 2)


def per_device(residual_q2, viscosity, pinned):
    fluid1 = 1.0 / viscosity
    pin1 = 4.0 * pinned.astype(jnp.float32) * fluid1
    rhs1 = coarsen(residual_q2.astype(jnp.float32))
    fluid2 = coarsen(fluid1) / 8.0
    pin2 = coarsen(pin1) / 4.0
    fluid3 = coarsen(fluid2) / 8.0
    pin3 = coarsen(pin2) / 4.0
    weights1 = couplings(fluid1, 1.0)
    weights2 = couplings(fluid2, 2.0)
    weights3 = couplings(fluid3, 4.0)
    diag1 = sum(weights1) + pin1
    diag2 = sum(weights2) + pin2
    diag3 = sum(weights3) + pin3
    coeffs = prepare_columns(weights3, diag3)
    corr1 = presmooth(rhs1, weights1, diag1)
    rhs2 = coarsen(rhs1 - apply_op(corr1, weights1, diag1))
    corr2 = presmooth(rhs2, weights2, diag2)
    rhs3 = coarsen(rhs2 - apply_op(corr2, weights2, diag2))
    corr3 = column_solve(rhs3, coeffs)
    corr3 = corr3 + column_solve(rhs3 - apply_op(corr3, weights3, diag3), coeffs)
    corr2 = postsmooth(corr2 + refine(corr3), rhs2, weights2, diag2)
    corr1 = postsmooth(corr1 + refine(corr2), rhs1, weights1, diag1)
    return diag1 * corr1


PLANE = (32, 32)
SPLIT = (2, 4)
ROWS = 8
LANES = 128
HALO = 16
NEAR = 8
PIECE = 8
TINY = 1e-30
F32 = jnp.float32


def iota(shape, dim):
    return lax.broadcasted_iota(jnp.int32, shape, dim)


def dot01(field, chosen, dims=(((1,), (0,)), ((), ()))):
    total = None
    rest = field
    for part in range(3):
        piece = rest.astype(jnp.bfloat16)
        term = lax.dot_general(piece, chosen, dims, preferred_element_type=F32)
        total = term if total is None else total + term
        if part < 2:
            rest = rest - piece.astype(F32)
    return total


def dot10(chosen, field):
    total = None
    rest = field
    for part in range(3):
        piece = rest.astype(jnp.bfloat16)
        term = lax.dot_general(
            chosen, piece, (((1,), (1,)), ((), ())), preferred_element_type=F32
        )
        total = term if total is None else total + term
        if part < 2:
            rest = rest - piece.astype(F32)
    return total


def where01(condition):
    return jnp.where(condition, 1.0, 0.0).astype(jnp.bfloat16)


def loop(low, high, size, body):
    for plane in range(low, high, size):
        body(plane, min(size, high - plane))


def inverse_of(field):
    first = pl.reciprocal(field, approx=True)
    return first * (2.0 - field * first)


class Level:
    def __init__(self, level):
        self.ny = PLANE[1] >> level
        self.xs = 4 >> level
        self.factor = float(2**level)

    def masks(self, shape):
        lane = iota(shape, 2)
        row = iota(shape, 1)
        within = (lane // self.ny) % self.xs
        y = lane % self.ny
        last_x = (row == ROWS - 1) & (within == self.xs - 1)
        return within, y == self.ny - 1, last_x

    def next_x(self, field):
        within = (iota(field.shape, 2) // self.ny) % self.xs
        moved = pltpu.roll(field, LANES - self.ny, 2)
        return jnp.where(within == self.xs - 1, pltpu.roll(moved, ROWS - 1, 1), moved)

    def last_x(self, field):
        within = (iota(field.shape, 2) // self.ny) % self.xs
        moved = pltpu.roll(field, self.ny, 2)
        return jnp.where(within == 0, pltpu.roll(moved, 1, 1), moved)

    def next_y(self, field):
        return pltpu.roll(field, LANES - 1, 2)

    def last_y(self, field):
        return pltpu.roll(field, 1, 2)

    def spread(self, field, scaled, plane, count):
        mid = field[1:-1]
        near = (
            self.next_x(mid), self.last_x(mid), self.next_y(mid), self.last_y(mid),
            field[2:], field[:-2],
        )
        terms = [weight[pl.ds(plane, count)] * value for weight, value in zip(scaled, near)]
        return mid, ((terms[0] + terms[1]) + (terms[2] + terms[3])) + (terms[4] + terms[5])


def mean_of(fluid, near, factor):
    return ((factor * 2.0) * fluid * near) * inverse_of(jnp.maximum(fluid + near, TINY))


def set_level(level, low, high, fluid, pin, rhs, fields):
    scaled, start, diag = fields

    def body(plane, count):
        wide = fluid[pl.ds(plane - 1, count + 2)]
        mid = wide[1:-1]
        within, end_y, end_x = level.masks(mid.shape)
        to_x = jnp.where(end_x, 0.0, mean_of(mid, level.next_x(mid), level.factor))
        to_y = jnp.where(end_y, 0.0, mean_of(mid, level.next_y(mid), level.factor))
        to_z = mean_of(wide[:-1], wide[1:], level.factor)
        weights = (to_x, level.last_x(to_x), to_y, level.last_y(to_y), to_z[1:], to_z[:-1])
        total = (
            (weights[0] + weights[1])
            + (weights[2] + weights[3])
            + (weights[4] + weights[5])
            + pin[pl.ds(plane, count)]
        )
        gain = OMEGA * inverse_of(jnp.maximum(total, TINY))
        for target, weight in zip(scaled, weights):
            target[pl.ds(plane, count)] = gain * weight
        start[pl.ds(plane, count)] = gain * rhs[pl.ds(plane, count)]
        diag[pl.ds(plane, count)] = total

    loop(low, high, PIECE, body)


def sweep(level, low, high, fields, source, target):
    scaled, start, _ = fields

    def body(plane, count):
        mid, total = level.spread(source[pl.ds(plane - 1, count + 2)], scaled, plane, count)
        target[pl.ds(plane, count)] = (1.0 - OMEGA) * mid + (start[pl.ds(plane, count)] + total)

    loop(low, high, PIECE, body)


def pair_sum(field):
    half = field.reshape((field.shape[0] // 2, 2) + field.shape[1:])
    return half[:, 0] + half[:, 1]


def coarse_residual(level, low, high, fields, corr, target):
    scaled, start, diag = fields

    def body(plane, count):
        mid, total = level.spread(corr[pl.ds(plane - 1, count + 2)], scaled, plane, count)
        rest = (start[pl.ds(plane, count)] + total) - OMEGA * mid
        rest = rest * (diag[pl.ds(plane, count)] * (1.0 / OMEGA))
        target[pl.ds((plane - low) // 2, count // 2)] = pair_sum(rest)

    loop(low, high, PIECE, body)


def lanes_down(level):
    fine = iota((LANES, LANES), 0)
    coarse = iota((LANES, LANES), 1)
    ny, xs = PLANE[1] >> level, 4 >> level
    half = xs // 2
    same_x = ((fine // ny) % xs) // 2 == (coarse // (ny // 2)) % half
    same_y = (fine % ny) // 2 == coarse % (ny // 2)
    return where01((fine < ny * xs) & same_x & same_y)


def in_lanes(field, chosen):
    flat = field.reshape(field.shape[0] * ROWS, LANES)
    return dot01(flat, chosen).reshape(field.shape)


def peer_at(rank):
    ny = SPLIT[1]
    ix, place_on_row = rank // ny, rank % ny
    return ix * ny + (ny - 1 - place_on_row if ix % 2 else place_on_row)


def peer_of(group, rank):
    return peer_at(SPLIT[0] * SPLIT[1] - 1 - rank if group % 2 else rank)


def own_peer_of(rank):
    return jnp.where(lax.axis_index("gz") % 2 == 1, peer_of(1, rank), peer_of(0, rank))


def slab_of(ix, iy, group):
    nx, ny = SPLIT
    rank = ix * ny + jnp.where(ix % 2 == 1, ny - 1 - iy, iy)
    return group * nx * ny + jnp.where(group % 2 == 1, nx * ny - 1 - rank, rank)


def device_of(slab):
    nx, ny = SPLIT
    group, rank = slab // (nx * ny), slab % (nx * ny)
    rank = jnp.where(group % 2 == 1, nx * ny - 1 - rank, rank)
    row, column = rank // ny, rank % ny
    return group * nx * ny + row * ny + jnp.where(row % 2 == 1, ny - 1 - column, column)


def prepare_kernel(
    share, res_in, visc_in, pin_in, out_ref, res_ref, visc_ref, pin_ref, arrived
):
    copies = [
        pltpu.make_async_copy(source, target, arrived.at[index])
        for index, (source, target) in enumerate(
            ((visc_in, visc_ref), (pin_in, pin_ref), (res_in, res_ref))
        )
    ]
    for copy in copies:
        copy.start()
    bx, by, depth = visc_ref.shape
    cells = bx * by
    groups = bx // 4

    def lane_of(x, y):
        return (x % 4) * (groups * by) + (x // 4) * by + y

    def send(index, field):
        for rank in range(depth // share):
            rows = slice(index * share, (index + 1) * share)
            out_ref[own_peer_of(rank), rows] = field[rank * share : (rank + 1) * share]

    cell = iota((cells, cells), 0)
    lane = iota((cells, cells), 1)
    chosen = where01(lane_of(cell // by, cell % by) == lane)
    copies[0].wait()
    fluid = 1.0 / visc_ref[...].reshape(cells, depth)
    send(0, dot01(fluid.T, chosen))
    copies[1].wait()
    pin = 4.0 * pin_ref[...].reshape(cells, depth).astype(F32) * fluid
    send(2, dot01(pin.T, chosen))
    pick = where01(iota((depth, 2 * depth), 1) // 2 == iota((depth, 2 * depth), 0))
    fine = iota((4 * cells, cells), 0)
    lane = iota((4 * cells, cells), 1)
    chosen = where01(lane_of(fine // (4 * by), (fine % (2 * by)) // 2) == lane)
    copies[2].wait()
    deep = lax.dot_general(
        pick, res_ref[...], (((1,), (1,)), ((), ())), preferred_element_type=F32
    )
    send(1, dot01(deep, chosen))


def spread_kernel(groups, by, gathered, own):
    for start in range(0, own.shape[0], ROWS):
        place(gathered, start, own, start, groups, by)


def place(gathered, row, target, plane, groups, by):
    group = (iota((ROWS, LANES), 1) // by) % groups
    nx, ny = SPLIT
    for ix in range(nx):
        found = [gathered[ix * ny + iy, pl.ds(row, ROWS), :] for iy in range(ny)]
        for part in range(groups):
            total = found[part]
            for iy in range(ny):
                if iy != part:
                    moved = pltpu.roll(found[iy], (by * (iy - part)) % LANES, 1)
                    total = jnp.where(group == iy, moved, total)
            target[pl.ds(plane, ROWS), ix * groups + part, :] = total


def down_kernel(
    groups, by, depth,
    own, inner, outer,
    xn1, xl1, yn1, yl1, zn1, zl1, start1, diag1, corr1,
    xn2, xl2, yn2, yl2, zn2, zl2, start2, diag2, corr2,
    packed,
    fluid1, rhs1, pin1, other1, fluid2, rhs2, pin2, other2, sums,
):
    planes = depth + 2 * HALO
    part = slab_of(lax.axis_index("gx"), lax.axis_index("gy"), lax.axis_index("gz"))
    odd = part % 2 == 1
    for index, target in enumerate((fluid1, rhs1, pin1)):
        rows = slice(index * depth, (index + 1) * depth)
        target[0:HALO] = jnp.where(odd, inner[rows], outer[rows])
        target[HALO : HALO + depth] = own[rows]
        target[HALO + depth :] = jnp.where(odd, outer[rows], inner[rows])

    fine, coarse = Level(0), Level(1)
    down1, down2 = lanes_down(0), lanes_down(1)
    fields1 = ((xn1, xl1, yn1, yl1, zn1, zl1), start1, diag1)
    fields2 = ((xn2, xl2, yn2, yl2, zn2, zl2), start2, diag2)
    set_level(fine, 1, planes - 1, fluid1, pin1, rhs1, fields1)
    sweep(fine, 2, planes - 2, fields1, start1, other1)
    sweep(fine, 3, planes - 3, fields1, other1, corr1)
    count2 = depth // 2 + 2 * NEAR
    begin = HALO - 2 * NEAR
    for source, target, share in ((fluid1, fluid2, 8.0), (pin1, pin2, 4.0)):
        whole = pair_sum(source[begin : begin + 2 * count2])
        target[...] = in_lanes(whole, down1) * (1.0 / share)
    low2, high2 = (begin + 4) // 2, count2 - (begin + 4) // 2
    inner = high2 - low2
    coarse_residual(fine, begin + 2 * low2, begin + 2 * high2, fields1, corr1, sums)
    rhs2[low2:high2] = in_lanes(sums[0:inner], down1)
    set_level(coarse, low2, high2, fluid2, pin2, rhs2, fields2)
    sweep(coarse, low2 + 1, high2 - 1, fields2, start2, other2)
    sweep(coarse, low2 + 2, high2 - 2, fields2, other2, corr2)
    coarse_residual(coarse, NEAR, NEAR + depth // 2, fields2, corr2, sums)
    count3 = depth // 4
    rhs3 = in_lanes(sums[0:count3], down2)
    fluid3 = in_lanes(pair_sum(fluid2[NEAR : NEAR + 2 * count3]), down2) * 0.125
    pin3 = in_lanes(pair_sum(pin2[NEAR : NEAR + 2 * count3]), down2) * 0.25
    lane = iota((count3, LANES), 1) // ROWS
    first = jnp.zeros((count3, LANES), F32)
    second = jnp.zeros((count3, LANES), F32)
    for row in range(ROWS):
        first = jnp.where(lane == row, rhs3[:, row, :], first)
        first = jnp.where(lane == ROWS + row, fluid3[:, row, :], first)
        second = jnp.where(lane % ROWS == row, pin3[:, row, :], second)
    packed[0] = first[0:2]
    packed[1] = first[2:4]
    packed[2] = jnp.where(lane[0:2] < ROWS, second[0:2], second[2:4])
    lane = iota((1, LANES), 1) // (LANES // 4)
    for index, plane in enumerate((NEAR + depth // 2 - 5, NEAR + 4)):
        for half in range(2):
            row = jnp.zeros((1, LANES), F32)
            for quarter in range(4):
                at = half * 4 + quarter
                row = jnp.where(lane == quarter, corr2[plane, at : at + 1, :], row)
            packed[3 + index, half : half + 1, :] = row


def rolled(field, shift):
    count = field.shape[0]
    shift %= count
    if shift % ROWS:
        return pltpu.roll(field, shift, 0)
    return jnp.concatenate([field[count - shift :], field[: count - shift]], axis=0)


def columns(rhs, fluid, pin):
    depth = fluid.shape[0]
    z, lane = iota(fluid.shape, 0), iota(fluid.shape, 1)
    y, x = lane % ROWS, (lane // ROWS) % ROWS

    def next_x(field):
        return pltpu.roll(field, LANES - ROWS, 1)

    def next_y(field):
        return pltpu.roll(field, LANES - 1, 1)

    wz = jnp.where(z == depth - 1, 0.0, mean_of(fluid, rolled(fluid, -1), 4.0))
    wy = jnp.where(y == ROWS - 1, 0.0, mean_of(fluid, next_y(fluid), 4.0))
    wx = jnp.where(x == ROWS - 1, 0.0, mean_of(fluid, next_x(fluid), 4.0))
    across = (wx + pltpu.roll(wx, ROWS, 1)) + (wy + pltpu.roll(wy, 1, 1)) + pin
    share = 1.0 / jnp.sum(across, axis=0, keepdims=True)

    above, below, own = rolled(wz, 1), wz, across
    steps = []
    stride = 1
    while stride < depth:
        inverse = inverse_of(above + below + own)
        up = above * rolled(inverse, stride)
        down = below * rolled(inverse, -stride)
        own = own + up * rolled(own, stride) + down * rolled(own, -stride)
        above = up * rolled(above, stride)
        below = down * rolled(below, -stride)
        steps.append((stride, up, down))
        stride *= 2
    inverse = inverse_of(above + below + own)

    def solve(right):
        mean = jnp.sum(right, axis=0, keepdims=True) * share
        for stride, up, down in steps:
            right = right + up * rolled(right, stride) + down * rolled(right, -stride)
        return right * inverse + mean

    corr = solve(rhs)
    flow_x = wx * (next_x(corr) - corr)
    flow_y = wy * (next_y(corr) - corr)
    flow_z = wz * (rolled(corr, -1) - corr)
    rest = (
        (rhs - pin * corr)
        + (flow_x - pltpu.roll(flow_x, ROWS, 1))
        + (flow_y - pltpu.roll(flow_y, 1, 1))
        + (flow_z - rolled(flow_z, 1))
    )
    return corr + solve(rest)


def up_kernel(
    groups, by, depth,
    packed,
    xn1, xl1, yn1, yl1, zn1, zl1, start1, diag1, corr1,
    xn2, xl2, yn2, yl2, zn2, zl2, start2, diag2, corr2,
    out_ref,
    one1, two1, one2, two2, lifted, first, second, solved,
):
    count3 = depth // 4
    shares = packed.shape[0]
    peers = SPLIT[0] * SPLIT[1]
    for slab in range(shares):
        index = slab // peers * peers + peer_of(slab // peers, slab % peers)
        row = slab * count3
        first[row : row + 2] = packed[index, 0]
        first[row + 2 : row + 4] = packed[index, 1]
        both = packed[index, 2]
        second[row : row + 2] = both
        second[row + 2 : row + 4] = pltpu.roll(both, LANES // 2, 1)
    half = iota((shares * count3, LANES), 1) < LANES // 2

    def low_half(field):
        return jnp.where(half, field, pltpu.roll(field, LANES // 2, 1))

    def high_half(field):
        return jnp.where(half, pltpu.roll(field, LANES // 2, 1), field)

    solved[NEAR : NEAR + shares * count3] = columns(
        low_half(first[...]), high_half(first[...]), low_half(second[...])
    )
    solved[0:NEAR] = jnp.zeros((NEAR, LANES), F32)
    solved[NEAR + shares * count3 :] = jnp.zeros((2 * NEAR, LANES), F32)

    nx, ny = SPLIT
    part = slab_of(lax.axis_index("gx"), lax.axis_index("gy"), lax.axis_index("gz"))
    count = count3 + 2 * NEAR
    tall = solved[pl.ds(part * count3, count + count3), :]
    fine, coarse = Level(0), Level(1)
    cell = iota((LANES, ROWS * LANES), 0)
    lane = iota((LANES, ROWS * LANES), 1)
    same_y = cell % ROWS == (lane % coarse.ny) // 2
    spread = where01((cell // ROWS == lane // LANES) & same_y)
    wide = dot01(tall, spread)
    for row in range(ROWS):
        lifted[0:count, row, :] = wide[:count, row * LANES : (row + 1) * LANES]

    fields1 = ((xn1, xl1, yn1, yl1, zn1, zl1), start1, diag1)
    fields2 = ((xn2, xl2, yn2, yl2, zn2, zl2), start2, diag2)
    low, high = NEAR - 4, NEAR + depth // 2 + 4
    parents = lifted[low // 2 + NEAR // 2 : high // 2 + NEAR // 2]
    twice = jnp.broadcast_to(parents[:, None], (parents.shape[0], 2, ROWS, LANES))
    reach = depth // 2 + NEAR
    quarter = iota((ROWS, LANES), 1) // (LANES // 4)
    row = iota((ROWS, LANES), 0)

    def unpacked(index, which):
        pair = packed[device_of(jnp.clip(index, 0, shares - 1)), which]
        total = None
        for shift in range(4):
            moved = pltpu.roll(pair, shift * (LANES // 4), 1)
            wide = jnp.where(row < 4, moved[0:1, :], moved[1:2, :])
            kept = jnp.where((quarter - shift) % 4 == row % 4, wide, 0.0)
            total = kept if total is None else total + kept
        return total

    before, after = unpacked(part - 1, 3), unpacked(part + 1, 4)
    one2[low - 1] = before + lifted[(low - 1) // 2 + NEAR // 2]
    one2[low:high] = corr2[low:high] + twice.reshape(high - low, ROWS, LANES)
    one2[high] = after + lifted[high // 2 + NEAR // 2]
    sweep(coarse, NEAR - 4, reach + 4, fields2, one2, two2)
    sweep(coarse, NEAR - 3, reach + 3, fields2, two2, one2)
    sweep(coarse, NEAR - 2, reach + 2, fields2, one2, two2)

    fine_lane, coarse_lane = iota((LANES, LANES), 1), iota((LANES, LANES), 0)
    x_of = (fine_lane // fine.ny) // 2
    y_of = (fine_lane % fine.ny) // 2
    up = where01(coarse_lane == x_of * coarse.ny + y_of)
    lifted[0 : depth // 2 + 4] = in_lanes(two2[NEAR - 2 : reach + 2], up)
    parents = lifted[0 : depth // 2 + 4]
    twice = jnp.broadcast_to(parents[:, None], (parents.shape[0], 2, ROWS, LANES))
    low, high = HALO - 4, HALO + depth + 4
    one1[low:high] = corr1[low:high] + twice.reshape(high - low, ROWS, LANES)
    reach = depth + HALO
    sweep(fine, HALO - 2, reach + 2, fields1, one1, two1)
    sweep(fine, HALO - 1, reach + 1, fields1, two1, one1)
    sweep(fine, HALO, reach, fields1, one1, two1)

    group = (iota((depth, LANES), 1) // by) % groups
    for ix in range(nx):
        scaled = [
            two1[HALO:reach, ix * groups + part, :] * diag1[HALO:reach, ix * groups + part, :]
            for part in range(groups)
        ]
        for iy in range(ny):
            total = scaled[iy]
            for part in range(groups):
                if part != iy:
                    moved = pltpu.roll(scaled[part], (by * (part - iy)) % LANES, 1)
                    total = jnp.where(group == part, moved, total)
            out_ref[ix * ny + iy] = total


def finish_kernel(blocks, out_ref):
    bx, by, depth = out_ref.shape
    cells = bx * by
    cell = iota((cells, cells), 0)
    lane = iota((cells, cells), 1)
    x, y = cell // by, cell % by
    chosen = where01((x % 4) * (bx // 4 * by) + (x // 4) * by + y == lane)
    peers = blocks.shape[0]
    ordered = jnp.concatenate([blocks[own_peer_of(rank)] for rank in range(peers)], axis=0)
    out_ref[...] = dot10(chosen, ordered).reshape(out_ref.shape)


def whole_planes(residual_q2, viscosity, pinned):
    bx, by, depth = viscosity.shape
    groups = bx // 4
    peers = SPLIT[0] * SPLIT[1]
    share = depth // peers
    planes = share + 2 * HALO
    count2 = share // 2 + 2 * NEAR
    limit = pltpu.CompilerParams(vmem_limit_bytes=32 * 2**20)

    def flat(rows):
        return jax.ShapeDtypeStruct((rows, LANES), F32)

    def blocks(count, rows):
        return jax.ShapeDtypeStruct((count, rows, LANES), F32)

    def room(count):
        return pltpu.VMEM((count, ROWS, LANES), F32)

    residual = residual_q2.reshape(4 * bx * by, 2 * depth)
    arguments = [
        pltpu.with_memory_space_constraint(field, pltpu.HBM)
        for field in (residual, viscosity, pinned)
    ]
    parcels = pl.pallas_call(
        functools.partial(prepare_kernel, share),
        in_specs=[pl.BlockSpec(memory_space=pltpu.HBM)] * 3,
        out_shape=blocks(peers, 3 * share),
        scratch_shapes=[pltpu.VMEM(field.shape, field.dtype) for field in arguments]
        + [pltpu.SemaphoreType.DMA((3,))],
        compiler_params=limit,
        name="prepare",
    )(*arguments)
    own = pl.pallas_call(
        functools.partial(spread_kernel, groups, by),
        out_shape=blocks(3 * share, ROWS),
        compiler_params=limit,
        name="spread",
    )(lax.all_to_all(parcels, ("gx", "gy"), 0, 0, tiled=True))
    length = lax.axis_size("gz")
    parts = length * peers

    device = [peer_of(i // peers, i % peers) * length + i // peers for i in range(parts)]

    def swap(field, first):
        pairs = [(device[i], device[i + 1]) for i in range(first, parts - 1, 2)]
        return lax.ppermute(field, ("gx", "gy", "gz"), pairs + [pair[::-1] for pair in pairs])

    inner, outer = swap(own, 0), swap(own, 1)
    saved = (blocks(planes, ROWS),) * 9 + (blocks(count2, ROWS),) * 9
    results = pl.pallas_call(
        functools.partial(down_kernel, groups, by, share),
        out_shape=saved + (blocks(5, 2),),
        scratch_shapes=[room(planes)] * 4 + [room(count2)] * 5,
        compiler_params=limit,
        name="down",
    )(own, inner, outer)
    copies = jnp.broadcast_to(results[-1], (parts,) + results[-1].shape)
    packed = lax.all_to_all(copies, ("gz", "gx", "gy"), 0, 0, tiled=True)
    depth3 = parts * share // 4
    mine = pl.pallas_call(
        functools.partial(up_kernel, groups, by, share),
        out_shape=blocks(peers, share),
        scratch_shapes=[room(planes), room(planes), room(count2), room(count2), room(count2)]
        + [pltpu.VMEM((rows, LANES), F32) for rows in (depth3, depth3, depth3 + 3 * NEAR)],
        compiler_params=limit,
        name="up",
    )(packed, *results[:-1])
    return pl.pallas_call(
        finish_kernel,
        out_shape=jax.ShapeDtypeStruct((bx, by, depth), F32),
        compiler_params=limit,
        name="finish",
    )(lax.all_to_all(mine, ("gx", "gy"), 0, 0, tiled=True))


def one_tile_planes(mesh, viscosity):
    split = (mesh.shape["gx"], mesh.shape["gy"])
    depth = viscosity.shape[2]
    fits = viscosity.shape[:2] == PLANE and split == SPLIT
    return fits and depth == 4 * LANES and depth // mesh.shape["gz"] == LANES


def solution(mesh):
    placed = (P("gx", "gy", "gz"), P("gx", "gy", "gz"), P("gx", "gy", "gz"))

    def cycle(residual_q2, viscosity, pinned):
        chosen = whole_planes if one_tile_planes(mesh, viscosity) else per_device
        return jax.shard_map(
            chosen, mesh=mesh, in_specs=placed, out_specs=P("gx", "gy", "gz"), check_vma=False
        )(residual_q2, viscosity, pinned)

    return cycle
```

```python
import functools

import jax
import jax.numpy as jnp
from jax import lax
from jax.experimental import pallas as pl
from jax.experimental.pallas import tpu as pltpu
from jax.sharding import PartitionSpec as P

NU = 3


OMEGA = 0.6


def with_halo(block, sides, width):
    for axis, dim in sides:
        count = lax.axis_size(axis)
        forward = [(i, i + 1) for i in range(count - 1)]
        backward = [(target, source) for source, target in forward]
        low = lax.ppermute(
            lax.slice_in_dim(block, block.shape[dim] - width, None, axis=dim), axis, forward
        )
        high = lax.ppermute(lax.slice_in_dim(block, 0, width, axis=dim), axis, backward)
        block = jnp.concatenate([low, block, high], axis=dim)
    return block


def coarsen(x):
    a, b, c = x.shape
    return x.reshape(a // 2, 2, b // 2, 2, c // 2, 2).sum(axis=(1, 3, 5))


def refine(x):
    return jnp.repeat(jnp.repeat(jnp.repeat(x, 2, 0), 2, 1), 2, 2)


def extended(field):
    return with_halo(field, (("gx", 0), ("gy", 1), ("gz", 2)), 1)


def shifted(padded):
    return [
        padded[2:, 1:-1, 1:-1],
        padded[:-2, 1:-1, 1:-1],
        padded[1:-1, 2:, 1:-1],
        padded[1:-1, :-2, 1:-1],
        padded[1:-1, 1:-1, 2:],
        padded[1:-1, 1:-1, :-2],
    ]


def neighbours(field):
    return shifted(extended(field))


def harmonic(fluid, near, factor):
    total = fluid + near
    return jnp.where(total > 0, factor * 2.0 * fluid * near / jnp.where(total > 0, total, 1.0), 0.0)


def couplings(fluid, factor):
    return [harmonic(fluid, near, factor) for near in neighbours(fluid)]


def apply_op(field, weights, diag):
    total = diag * field
    for weight, near in zip(weights, neighbours(field)):
        total = total - weight * near
    return total


def presmooth(rhs, weights, diag):
    corr = OMEGA * rhs / diag
    for sweep in range(NU - 1):
        corr = corr + OMEGA * (rhs - apply_op(corr, weights, diag)) / diag
    return corr


def postsmooth(corr, rhs, weights, diag):
    for sweep in range(NU):
        corr = corr + OMEGA * (rhs - apply_op(corr, weights, diag)) / diag
    return corr


def tridiag(coeffs, rhs):
    solved = lax.linalg.tridiagonal_solve(coeffs[0], coeffs[1], coeffs[2], rhs[..., None])[..., 0]
    last = rhs.ndim - 1
    shift_col = jnp.sum(rhs, axis=last, keepdims=True) / jnp.sum(
        coeffs[3], axis=last, keepdims=True
    )
    return solved + shift_col


def prepare_columns(weights, diag):
    lower = -weights[5]
    upper = -weights[4]
    across = diag + lower + upper
    return (
        lax.all_gather(lower, "gz", axis=2, tiled=True),
        lax.all_gather(diag, "gz", axis=2, tiled=True),
        lax.all_gather(upper, "gz", axis=2, tiled=True),
        lax.all_gather(across, "gz", axis=2, tiled=True),
    )


def column_solve(rhs, coeffs):
    depth = rhs.shape[2]
    whole = lax.all_gather(rhs, "gz", axis=2, tiled=True)
    solved = tridiag(coeffs, whole)
    return lax.dynamic_slice_in_dim(solved, lax.axis_index("gz") * depth, depth, 2)


def per_device(residual_q2, viscosity, pinned):
    fluid1 = 1.0 / viscosity
    pin1 = 4.0 * pinned.astype(jnp.float32) * fluid1
    rhs1 = coarsen(residual_q2.astype(jnp.float32))
    fluid2 = coarsen(fluid1) / 8.0
    pin2 = coarsen(pin1) / 4.0
    fluid3 = coarsen(fluid2) / 8.0
    pin3 = coarsen(pin2) / 4.0
    weights1 = couplings(fluid1, 1.0)
    weights2 = couplings(fluid2, 2.0)
    weights3 = couplings(fluid3, 4.0)
    diag1 = sum(weights1) + pin1
    diag2 = sum(weights2) + pin2
    diag3 = sum(weights3) + pin3
    coeffs = prepare_columns(weights3, diag3)
    corr1 = presmooth(rhs1, weights1, diag1)
    rhs2 = coarsen(rhs1 - apply_op(corr1, weights1, diag1))
    corr2 = presmooth(rhs2, weights2, diag2)
    rhs3 = coarsen(rhs2 - apply_op(corr2, weights2, diag2))
    corr3 = column_solve(rhs3, coeffs)
    corr3 = corr3 + column_solve(rhs3 - apply_op(corr3, weights3, diag3), coeffs)
    corr2 = postsmooth(corr2 + refine(corr3), rhs2, weights2, diag2)
    corr1 = postsmooth(corr1 + refine(corr2), rhs1, weights1, diag1)
    return diag1 * corr1


PLANE = (32, 32)
SPLIT = (2, 4)
ROWS = 8
LANES = 128
HALO = 16
NEAR = 8
PIECE = 8
TINY = 1e-30
F32 = jnp.float32


def iota(shape, dim):
    return lax.broadcasted_iota(jnp.int32, shape, dim)


def dot01(field, chosen, dims=(((1,), (0,)), ((), ()))):
    total = None
    rest = field
    for part in range(3):
        piece = rest.astype(jnp.bfloat16)
        term = lax.dot_general(piece, chosen, dims, preferred_element_type=F32)
        total = term if total is None else total + term
        if part < 2:
            rest = rest - piece.astype(F32)
    return total


def dot10(chosen, field):
    total = None
    rest = field
    for part in range(3):
        piece = rest.astype(jnp.bfloat16)
        term = lax.dot_general(
            chosen, piece, (((1,), (1,)), ((), ())), preferred_element_type=F32
        )
        total = term if total is None else total + term
        if part < 2:
            rest = rest - piece.astype(F32)
    return total


def where01(condition):
    return jnp.where(condition, 1.0, 0.0).astype(jnp.bfloat16)


def loop(low, high, size, body):
    for plane in range(low, high, size):
        body(plane, min(size, high - plane))


def inverse_of(field):
    first = pl.reciprocal(field, approx=True)
    return first * (2.0 - field * first)


class Level:
    def __init__(self, level):
        self.ny = PLANE[1] >> level
        self.xs = 4 >> level
        self.factor = float(2**level)

    def masks(self, shape):
        lane = iota(shape, 2)
        row = iota(shape, 1)
        within = (lane // self.ny) % self.xs
        y = lane % self.ny
        last_x = (row == ROWS - 1) & (within == self.xs - 1)
        return within, y == self.ny - 1, last_x

    def next_x(self, field):
        within = (iota(field.shape, 2) // self.ny) % self.xs
        moved = pltpu.roll(field, LANES - self.ny, 2)
        return jnp.where(within == self.xs - 1, pltpu.roll(moved, ROWS - 1, 1), moved)

    def last_x(self, field):
        within = (iota(field.shape, 2) // self.ny) % self.xs
        moved = pltpu.roll(field, self.ny, 2)
        return jnp.where(within == 0, pltpu.roll(moved, 1, 1), moved)

    def next_y(self, field):
        return pltpu.roll(field, LANES - 1, 2)

    def last_y(self, field):
        return pltpu.roll(field, 1, 2)

    def spread(self, field, scaled, plane, count):
        mid = field[1:-1]
        near = (
            self.next_x(mid), self.last_x(mid), self.next_y(mid), self.last_y(mid),
            field[2:], field[:-2],
        )
        terms = [weight[pl.ds(plane, count)] * value for weight, value in zip(scaled, near)]
        return mid, ((terms[0] + terms[1]) + (terms[2] + terms[3])) + (terms[4] + terms[5])


def mean_of(fluid, near, factor):
    return ((factor * 2.0) * fluid * near) * inverse_of(jnp.maximum(fluid + near, TINY))


def set_level(level, low, high, fluid, pin, rhs, fields):
    scaled, start, diag = fields

    def body(plane, count):
        wide = fluid[pl.ds(plane - 1, count + 2)]
        mid = wide[1:-1]
        within, end_y, end_x = level.masks(mid.shape)
        to_x = jnp.where(end_x, 0.0, mean_of(mid, level.next_x(mid), level.factor))
        to_y = jnp.where(end_y, 0.0, mean_of(mid, level.next_y(mid), level.factor))
        to_z = mean_of(wide[:-1], wide[1:], level.factor)
        weights = (to_x, level.last_x(to_x), to_y, level.last_y(to_y), to_z[1:], to_z[:-1])
        total = (
            (weights[0] + weights[1])
            + (weights[2] + weights[3])
            + (weights[4] + weights[5])
            + pin[pl.ds(plane, count)]
        )
        gain = OMEGA * inverse_of(jnp.maximum(total, TINY))
        for target, weight in zip(scaled, weights):
            target[pl.ds(plane, count)] = gain * weight
        start[pl.ds(plane, count)] = gain * rhs[pl.ds(plane, count)]
        diag[pl.ds(plane, count)] = total

    loop(low, high, PIECE, body)


def sweep(level, low, high, fields, source, target):
    scaled, start, _ = fields

    def body(plane, count):
        mid, total = level.spread(source[pl.ds(plane - 1, count + 2)], scaled, plane, count)
        target[pl.ds(plane, count)] = (1.0 - OMEGA) * mid + (start[pl.ds(plane, count)] + total)

    loop(low, high, PIECE, body)


def pair_sum(field):
    half = field.reshape((field.shape[0] // 2, 2) + field.shape[1:])
    return half[:, 0] + half[:, 1]


def coarse_residual(level, low, high, fields, corr, target):
    scaled, start, diag = fields

    def body(plane, count):
        mid, total = level.spread(corr[pl.ds(plane - 1, count + 2)], scaled, plane, count)
        rest = (start[pl.ds(plane, count)] + total) - OMEGA * mid
        rest = rest * (diag[pl.ds(plane, count)] * (1.0 / OMEGA))
        target[pl.ds((plane - low) // 2, count // 2)] = pair_sum(rest)

    loop(low, high, PIECE, body)


def lanes_down(level):
    fine = iota((LANES, LANES), 0)
    coarse = iota((LANES, LANES), 1)
    ny, xs = PLANE[1] >> level, 4 >> level
    half = xs // 2
    same_x = ((fine // ny) % xs) // 2 == (coarse // (ny // 2)) % half
    same_y = (fine % ny) // 2 == coarse % (ny // 2)
    return where01((fine < ny * xs) & same_x & same_y)


def in_lanes(field, chosen):
    flat = field.reshape(field.shape[0] * ROWS, LANES)
    return dot01(flat, chosen).reshape(field.shape)


def peer_at(rank):
    ny = SPLIT[1]
    ix, place_on_row = rank // ny, rank % ny
    return ix * ny + (ny - 1 - place_on_row if ix % 2 else place_on_row)


def peer_of(group, rank):
    return peer_at(SPLIT[0] * SPLIT[1] - 1 - rank if group % 2 else rank)


def own_peer_of(rank):
    return jnp.where(lax.axis_index("gz") % 2 == 1, peer_of(1, rank), peer_of(0, rank))


def slab_of(ix, iy, group):
    nx, ny = SPLIT
    rank = ix * ny + jnp.where(ix % 2 == 1, ny - 1 - iy, iy)
    return group * nx * ny + jnp.where(group % 2 == 1, nx * ny - 1 - rank, rank)


def device_of(slab):
    nx, ny = SPLIT
    group, rank = slab // (nx * ny), slab % (nx * ny)
    rank = jnp.where(group % 2 == 1, nx * ny - 1 - rank, rank)
    row, column = rank // ny, rank % ny
    peer = row * ny + jnp.where(row % 2 == 1, ny - 1 - column, column)
    return peer * lax.axis_size("gz") + group


def prepare_kernel(share, res_ref, fluid_ref, pin_ref, out_ref):
    bx, by, depth = fluid_ref.shape
    cells = bx * by
    groups = bx // 4
    pick = where01(iota((depth, 2 * depth), 1) // 2 == iota((depth, 2 * depth), 0))
    deep = lax.dot_general(
        pick, res_ref[...], (((1,), (1,)), ((), ())), preferred_element_type=F32
    )

    def lane_of(x, y):
        return (x % 4) * (groups * by) + (x // 4) * by + y

    fine = iota((4 * cells, cells), 0)
    lane = iota((4 * cells, cells), 1)
    chosen = where01(lane_of(fine // (4 * by), (fine % (2 * by)) // 2) == lane)
    rhs = dot01(deep, chosen)
    cell = iota((cells, cells), 0)
    lane = iota((cells, cells), 1)
    chosen = where01(lane_of(cell // by, cell % by) == lane)
    fluid = dot01(fluid_ref[...].reshape(cells, depth).T, chosen)
    pin = dot01(pin_ref[...].reshape(cells, depth).T, chosen)
    for rank in range(depth // share):
        peer, begin = own_peer_of(rank), rank * share
        for index, field in enumerate((fluid, rhs, pin)):
            out_ref[peer, index * share : (index + 1) * share] = field[begin : begin + share]


def spread_kernel(groups, by, gathered, own):
    for start in range(0, own.shape[0], ROWS):
        place(gathered, start, own, start, groups, by)


def place(gathered, row, target, plane, groups, by):
    group = (iota((ROWS, LANES), 1) // by) % groups
    nx, ny = SPLIT
    for ix in range(nx):
        found = [gathered[ix * ny + iy, pl.ds(row, ROWS), :] for iy in range(ny)]
        for part in range(groups):
            total = found[part]
            for iy in range(ny):
                if iy != part:
                    moved = pltpu.roll(found[iy], (by * (iy - part)) % LANES, 1)
                    total = jnp.where(group == iy, moved, total)
            target[pl.ds(plane, ROWS), ix * groups + part, :] = total


def down_kernel(
    groups, by, depth,
    own, outer, inner,
    xn1, xl1, yn1, yl1, zn1, zl1, start1, diag1, corr1,
    xn2, xl2, yn2, yl2, zn2, zl2, start2, diag2, corr2,
    packed,
    fluid1, rhs1, pin1, other1, fluid2, rhs2, pin2, other2, sums,
):
    planes = depth + 2 * HALO
    part = slab_of(lax.axis_index("gx"), lax.axis_index("gy"), lax.axis_index("gz"))
    odd = part % 2 == 1
    for index, target in enumerate((fluid1, rhs1, pin1)):
        rows = slice(index * depth, (index + 1) * depth)
        target[0:HALO] = jnp.where(odd, inner[rows], outer[rows])
        target[HALO : HALO + depth] = own[rows]
        target[HALO + depth :] = jnp.where(odd, outer[rows], inner[rows])

    fine, coarse = Level(0), Level(1)
    down1, down2 = lanes_down(0), lanes_down(1)
    fields1 = ((xn1, xl1, yn1, yl1, zn1, zl1), start1, diag1)
    fields2 = ((xn2, xl2, yn2, yl2, zn2, zl2), start2, diag2)
    set_level(fine, 1, planes - 1, fluid1, pin1, rhs1, fields1)
    sweep(fine, 2, planes - 2, fields1, start1, other1)
    sweep(fine, 3, planes - 3, fields1, other1, corr1)
    count2 = depth // 2 + 2 * NEAR
    begin = HALO - 2 * NEAR
    for source, target, share in ((fluid1, fluid2, 8.0), (pin1, pin2, 4.0)):
        whole = pair_sum(source[begin : begin + 2 * count2])
        target[...] = in_lanes(whole, down1) * (1.0 / share)
    low2, high2 = (begin + 4) // 2, count2 - (begin + 4) // 2
    inner = high2 - low2
    coarse_residual(fine, begin + 2 * low2, begin + 2 * high2, fields1, corr1, sums)
    rhs2[low2:high2] = in_lanes(sums[0:inner], down1)
    set_level(coarse, low2, high2, fluid2, pin2, rhs2, fields2)
    sweep(coarse, low2 + 1, high2 - 1, fields2, start2, other2)
    sweep(coarse, low2 + 2, high2 - 2, fields2, other2, corr2)
    coarse_residual(coarse, NEAR, NEAR + depth // 2, fields2, corr2, sums)
    count3 = depth // 4
    rhs3 = in_lanes(sums[0:count3], down2)
    fluid3 = in_lanes(pair_sum(fluid2[NEAR : NEAR + 2 * count3]), down2) * 0.125
    pin3 = in_lanes(pair_sum(pin2[NEAR : NEAR + 2 * count3]), down2) * 0.25
    lane = iota((count3, LANES), 1) // ROWS
    first = jnp.zeros((count3, LANES), F32)
    second = jnp.zeros((count3, LANES), F32)
    for row in range(ROWS):
        first = jnp.where(lane == row, rhs3[:, row, :], first)
        first = jnp.where(lane == ROWS + row, fluid3[:, row, :], first)
        second = jnp.where(lane % ROWS == row, pin3[:, row, :], second)
    packed[0] = first[0:2]
    packed[1] = first[2:4]
    packed[2] = jnp.where(lane[0:2] < ROWS, second[0:2], second[2:4])
    lane = iota((1, LANES), 1) // (LANES // 4)
    for index, plane in enumerate((NEAR + depth // 2 - 5, NEAR + 4)):
        for half in range(2):
            row = jnp.zeros((1, LANES), F32)
            for quarter in range(4):
                at = half * 4 + quarter
                row = jnp.where(lane == quarter, corr2[plane, at : at + 1, :], row)
            packed[3 + index, half : half + 1, :] = row


def rolled(field, shift):
    count = field.shape[0]
    shift %= count
    if shift % ROWS:
        return pltpu.roll(field, shift, 0)
    return jnp.concatenate([field[count - shift :], field[: count - shift]], axis=0)


def columns(rhs, fluid, pin):
    depth = fluid.shape[0]
    z, lane = iota(fluid.shape, 0), iota(fluid.shape, 1)
    y, x = lane % ROWS, (lane // ROWS) % ROWS

    def next_x(field):
        return pltpu.roll(field, LANES - ROWS, 1)

    def next_y(field):
        return pltpu.roll(field, LANES - 1, 1)

    wz = jnp.where(z == depth - 1, 0.0, mean_of(fluid, rolled(fluid, -1), 4.0))
    wy = jnp.where(y == ROWS - 1, 0.0, mean_of(fluid, next_y(fluid), 4.0))
    wx = jnp.where(x == ROWS - 1, 0.0, mean_of(fluid, next_x(fluid), 4.0))
    across = (wx + pltpu.roll(wx, ROWS, 1)) + (wy + pltpu.roll(wy, 1, 1)) + pin
    share = 1.0 / jnp.sum(across, axis=0, keepdims=True)

    above, below, own = rolled(wz, 1), wz, across
    steps = []
    stride = 1
    while stride < depth:
        inverse = inverse_of(above + below + own)
        up = above * rolled(inverse, stride)
        down = below * rolled(inverse, -stride)
        own = own + up * rolled(own, stride) + down * rolled(own, -stride)
        above = up * rolled(above, stride)
        below = down * rolled(below, -stride)
        steps.append((stride, up, down))
        stride *= 2
    inverse = inverse_of(above + below + own)

    def solve(right):
        mean = jnp.sum(right, axis=0, keepdims=True) * share
        for stride, up, down in steps:
            right = right + up * rolled(right, stride) + down * rolled(right, -stride)
        return right * inverse + mean

    corr = solve(rhs)
    flow_x = wx * (next_x(corr) - corr)
    flow_y = wy * (next_y(corr) - corr)
    flow_z = wz * (rolled(corr, -1) - corr)
    rest = (
        (rhs - pin * corr)
        + (flow_x - pltpu.roll(flow_x, ROWS, 1))
        + (flow_y - pltpu.roll(flow_y, 1, 1))
        + (flow_z - rolled(flow_z, 1))
    )
    return corr + solve(rest)


def up_kernel(
    groups, by, depth,
    packed,
    xn1, xl1, yn1, yl1, zn1, zl1, start1, diag1, corr1,
    xn2, xl2, yn2, yl2, zn2, zl2, start2, diag2, corr2,
    out_ref,
    one1, two1, one2, two2, lifted, first, second, solved,
):
    count3 = depth // 4
    shares = packed.shape[0]
    peers = SPLIT[0] * SPLIT[1]
    for slab in range(shares):
        index = peer_of(slab // peers, slab % peers) * (shares // peers) + slab // peers
        row = slab * count3
        first[row : row + 2] = packed[index, 0]
        first[row + 2 : row + 4] = packed[index, 1]
        both = packed[index, 2]
        second[row : row + 2] = both
        second[row + 2 : row + 4] = pltpu.roll(both, LANES // 2, 1)
    half = iota((shares * count3, LANES), 1) < LANES // 2

    def low_half(field):
        return jnp.where(half, field, pltpu.roll(field, LANES // 2, 1))

    def high_half(field):
        return jnp.where(half, pltpu.roll(field, LANES // 2, 1), field)

    solved[NEAR : NEAR + shares * count3] = columns(
        low_half(first[...]), high_half(first[...]), low_half(second[...])
    )
    solved[0:NEAR] = jnp.zeros((NEAR, LANES), F32)
    solved[NEAR + shares * count3 :] = jnp.zeros((2 * NEAR, LANES), F32)

    nx, ny = SPLIT
    part = slab_of(lax.axis_index("gx"), lax.axis_index("gy"), lax.axis_index("gz"))
    count = count3 + 2 * NEAR
    tall = solved[pl.ds(part * count3, count + count3), :]
    fine, coarse = Level(0), Level(1)
    cell = iota((LANES, ROWS * LANES), 0)
    lane = iota((LANES, ROWS * LANES), 1)
    same_y = cell % ROWS == (lane % coarse.ny) // 2
    spread = where01((cell // ROWS == lane // LANES) & same_y)
    wide = dot01(tall, spread)
    for row in range(ROWS):
        lifted[0:count, row, :] = wide[:count, row * LANES : (row + 1) * LANES]

    fields1 = ((xn1, xl1, yn1, yl1, zn1, zl1), start1, diag1)
    fields2 = ((xn2, xl2, yn2, yl2, zn2, zl2), start2, diag2)
    low, high = NEAR - 4, NEAR + depth // 2 + 4
    parents = lifted[low // 2 + NEAR // 2 : high // 2 + NEAR // 2]
    twice = jnp.broadcast_to(parents[:, None], (parents.shape[0], 2, ROWS, LANES))
    reach = depth // 2 + NEAR
    quarter = iota((ROWS, LANES), 1) // (LANES // 4)
    row = iota((ROWS, LANES), 0)

    def unpacked(index, which):
        pair = packed[device_of(jnp.clip(index, 0, shares - 1)), which]
        total = None
        for shift in range(4):
            moved = pltpu.roll(pair, shift * (LANES // 4), 1)
            wide = jnp.where(row < 4, moved[0:1, :], moved[1:2, :])
            kept = jnp.where((quarter - shift) % 4 == row % 4, wide, 0.0)
            total = kept if total is None else total + kept
        return total

    before, after = unpacked(part - 1, 3), unpacked(part + 1, 4)
    one2[low - 1] = before + lifted[(low - 1) // 2 + NEAR // 2]
    one2[low:high] = corr2[low:high] + twice.reshape(high - low, ROWS, LANES)
    one2[high] = after + lifted[high // 2 + NEAR // 2]
    sweep(coarse, NEAR - 4, reach + 4, fields2, one2, two2)
    sweep(coarse, NEAR - 3, reach + 3, fields2, two2, one2)
    sweep(coarse, NEAR - 2, reach + 2, fields2, one2, two2)

    fine_lane, coarse_lane = iota((LANES, LANES), 1), iota((LANES, LANES), 0)
    x_of = (fine_lane // fine.ny) // 2
    y_of = (fine_lane % fine.ny) // 2
    up = where01(coarse_lane == x_of * coarse.ny + y_of)
    lifted[0 : depth // 2 + 4] = in_lanes(two2[NEAR - 2 : reach + 2], up)
    parents = lifted[0 : depth // 2 + 4]
    twice = jnp.broadcast_to(parents[:, None], (parents.shape[0], 2, ROWS, LANES))
    low, high = HALO - 4, HALO + depth + 4
    one1[low:high] = corr1[low:high] + twice.reshape(high - low, ROWS, LANES)
    reach = depth + HALO
    sweep(fine, HALO - 2, reach + 2, fields1, one1, two1)
    sweep(fine, HALO - 1, reach + 1, fields1, two1, one1)
    sweep(fine, HALO, reach, fields1, one1, two1)

    group = (iota((depth, LANES), 1) // by) % groups
    for ix in range(nx):
        scaled = [
            two1[HALO:reach, ix * groups + part, :] * diag1[HALO:reach, ix * groups + part, :]
            for part in range(groups)
        ]
        for iy in range(ny):
            total = scaled[iy]
            for part in range(groups):
                if part != iy:
                    moved = pltpu.roll(scaled[part], (by * (part - iy)) % LANES, 1)
                    total = jnp.where(group == part, moved, total)
            out_ref[ix * ny + iy] = total


def finish_kernel(blocks, out_ref):
    bx, by, depth = out_ref.shape
    cells = bx * by
    cell = iota((cells, cells), 0)
    lane = iota((cells, cells), 1)
    x, y = cell // by, cell % by
    chosen = where01((x % 4) * (bx // 4 * by) + (x // 4) * by + y == lane)
    peers = blocks.shape[0]
    ordered = jnp.concatenate([blocks[own_peer_of(rank)] for rank in range(peers)], axis=0)
    out_ref[...] = dot10(chosen, ordered).reshape(out_ref.shape)


def whole_planes(residual_q2, viscosity, pinned):
    bx, by, depth = viscosity.shape
    groups = bx // 4
    peers = SPLIT[0] * SPLIT[1]
    share = depth // peers
    planes = share + 2 * HALO
    count2 = share // 2 + 2 * NEAR
    limit = pltpu.CompilerParams(vmem_limit_bytes=32 * 2**20)

    def flat(rows):
        return jax.ShapeDtypeStruct((rows, LANES), F32)

    def blocks(count, rows):
        return jax.ShapeDtypeStruct((count, rows, LANES), F32)

    def room(count):
        return pltpu.VMEM((count, ROWS, LANES), F32)

    fluid = 1.0 / viscosity
    pin = 4.0 * pinned.astype(F32) * fluid
    parcels = pl.pallas_call(
        functools.partial(prepare_kernel, share),
        out_shape=blocks(peers, 3 * share),
        compiler_params=limit,
        name="prepare",
    )(residual_q2.reshape(4 * bx * by, 2 * depth), fluid, pin)
    own = pl.pallas_call(
        functools.partial(spread_kernel, groups, by),
        out_shape=blocks(3 * share, ROWS),
        compiler_params=limit,
        name="spread",
    )(lax.all_to_all(parcels, ("gx", "gy"), 0, 0, tiled=True))
    length = lax.axis_size("gz")
    parts = length * peers

    device = [peer_of(i // peers, i % peers) * length + i // peers for i in range(parts)]

    def swap(field, first):
        pairs = [(device[i], device[i + 1]) for i in range(first, parts - 1, 2)]
        return lax.ppermute(field, ("gx", "gy", "gz"), pairs + [pair[::-1] for pair in pairs])

    outer, inner = swap(own, 1), swap(own, 0)
    saved = (blocks(planes, ROWS),) * 9 + (blocks(count2, ROWS),) * 9
    results = pl.pallas_call(
        functools.partial(down_kernel, groups, by, share),
        out_shape=saved + (blocks(5, 2),),
        scratch_shapes=[room(planes)] * 4 + [room(count2)] * 5,
        compiler_params=limit,
        name="down",
    )(own, outer, inner)
    copies = jnp.broadcast_to(results[-1], (parts,) + results[-1].shape)
    packed = lax.all_to_all(copies, ("gx", "gy", "gz"), 0, 0, tiled=True)
    depth3 = parts * share // 4
    mine = pl.pallas_call(
        functools.partial(up_kernel, groups, by, share),
        out_shape=blocks(peers, share),
        scratch_shapes=[room(planes), room(planes), room(count2), room(count2), room(count2)]
        + [pltpu.VMEM((rows, LANES), F32) for rows in (depth3, depth3, depth3 + 3 * NEAR)],
        compiler_params=limit,
        name="up",
    )(packed, *results[:-1])
    return pl.pallas_call(
        finish_kernel,
        out_shape=jax.ShapeDtypeStruct((bx, by, depth), F32),
        compiler_params=limit,
        name="finish",
    )(lax.all_to_all(mine, ("gx", "gy"), 0, 0, tiled=True))


def one_tile_planes(mesh, viscosity):
    split = (mesh.shape["gx"], mesh.shape["gy"])
    depth = viscosity.shape[2]
    fits = viscosity.shape[:2] == PLANE and split == SPLIT
    return fits and depth == 4 * LANES and depth // mesh.shape["gz"] == LANES


def solution(mesh):
    placed = (P("gx", "gy", "gz"), P("gx", "gy", "gz"), P("gx", "gy", "gz"))

    def cycle(residual_q2, viscosity, pinned):
        chosen = whole_planes if one_tile_planes(mesh, viscosity) else per_device
        return jax.shard_map(
            chosen, mesh=mesh, in_specs=placed, out_specs=P("gx", "gy", "gz"), check_vma=False
        )(residual_q2, viscosity, pinned)

    return cycle
```

```python
import functools

import jax
import jax.numpy as jnp
from jax import lax
from jax.experimental import pallas as pl
from jax.experimental.pallas import tpu as pltpu
from jax.sharding import PartitionSpec as P

NU = 3


OMEGA = 0.6


def with_halo(block, sides, width):
    for axis, dim in sides:
        count = lax.axis_size(axis)
        forward = [(i, i + 1) for i in range(count - 1)]
        backward = [(target, source) for source, target in forward]
        low = lax.ppermute(
            lax.slice_in_dim(block, block.shape[dim] - width, None, axis=dim), axis, forward
        )
        high = lax.ppermute(lax.slice_in_dim(block, 0, width, axis=dim), axis, backward)
        block = jnp.concatenate([low, block, high], axis=dim)
    return block


def coarsen(x):
    a, b, c = x.shape
    return x.reshape(a // 2, 2, b // 2, 2, c // 2, 2).sum(axis=(1, 3, 5))


def refine(x):
    return jnp.repeat(jnp.repeat(jnp.repeat(x, 2, 0), 2, 1), 2, 2)


def extended(field):
    return with_halo(field, (("gx", 0), ("gy", 1), ("gz", 2)), 1)


def shifted(padded):
    return [
        padded[2:, 1:-1, 1:-1],
        padded[:-2, 1:-1, 1:-1],
        padded[1:-1, 2:, 1:-1],
        padded[1:-1, :-2, 1:-1],
        padded[1:-1, 1:-1, 2:],
        padded[1:-1, 1:-1, :-2],
    ]


def neighbours(field):
    return shifted(extended(field))


def harmonic(fluid, near, factor):
    total = fluid + near
    return jnp.where(total > 0, factor * 2.0 * fluid * near / jnp.where(total > 0, total, 1.0), 0.0)


def couplings(fluid, factor):
    return [harmonic(fluid, near, factor) for near in neighbours(fluid)]


def apply_op(field, weights, diag):
    total = diag * field
    for weight, near in zip(weights, neighbours(field)):
        total = total - weight * near
    return total


def presmooth(rhs, weights, diag):
    corr = OMEGA * rhs / diag
    for sweep in range(NU - 1):
        corr = corr + OMEGA * (rhs - apply_op(corr, weights, diag)) / diag
    return corr


def postsmooth(corr, rhs, weights, diag):
    for sweep in range(NU):
        corr = corr + OMEGA * (rhs - apply_op(corr, weights, diag)) / diag
    return corr


def tridiag(coeffs, rhs):
    solved = lax.linalg.tridiagonal_solve(coeffs[0], coeffs[1], coeffs[2], rhs[..., None])[..., 0]
    last = rhs.ndim - 1
    shift_col = jnp.sum(rhs, axis=last, keepdims=True) / jnp.sum(
        coeffs[3], axis=last, keepdims=True
    )
    return solved + shift_col


def prepare_columns(weights, diag):
    lower = -weights[5]
    upper = -weights[4]
    across = diag + lower + upper
    return (
        lax.all_gather(lower, "gz", axis=2, tiled=True),
        lax.all_gather(diag, "gz", axis=2, tiled=True),
        lax.all_gather(upper, "gz", axis=2, tiled=True),
        lax.all_gather(across, "gz", axis=2, tiled=True),
    )


def column_solve(rhs, coeffs):
    depth = rhs.shape[2]
    whole = lax.all_gather(rhs, "gz", axis=2, tiled=True)
    solved = tridiag(coeffs, whole)
    return lax.dynamic_slice_in_dim(solved, lax.axis_index("gz") * depth, depth, 2)


def per_device(residual_q2, viscosity, pinned):
    fluid1 = 1.0 / viscosity
    pin1 = 4.0 * pinned.astype(jnp.float32) * fluid1
    rhs1 = coarsen(residual_q2.astype(jnp.float32))
    fluid2 = coarsen(fluid1) / 8.0
    pin2 = coarsen(pin1) / 4.0
    fluid3 = coarsen(fluid2) / 8.0
    pin3 = coarsen(pin2) / 4.0
    weights1 = couplings(fluid1, 1.0)
    weights2 = couplings(fluid2, 2.0)
    weights3 = couplings(fluid3, 4.0)
    diag1 = sum(weights1) + pin1
    diag2 = sum(weights2) + pin2
    diag3 = sum(weights3) + pin3
    coeffs = prepare_columns(weights3, diag3)
    corr1 = presmooth(rhs1, weights1, diag1)
    rhs2 = coarsen(rhs1 - apply_op(corr1, weights1, diag1))
    corr2 = presmooth(rhs2, weights2, diag2)
    rhs3 = coarsen(rhs2 - apply_op(corr2, weights2, diag2))
    corr3 = column_solve(rhs3, coeffs)
    corr3 = corr3 + column_solve(rhs3 - apply_op(corr3, weights3, diag3), coeffs)
    corr2 = postsmooth(corr2 + refine(corr3), rhs2, weights2, diag2)
    corr1 = postsmooth(corr1 + refine(corr2), rhs1, weights1, diag1)
    return diag1 * corr1


PLANE = (32, 32)
SPLIT = (2, 4)
ROWS = 8
LANES = 128
HALO = 16
NEAR = 8
PIECE = 8
TINY = 1e-30
F32 = jnp.float32


def iota(shape, dim):
    return lax.broadcasted_iota(jnp.int32, shape, dim)


def dot01(field, chosen, dims=(((1,), (0,)), ((), ()))):
    total = None
    rest = field
    for part in range(3):
        piece = rest.astype(jnp.bfloat16)
        term = lax.dot_general(piece, chosen, dims, preferred_element_type=F32)
        total = term if total is None else total + term
        if part < 2:
            rest = rest - piece.astype(F32)
    return total


def dot10(chosen, field):
    total = None
    rest = field
    for part in range(3):
        piece = rest.astype(jnp.bfloat16)
        term = lax.dot_general(
            chosen, piece, (((1,), (1,)), ((), ())), preferred_element_type=F32
        )
        total = term if total is None else total + term
        if part < 2:
            rest = rest - piece.astype(F32)
    return total


def where01(condition):
    return jnp.where(condition, 1.0, 0.0).astype(jnp.bfloat16)


def loop(low, high, size, body):
    for plane in range(low, high, size):
        body(plane, min(size, high - plane))


def inverse_of(field):
    first = pl.reciprocal(field, approx=True)
    return first * (2.0 - field * first)


class Level:
    def __init__(self, level):
        self.ny = PLANE[1] >> level
        self.xs = 4 >> level
        self.factor = float(2**level)

    def masks(self, shape):
        lane = iota(shape, 2)
        row = iota(shape, 1)
        within = (lane // self.ny) % self.xs
        y = lane % self.ny
        last_x = (row == ROWS - 1) & (within == self.xs - 1)
        return within, y == self.ny - 1, last_x

    def next_x(self, field):
        within = (iota(field.shape, 2) // self.ny) % self.xs
        moved = pltpu.roll(field, LANES - self.ny, 2)
        return jnp.where(within == self.xs - 1, pltpu.roll(moved, ROWS - 1, 1), moved)

    def last_x(self, field):
        within = (iota(field.shape, 2) // self.ny) % self.xs
        moved = pltpu.roll(field, self.ny, 2)
        return jnp.where(within == 0, pltpu.roll(moved, 1, 1), moved)

    def next_y(self, field):
        return pltpu.roll(field, LANES - 1, 2)

    def last_y(self, field):
        return pltpu.roll(field, 1, 2)

    def spread(self, field, scaled, plane, count):
        mid = field[1:-1]
        near = (
            self.next_x(mid), self.last_x(mid), self.next_y(mid), self.last_y(mid),
            field[2:], field[:-2],
        )
        terms = [weight[pl.ds(plane, count)] * value for weight, value in zip(scaled, near)]
        return mid, ((terms[0] + terms[1]) + (terms[2] + terms[3])) + (terms[4] + terms[5])


def mean_of(fluid, near, factor):
    return ((factor * 2.0) * fluid * near) * inverse_of(jnp.maximum(fluid + near, TINY))


def set_level(level, low, high, fluid, pin, rhs, fields):
    scaled, start, diag = fields

    def body(plane, count):
        wide = fluid[pl.ds(plane - 1, count + 2)]
        mid = wide[1:-1]
        within, end_y, end_x = level.masks(mid.shape)
        to_x = jnp.where(end_x, 0.0, mean_of(mid, level.next_x(mid), level.factor))
        to_y = jnp.where(end_y, 0.0, mean_of(mid, level.next_y(mid), level.factor))
        to_z = mean_of(wide[:-1], wide[1:], level.factor)
        weights = (to_x, level.last_x(to_x), to_y, level.last_y(to_y), to_z[1:], to_z[:-1])
        total = (
            (weights[0] + weights[1])
            + (weights[2] + weights[3])
            + (weights[4] + weights[5])
            + pin[pl.ds(plane, count)]
        )
        gain = OMEGA * inverse_of(jnp.maximum(total, TINY))
        for target, weight in zip(scaled, weights):
            target[pl.ds(plane, count)] = gain * weight
        start[pl.ds(plane, count)] = gain * rhs[pl.ds(plane, count)]
        diag[pl.ds(plane, count)] = total

    loop(low, high, PIECE, body)


def sweep(level, low, high, fields, source, target):
    scaled, start, _ = fields

    def body(plane, count):
        mid, total = level.spread(source[pl.ds(plane - 1, count + 2)], scaled, plane, count)
        target[pl.ds(plane, count)] = (1.0 - OMEGA) * mid + (start[pl.ds(plane, count)] + total)

    loop(low, high, PIECE, body)


def pair_sum(field):
    half = field.reshape((field.shape[0] // 2, 2) + field.shape[1:])
    return half[:, 0] + half[:, 1]


def coarse_residual(level, low, high, fields, corr, target):
    scaled, start, diag = fields

    def body(plane, count):
        mid, total = level.spread(corr[pl.ds(plane - 1, count + 2)], scaled, plane, count)
        rest = (start[pl.ds(plane, count)] + total) - OMEGA * mid
        rest = rest * (diag[pl.ds(plane, count)] * (1.0 / OMEGA))
        target[pl.ds((plane - low) // 2, count // 2)] = pair_sum(rest)

    loop(low, high, PIECE, body)


def lanes_down(level):
    fine = iota((LANES, LANES), 0)
    coarse = iota((LANES, LANES), 1)
    ny, xs = PLANE[1] >> level, 4 >> level
    half = xs // 2
    same_x = ((fine // ny) % xs) // 2 == (coarse // (ny // 2)) % half
    same_y = (fine % ny) // 2 == coarse % (ny // 2)
    return where01((fine < ny * xs) & same_x & same_y)


def in_lanes(field, chosen):
    flat = field.reshape(field.shape[0] * ROWS, LANES)
    return dot01(flat, chosen).reshape(field.shape)


def path_of(group):
    nx, ny = SPLIT
    row, column = 0, 0
    for index in range(group + 1):
        columns = list(range(ny)) if column == 0 else list(range(ny))[::-1]
        if index % 2:
            path = [(row, at) for at in columns] + [(1 - row, at) for at in columns[::-1]]
        else:
            path = []
            for at in columns:
                path += [(row, at), (1 - row, at)]
                row = 1 - row
        row, column = path[-1]
    return [row * ny + column for row, column in path]


def lookup(table, index):
    found = table[0]
    for at, value in enumerate(table[1:], 1):
        found = jnp.where(index == at, value, found)
    return found


def own_peer_of(rank):
    return lookup([path_of(group)[rank] for group in range(lax.axis_size("gz"))], lax.axis_index("gz"))


def slabs_of(groups):
    peers = SPLIT[0] * SPLIT[1]
    return [
        group * peers + path_of(group).index(peer) for peer in range(peers) for group in range(groups)
    ]


def own_slab():
    nx, ny = SPLIT
    groups = lax.axis_size("gz")
    device = (lax.axis_index("gx") * ny + lax.axis_index("gy")) * groups + lax.axis_index("gz")
    return lookup(slabs_of(groups), device)


def devices_of(groups):
    slabs = slabs_of(groups)
    return [slabs.index(slab) for slab in range(len(slabs))]


def prepare_kernel(share, res_ref, fluid_ref, pin_ref, out_ref):
    bx, by, depth = fluid_ref.shape
    cells = bx * by
    groups = bx // 4
    pick = where01(iota((depth, 2 * depth), 1) // 2 == iota((depth, 2 * depth), 0))
    deep = lax.dot_general(
        pick, res_ref[...], (((1,), (1,)), ((), ())), preferred_element_type=F32
    )

    def lane_of(x, y):
        return (x % 4) * (groups * by) + (x // 4) * by + y

    fine = iota((4 * cells, cells), 0)
    lane = iota((4 * cells, cells), 1)
    chosen = where01(lane_of(fine // (4 * by), (fine % (2 * by)) // 2) == lane)
    rhs = dot01(deep, chosen)
    cell = iota((cells, cells), 0)
    lane = iota((cells, cells), 1)
    chosen = where01(lane_of(cell // by, cell % by) == lane)
    fluid = dot01(fluid_ref[...].reshape(cells, depth).T, chosen)
    pin = dot01(pin_ref[...].reshape(cells, depth).T, chosen)
    for rank in range(depth // share):
        peer, begin = own_peer_of(rank), rank * share
        for index, field in enumerate((fluid, rhs, pin)):
            out_ref[peer, index * share : (index + 1) * share] = field[begin : begin + share]


def spread_kernel(groups, by, gathered, own):
    for start in range(0, own.shape[0], ROWS):
        place(gathered, start, own, start, groups, by)


def place(gathered, row, target, plane, groups, by):
    group = (iota((ROWS, LANES), 1) // by) % groups
    nx, ny = SPLIT
    for ix in range(nx):
        found = [gathered[ix * ny + iy, pl.ds(row, ROWS), :] for iy in range(ny)]
        for part in range(groups):
            total = found[part]
            for iy in range(ny):
                if iy != part:
                    moved = pltpu.roll(found[iy], (by * (iy - part)) % LANES, 1)
                    total = jnp.where(group == iy, moved, total)
            target[pl.ds(plane, ROWS), ix * groups + part, :] = total


def down_kernel(
    groups, by, depth,
    own, outer, inner,
    xn1, xl1, yn1, yl1, zn1, zl1, start1, diag1, corr1,
    xn2, xl2, yn2, yl2, zn2, zl2, start2, diag2, corr2,
    packed,
    fluid1, rhs1, pin1, other1, fluid2, rhs2, pin2, other2, sums,
):
    planes = depth + 2 * HALO
    part = own_slab()
    odd = part % 2 == 1
    for index, target in enumerate((fluid1, rhs1, pin1)):
        rows = slice(index * depth, (index + 1) * depth)
        target[0:HALO] = jnp.where(odd, inner[rows], outer[rows])
        target[HALO : HALO + depth] = own[rows]
        target[HALO + depth :] = jnp.where(odd, outer[rows], inner[rows])

    fine, coarse = Level(0), Level(1)
    down1, down2 = lanes_down(0), lanes_down(1)
    fields1 = ((xn1, xl1, yn1, yl1, zn1, zl1), start1, diag1)
    fields2 = ((xn2, xl2, yn2, yl2, zn2, zl2), start2, diag2)
    set_level(fine, 1, planes - 1, fluid1, pin1, rhs1, fields1)
    sweep(fine, 2, planes - 2, fields1, start1, other1)
    sweep(fine, 3, planes - 3, fields1, other1, corr1)
    count2 = depth // 2 + 2 * NEAR
    begin = HALO - 2 * NEAR
    for source, target, share in ((fluid1, fluid2, 8.0), (pin1, pin2, 4.0)):
        whole = pair_sum(source[begin : begin + 2 * count2])
        target[...] = in_lanes(whole, down1) * (1.0 / share)
    low2, high2 = (begin + 4) // 2, count2 - (begin + 4) // 2
    inner = high2 - low2
    coarse_residual(fine, begin + 2 * low2, begin + 2 * high2, fields1, corr1, sums)
    rhs2[low2:high2] = in_lanes(sums[0:inner], down1)
    set_level(coarse, low2, high2, fluid2, pin2, rhs2, fields2)
    sweep(coarse, low2 + 1, high2 - 1, fields2, start2, other2)
    sweep(coarse, low2 + 2, high2 - 2, fields2, other2, corr2)
    coarse_residual(coarse, NEAR, NEAR + depth // 2, fields2, corr2, sums)
    count3 = depth // 4
    rhs3 = in_lanes(sums[0:count3], down2)
    fluid3 = in_lanes(pair_sum(fluid2[NEAR : NEAR + 2 * count3]), down2) * 0.125
    pin3 = in_lanes(pair_sum(pin2[NEAR : NEAR + 2 * count3]), down2) * 0.25
    lane = iota((count3, LANES), 1) // ROWS
    first = jnp.zeros((count3, LANES), F32)
    second = jnp.zeros((count3, LANES), F32)
    for row in range(ROWS):
        first = jnp.where(lane == row, rhs3[:, row, :], first)
        first = jnp.where(lane == ROWS + row, fluid3[:, row, :], first)
        second = jnp.where(lane % ROWS == row, pin3[:, row, :], second)
    packed[0] = first[0:2]
    packed[1] = first[2:4]
    packed[2] = jnp.where(lane[0:2] < ROWS, second[0:2], second[2:4])
    lane = iota((1, LANES), 1) // (LANES // 4)
    for index, plane in enumerate((NEAR + depth // 2 - 5, NEAR + 4)):
        for half in range(2):
            row = jnp.zeros((1, LANES), F32)
            for quarter in range(4):
                at = half * 4 + quarter
                row = jnp.where(lane == quarter, corr2[plane, at : at + 1, :], row)
            packed[3 + index, half : half + 1, :] = row


def rolled(field, shift):
    count = field.shape[0]
    shift %= count
    if shift % ROWS:
        return pltpu.roll(field, shift, 0)
    return jnp.concatenate([field[count - shift :], field[: count - shift]], axis=0)


def columns(rhs, fluid, pin):
    depth = fluid.shape[0]
    z, lane = iota(fluid.shape, 0), iota(fluid.shape, 1)
    y, x = lane % ROWS, (lane // ROWS) % ROWS

    def next_x(field):
        return pltpu.roll(field, LANES - ROWS, 1)

    def next_y(field):
        return pltpu.roll(field, LANES - 1, 1)

    wz = jnp.where(z == depth - 1, 0.0, mean_of(fluid, rolled(fluid, -1), 4.0))
    wy = jnp.where(y == ROWS - 1, 0.0, mean_of(fluid, next_y(fluid), 4.0))
    wx = jnp.where(x == ROWS - 1, 0.0, mean_of(fluid, next_x(fluid), 4.0))
    across = (wx + pltpu.roll(wx, ROWS, 1)) + (wy + pltpu.roll(wy, 1, 1)) + pin
    share = 1.0 / jnp.sum(across, axis=0, keepdims=True)

    above, below, own = rolled(wz, 1), wz, across
    steps = []
    stride = 1
    while stride < depth:
        inverse = inverse_of(above + below + own)
        up = above * rolled(inverse, stride)
        down = below * rolled(inverse, -stride)
        own = own + up * rolled(own, stride) + down * rolled(own, -stride)
        above = up * rolled(above, stride)
        below = down * rolled(below, -stride)
        steps.append((stride, up, down))
        stride *= 2
    inverse = inverse_of(above + below + own)

    def solve(right):
        mean = jnp.sum(right, axis=0, keepdims=True) * share
        for stride, up, down in steps:
            right = right + up * rolled(right, stride) + down * rolled(right, -stride)
        return right * inverse + mean

    corr = solve(rhs)
    flow_x = wx * (next_x(corr) - corr)
    flow_y = wy * (next_y(corr) - corr)
    flow_z = wz * (rolled(corr, -1) - corr)
    rest = (
        (rhs - pin * corr)
        + (flow_x - pltpu.roll(flow_x, ROWS, 1))
        + (flow_y - pltpu.roll(flow_y, 1, 1))
        + (flow_z - rolled(flow_z, 1))
    )
    return corr + solve(rest)


def up_kernel(
    groups, by, depth,
    packed,
    xn1, xl1, yn1, yl1, zn1, zl1, start1, diag1, corr1,
    xn2, xl2, yn2, yl2, zn2, zl2, start2, diag2, corr2,
    out_ref,
    one1, two1, one2, two2, lifted, first, second, solved,
):
    count3 = depth // 4
    shares = packed.shape[0]
    peers = SPLIT[0] * SPLIT[1]
    devices = devices_of(shares // peers)
    for slab, index in enumerate(devices):
        row = slab * count3
        first[row : row + 2] = packed[index, 0]
        first[row + 2 : row + 4] = packed[index, 1]
        both = packed[index, 2]
        second[row : row + 2] = both
        second[row + 2 : row + 4] = pltpu.roll(both, LANES // 2, 1)
    half = iota((shares * count3, LANES), 1) < LANES // 2

    def low_half(field):
        return jnp.where(half, field, pltpu.roll(field, LANES // 2, 1))

    def high_half(field):
        return jnp.where(half, pltpu.roll(field, LANES // 2, 1), field)

    solved[NEAR : NEAR + shares * count3] = columns(
        low_half(first[...]), high_half(first[...]), low_half(second[...])
    )
    solved[0:NEAR] = jnp.zeros((NEAR, LANES), F32)
    solved[NEAR + shares * count3 :] = jnp.zeros((2 * NEAR, LANES), F32)

    nx, ny = SPLIT
    part = own_slab()
    count = count3 + 2 * NEAR
    tall = solved[pl.ds(part * count3, count + count3), :]
    fine, coarse = Level(0), Level(1)
    cell = iota((LANES, LANES), 0)
    lane = iota((LANES, LANES), 1)
    spread = where01((cell < ROWS) & (cell == (lane % coarse.ny) // 2))
    rows = tall.shape[0]
    turned = [tall] + [pltpu.roll(tall, LANES - ROWS * row, 1) for row in range(1, ROWS)]
    wide = dot01(jnp.concatenate(turned, axis=0), spread)
    for row in range(ROWS):
        lifted[0:rows, row, :] = wide[row * rows : (row + 1) * rows]

    fields1 = ((xn1, xl1, yn1, yl1, zn1, zl1), start1, diag1)
    fields2 = ((xn2, xl2, yn2, yl2, zn2, zl2), start2, diag2)
    low, high = NEAR - 4, NEAR + depth // 2 + 4
    parents = lifted[low // 2 + NEAR // 2 : high // 2 + NEAR // 2]
    twice = jnp.broadcast_to(parents[:, None], (parents.shape[0], 2, ROWS, LANES))
    reach = depth // 2 + NEAR
    quarter = iota((ROWS, LANES), 1) // (LANES // 4)
    row = iota((ROWS, LANES), 0)

    def unpacked(index, which):
        pair = packed[lookup(devices, jnp.clip(index, 0, shares - 1)), which]
        total = None
        for shift in range(4):
            moved = pltpu.roll(pair, shift * (LANES // 4), 1)
            wide = jnp.where(row < 4, moved[0:1, :], moved[1:2, :])
            kept = jnp.where((quarter - shift) % 4 == row % 4, wide, 0.0)
            total = kept if total is None else total + kept
        return total

    before, after = unpacked(part - 1, 3), unpacked(part + 1, 4)
    one2[low - 1] = before + lifted[(low - 1) // 2 + NEAR // 2]
    one2[low:high] = corr2[low:high] + twice.reshape(high - low, ROWS, LANES)
    one2[high] = after + lifted[high // 2 + NEAR // 2]
    sweep(coarse, NEAR - 4, reach + 4, fields2, one2, two2)
    sweep(coarse, NEAR - 3, reach + 3, fields2, two2, one2)
    sweep(coarse, NEAR - 2, reach + 2, fields2, one2, two2)

    fine_lane, coarse_lane = iota((LANES, LANES), 1), iota((LANES, LANES), 0)
    x_of = (fine_lane // fine.ny) // 2
    y_of = (fine_lane % fine.ny) // 2
    up = where01(coarse_lane == x_of * coarse.ny + y_of)
    lifted[0 : depth // 2 + 4] = in_lanes(two2[NEAR - 2 : reach + 2], up)
    parents = lifted[0 : depth // 2 + 4]
    twice = jnp.broadcast_to(parents[:, None], (parents.shape[0], 2, ROWS, LANES))
    low, high = HALO - 4, HALO + depth + 4
    one1[low:high] = corr1[low:high] + twice.reshape(high - low, ROWS, LANES)
    reach = depth + HALO
    sweep(fine, HALO - 2, reach + 2, fields1, one1, two1)
    sweep(fine, HALO - 1, reach + 1, fields1, two1, one1)
    sweep(fine, HALO, reach, fields1, one1, two1)

    group = (iota((depth, LANES), 1) // by) % groups
    for ix in range(nx):
        scaled = [
            two1[HALO:reach, ix * groups + part, :] * diag1[HALO:reach, ix * groups + part, :]
            for part in range(groups)
        ]
        for iy in range(ny):
            total = scaled[iy]
            for part in range(groups):
                if part != iy:
                    moved = pltpu.roll(scaled[part], (by * (part - iy)) % LANES, 1)
                    total = jnp.where(group == part, moved, total)
            out_ref[ix * ny + iy] = total


def finish_kernel(blocks, out_ref):
    bx, by, depth = out_ref.shape
    cells = bx * by
    cell = iota((cells, cells), 0)
    lane = iota((cells, cells), 1)
    x, y = cell // by, cell % by
    chosen = where01((x % 4) * (bx // 4 * by) + (x // 4) * by + y == lane)
    peers = blocks.shape[0]
    ordered = jnp.concatenate([blocks[own_peer_of(rank)] for rank in range(peers)], axis=0)
    out_ref[...] = dot10(chosen, ordered).reshape(out_ref.shape)


def whole_planes(residual_q2, viscosity, pinned):
    bx, by, depth = viscosity.shape
    groups = bx // 4
    peers = SPLIT[0] * SPLIT[1]
    share = depth // peers
    planes = share + 2 * HALO
    count2 = share // 2 + 2 * NEAR
    limit = pltpu.CompilerParams(vmem_limit_bytes=32 * 2**20)

    def flat(rows):
        return jax.ShapeDtypeStruct((rows, LANES), F32)

    def blocks(count, rows):
        return jax.ShapeDtypeStruct((count, rows, LANES), F32)

    def room(count):
        return pltpu.VMEM((count, ROWS, LANES), F32)

    fluid = 1.0 / viscosity
    pin = 4.0 * pinned.astype(F32) * fluid
    parcels = pl.pallas_call(
        functools.partial(prepare_kernel, share),
        out_shape=blocks(peers, 3 * share),
        compiler_params=limit,
        name="prepare",
    )(residual_q2.reshape(4 * bx * by, 2 * depth), fluid, pin)
    own = pl.pallas_call(
        functools.partial(spread_kernel, groups, by),
        out_shape=blocks(3 * share, ROWS),
        compiler_params=limit,
        name="spread",
    )(lax.all_to_all(parcels, ("gx", "gy"), 0, 0, tiled=True))
    length = lax.axis_size("gz")
    parts = length * peers

    device = devices_of(length)

    def swap(field, first):
        pairs = [(device[i], device[i + 1]) for i in range(first, parts - 1, 2)]
        return lax.ppermute(field, ("gx", "gy", "gz"), pairs + [pair[::-1] for pair in pairs])

    outer, inner = swap(own, 1), swap(own, 0)
    saved = (blocks(planes, ROWS),) * 9 + (blocks(count2, ROWS),) * 9
    results = pl.pallas_call(
        functools.partial(down_kernel, groups, by, share),
        out_shape=saved + (blocks(5, 2),),
        scratch_shapes=[room(planes)] * 4 + [room(count2)] * 5,
        compiler_params=limit,
        name="down",
    )(own, outer, inner)
    copies = jnp.broadcast_to(results[-1], (parts,) + results[-1].shape)
    packed = lax.all_to_all(copies, ("gx", "gy", "gz"), 0, 0, tiled=True)
    depth3 = parts * share // 4
    mine = pl.pallas_call(
        functools.partial(up_kernel, groups, by, share),
        out_shape=blocks(peers, share),
        scratch_shapes=[room(planes), room(planes), room(count2), room(count2), room(count2)]
        + [pltpu.VMEM((rows, LANES), F32) for rows in (depth3, depth3, depth3 + 3 * NEAR)],
        compiler_params=limit,
        name="up",
    )(packed, *results[:-1])
    return pl.pallas_call(
        finish_kernel,
        out_shape=jax.ShapeDtypeStruct((bx, by, depth), F32),
        compiler_params=limit,
        name="finish",
    )(lax.all_to_all(mine, ("gx", "gy"), 0, 0, tiled=True))


def one_tile_planes(mesh, viscosity):
    split = (mesh.shape["gx"], mesh.shape["gy"])
    depth = viscosity.shape[2]
    fits = viscosity.shape[:2] == PLANE and split == SPLIT
    return fits and depth == 4 * LANES and depth // mesh.shape["gz"] == LANES


def solution(mesh):
    placed = (P("gx", "gy", "gz"), P("gx", "gy", "gz"), P("gx", "gy", "gz"))

    def cycle(residual_q2, viscosity, pinned):
        chosen = whole_planes if one_tile_planes(mesh, viscosity) else per_device
        return jax.shard_map(
            chosen, mesh=mesh, in_specs=placed, out_specs=P("gx", "gy", "gz"), check_vma=False
        )(residual_q2, viscosity, pinned)

    return cycle
```

```python
import functools

import jax
import jax.numpy as jnp
from jax import lax
from jax.experimental import pallas as pl
from jax.experimental.pallas import tpu as pltpu
from jax.sharding import PartitionSpec as P

NU = 3


OMEGA = 0.6


def with_halo(block, sides, width):
    for axis, dim in sides:
        count = lax.axis_size(axis)
        forward = [(i, i + 1) for i in range(count - 1)]
        backward = [(target, source) for source, target in forward]
        low = lax.ppermute(
            lax.slice_in_dim(block, block.shape[dim] - width, None, axis=dim), axis, forward
        )
        high = lax.ppermute(lax.slice_in_dim(block, 0, width, axis=dim), axis, backward)
        block = jnp.concatenate([low, block, high], axis=dim)
    return block


def coarsen(x):
    a, b, c = x.shape
    return x.reshape(a // 2, 2, b // 2, 2, c // 2, 2).sum(axis=(1, 3, 5))


def refine(x):
    return jnp.repeat(jnp.repeat(jnp.repeat(x, 2, 0), 2, 1), 2, 2)


def extended(field):
    return with_halo(field, (("gx", 0), ("gy", 1), ("gz", 2)), 1)


def shifted(padded):
    return [
        padded[2:, 1:-1, 1:-1],
        padded[:-2, 1:-1, 1:-1],
        padded[1:-1, 2:, 1:-1],
        padded[1:-1, :-2, 1:-1],
        padded[1:-1, 1:-1, 2:],
        padded[1:-1, 1:-1, :-2],
    ]


def neighbours(field):
    return shifted(extended(field))


def harmonic(fluid, near, factor):
    total = fluid + near
    return jnp.where(total > 0, factor * 2.0 * fluid * near / jnp.where(total > 0, total, 1.0), 0.0)


def couplings(fluid, factor):
    return [harmonic(fluid, near, factor) for near in neighbours(fluid)]


def apply_op(field, weights, diag):
    total = diag * field
    for weight, near in zip(weights, neighbours(field)):
        total = total - weight * near
    return total


def presmooth(rhs, weights, diag):
    corr = OMEGA * rhs / diag
    for sweep in range(NU - 1):
        corr = corr + OMEGA * (rhs - apply_op(corr, weights, diag)) / diag
    return corr


def postsmooth(corr, rhs, weights, diag):
    for sweep in range(NU):
        corr = corr + OMEGA * (rhs - apply_op(corr, weights, diag)) / diag
    return corr


def tridiag(coeffs, rhs):
    solved = lax.linalg.tridiagonal_solve(coeffs[0], coeffs[1], coeffs[2], rhs[..., None])[..., 0]
    last = rhs.ndim - 1
    shift_col = jnp.sum(rhs, axis=last, keepdims=True) / jnp.sum(
        coeffs[3], axis=last, keepdims=True
    )
    return solved + shift_col


def prepare_columns(weights, diag):
    lower = -weights[5]
    upper = -weights[4]
    across = diag + lower + upper
    return (
        lax.all_gather(lower, "gz", axis=2, tiled=True),
        lax.all_gather(diag, "gz", axis=2, tiled=True),
        lax.all_gather(upper, "gz", axis=2, tiled=True),
        lax.all_gather(across, "gz", axis=2, tiled=True),
    )


def column_solve(rhs, coeffs):
    depth = rhs.shape[2]
    whole = lax.all_gather(rhs, "gz", axis=2, tiled=True)
    solved = tridiag(coeffs, whole)
    return lax.dynamic_slice_in_dim(solved, lax.axis_index("gz") * depth, depth, 2)


def per_device(residual_q2, viscosity, pinned):
    fluid1 = 1.0 / viscosity
    pin1 = 4.0 * pinned.astype(jnp.float32) * fluid1
    rhs1 = coarsen(residual_q2.astype(jnp.float32))
    fluid2 = coarsen(fluid1) / 8.0
    pin2 = coarsen(pin1) / 4.0
    fluid3 = coarsen(fluid2) / 8.0
    pin3 = coarsen(pin2) / 4.0
    weights1 = couplings(fluid1, 1.0)
    weights2 = couplings(fluid2, 2.0)
    weights3 = couplings(fluid3, 4.0)
    diag1 = sum(weights1) + pin1
    diag2 = sum(weights2) + pin2
    diag3 = sum(weights3) + pin3
    coeffs = prepare_columns(weights3, diag3)
    corr1 = presmooth(rhs1, weights1, diag1)
    rhs2 = coarsen(rhs1 - apply_op(corr1, weights1, diag1))
    corr2 = presmooth(rhs2, weights2, diag2)
    rhs3 = coarsen(rhs2 - apply_op(corr2, weights2, diag2))
    corr3 = column_solve(rhs3, coeffs)
    corr3 = corr3 + column_solve(rhs3 - apply_op(corr3, weights3, diag3), coeffs)
    corr2 = postsmooth(corr2 + refine(corr3), rhs2, weights2, diag2)
    corr1 = postsmooth(corr1 + refine(corr2), rhs1, weights1, diag1)
    return diag1 * corr1


PLANE = (32, 32)
SPLIT = (2, 4)
ROWS = 8
LANES = 128
HALO = 10
NEAR = 8
PIECE = 8
TINY = 1e-30
F32 = jnp.float32


def iota(shape, dim):
    return lax.broadcasted_iota(jnp.int32, shape, dim)


def dot01(field, chosen, dims=(((1,), (0,)), ((), ()))):
    total = None
    rest = field
    for part in range(3):
        piece = rest.astype(jnp.bfloat16)
        term = lax.dot_general(piece, chosen, dims, preferred_element_type=F32)
        total = term if total is None else total + term
        if part < 2:
            rest = rest - piece.astype(F32)
    return total


def dot10(chosen, field):
    total = None
    rest = field
    for part in range(3):
        piece = rest.astype(jnp.bfloat16)
        term = lax.dot_general(
            chosen, piece, (((1,), (1,)), ((), ())), preferred_element_type=F32
        )
        total = term if total is None else total + term
        if part < 2:
            rest = rest - piece.astype(F32)
    return total


def where01(condition):
    return jnp.where(condition, 1.0, 0.0).astype(jnp.bfloat16)


def loop(low, high, size, body):
    for plane in range(low, high, size):
        body(plane, min(size, high - plane))


def inverse_of(field):
    first = pl.reciprocal(field, approx=True)
    return first * (2.0 - field * first)


class Level:
    def __init__(self, level):
        self.ny = PLANE[1] >> level
        self.xs = 4 >> level
        self.factor = float(2**level)

    def masks(self, shape):
        lane = iota(shape, 2)
        row = iota(shape, 1)
        within = (lane // self.ny) % self.xs
        y = lane % self.ny
        last_x = (row == ROWS - 1) & (within == self.xs - 1)
        return within, y == self.ny - 1, last_x

    def next_x(self, field):
        within = (iota(field.shape, 2) // self.ny) % self.xs
        moved = pltpu.roll(field, LANES - self.ny, 2)
        return jnp.where(within == self.xs - 1, pltpu.roll(moved, ROWS - 1, 1), moved)

    def last_x(self, field):
        within = (iota(field.shape, 2) // self.ny) % self.xs
        moved = pltpu.roll(field, self.ny, 2)
        return jnp.where(within == 0, pltpu.roll(moved, 1, 1), moved)

    def next_y(self, field):
        return pltpu.roll(field, LANES - 1, 2)

    def last_y(self, field):
        return pltpu.roll(field, 1, 2)

    def spread(self, field, scaled, plane, count):
        mid = field[1:-1]
        near = (
            self.next_x(mid), self.last_x(mid), self.next_y(mid), self.last_y(mid),
            field[2:], field[:-2],
        )
        terms = [weight[pl.ds(plane, count)] * value for weight, value in zip(scaled, near)]
        return mid, ((terms[0] + terms[1]) + (terms[2] + terms[3])) + (terms[4] + terms[5])


def mean_of(fluid, near, factor):
    return ((factor * 2.0) * fluid * near) * inverse_of(jnp.maximum(fluid + near, TINY))


def set_level(level, low, high, fluid, pin, rhs, fields):
    scaled, start, diag = fields

    def body(plane, count):
        wide = fluid[pl.ds(plane - 1, count + 2)]
        mid = wide[1:-1]
        within, end_y, end_x = level.masks(mid.shape)
        to_x = jnp.where(end_x, 0.0, mean_of(mid, level.next_x(mid), level.factor))
        to_y = jnp.where(end_y, 0.0, mean_of(mid, level.next_y(mid), level.factor))
        to_z = mean_of(wide[:-1], wide[1:], level.factor)
        weights = (to_x, level.last_x(to_x), to_y, level.last_y(to_y), to_z[1:], to_z[:-1])
        total = (
            (weights[0] + weights[1])
            + (weights[2] + weights[3])
            + (weights[4] + weights[5])
            + pin[pl.ds(plane, count)]
        )
        gain = OMEGA * inverse_of(jnp.maximum(total, TINY))
        for target, weight in zip(scaled, weights):
            target[pl.ds(plane, count)] = gain * weight
        start[pl.ds(plane, count)] = gain * rhs[pl.ds(plane, count)]
        diag[pl.ds(plane, count)] = total

    loop(low, high, PIECE, body)


def sweep(level, low, high, fields, source, target):
    scaled, start, _ = fields

    def body(plane, count):
        mid, total = level.spread(source[pl.ds(plane - 1, count + 2)], scaled, plane, count)
        target[pl.ds(plane, count)] = (1.0 - OMEGA) * mid + (start[pl.ds(plane, count)] + total)

    loop(low, high, PIECE, body)


def pair_sum(field):
    half = field.reshape((field.shape[0] // 2, 2) + field.shape[1:])
    return half[:, 0] + half[:, 1]


def coarse_residual(level, low, high, fields, corr, target):
    scaled, start, diag = fields

    def body(plane, count):
        mid, total = level.spread(corr[pl.ds(plane - 1, count + 2)], scaled, plane, count)
        rest = (start[pl.ds(plane, count)] + total) - OMEGA * mid
        rest = rest * (diag[pl.ds(plane, count)] * (1.0 / OMEGA))
        target[pl.ds((plane - low) // 2, count // 2)] = pair_sum(rest)

    loop(low, high, PIECE, body)


def lanes_down(level):
    fine = iota((LANES, LANES), 0)
    coarse = iota((LANES, LANES), 1)
    ny, xs = PLANE[1] >> level, 4 >> level
    half = xs // 2
    same_x = ((fine // ny) % xs) // 2 == (coarse // (ny // 2)) % half
    same_y = (fine % ny) // 2 == coarse % (ny // 2)
    return where01((fine < ny * xs) & same_x & same_y)


def in_lanes(field, chosen):
    flat = field.reshape(field.shape[0] * ROWS, LANES)
    return dot01(flat, chosen).reshape(field.shape)


def path_of(group):
    nx, ny = SPLIT
    row, column = 0, 0
    for index in range(group + 1):
        columns = list(range(ny)) if column == 0 else list(range(ny))[::-1]
        if index % 2:
            path = [(row, at) for at in columns] + [(1 - row, at) for at in columns[::-1]]
        else:
            path = []
            for at in columns:
                path += [(row, at), (1 - row, at)]
                row = 1 - row
        row, column = path[-1]
    return [row * ny + column for row, column in path]


def lookup(table, index):
    found = table[0]
    for at, value in enumerate(table[1:], 1):
        found = jnp.where(index == at, value, found)
    return found


def own_peer_of(rank):
    return lookup([path_of(group)[rank] for group in range(lax.axis_size("gz"))], lax.axis_index("gz"))


def slabs_of(groups):
    peers = SPLIT[0] * SPLIT[1]
    return [
        group * peers + path_of(group).index(peer) for peer in range(peers) for group in range(groups)
    ]


def own_slab():
    nx, ny = SPLIT
    groups = lax.axis_size("gz")
    device = (lax.axis_index("gx") * ny + lax.axis_index("gy")) * groups + lax.axis_index("gz")
    return lookup(slabs_of(groups), device)


def devices_of(groups):
    slabs = slabs_of(groups)
    return [slabs.index(slab) for slab in range(len(slabs))]


def prepare_kernel(share, res_ref, fluid_ref, pin_ref, out_ref):
    bx, by, depth = fluid_ref.shape
    cells = bx * by
    groups = bx // 4
    pick = where01(iota((depth, 2 * depth), 1) // 2 == iota((depth, 2 * depth), 0))
    deep = lax.dot_general(
        pick, res_ref[...], (((1,), (1,)), ((), ())), preferred_element_type=F32
    )

    def lane_of(x, y):
        return (x % 4) * (groups * by) + (x // 4) * by + y

    fine = iota((4 * cells, cells), 0)
    lane = iota((4 * cells, cells), 1)
    chosen = where01(lane_of(fine // (4 * by), (fine % (2 * by)) // 2) == lane)
    rhs = dot01(deep, chosen)
    cell = iota((cells, cells), 0)
    lane = iota((cells, cells), 1)
    chosen = where01(lane_of(cell // by, cell % by) == lane)
    fluid = dot01(fluid_ref[...].reshape(cells, depth).T, chosen)
    pin = dot01(pin_ref[...].reshape(cells, depth).T, chosen)
    for rank in range(depth // share):
        peer, begin = own_peer_of(rank), rank * share
        for index, field in enumerate((fluid, rhs, pin)):
            out_ref[peer, index * share : (index + 1) * share] = field[begin : begin + share]


def spread_kernel(groups, by, gathered, own, inner, outer):
    for start in range(0, own.shape[0], ROWS):
        place(gathered, start, own, start, groups, by)
    share = own.shape[0] // 3
    odd = own_slab() % 2 == 1
    top = share - HALO
    for index in range(3):
        rows = slice(index * HALO, (index + 1) * HALO)
        inner[rows] = own[pl.ds(index * share + jnp.where(odd, 0, top), HALO)]
        outer[rows] = own[pl.ds(index * share + jnp.where(odd, top, 0), HALO)]


def place(gathered, row, target, plane, groups, by):
    group = (iota((ROWS, LANES), 1) // by) % groups
    nx, ny = SPLIT
    for ix in range(nx):
        found = [gathered[ix * ny + iy, pl.ds(row, ROWS), :] for iy in range(ny)]
        for part in range(groups):
            total = found[part]
            for iy in range(ny):
                if iy != part:
                    moved = pltpu.roll(found[iy], (by * (iy - part)) % LANES, 1)
                    total = jnp.where(group == iy, moved, total)
            target[pl.ds(plane, ROWS), ix * groups + part, :] = total


def down_kernel(
    groups, by, depth,
    own, inner, outer,
    xn1, xl1, yn1, yl1, zn1, zl1, start1, diag1, corr1,
    xn2, xl2, yn2, yl2, zn2, zl2, start2, diag2, corr2,
    packed, inner2, outer2,
    fluid1, rhs1, pin1, other1, fluid2, rhs2, pin2, other2, sums,
):
    planes = depth + 2 * HALO
    part = own_slab()
    odd = part % 2 == 1
    for index, target in enumerate((fluid1, rhs1, pin1)):
        rows = slice(index * HALO, (index + 1) * HALO)
        target[0:HALO] = jnp.where(odd, inner[rows], outer[rows])
        target[HALO : HALO + depth] = own[index * depth : (index + 1) * depth]
        target[HALO + depth :] = jnp.where(odd, outer[rows], inner[rows])

    fine, coarse = Level(0), Level(1)
    down1, down2 = lanes_down(0), lanes_down(1)
    fields1 = ((xn1, xl1, yn1, yl1, zn1, zl1), start1, diag1)
    fields2 = ((xn2, xl2, yn2, yl2, zn2, zl2), start2, diag2)
    set_level(fine, 1, planes - 1, fluid1, pin1, rhs1, fields1)
    sweep(fine, 2, planes - 2, fields1, start1, other1)
    sweep(fine, 3, planes - 3, fields1, other1, corr1)
    first2, last2 = NEAR - HALO // 2, NEAR + depth // 2 + HALO // 2
    for source, target, share in ((fluid1, fluid2, 8.0), (pin1, pin2, 4.0)):
        target[first2:last2] = in_lanes(pair_sum(source[...]), down1) * (1.0 / share)
    low2, high2 = first2 + 2, last2 - 2
    coarse_residual(fine, 4, planes - 4, fields1, corr1, sums)
    rhs2[low2:high2] = in_lanes(sums[0 : high2 - low2], down1)
    set_level(coarse, low2 - 1, high2 + 1, fluid2, pin2, rhs2, fields2)
    sweep(coarse, low2 + 1, high2 - 1, fields2, start2, other2)
    sweep(coarse, low2 + 2, high2 - 2, fields2, other2, corr2)
    half = depth // 2
    above, below = NEAR + half - 5, NEAR + 1
    inner2[0:4] = corr2[pl.ds(jnp.where(odd, below, above), 4)]
    outer2[0:4] = corr2[pl.ds(jnp.where(odd, above, below), 4)]
    above, below = NEAR + half - 4, NEAR + 3
    inner2[4] = start2[jnp.where(odd, below, above)]
    outer2[4] = start2[jnp.where(odd, above, below)]
    coarse_residual(coarse, NEAR, NEAR + half, fields2, corr2, sums)
    count3 = depth // 4
    rhs3 = in_lanes(sums[0:count3], down2)
    fluid3 = in_lanes(pair_sum(fluid2[NEAR : NEAR + 2 * count3]), down2) * 0.125
    pin3 = in_lanes(pair_sum(pin2[NEAR : NEAR + 2 * count3]), down2) * 0.25
    lane = iota((count3, LANES), 1) // ROWS
    first = jnp.zeros((count3, LANES), F32)
    second = jnp.zeros((count3, LANES), F32)
    for row in range(ROWS):
        first = jnp.where(lane == row, rhs3[:, row, :], first)
        first = jnp.where(lane == ROWS + row, fluid3[:, row, :], first)
        second = jnp.where(lane % ROWS == row, pin3[:, row, :], second)
    packed[0] = first[0:2]
    packed[1] = first[2:4]
    packed[2] = jnp.where(lane[0:2] < ROWS, second[0:2], second[2:4])


def rolled(field, shift):
    count = field.shape[0]
    shift %= count
    if shift % ROWS:
        return pltpu.roll(field, shift, 0)
    return jnp.concatenate([field[count - shift :], field[: count - shift]], axis=0)


def columns(rhs, fluid, pin):
    depth = fluid.shape[0]
    z, lane = iota(fluid.shape, 0), iota(fluid.shape, 1)
    y, x = lane % ROWS, (lane // ROWS) % ROWS

    def next_x(field):
        return pltpu.roll(field, LANES - ROWS, 1)

    def next_y(field):
        return pltpu.roll(field, LANES - 1, 1)

    wz = jnp.where(z == depth - 1, 0.0, mean_of(fluid, rolled(fluid, -1), 4.0))
    wy = jnp.where(y == ROWS - 1, 0.0, mean_of(fluid, next_y(fluid), 4.0))
    wx = jnp.where(x == ROWS - 1, 0.0, mean_of(fluid, next_x(fluid), 4.0))
    across = (wx + pltpu.roll(wx, ROWS, 1)) + (wy + pltpu.roll(wy, 1, 1)) + pin
    share = 1.0 / jnp.sum(across, axis=0, keepdims=True)

    above, below, own = rolled(wz, 1), wz, across
    steps = []
    stride = 1
    while stride < depth:
        inverse = inverse_of(above + below + own)
        up = above * rolled(inverse, stride)
        down = below * rolled(inverse, -stride)
        own = own + up * rolled(own, stride) + down * rolled(own, -stride)
        above = up * rolled(above, stride)
        below = down * rolled(below, -stride)
        steps.append((stride, up, down))
        stride *= 2
    inverse = inverse_of(above + below + own)

    def solve(right):
        mean = jnp.sum(right, axis=0, keepdims=True) * share
        for stride, up, down in steps:
            right = right + up * rolled(right, stride) + down * rolled(right, -stride)
        return right * inverse + mean

    corr = solve(rhs)
    flow_x = wx * (next_x(corr) - corr)
    flow_y = wy * (next_y(corr) - corr)
    flow_z = wz * (rolled(corr, -1) - corr)
    rest = (
        (rhs - pin * corr)
        + (flow_x - pltpu.roll(flow_x, ROWS, 1))
        + (flow_y - pltpu.roll(flow_y, 1, 1))
        + (flow_z - rolled(flow_z, 1))
    )
    return corr + solve(rest)


def up_kernel(
    groups, by, depth,
    packed, inner2, outer2,
    xn1, xl1, yn1, yl1, zn1, zl1, start1, diag1, corr1,
    xn2, xl2, yn2, yl2, zn2, zl2, start2, diag2, corr2,
    out_ref,
    one1, two1, one2, two2, lifted, begun, first, second, solved,
):
    count3 = depth // 4
    shares = packed.shape[0]
    peers = SPLIT[0] * SPLIT[1]
    devices = devices_of(shares // peers)
    for slab, index in enumerate(devices):
        row = slab * count3
        first[row : row + 2] = packed[index, 0]
        first[row + 2 : row + 4] = packed[index, 1]
        both = packed[index, 2]
        second[row : row + 2] = both
        second[row + 2 : row + 4] = pltpu.roll(both, LANES // 2, 1)
    half = iota((shares * count3, LANES), 1) < LANES // 2

    def low_half(field):
        return jnp.where(half, field, pltpu.roll(field, LANES // 2, 1))

    def high_half(field):
        return jnp.where(half, pltpu.roll(field, LANES // 2, 1), field)

    solved[NEAR : NEAR + shares * count3] = columns(
        low_half(first[...]), high_half(first[...]), low_half(second[...])
    )
    solved[0:NEAR] = jnp.zeros((NEAR, LANES), F32)
    solved[NEAR + shares * count3 :] = jnp.zeros((2 * NEAR, LANES), F32)

    nx, ny = SPLIT
    part = own_slab()
    count = count3 + 2 * NEAR
    tall = solved[pl.ds(part * count3, count + count3), :]
    fine, coarse = Level(0), Level(1)
    cell = iota((LANES, LANES), 0)
    lane = iota((LANES, LANES), 1)
    spread = where01((cell < ROWS) & (cell == (lane % coarse.ny) // 2))
    rows = tall.shape[0]
    turned = [tall] + [pltpu.roll(tall, LANES - ROWS * row, 1) for row in range(1, ROWS)]
    wide = dot01(jnp.concatenate(turned, axis=0), spread)
    for row in range(ROWS):
        lifted[0:rows, row, :] = wide[row * rows : (row + 1) * rows]

    fields1 = ((xn1, xl1, yn1, yl1, zn1, zl1), start1, diag1)
    fields2 = ((xn2, xl2, yn2, yl2, zn2, zl2), begun, diag2)
    reach = depth // 2 + NEAR
    odd = part % 2 == 1
    below = jnp.where(odd, inner2[...], outer2[...])
    above = jnp.where(odd, outer2[...], inner2[...])
    for plane in range(NEAR - 5, reach + 5):
        if plane < NEAR - 1:
            corr = below[plane - (NEAR - 5)]
        elif plane > reach:
            corr = above[plane - (reach + 1)]
        else:
            corr = corr2[plane]
        one2[plane] = corr + lifted[plane // 2 + NEAR // 2]
    begun[NEAR - 4] = below[4]
    begun[NEAR - 3 : reach + 3] = start2[NEAR - 3 : reach + 3]
    begun[reach + 3] = above[4]
    sweep(coarse, NEAR - 4, reach + 4, fields2, one2, two2)
    sweep(coarse, NEAR - 3, reach + 3, fields2, two2, one2)
    sweep(coarse, NEAR - 2, reach + 2, fields2, one2, two2)

    fine_lane, coarse_lane = iota((LANES, LANES), 1), iota((LANES, LANES), 0)
    x_of = (fine_lane // fine.ny) // 2
    y_of = (fine_lane % fine.ny) // 2
    up = where01(coarse_lane == x_of * coarse.ny + y_of)
    lifted[0 : depth // 2 + 4] = in_lanes(two2[NEAR - 2 : reach + 2], up)
    parents = lifted[0 : depth // 2 + 4]
    twice = jnp.broadcast_to(parents[:, None], (parents.shape[0], 2, ROWS, LANES))
    low, high = HALO - 4, HALO + depth + 4
    one1[low:high] = corr1[low:high] + twice.reshape(high - low, ROWS, LANES)
    reach = depth + HALO
    sweep(fine, HALO - 2, reach + 2, fields1, one1, two1)
    sweep(fine, HALO - 1, reach + 1, fields1, two1, one1)
    sweep(fine, HALO, reach, fields1, one1, two1)

    group = (iota((depth, LANES), 1) // by) % groups
    for ix in range(nx):
        scaled = [
            two1[HALO:reach, ix * groups + part, :] * diag1[HALO:reach, ix * groups + part, :]
            for part in range(groups)
        ]
        for iy in range(ny):
            total = scaled[iy]
            for part in range(groups):
                if part != iy:
                    moved = pltpu.roll(scaled[part], (by * (part - iy)) % LANES, 1)
                    total = jnp.where(group == part, moved, total)
            out_ref[ix * ny + iy] = total


def finish_kernel(blocks, out_ref):
    bx, by, depth = out_ref.shape
    cells = bx * by
    cell = iota((cells, cells), 0)
    lane = iota((cells, cells), 1)
    x, y = cell // by, cell % by
    chosen = where01((x % 4) * (bx // 4 * by) + (x // 4) * by + y == lane)
    peers = blocks.shape[0]
    ordered = jnp.concatenate([blocks[own_peer_of(rank)] for rank in range(peers)], axis=0)
    out_ref[...] = dot10(chosen, ordered).reshape(out_ref.shape)


def whole_planes(residual_q2, viscosity, pinned):
    bx, by, depth = viscosity.shape
    groups = bx // 4
    peers = SPLIT[0] * SPLIT[1]
    share = depth // peers
    planes = share + 2 * HALO
    count2 = share // 2 + 2 * NEAR
    limit = pltpu.CompilerParams(vmem_limit_bytes=32 * 2**20)

    def flat(rows):
        return jax.ShapeDtypeStruct((rows, LANES), F32)

    def blocks(count, rows):
        return jax.ShapeDtypeStruct((count, rows, LANES), F32)

    def room(count):
        return pltpu.VMEM((count, ROWS, LANES), F32)

    fluid = 1.0 / viscosity
    pin = 4.0 * pinned.astype(F32) * fluid
    parcels = pl.pallas_call(
        functools.partial(prepare_kernel, share),
        out_shape=blocks(peers, 3 * share),
        compiler_params=limit,
        name="prepare",
    )(residual_q2.reshape(4 * bx * by, 2 * depth), fluid, pin)
    own, inner, outer = pl.pallas_call(
        functools.partial(spread_kernel, groups, by),
        out_shape=(blocks(3 * share, ROWS), blocks(3 * HALO, ROWS), blocks(3 * HALO, ROWS)),
        compiler_params=limit,
        name="spread",
    )(lax.all_to_all(parcels, ("gx", "gy"), 0, 0, tiled=True))
    length = lax.axis_size("gz")
    parts = length * peers

    device = devices_of(length)

    def swap(field, first):
        pairs = [(device[i], device[i + 1]) for i in range(first, parts - 1, 2)]
        return lax.ppermute(field, ("gx", "gy", "gz"), pairs + [pair[::-1] for pair in pairs])

    outer, inner = swap(outer, 1), swap(inner, 0)
    saved = (blocks(planes, ROWS),) * 9 + (blocks(count2, ROWS),) * 9
    results = pl.pallas_call(
        functools.partial(down_kernel, groups, by, share),
        out_shape=saved + (blocks(3, 2), blocks(5, ROWS), blocks(5, ROWS)),
        scratch_shapes=[room(planes)] * 4 + [room(count2)] * 5,
        compiler_params=limit,
        name="down",
    )(own, inner, outer)
    saved, (parcel, inner, outer) = results[:-3], results[-3:]
    outer, inner = swap(outer, 1), swap(inner, 0)
    copies = jnp.broadcast_to(parcel, (parts,) + parcel.shape)
    packed = lax.all_to_all(copies, ("gx", "gy", "gz"), 0, 0, tiled=True)
    depth3 = parts * share // 4
    mine = pl.pallas_call(
        functools.partial(up_kernel, groups, by, share),
        out_shape=blocks(peers, share),
        scratch_shapes=[room(planes)] * 2 + [room(count2)] * 4
        + [pltpu.VMEM((rows, LANES), F32) for rows in (depth3, depth3, depth3 + 3 * NEAR)],
        compiler_params=limit,
        name="up",
    )(packed, inner, outer, *saved)
    return pl.pallas_call(
        finish_kernel,
        out_shape=jax.ShapeDtypeStruct((bx, by, depth), F32),
        compiler_params=limit,
        name="finish",
    )(lax.all_to_all(mine, ("gx", "gy"), 0, 0, tiled=True))


def one_tile_planes(mesh, viscosity):
    split = (mesh.shape["gx"], mesh.shape["gy"])
    depth = viscosity.shape[2]
    fits = viscosity.shape[:2] == PLANE and split == SPLIT
    return fits and depth == 4 * LANES and depth // mesh.shape["gz"] == LANES


def solution(mesh):
    placed = (P("gx", "gy", "gz"), P("gx", "gy", "gz"), P("gx", "gy", "gz"))

    def cycle(residual_q2, viscosity, pinned):
        chosen = whole_planes if one_tile_planes(mesh, viscosity) else per_device
        return jax.shard_map(
            chosen, mesh=mesh, in_specs=placed, out_specs=P("gx", "gy", "gz"), check_vma=False
        )(residual_q2, viscosity, pinned)

    return cycle
```

```python
import functools

import jax
import jax.numpy as jnp
from jax import lax
from jax.experimental import pallas as pl
from jax.experimental.pallas import tpu as pltpu
from jax.sharding import PartitionSpec as P

NU = 3


OMEGA = 0.6


def with_halo(block, sides, width):
    for axis, dim in sides:
        count = lax.axis_size(axis)
        forward = [(i, i + 1) for i in range(count - 1)]
        backward = [(target, source) for source, target in forward]
        low = lax.ppermute(
            lax.slice_in_dim(block, block.shape[dim] - width, None, axis=dim), axis, forward
        )
        high = lax.ppermute(lax.slice_in_dim(block, 0, width, axis=dim), axis, backward)
        block = jnp.concatenate([low, block, high], axis=dim)
    return block


def coarsen(x):
    a, b, c = x.shape
    return x.reshape(a // 2, 2, b // 2, 2, c // 2, 2).sum(axis=(1, 3, 5))


def refine(x):
    return jnp.repeat(jnp.repeat(jnp.repeat(x, 2, 0), 2, 1), 2, 2)


def extended(field):
    return with_halo(field, (("gx", 0), ("gy", 1), ("gz", 2)), 1)


def shifted(padded):
    return [
        padded[2:, 1:-1, 1:-1],
        padded[:-2, 1:-1, 1:-1],
        padded[1:-1, 2:, 1:-1],
        padded[1:-1, :-2, 1:-1],
        padded[1:-1, 1:-1, 2:],
        padded[1:-1, 1:-1, :-2],
    ]


def neighbours(field):
    return shifted(extended(field))


def harmonic(fluid, near, factor):
    total = fluid + near
    return jnp.where(total > 0, factor * 2.0 * fluid * near / jnp.where(total > 0, total, 1.0), 0.0)


def couplings(fluid, factor):
    return [harmonic(fluid, near, factor) for near in neighbours(fluid)]


def apply_op(field, weights, diag):
    total = diag * field
    for weight, near in zip(weights, neighbours(field)):
        total = total - weight * near
    return total


def presmooth(rhs, weights, diag):
    corr = OMEGA * rhs / diag
    for sweep in range(NU - 1):
        corr = corr + OMEGA * (rhs - apply_op(corr, weights, diag)) / diag
    return corr


def postsmooth(corr, rhs, weights, diag):
    for sweep in range(NU):
        corr = corr + OMEGA * (rhs - apply_op(corr, weights, diag)) / diag
    return corr


def tridiag(coeffs, rhs):
    solved = lax.linalg.tridiagonal_solve(coeffs[0], coeffs[1], coeffs[2], rhs[..., None])[..., 0]
    last = rhs.ndim - 1
    shift_col = jnp.sum(rhs, axis=last, keepdims=True) / jnp.sum(
        coeffs[3], axis=last, keepdims=True
    )
    return solved + shift_col


def prepare_columns(weights, diag):
    lower = -weights[5]
    upper = -weights[4]
    across = diag + lower + upper
    return (
        lax.all_gather(lower, "gz", axis=2, tiled=True),
        lax.all_gather(diag, "gz", axis=2, tiled=True),
        lax.all_gather(upper, "gz", axis=2, tiled=True),
        lax.all_gather(across, "gz", axis=2, tiled=True),
    )


def column_solve(rhs, coeffs):
    depth = rhs.shape[2]
    whole = lax.all_gather(rhs, "gz", axis=2, tiled=True)
    solved = tridiag(coeffs, whole)
    return lax.dynamic_slice_in_dim(solved, lax.axis_index("gz") * depth, depth, 2)


def per_device(residual_q2, viscosity, pinned):
    fluid1 = 1.0 / viscosity
    pin1 = 4.0 * pinned.astype(jnp.float32) * fluid1
    rhs1 = coarsen(residual_q2.astype(jnp.float32))
    fluid2 = coarsen(fluid1) / 8.0
    pin2 = coarsen(pin1) / 4.0
    fluid3 = coarsen(fluid2) / 8.0
    pin3 = coarsen(pin2) / 4.0
    weights1 = couplings(fluid1, 1.0)
    weights2 = couplings(fluid2, 2.0)
    weights3 = couplings(fluid3, 4.0)
    diag1 = sum(weights1) + pin1
    diag2 = sum(weights2) + pin2
    diag3 = sum(weights3) + pin3
    coeffs = prepare_columns(weights3, diag3)
    corr1 = presmooth(rhs1, weights1, diag1)
    rhs2 = coarsen(rhs1 - apply_op(corr1, weights1, diag1))
    corr2 = presmooth(rhs2, weights2, diag2)
    rhs3 = coarsen(rhs2 - apply_op(corr2, weights2, diag2))
    corr3 = column_solve(rhs3, coeffs)
    corr3 = corr3 + column_solve(rhs3 - apply_op(corr3, weights3, diag3), coeffs)
    corr2 = postsmooth(corr2 + refine(corr3), rhs2, weights2, diag2)
    corr1 = postsmooth(corr1 + refine(corr2), rhs1, weights1, diag1)
    return diag1 * corr1


PLANE = (32, 32)
SPLIT = (2, 4)
ROWS = 8
LANES = 128
HALO = 16
NEAR = 8
PIECE = 8
TINY = 1e-30
F32 = jnp.float32


def iota(shape, dim):
    return lax.broadcasted_iota(jnp.int32, shape, dim)


def dot01(field, chosen, dims=(((1,), (0,)), ((), ()))):
    total = None
    rest = field
    for part in range(3):
        piece = rest.astype(jnp.bfloat16)
        term = lax.dot_general(piece, chosen, dims, preferred_element_type=F32)
        total = term if total is None else total + term
        if part < 2:
            rest = rest - piece.astype(F32)
    return total


def dot10(chosen, field):
    total = None
    rest = field
    for part in range(3):
        piece = rest.astype(jnp.bfloat16)
        term = lax.dot_general(
            chosen, piece, (((1,), (1,)), ((), ())), preferred_element_type=F32
        )
        total = term if total is None else total + term
        if part < 2:
            rest = rest - piece.astype(F32)
    return total


def where01(condition):
    return jnp.where(condition, 1.0, 0.0).astype(jnp.bfloat16)


def loop(low, high, size, body):
    for plane in range(low, high, size):
        body(plane, min(size, high - plane))


def inverse_of(field):
    first = pl.reciprocal(field, approx=True)
    return first * (2.0 - field * first)


class Level:
    def __init__(self, level):
        self.ny = PLANE[1] >> level
        self.xs = 4 >> level
        self.factor = float(2**level)

    def masks(self, shape):
        lane = iota(shape, 2)
        row = iota(shape, 1)
        within = (lane // self.ny) % self.xs
        y = lane % self.ny
        last_x = (row == ROWS - 1) & (within == self.xs - 1)
        return within, y == self.ny - 1, last_x

    def next_x(self, field):
        within = (iota(field.shape, 2) // self.ny) % self.xs
        moved = pltpu.roll(field, LANES - self.ny, 2)
        return jnp.where(within == self.xs - 1, pltpu.roll(moved, ROWS - 1, 1), moved)

    def last_x(self, field):
        within = (iota(field.shape, 2) // self.ny) % self.xs
        moved = pltpu.roll(field, self.ny, 2)
        return jnp.where(within == 0, pltpu.roll(moved, 1, 1), moved)

    def next_y(self, field):
        return pltpu.roll(field, LANES - 1, 2)

    def last_y(self, field):
        return pltpu.roll(field, 1, 2)

    def spread(self, field, scaled, plane, count):
        mid = field[1:-1]
        near = (
            self.next_x(mid), self.last_x(mid), self.next_y(mid), self.last_y(mid),
            field[2:], field[:-2],
        )
        terms = [weight[pl.ds(plane, count)] * value for weight, value in zip(scaled, near)]
        return mid, ((terms[0] + terms[1]) + (terms[2] + terms[3])) + (terms[4] + terms[5])


def mean_of(fluid, near, factor):
    return ((factor * 2.0) * fluid * near) * inverse_of(jnp.maximum(fluid + near, TINY))


def set_level(level, low, high, fluid, pin, rhs, fields):
    scaled, start, diag = fields

    def body(plane, count):
        wide = fluid[pl.ds(plane - 1, count + 2)]
        mid = wide[1:-1]
        within, end_y, end_x = level.masks(mid.shape)
        to_x = jnp.where(end_x, 0.0, mean_of(mid, level.next_x(mid), level.factor))
        to_y = jnp.where(end_y, 0.0, mean_of(mid, level.next_y(mid), level.factor))
        to_z = mean_of(wide[:-1], wide[1:], level.factor)
        weights = (to_x, level.last_x(to_x), to_y, level.last_y(to_y), to_z[1:], to_z[:-1])
        total = (
            (weights[0] + weights[1])
            + (weights[2] + weights[3])
            + (weights[4] + weights[5])
            + pin[pl.ds(plane, count)]
        )
        gain = OMEGA * inverse_of(jnp.maximum(total, TINY))
        for target, weight in zip(scaled, weights):
            target[pl.ds(plane, count)] = gain * weight
        start[pl.ds(plane, count)] = gain * rhs[pl.ds(plane, count)]
        diag[pl.ds(plane, count)] = total

    loop(low, high, PIECE, body)


def swept(level, plane, count, fields, source, shift=0):
    scaled, start, _ = fields
    mid, total = level.spread(source[pl.ds(plane - 1, count + 2)], scaled, plane - shift, count)
    return (1.0 - OMEGA) * mid + (start[pl.ds(plane - shift, count)] + total)


def sweep(level, low, high, fields, source, target, shift=0):
    def body(plane, count):
        target[pl.ds(plane, count)] = swept(level, plane, count, fields, source, shift)

    loop(low, high, PIECE, body)


def pair_sum(field):
    half = field.reshape((field.shape[0] // 2, 2) + field.shape[1:])
    return half[:, 0] + half[:, 1]


def coarse_residual(level, low, high, fields, corr, target):
    scaled, start, diag = fields

    def body(plane, count):
        mid, total = level.spread(corr[pl.ds(plane - 1, count + 2)], scaled, plane, count)
        rest = (start[pl.ds(plane, count)] + total) - OMEGA * mid
        rest = rest * (diag[pl.ds(plane, count)] * (1.0 / OMEGA))
        target[pl.ds((plane - low) // 2, count // 2)] = pair_sum(rest)

    loop(low, high, PIECE, body)


def lanes_down(level):
    fine = iota((LANES, LANES), 0)
    coarse = iota((LANES, LANES), 1)
    ny, xs = PLANE[1] >> level, 4 >> level
    half = xs // 2
    same_x = ((fine // ny) % xs) // 2 == (coarse // (ny // 2)) % half
    same_y = (fine % ny) // 2 == coarse % (ny // 2)
    return where01((fine < ny * xs) & same_x & same_y)


def in_lanes(field, chosen):
    flat = field.reshape(field.shape[0] * ROWS, LANES)
    return dot01(flat, chosen).reshape(field.shape)


def path_of(group):
    nx, ny = SPLIT
    row, column = 0, 0
    for index in range(group + 1):
        columns = list(range(ny)) if column == 0 else list(range(ny))[::-1]
        if index % 2:
            path = [(row, at) for at in columns] + [(1 - row, at) for at in columns[::-1]]
        else:
            path = []
            for at in columns:
                path += [(row, at), (1 - row, at)]
                row = 1 - row
        row, column = path[-1]
    return [row * ny + column for row, column in path]


def lookup(table, index):
    found = table[0]
    for at, value in enumerate(table[1:], 1):
        found = jnp.where(index == at, value, found)
    return found


def own_peer_of(rank):
    return lookup([path_of(group)[rank] for group in range(lax.axis_size("gz"))], lax.axis_index("gz"))


def slabs_of(groups):
    peers = SPLIT[0] * SPLIT[1]
    return [
        group * peers + path_of(group).index(peer) for peer in range(peers) for group in range(groups)
    ]


def own_slab():
    nx, ny = SPLIT
    groups = lax.axis_size("gz")
    device = (lax.axis_index("gx") * ny + lax.axis_index("gy")) * groups + lax.axis_index("gz")
    return lookup(slabs_of(groups), device)


def devices_of(groups):
    slabs = slabs_of(groups)
    return [slabs.index(slab) for slab in range(len(slabs))]


def prepare_kernel(share, res_ref, fluid_ref, pin_ref, out_ref):
    bx, by, depth = fluid_ref.shape
    cells = bx * by
    groups = bx // 4
    pick = where01(iota((depth, 2 * depth), 1) // 2 == iota((depth, 2 * depth), 0))
    deep = lax.dot_general(
        pick, res_ref[...], (((1,), (1,)), ((), ())), preferred_element_type=F32
    )

    def lane_of(x, y):
        return (x % 4) * (groups * by) + (x // 4) * by + y

    fine = iota((4 * cells, cells), 0)
    lane = iota((4 * cells, cells), 1)
    chosen = where01(lane_of(fine // (4 * by), (fine % (2 * by)) // 2) == lane)
    rhs = dot01(deep, chosen)
    cell = iota((cells, cells), 0)
    lane = iota((cells, cells), 1)
    chosen = where01(lane_of(cell // by, cell % by) == lane)
    fluid = dot01(fluid_ref[...].reshape(cells, depth).T, chosen)
    pin = dot01(pin_ref[...].reshape(cells, depth).T, chosen)
    for rank in range(depth // share):
        peer, begin = own_peer_of(rank), rank * share
        for index, field in enumerate((fluid, rhs, pin)):
            out_ref[peer, index * share : (index + 1) * share] = field[begin : begin + share]


def spread_kernel(groups, by, gathered, own, straight):
    for start in range(0, own.shape[0], ROWS):
        place(gathered, start, straight, start, groups, by)
    share = own.shape[0] // 3
    odd = own_slab() % 2 == 1
    for index in range(3):
        for plane in range(share):
            at = jnp.where(odd, share - 1 - plane, plane)
            own[index * share + plane] = straight[index * share + at]


def place(gathered, row, target, plane, groups, by):
    group = (iota((ROWS, LANES), 1) // by) % groups
    nx, ny = SPLIT
    for ix in range(nx):
        found = [gathered[ix * ny + iy, pl.ds(row, ROWS), :] for iy in range(ny)]
        for part in range(groups):
            total = found[part]
            for iy in range(ny):
                if iy != part:
                    moved = pltpu.roll(found[iy], (by * (iy - part)) % LANES, 1)
                    total = jnp.where(group == iy, moved, total)
            target[pl.ds(plane, ROWS), ix * groups + part, :] = total


def near_kernel(
    depth,
    own, inner,
    saved1, saved2, fluid2, pin2, fluid3, pin3,
    fluid1, rhs1, pin1, other1, rhs2, sums,
):
    for index, target in enumerate((fluid1, rhs1, pin1)):
        target[0:depth] = own[index * depth : (index + 1) * depth]
        for plane in range(HALO):
            target[depth + plane] = inner[(index + 1) * depth - 1 - plane]
    fine, coarse = Level(0), Level(1)
    down1, down2 = lanes_down(0), lanes_down(1)
    fields1, corr1 = (saved1[0:6], saved1[6], saved1[7]), saved1[8]
    fields2 = (saved2[0:6], saved2[6], saved2[7])
    planes = depth + HALO
    set_level(fine, 1, planes - 1, fluid1, pin1, rhs1, fields1)
    sweep(fine, 2, planes - 2, fields1, fields1[1], other1)
    sweep(fine, 3, planes - 3, fields1, other1, corr1)
    coarse_residual(fine, 4, planes - 4, fields1, corr1, sums)
    count2 = planes // 2
    for source, target, share in ((fluid1, fluid2, 8.0), (pin1, pin2, 4.0)):
        target[NEAR : NEAR + count2] = in_lanes(pair_sum(source[...]), down1) * (1.0 / share)
    low2, high2 = NEAR + 2, NEAR + count2 - 2
    rhs2[low2:high2] = in_lanes(sums[0 : high2 - low2], down1)
    set_level(coarse, low2, high2, fluid2, pin2, rhs2, fields2)
    for source, target, scale in ((fluid2, fluid3, 0.125), (pin2, pin3, 0.25)):
        target[...] = in_lanes(pair_sum(source[NEAR : NEAR + depth // 2]), down2) * scale


def down_kernel(
    depth,
    own, outer, near2, near_fluid2, near_pin2, fluid3, pin3,
    saved1, saved2,
    packed,
    fluid1, rhs1, pin1, other1, fluid2, rhs2, pin2, other2, sums,
):
    planes = fluid1.shape[0]
    for index, target in enumerate((fluid1, rhs1, pin1)):
        for plane in range(HALO):
            target[plane] = outer[index * depth + HALO - 1 - plane]
        target[HALO:planes] = own[index * depth : index * depth + planes - HALO]

    fine, coarse = Level(0), Level(1)
    down1, down2 = lanes_down(0), lanes_down(1)
    fields1, corr1 = (saved1[0:6], saved1[6], saved1[7]), saved1[8]
    fields2, corr2 = (saved2[0:6], saved2[6], saved2[7]), saved2[8]
    set_level(fine, 1, planes - 1, fluid1, pin1, rhs1, fields1)
    sweep(fine, 2, planes - 2, fields1, fields1[1], other1)
    sweep(fine, 3, planes - 3, fields1, other1, corr1)
    count2 = depth // 2 + 2 * NEAR
    low2, done, high2 = 2, NEAR + 2, count2 - 2
    coarse_residual(fine, 2 * low2, 2 * done, fields1, corr1, sums)
    for source, ready, target, share in (
        (fluid1, near_fluid2, fluid2, 8.0), (pin1, near_pin2, pin2, 4.0)
    ):
        target[0:NEAR] = in_lanes(pair_sum(source[0:HALO]), down1) * (1.0 / share)
        target[NEAR : done + 1] = ready[NEAR : done + 1]
    rhs2[low2:done] = in_lanes(sums[0 : done - low2], down1)
    set_level(coarse, low2, done, fluid2, pin2, rhs2, fields2)
    for source, target in zip(near2, saved2[0:8]):
        target[done:high2] = source[done:high2]
    sweep(coarse, low2 + 1, high2 - 1, fields2, fields2[1], other2)
    sweep(coarse, low2 + 2, high2 - 2, fields2, other2, corr2)
    coarse_residual(coarse, NEAR, NEAR + depth // 2, fields2, corr2, sums)
    count3 = depth // 4
    rhs3 = in_lanes(sums[0:count3], down2)
    lane = iota((count3, LANES), 1) // ROWS
    first = jnp.zeros((count3, LANES), F32)
    second = jnp.zeros((count3, LANES), F32)
    for row in range(ROWS):
        first = jnp.where(lane == row, rhs3[:, row, :], first)
        first = jnp.where(lane == ROWS + row, fluid3[:, row, :], first)
        second = jnp.where(lane % ROWS == row, pin3[:, row, :], second)
    packed[0] = first[0:2]
    packed[1] = first[2:4]
    packed[2] = jnp.where(lane[0:2] < ROWS, second[0:2], second[2:4])
    lane = iota((1, LANES), 1) // (LANES // 4)
    for index, plane in enumerate((NEAR + depth // 2 - 5, NEAR + 4)):
        for half in range(2):
            row = jnp.zeros((1, LANES), F32)
            for quarter in range(4):
                at = half * 4 + quarter
                row = jnp.where(lane == quarter, corr2[plane, at : at + 1, :], row)
            packed[3 + index, half : half + 1, :] = row


def rolled(field, shift):
    count = field.shape[0]
    shift %= count
    if shift % ROWS:
        return pltpu.roll(field, shift, 0)
    return jnp.concatenate([field[count - shift :], field[: count - shift]], axis=0)


def columns(rhs, fluid, pin):
    depth = fluid.shape[0]
    z, lane = iota(fluid.shape, 0), iota(fluid.shape, 1)
    y, x = lane % ROWS, (lane // ROWS) % ROWS

    def next_x(field):
        return pltpu.roll(field, LANES - ROWS, 1)

    def next_y(field):
        return pltpu.roll(field, LANES - 1, 1)

    wz = jnp.where(z == depth - 1, 0.0, mean_of(fluid, rolled(fluid, -1), 4.0))
    wy = jnp.where(y == ROWS - 1, 0.0, mean_of(fluid, next_y(fluid), 4.0))
    wx = jnp.where(x == ROWS - 1, 0.0, mean_of(fluid, next_x(fluid), 4.0))
    across = (wx + pltpu.roll(wx, ROWS, 1)) + (wy + pltpu.roll(wy, 1, 1)) + pin
    share = 1.0 / jnp.sum(across, axis=0, keepdims=True)

    above, below, own = rolled(wz, 1), wz, across
    steps = []
    stride = 1
    while stride < depth:
        inverse = inverse_of(above + below + own)
        up = above * rolled(inverse, stride)
        down = below * rolled(inverse, -stride)
        own = own + up * rolled(own, stride) + down * rolled(own, -stride)
        above = up * rolled(above, stride)
        below = down * rolled(below, -stride)
        steps.append((stride, up, down))
        stride *= 2
    inverse = inverse_of(above + below + own)

    def solve(right):
        mean = jnp.sum(right, axis=0, keepdims=True) * share
        for stride, up, down in steps:
            right = right + up * rolled(right, stride) + down * rolled(right, -stride)
        return right * inverse + mean

    corr = solve(rhs)
    flow_x = wx * (next_x(corr) - corr)
    flow_y = wy * (next_y(corr) - corr)
    flow_z = wz * (rolled(corr, -1) - corr)
    rest = (
        (rhs - pin * corr)
        + (flow_x - pltpu.roll(flow_x, ROWS, 1))
        + (flow_y - pltpu.roll(flow_y, 1, 1))
        + (flow_z - rolled(flow_z, 1))
    )
    return corr + solve(rest)


def up_kernel(
    groups, by, depth,
    packed, near1, far1, far2,
    out_ref,
    one1, two1, one2, two2, lifted, first, second, solved, final,
):
    count3 = depth // 4
    shares = packed.shape[0]
    peers = SPLIT[0] * SPLIT[1]
    devices = devices_of(shares // peers)
    for slab, index in enumerate(devices):
        row = slab * count3
        low, high, both = packed[index, 0], packed[index, 1], packed[index, 2]
        rest = pltpu.roll(both, LANES // 2, 1)
        if slab % 2:
            for at, (level3, pin) in enumerate(((high, rest), (low, both))):
                begin = row + 2 * at
                first[begin : begin + 1] = level3[1:2]
                first[begin + 1 : begin + 2] = level3[0:1]
                second[begin : begin + 1] = pin[1:2]
                second[begin + 1 : begin + 2] = pin[0:1]
        else:
            first[row : row + 2] = low
            first[row + 2 : row + 4] = high
            second[row : row + 2] = both
            second[row + 2 : row + 4] = rest
    half = iota((shares * count3, LANES), 1) < LANES // 2

    def low_half(field):
        return jnp.where(half, field, pltpu.roll(field, LANES // 2, 1))

    def high_half(field):
        return jnp.where(half, pltpu.roll(field, LANES // 2, 1), field)

    solved[NEAR : NEAR + shares * count3] = columns(
        low_half(first[...]), high_half(first[...]), low_half(second[...])
    )
    solved[0:NEAR] = jnp.zeros((NEAR, LANES), F32)
    solved[NEAR + shares * count3 :] = jnp.zeros((2 * NEAR, LANES), F32)

    nx, ny = SPLIT
    part = own_slab()
    count = count3 + 2 * NEAR
    tall = solved[pl.ds(part * count3, count + count3), :]
    fine, coarse = Level(0), Level(1)
    cell = iota((LANES, LANES), 0)
    lane = iota((LANES, LANES), 1)
    spread = where01((cell < ROWS) & (cell == (lane % coarse.ny) // 2))
    rows = tall.shape[0]
    turned = [tall] + [pltpu.roll(tall, LANES - ROWS * row, 1) for row in range(1, ROWS)]
    wide = dot01(jnp.concatenate(turned, axis=0), spread)
    for row in range(ROWS):
        lifted[0:rows, row, :] = wide[row * rows : (row + 1) * rows]

    odd = part % 2 == 1

    def lifted_to(plane):
        parent = plane // 2 + NEAR // 2
        return lifted[jnp.where(odd, count - 1 - parent, parent)]

    near_fields, near_corr1 = (near1[0:6], near1[6], near1[7]), near1[8]
    far_fields, far_corr1 = (far1[0:6], far1[6], far1[7]), far1[8]
    fields2, corr2 = (far2[0:6], far2[6], far2[7]), far2[8]
    low, high = NEAR - 4, NEAR + depth // 2 + 4
    reach = depth // 2 + NEAR
    quarter = iota((ROWS, LANES), 1) // (LANES // 4)
    row = iota((ROWS, LANES), 0)

    def unpacked(index, which):
        pair = packed[lookup(devices, jnp.clip(index, 0, shares - 1)), which]
        total = None
        for shift in range(4):
            moved = pltpu.roll(pair, shift * (LANES // 4), 1)
            wide = jnp.where(row < 4, moved[0:1, :], moved[1:2, :])
            kept = jnp.where((quarter - shift) % 4 == row % 4, wide, 0.0)
            total = kept if total is None else total + kept
        return total

    one2[low - 1] = unpacked(jnp.where(odd, part + 1, part - 1), 4) + lifted_to(low - 1)
    for plane in range(low, high):
        one2[plane] = corr2[plane] + lifted_to(plane)
    one2[high] = unpacked(jnp.where(odd, part - 1, part + 1), 3) + lifted_to(high)
    sweep(coarse, NEAR - 4, reach + 4, fields2, one2, two2)
    sweep(coarse, NEAR - 3, reach + 3, fields2, two2, one2)
    sweep(coarse, NEAR - 2, reach + 2, fields2, one2, two2)

    fine_lane, coarse_lane = iota((LANES, LANES), 1), iota((LANES, LANES), 0)
    x_of = (fine_lane // fine.ny) // 2
    y_of = (fine_lane % fine.ny) // 2
    up = where01(coarse_lane == x_of * coarse.ny + y_of)
    lifted[0 : depth // 2 + 4] = in_lanes(two2[NEAR - 2 : reach + 2], up)
    parents = lifted[0 : depth // 2 + 4]
    twice = jnp.broadcast_to(parents[:, None], (parents.shape[0], 2, ROWS, LANES))
    low, high = HALO - 4, HALO + depth + 4
    turn = HALO + 3
    for plane in range(low, high):
        corr = far_corr1[plane] if plane < turn else near_corr1[plane - HALO]
        one1[plane] = corr + lifted[(plane - low) // 2]
    reach = depth + HALO
    for more, source, target in ((2, one1, two1), (1, two1, one1)):
        sweep(fine, HALO - more, turn, far_fields, source, target)
        sweep(fine, turn, reach + more, near_fields, source, target, HALO)

    def last(fields, shift):
        def body(plane, count):
            value = swept(fine, plane, count, fields, one1, shift)
            value = value * fields[2][pl.ds(plane - shift, count)]
            for index in range(count):
                at = plane - HALO + index
                final[jnp.where(odd, depth - 1 - at, at)] = value[index]

        return body

    loop(HALO, turn, PIECE, last(far_fields, 0))
    loop(turn, reach, PIECE, last(near_fields, HALO))

    group = (iota((depth, LANES), 1) // by) % groups
    for ix in range(nx):
        scaled = [final[:, ix * groups + part, :] for part in range(groups)]
        for iy in range(ny):
            total = scaled[iy]
            for part in range(groups):
                if part != iy:
                    moved = pltpu.roll(scaled[part], (by * (part - iy)) % LANES, 1)
                    total = jnp.where(group == part, moved, total)
            out_ref[ix * ny + iy] = total


def finish_kernel(blocks, out_ref):
    bx, by, depth = out_ref.shape
    cells = bx * by
    cell = iota((cells, cells), 0)
    lane = iota((cells, cells), 1)
    x, y = cell // by, cell % by
    chosen = where01((x % 4) * (bx // 4 * by) + (x // 4) * by + y == lane)
    peers = blocks.shape[0]
    ordered = jnp.concatenate([blocks[own_peer_of(rank)] for rank in range(peers)], axis=0)
    out_ref[...] = dot10(chosen, ordered).reshape(out_ref.shape)


def whole_planes(residual_q2, viscosity, pinned):
    bx, by, depth = viscosity.shape
    groups = bx // 4
    peers = SPLIT[0] * SPLIT[1]
    share = depth // peers
    planes = share + 2 * HALO
    count2 = share // 2 + 2 * NEAR
    limit = pltpu.CompilerParams(vmem_limit_bytes=32 * 2**20)

    def flat(rows):
        return jax.ShapeDtypeStruct((rows, LANES), F32)

    def blocks(count, rows):
        return jax.ShapeDtypeStruct((count, rows, LANES), F32)

    def room(count):
        return pltpu.VMEM((count, ROWS, LANES), F32)

    fluid = 1.0 / viscosity
    pin = 4.0 * pinned.astype(F32) * fluid
    parcels = pl.pallas_call(
        functools.partial(prepare_kernel, share),
        out_shape=blocks(peers, 3 * share),
        compiler_params=limit,
        name="prepare",
    )(residual_q2.reshape(4 * bx * by, 2 * depth), fluid, pin)
    own = pl.pallas_call(
        functools.partial(spread_kernel, groups, by),
        out_shape=blocks(3 * share, ROWS),
        scratch_shapes=[room(3 * share)],
        compiler_params=limit,
        name="spread",
    )(lax.all_to_all(parcels, ("gx", "gy"), 0, 0, tiled=True))
    length = lax.axis_size("gz")
    parts = length * peers

    device = devices_of(length)

    def swap(field, first):
        pairs = [(device[i], device[i + 1]) for i in range(first, parts - 1, 2)]
        return lax.ppermute(field, ("gx", "gy", "gz"), pairs + [pair[::-1] for pair in pairs])

    outer, inner = swap(own, 1), swap(own, 0)
    count3 = share // 4
    near1, near2, far1, far2 = (
        (blocks(count, ROWS),) * fields
        for count, fields in ((share + HALO, 9), (count2, 8), (HALO + 8, 9), (count2, 9))
    )
    near1, near2, fluid2, pin2, fluid3, pin3 = pl.pallas_call(
        functools.partial(near_kernel, share),
        out_shape=(near1, near2) + (blocks(count2, ROWS),) * 2 + (blocks(count3, ROWS),) * 2,
        scratch_shapes=[room(share + HALO)] * 4 + [room(count2)] * 2,
        compiler_params=limit,
        name="near",
    )(own, inner)
    far1, far2, parcel = pl.pallas_call(
        functools.partial(down_kernel, share),
        out_shape=(far1, far2, blocks(5, 2)),
        scratch_shapes=[room(HALO + 8)] * 4 + [room(count2)] * 5,
        compiler_params=limit,
        name="down",
    )(own, outer, near2, fluid2, pin2, fluid3, pin3)
    copies = jnp.broadcast_to(parcel, (parts,) + parcel.shape)
    packed = lax.all_to_all(copies, ("gx", "gy", "gz"), 0, 0, tiled=True)
    depth3 = parts * count3
    mine = pl.pallas_call(
        functools.partial(up_kernel, groups, by, share),
        out_shape=blocks(peers, share),
        scratch_shapes=[room(planes), room(planes), room(count2), room(count2), room(count2)]
        + [pltpu.VMEM((rows, LANES), F32) for rows in (depth3, depth3, depth3 + 3 * NEAR)]
        + [room(share)],
        compiler_params=limit,
        name="up",
    )(packed, near1, far1, far2)
    return pl.pallas_call(
        finish_kernel,
        out_shape=jax.ShapeDtypeStruct((bx, by, depth), F32),
        compiler_params=limit,
        name="finish",
    )(lax.all_to_all(mine, ("gx", "gy"), 0, 0, tiled=True))


def one_tile_planes(mesh, viscosity):
    split = (mesh.shape["gx"], mesh.shape["gy"])
    depth = viscosity.shape[2]
    fits = viscosity.shape[:2] == PLANE and split == SPLIT
    return fits and depth == 4 * LANES and depth // mesh.shape["gz"] == LANES


def solution(mesh):
    placed = (P("gx", "gy", "gz"), P("gx", "gy", "gz"), P("gx", "gy", "gz"))

    def cycle(residual_q2, viscosity, pinned):
        chosen = whole_planes if one_tile_planes(mesh, viscosity) else per_device
        return jax.shard_map(
            chosen, mesh=mesh, in_specs=placed, out_specs=P("gx", "gy", "gz"), check_vma=False
        )(residual_q2, viscosity, pinned)

    return cycle
```

```python
import functools

import jax
import jax.numpy as jnp
from jax import lax
from jax.experimental import pallas as pl
from jax.experimental.pallas import tpu as pltpu
from jax.sharding import PartitionSpec as P

NU = 3


OMEGA = 0.6


def with_halo(block, sides, width):
    for axis, dim in sides:
        count = lax.axis_size(axis)
        forward = [(i, i + 1) for i in range(count - 1)]
        backward = [(target, source) for source, target in forward]
        low = lax.ppermute(
            lax.slice_in_dim(block, block.shape[dim] - width, None, axis=dim), axis, forward
        )
        high = lax.ppermute(lax.slice_in_dim(block, 0, width, axis=dim), axis, backward)
        block = jnp.concatenate([low, block, high], axis=dim)
    return block


def coarsen(x):
    a, b, c = x.shape
    return x.reshape(a // 2, 2, b // 2, 2, c // 2, 2).sum(axis=(1, 3, 5))


def refine(x):
    return jnp.repeat(jnp.repeat(jnp.repeat(x, 2, 0), 2, 1), 2, 2)


def extended(field):
    return with_halo(field, (("gx", 0), ("gy", 1), ("gz", 2)), 1)


def shifted(padded):
    return [
        padded[2:, 1:-1, 1:-1],
        padded[:-2, 1:-1, 1:-1],
        padded[1:-1, 2:, 1:-1],
        padded[1:-1, :-2, 1:-1],
        padded[1:-1, 1:-1, 2:],
        padded[1:-1, 1:-1, :-2],
    ]


def neighbours(field):
    return shifted(extended(field))


def harmonic(fluid, near, factor):
    total = fluid + near
    return jnp.where(total > 0, factor * 2.0 * fluid * near / jnp.where(total > 0, total, 1.0), 0.0)


def couplings(fluid, factor):
    return [harmonic(fluid, near, factor) for near in neighbours(fluid)]


def apply_op(field, weights, diag):
    total = diag * field
    for weight, near in zip(weights, neighbours(field)):
        total = total - weight * near
    return total


def presmooth(rhs, weights, diag):
    corr = OMEGA * rhs / diag
    for sweep in range(NU - 1):
        corr = corr + OMEGA * (rhs - apply_op(corr, weights, diag)) / diag
    return corr


def postsmooth(corr, rhs, weights, diag):
    for sweep in range(NU):
        corr = corr + OMEGA * (rhs - apply_op(corr, weights, diag)) / diag
    return corr


def tridiag(coeffs, rhs):
    solved = lax.linalg.tridiagonal_solve(coeffs[0], coeffs[1], coeffs[2], rhs[..., None])[..., 0]
    last = rhs.ndim - 1
    shift_col = jnp.sum(rhs, axis=last, keepdims=True) / jnp.sum(
        coeffs[3], axis=last, keepdims=True
    )
    return solved + shift_col


def prepare_columns(weights, diag):
    lower = -weights[5]
    upper = -weights[4]
    across = diag + lower + upper
    return (
        lax.all_gather(lower, "gz", axis=2, tiled=True),
        lax.all_gather(diag, "gz", axis=2, tiled=True),
        lax.all_gather(upper, "gz", axis=2, tiled=True),
        lax.all_gather(across, "gz", axis=2, tiled=True),
    )


def column_solve(rhs, coeffs):
    depth = rhs.shape[2]
    whole = lax.all_gather(rhs, "gz", axis=2, tiled=True)
    solved = tridiag(coeffs, whole)
    return lax.dynamic_slice_in_dim(solved, lax.axis_index("gz") * depth, depth, 2)


def per_device(residual_q2, viscosity, pinned):
    fluid1 = 1.0 / viscosity
    pin1 = 4.0 * pinned.astype(jnp.float32) * fluid1
    rhs1 = coarsen(residual_q2.astype(jnp.float32))
    fluid2 = coarsen(fluid1) / 8.0
    pin2 = coarsen(pin1) / 4.0
    fluid3 = coarsen(fluid2) / 8.0
    pin3 = coarsen(pin2) / 4.0
    weights1 = couplings(fluid1, 1.0)
    weights2 = couplings(fluid2, 2.0)
    weights3 = couplings(fluid3, 4.0)
    diag1 = sum(weights1) + pin1
    diag2 = sum(weights2) + pin2
    diag3 = sum(weights3) + pin3
    coeffs = prepare_columns(weights3, diag3)
    corr1 = presmooth(rhs1, weights1, diag1)
    rhs2 = coarsen(rhs1 - apply_op(corr1, weights1, diag1))
    corr2 = presmooth(rhs2, weights2, diag2)
    rhs3 = coarsen(rhs2 - apply_op(corr2, weights2, diag2))
    corr3 = column_solve(rhs3, coeffs)
    corr3 = corr3 + column_solve(rhs3 - apply_op(corr3, weights3, diag3), coeffs)
    corr2 = postsmooth(corr2 + refine(corr3), rhs2, weights2, diag2)
    corr1 = postsmooth(corr1 + refine(corr2), rhs1, weights1, diag1)
    return diag1 * corr1


PLANE = (32, 32)
SPLIT = (2, 4)
ROWS = 8
LANES = 128
HALO = 16
NEAR = 8
PIECE = 8
TINY = 1e-30
F32 = jnp.float32


def iota(shape, dim):
    return lax.broadcasted_iota(jnp.int32, shape, dim)


def dot01(field, chosen, parts=3):
    total = None
    rest = field
    for part in range(parts):
        piece = rest.astype(jnp.bfloat16)
        term = jnp.dot(piece, chosen, preferred_element_type=F32)
        total = term if total is None else total + term
        if part < parts - 1:
            rest = rest - piece.astype(F32)
    return total


def dot10(chosen, field):
    total = None
    rest = field
    for part in range(3):
        piece = rest.astype(jnp.bfloat16)
        term = lax.dot_general(
            chosen, piece, (((1,), (1,)), ((), ())), preferred_element_type=F32
        )
        total = term if total is None else total + term
        if part < 2:
            rest = rest - piece.astype(F32)
    return total


def where01(condition):
    return jnp.where(condition, 1.0, 0.0).astype(jnp.bfloat16)


def loop(low, high, size, body):
    for plane in range(low, high, size):
        body(plane, min(size, high - plane))


def inverse_of(field):
    first = pl.reciprocal(field, approx=True)
    return first * (2.0 - field * first)


class Level:
    def __init__(self, level):
        self.ny = PLANE[1] >> level
        self.xs = 4 >> level
        self.factor = float(2**level)

    def masks(self, shape):
        lane = iota(shape, 2)
        row = iota(shape, 1)
        within = (lane // self.ny) % self.xs
        y = lane % self.ny
        last_x = (row == ROWS - 1) & (within == self.xs - 1)
        return within, y == self.ny - 1, last_x

    def next_x(self, field):
        within = (iota(field.shape, 2) // self.ny) % self.xs
        moved = pltpu.roll(field, LANES - self.ny, 2)
        return jnp.where(within == self.xs - 1, pltpu.roll(moved, ROWS - 1, 1), moved)

    def last_x(self, field):
        within = (iota(field.shape, 2) // self.ny) % self.xs
        moved = pltpu.roll(field, self.ny, 2)
        return jnp.where(within == 0, pltpu.roll(moved, 1, 1), moved)

    def next_y(self, field):
        return pltpu.roll(field, LANES - 1, 2)

    def last_y(self, field):
        return pltpu.roll(field, 1, 2)

    def spread(self, field, scaled, plane, count):
        mid = field[1:-1]
        near = (
            self.next_x(mid), self.last_x(mid), self.next_y(mid), self.last_y(mid),
            field[2:], field[:-2],
        )
        terms = [weight[pl.ds(plane, count)] * value for weight, value in zip(scaled, near)]
        return mid, ((terms[0] + terms[1]) + (terms[2] + terms[3])) + (terms[4] + terms[5])


def mean_of(fluid, near, factor):
    return ((factor * 2.0) * fluid * near) * inverse_of(jnp.maximum(fluid + near, TINY))


def set_level(level, low, high, fluid, pin, rhs, fields):
    scaled, start, diag = fields

    def body(plane, count):
        wide = fluid[pl.ds(plane - 1, count + 2)]
        mid = wide[1:-1]
        within, end_y, end_x = level.masks(mid.shape)
        to_x = jnp.where(end_x, 0.0, mean_of(mid, level.next_x(mid), level.factor))
        to_y = jnp.where(end_y, 0.0, mean_of(mid, level.next_y(mid), level.factor))
        to_z = mean_of(wide[:-1], wide[1:], level.factor)
        weights = (to_x, level.last_x(to_x), to_y, level.last_y(to_y), to_z[1:], to_z[:-1])
        total = (
            (weights[0] + weights[1])
            + (weights[2] + weights[3])
            + (weights[4] + weights[5])
            + pin[pl.ds(plane, count)]
        )
        gain = OMEGA * inverse_of(jnp.maximum(total, TINY))
        for target, weight in zip(scaled, weights):
            target[pl.ds(plane, count)] = gain * weight
        start[pl.ds(plane, count)] = gain * rhs[pl.ds(plane, count)]
        diag[pl.ds(plane, count)] = total

    loop(low, high, PIECE, body)


def swept(level, plane, count, fields, source, shift=0):
    scaled, start, _ = fields
    mid, total = level.spread(source[pl.ds(plane - 1, count + 2)], scaled, plane - shift, count)
    return (1.0 - OMEGA) * mid + (start[pl.ds(plane - shift, count)] + total)


def sweep(level, low, high, fields, source, target, shift=0):
    def body(plane, count):
        target[pl.ds(plane, count)] = swept(level, plane, count, fields, source, shift)

    loop(low, high, PIECE, body)


def pair_sum(field):
    half = field.reshape((field.shape[0] // 2, 2) + field.shape[1:])
    return half[:, 0] + half[:, 1]


def coarse_residual(level, low, high, fields, corr, target):
    scaled, start, diag = fields

    def body(plane, count):
        mid, total = level.spread(corr[pl.ds(plane - 1, count + 2)], scaled, plane, count)
        rest = (start[pl.ds(plane, count)] + total) - OMEGA * mid
        rest = rest * (diag[pl.ds(plane, count)] * (1.0 / OMEGA))
        target[pl.ds((plane - low) // 2, count // 2)] = pair_sum(rest)

    loop(low, high, PIECE, body)


def lanes_down(level):
    fine = iota((LANES, LANES), 0)
    coarse = iota((LANES, LANES), 1)
    ny, xs = PLANE[1] >> level, 4 >> level
    half = xs // 2
    same_x = ((fine // ny) % xs) // 2 == (coarse // (ny // 2)) % half
    same_y = (fine % ny) // 2 == coarse % (ny // 2)
    return where01((fine < ny * xs) & same_x & same_y)


def in_lanes(field, chosen, parts=3):
    flat = field.reshape(field.shape[0] * ROWS, LANES)
    return dot01(flat, chosen, parts).reshape(field.shape)


def path_of(group):
    nx, ny = SPLIT
    row, column = 0, 0
    for index in range(group + 1):
        columns = list(range(ny)) if column == 0 else list(range(ny))[::-1]
        if index % 2:
            path = [(row, at) for at in columns] + [(1 - row, at) for at in columns[::-1]]
        else:
            path = []
            for at in columns:
                path += [(row, at), (1 - row, at)]
                row = 1 - row
        row, column = path[-1]
    return [row * ny + column for row, column in path]


def lookup(table, index):
    found = table[0]
    for at, value in enumerate(table[1:], 1):
        found = jnp.where(index == at, value, found)
    return found


def own_peer_of(rank):
    return lookup([path_of(group)[rank] for group in range(lax.axis_size("gz"))], lax.axis_index("gz"))


def slabs_of(groups):
    peers = SPLIT[0] * SPLIT[1]
    return [
        group * peers + path_of(group).index(peer) for peer in range(peers) for group in range(groups)
    ]


def own_slab():
    nx, ny = SPLIT
    groups = lax.axis_size("gz")
    device = (lax.axis_index("gx") * ny + lax.axis_index("gy")) * groups + lax.axis_index("gz")
    return lookup(slabs_of(groups), device)


def devices_of(groups):
    slabs = slabs_of(groups)
    return [slabs.index(slab) for slab in range(len(slabs))]


def prepare_kernel(share, res_ref, fluid_ref, pin_ref, out_ref):
    bx, by, depth = fluid_ref.shape
    cells = bx * by
    groups = bx // 4
    order = [x for low in range(4) for x in range(low, bx, 4)]
    fine = iota((cells, 4 * cells), 1)
    x, y = fine // (4 * by), (fine % (2 * by)) // 2
    chosen = where01((x % 4) * (groups * by) + (x // 4) * by + y == iota((cells, 4 * cells), 0))
    wide = lax.dot_general(
        chosen, res_ref[...], (((1,), (0,)), ((), ())), preferred_element_type=F32
    )
    rhs = dot10(where01(iota((depth, 2 * depth), 1) // 2 == iota((depth, 2 * depth), 0)), wide)

    def turned(field_ref):
        field = jnp.concatenate([field_ref[x : x + 1] for x in order], axis=0)
        return field.reshape(cells, depth).T

    fluid, pin = turned(fluid_ref), turned(pin_ref)
    for rank in range(depth // share):
        peer, begin = own_peer_of(rank), rank * share
        for index, field in enumerate((fluid, rhs, pin)):
            out_ref[peer, index * share : (index + 1) * share] = field[begin : begin + share]


def spread_kernel(groups, by, gathered, own, straight):
    for start in range(0, own.shape[0], ROWS):
        place(gathered, start, straight, start, groups, by)
    share = own.shape[0] // 3
    odd = own_slab() % 2 == 1
    for index in range(3):
        for plane in range(share):
            at = jnp.where(odd, share - 1 - plane, plane)
            own[index * share + plane] = straight[index * share + at]


def place(gathered, row, target, plane, groups, by):
    group = (iota((ROWS, LANES), 1) // by) % groups
    nx, ny = SPLIT
    for ix in range(nx):
        found = [gathered[ix * ny + iy, pl.ds(row, ROWS), :] for iy in range(ny)]
        for part in range(groups):
            total = found[part]
            for iy in range(ny):
                if iy != part:
                    moved = pltpu.roll(found[iy], (by * (iy - part)) % LANES, 1)
                    total = jnp.where(group == iy, moved, total)
            target[pl.ds(plane, ROWS), ix * groups + part, :] = total


def near_kernel(
    depth,
    own, inner,
    saved1, saved2, fluid2, pin2, fluid3, pin3,
    fluid1, rhs1, pin1, other1, rhs2, sums,
):
    for index, target in enumerate((fluid1, rhs1, pin1)):
        target[0:depth] = own[index * depth : (index + 1) * depth]
        for plane in range(HALO):
            target[depth + plane] = inner[(index + 1) * depth - 1 - plane]
    fine, coarse = Level(0), Level(1)
    down1, down2 = lanes_down(0), lanes_down(1)
    fields1, corr1 = (saved1[0:6], saved1[6], saved1[7]), saved1[8]
    fields2 = (saved2[0:6], saved2[6], saved2[7])
    planes = depth + HALO
    set_level(fine, 1, planes - 1, fluid1, pin1, rhs1, fields1)
    sweep(fine, 2, planes - 2, fields1, fields1[1], other1)
    sweep(fine, 3, planes - 3, fields1, other1, corr1)
    coarse_residual(fine, 4, planes - 4, fields1, corr1, sums)
    count2 = planes // 2
    for source, target, share in ((fluid1, fluid2, 8.0), (pin1, pin2, 4.0)):
        target[NEAR : NEAR + count2] = in_lanes(pair_sum(source[...]), down1) * (1.0 / share)
    low2, high2 = NEAR + 2, NEAR + count2 - 2
    rhs2[low2:high2] = in_lanes(sums[0 : high2 - low2], down1)
    set_level(coarse, low2, high2, fluid2, pin2, rhs2, fields2)
    for source, target, scale in ((fluid2, fluid3, 0.125), (pin2, pin3, 0.25)):
        target[...] = in_lanes(pair_sum(source[NEAR : NEAR + depth // 2]), down2) * scale


def down_kernel(
    depth,
    own, outer, near2, near_fluid2, near_pin2, fluid3, pin3,
    saved1, saved2,
    packed,
    fluid1, rhs1, pin1, other1, fluid2, rhs2, pin2, other2, sums,
):
    planes = fluid1.shape[0]
    for index, target in enumerate((fluid1, rhs1, pin1)):
        for plane in range(HALO):
            target[plane] = outer[index * depth + HALO - 1 - plane]
        target[HALO:planes] = own[index * depth : index * depth + planes - HALO]

    fine, coarse = Level(0), Level(1)
    down1, down2 = lanes_down(0), lanes_down(1)
    fields1, corr1 = (saved1[0:6], saved1[6], saved1[7]), saved1[8]
    fields2, corr2 = (saved2[0:6], saved2[6], saved2[7]), saved2[8]
    set_level(fine, 1, planes - 1, fluid1, pin1, rhs1, fields1)
    sweep(fine, 2, planes - 2, fields1, fields1[1], other1)
    sweep(fine, 3, planes - 3, fields1, other1, corr1)
    count2 = depth // 2 + 2 * NEAR
    low2, done, high2 = 2, NEAR + 2, count2 - 2
    coarse_residual(fine, 2 * low2, 2 * done, fields1, corr1, sums)
    for source, ready, target, share in (
        (fluid1, near_fluid2, fluid2, 8.0), (pin1, near_pin2, pin2, 4.0)
    ):
        target[0:NEAR] = in_lanes(pair_sum(source[0:HALO]), down1) * (1.0 / share)
        target[NEAR : done + 1] = ready[NEAR : done + 1]
    rhs2[low2:done] = in_lanes(sums[0 : done - low2], down1)
    set_level(coarse, low2, done, fluid2, pin2, rhs2, fields2)
    for source, target in zip(near2, saved2[0:8]):
        target[done:high2] = source[done:high2]
    sweep(coarse, low2 + 1, high2 - 1, fields2, fields2[1], other2)
    sweep(coarse, low2 + 2, high2 - 2, fields2, other2, corr2)
    coarse_residual(coarse, NEAR, NEAR + depth // 2, fields2, corr2, sums)
    count3 = depth // 4
    rhs3 = in_lanes(sums[0:count3], down2)
    lane = iota((count3, LANES), 1) // ROWS
    first = jnp.zeros((count3, LANES), F32)
    second = jnp.zeros((count3, LANES), F32)
    for row in range(ROWS):
        first = jnp.where(lane == row, rhs3[:, row, :], first)
        first = jnp.where(lane == ROWS + row, fluid3[:, row, :], first)
        second = jnp.where(lane % ROWS == row, pin3[:, row, :], second)
    packed[0] = first[0:2]
    packed[1] = first[2:4]
    packed[2] = jnp.where(lane[0:2] < ROWS, second[0:2], second[2:4])
    lane = iota((1, LANES), 1) // (LANES // 4)
    for index, plane in enumerate((NEAR + depth // 2 - 5, NEAR + 4)):
        for half in range(2):
            row = jnp.zeros((1, LANES), F32)
            for quarter in range(4):
                at = half * 4 + quarter
                row = jnp.where(lane == quarter, corr2[plane, at : at + 1, :], row)
            packed[3 + index, half : half + 1, :] = row


def swapped(field):
    return pltpu.roll(field, LANES // 2, 1)


def rolled(field, shift):
    count = field.shape[0]
    if abs(shift) == count:
        return swapped(field)
    if shift % ROWS:
        moved = pltpu.roll(field, shift % count, 0)
        row = iota(field.shape, 0)
        crossed = row < shift if shift > 0 else row >= count + shift
        return jnp.where(crossed, swapped(moved), moved)
    cut = count - shift if shift > 0 else -shift
    low, high = field[:cut], field[cut:]
    return jnp.concatenate([swapped(high), low] if shift > 0 else [high, swapped(low)], axis=0)


def columns(rhs, fluid, pin):
    count = fluid.shape[0]
    depth = 2 * count
    row, lane = iota(fluid.shape, 0), iota(fluid.shape, 1)
    y, x = lane % ROWS, (lane // ROWS) % ROWS
    last = (row == count - 1) & (lane >= LANES // 2)

    def next_x(field):
        return pltpu.roll(field, LANES - ROWS, 1)

    def next_y(field):
        return pltpu.roll(field, LANES - 1, 1)

    def total(field):
        part = jnp.sum(field, axis=0, keepdims=True)
        return part + swapped(part)

    wz = jnp.where(last, 0.0, mean_of(fluid, rolled(fluid, -1), 4.0))
    wy = jnp.where(y == ROWS - 1, 0.0, mean_of(fluid, next_y(fluid), 4.0))
    wx = jnp.where(x == ROWS - 1, 0.0, mean_of(fluid, next_x(fluid), 4.0))
    across = (wx + pltpu.roll(wx, ROWS, 1)) + (wy + pltpu.roll(wy, 1, 1)) + pin
    share = 1.0 / total(across)

    above, below, own = rolled(wz, 1), wz, across
    steps = []
    stride = 1
    while stride < depth:
        inverse = inverse_of(above + below + own)
        up = above * rolled(inverse, stride)
        down = below * rolled(inverse, -stride)
        own = own + up * rolled(own, stride) + down * rolled(own, -stride)
        above = up * rolled(above, stride)
        below = down * rolled(below, -stride)
        steps.append((stride, up, down))
        stride *= 2
    inverse = inverse_of(above + below + own)

    def solve(right):
        mean = total(right) * share
        for stride, up, down in steps:
            right = right + up * rolled(right, stride) + down * rolled(right, -stride)
        return right * inverse + mean

    corr = solve(rhs)
    flow_x = wx * (next_x(corr) - corr)
    flow_y = wy * (next_y(corr) - corr)
    flow_z = wz * (rolled(corr, -1) - corr)
    rest = (
        (rhs - pin * corr)
        + (flow_x - pltpu.roll(flow_x, ROWS, 1))
        + (flow_y - pltpu.roll(flow_y, 1, 1))
        + (flow_z - rolled(flow_z, 1))
    )
    return corr + solve(rest)


def up_kernel(
    groups, by, depth,
    packed, near1, far1, far2,
    out_ref,
    one1, two1, one2, two2, lifted, first, second, solved, final,
):
    count3 = depth // 4
    shares = packed.shape[0]
    peers = SPLIT[0] * SPLIT[1]
    devices = devices_of(shares // peers)
    for slab, index in enumerate(devices):
        row = slab * count3
        low, high, both = packed[index, 0], packed[index, 1], packed[index, 2]
        rest = pltpu.roll(both, LANES // 2, 1)
        if slab % 2:
            for at, (level3, pin) in enumerate(((high, rest), (low, both))):
                begin = row + 2 * at
                first[begin : begin + 1] = level3[1:2]
                first[begin + 1 : begin + 2] = level3[0:1]
                second[begin : begin + 1] = pin[1:2]
                second[begin + 1 : begin + 2] = pin[0:1]
        else:
            first[row : row + 2] = low
            first[row + 2 : row + 4] = high
            second[row : row + 2] = both
            second[row + 2 : row + 4] = rest
    count = shares * count3 // 2
    low, high = first[:count], first[count:]
    half = iota((count, LANES), 1) < LANES // 2
    corr3 = columns(
        jnp.where(half, low, swapped(high)),
        jnp.where(half, swapped(low), high),
        jnp.where(half, second[:count], swapped(second[count:])),
    )
    solved[0:NEAR] = jnp.zeros((NEAR, LANES), F32)
    solved[NEAR : NEAR + count] = corr3
    solved[NEAR + count : NEAR + 2 * count] = swapped(corr3)
    solved[NEAR + 2 * count :] = jnp.zeros((2 * NEAR, LANES), F32)

    nx, ny = SPLIT
    part = own_slab()
    count = count3 + 2 * NEAR
    tall = solved[pl.ds(part * count3, count + count3), :]
    fine, coarse = Level(0), Level(1)
    cell = iota((LANES, LANES), 0)
    lane = iota((LANES, LANES), 1)
    spread = where01((cell < ROWS) & (cell == (lane % coarse.ny) // 2))
    rows = tall.shape[0]
    turned = [tall] + [pltpu.roll(tall, LANES - ROWS * row, 1) for row in range(1, ROWS)]
    wide = dot01(jnp.concatenate(turned, axis=0), spread, 2)
    for row in range(ROWS):
        lifted[0:rows, row, :] = wide[row * rows : (row + 1) * rows]

    odd = part % 2 == 1

    def lifted_to(plane):
        parent = plane // 2 + NEAR // 2
        return lifted[jnp.where(odd, count - 1 - parent, parent)]

    near_fields, near_corr1 = (near1[0:6], near1[6], near1[7]), near1[8]
    far_fields, far_corr1 = (far1[0:6], far1[6], far1[7]), far1[8]
    fields2, corr2 = (far2[0:6], far2[6], far2[7]), far2[8]
    low, high = NEAR - 4, NEAR + depth // 2 + 4
    reach = depth // 2 + NEAR
    quarter = iota((ROWS, LANES), 1) // (LANES // 4)
    row = iota((ROWS, LANES), 0)

    def unpacked(index, which):
        pair = packed[lookup(devices, jnp.clip(index, 0, shares - 1)), which]
        total = None
        for shift in range(4):
            moved = pltpu.roll(pair, shift * (LANES // 4), 1)
            wide = jnp.where(row < 4, moved[0:1, :], moved[1:2, :])
            kept = jnp.where((quarter - shift) % 4 == row % 4, wide, 0.0)
            total = kept if total is None else total + kept
        return total

    one2[low - 1] = unpacked(jnp.where(odd, part + 1, part - 1), 4) + lifted_to(low - 1)
    for plane in range(low, high):
        one2[plane] = corr2[plane] + lifted_to(plane)
    one2[high] = unpacked(jnp.where(odd, part - 1, part + 1), 3) + lifted_to(high)
    sweep(coarse, NEAR - 4, reach + 4, fields2, one2, two2)
    sweep(coarse, NEAR - 3, reach + 3, fields2, two2, one2)
    sweep(coarse, NEAR - 2, reach + 2, fields2, one2, two2)

    fine_lane, coarse_lane = iota((LANES, LANES), 1), iota((LANES, LANES), 0)
    x_of = (fine_lane // fine.ny) // 2
    y_of = (fine_lane % fine.ny) // 2
    up = where01(coarse_lane == x_of * coarse.ny + y_of)
    lifted[0 : depth // 2 + 4] = in_lanes(two2[NEAR - 2 : reach + 2], up, 2)
    parents = lifted[0 : depth // 2 + 4]
    twice = jnp.broadcast_to(parents[:, None], (parents.shape[0], 2, ROWS, LANES))
    low, high = HALO - 4, HALO + depth + 4
    turn = HALO + 3
    for plane in range(low, high):
        corr = far_corr1[plane] if plane < turn else near_corr1[plane - HALO]
        one1[plane] = corr + lifted[(plane - low) // 2]
    reach = depth + HALO
    for more, source, target in ((2, one1, two1), (1, two1, one1)):
        sweep(fine, HALO - more, turn, far_fields, source, target)
        sweep(fine, turn, reach + more, near_fields, source, target, HALO)

    def last(fields, shift):
        def body(plane, count):
            value = swept(fine, plane, count, fields, one1, shift)
            value = value * fields[2][pl.ds(plane - shift, count)]
            for index in range(count):
                at = plane - HALO + index
                final[jnp.where(odd, depth - 1 - at, at)] = value[index]

        return body

    loop(HALO, turn, PIECE, last(far_fields, 0))
    loop(turn, reach, PIECE, last(near_fields, HALO))

    group = (iota((depth, LANES), 1) // by) % groups
    for ix in range(nx):
        scaled = [final[:, ix * groups + part, :] for part in range(groups)]
        for iy in range(ny):
            total = scaled[iy]
            for part in range(groups):
                if part != iy:
                    moved = pltpu.roll(scaled[part], (by * (part - iy)) % LANES, 1)
                    total = jnp.where(group == part, moved, total)
            out_ref[ix * ny + iy] = total


def finish_kernel(blocks, out_ref):
    bx, by, depth = out_ref.shape
    peers = blocks.shape[0]
    ordered = jnp.concatenate([blocks[own_peer_of(rank)] for rank in range(peers)], axis=0)
    turned = ordered.T
    for x in range(bx):
        row = ((x % 4) * (bx // 4) + x // 4) * by
        out_ref[x] = turned[row : row + by]


def whole_planes(residual_q2, viscosity, pinned):
    bx, by, depth = viscosity.shape
    groups = bx // 4
    peers = SPLIT[0] * SPLIT[1]
    share = depth // peers
    planes = share + 2 * HALO
    count2 = share // 2 + 2 * NEAR
    limit = pltpu.CompilerParams(vmem_limit_bytes=32 * 2**20)

    def flat(rows):
        return jax.ShapeDtypeStruct((rows, LANES), F32)

    def blocks(count, rows):
        return jax.ShapeDtypeStruct((count, rows, LANES), F32)

    def room(count):
        return pltpu.VMEM((count, ROWS, LANES), F32)

    fluid = 1.0 / viscosity
    pin = 4.0 * pinned.astype(F32) * fluid
    parcels = pl.pallas_call(
        functools.partial(prepare_kernel, share),
        out_shape=blocks(peers, 3 * share),
        compiler_params=limit,
        name="prepare",
    )(residual_q2.reshape(4 * bx * by, 2 * depth), fluid, pin)
    own = pl.pallas_call(
        functools.partial(spread_kernel, groups, by),
        out_shape=blocks(3 * share, ROWS),
        scratch_shapes=[room(3 * share)],
        compiler_params=limit,
        name="spread",
    )(lax.all_to_all(parcels, ("gx", "gy"), 0, 0, tiled=True))
    length = lax.axis_size("gz")
    parts = length * peers

    device = devices_of(length)

    def swap(field, first):
        pairs = [(device[i], device[i + 1]) for i in range(first, parts - 1, 2)]
        return lax.ppermute(field, ("gx", "gy", "gz"), pairs + [pair[::-1] for pair in pairs])

    outer, inner = swap(own, 1), swap(own, 0)
    count3 = share // 4
    near1, near2, far1, far2 = (
        (blocks(count, ROWS),) * fields
        for count, fields in ((share + HALO, 9), (count2, 8), (HALO + 8, 9), (count2, 9))
    )
    near1, near2, fluid2, pin2, fluid3, pin3 = pl.pallas_call(
        functools.partial(near_kernel, share),
        out_shape=(near1, near2) + (blocks(count2, ROWS),) * 2 + (blocks(count3, ROWS),) * 2,
        scratch_shapes=[room(share + HALO)] * 4 + [room(count2)] * 2,
        compiler_params=limit,
        name="near",
    )(own, inner)
    far1, far2, parcel = pl.pallas_call(
        functools.partial(down_kernel, share),
        out_shape=(far1, far2, blocks(5, 2)),
        scratch_shapes=[room(HALO + 8)] * 4 + [room(count2)] * 5,
        compiler_params=limit,
        name="down",
    )(own, outer, near2, fluid2, pin2, fluid3, pin3)
    copies = jnp.broadcast_to(parcel, (parts,) + parcel.shape)
    packed = lax.all_to_all(copies, ("gx", "gy", "gz"), 0, 0, tiled=True)
    depth3 = parts * count3
    mine = pl.pallas_call(
        functools.partial(up_kernel, groups, by, share),
        out_shape=blocks(peers, share),
        scratch_shapes=[room(planes), room(planes), room(count2), room(count2), room(count2)]
        + [pltpu.VMEM((rows, LANES), F32) for rows in (depth3, depth3, depth3 + 3 * NEAR)]
        + [room(share)],
        compiler_params=limit,
        name="up",
    )(packed, near1, far1, far2)
    return pl.pallas_call(
        finish_kernel,
        out_shape=jax.ShapeDtypeStruct((bx, by, depth), F32),
        compiler_params=limit,
        name="finish",
    )(lax.all_to_all(mine, ("gx", "gy"), 0, 0, tiled=True))


def one_tile_planes(mesh, viscosity):
    split = (mesh.shape["gx"], mesh.shape["gy"])
    depth = viscosity.shape[2]
    fits = viscosity.shape[:2] == PLANE and split == SPLIT
    return fits and depth == 4 * LANES and depth // mesh.shape["gz"] == LANES


def solution(mesh):
    placed = (P("gx", "gy", "gz"), P("gx", "gy", "gz"), P("gx", "gy", "gz"))

    def cycle(residual_q2, viscosity, pinned):
        chosen = whole_planes if one_tile_planes(mesh, viscosity) else per_device
        return jax.shard_map(
            chosen, mesh=mesh, in_specs=placed, out_specs=P("gx", "gy", "gz"), check_vma=False
        )(residual_q2, viscosity, pinned)

    return cycle
```

```python
import functools

import jax
import jax.numpy as jnp
from jax import lax
from jax.experimental import pallas as pl
from jax.experimental.pallas import tpu as pltpu
from jax.sharding import PartitionSpec as P

NU = 3


OMEGA = 0.6


def with_halo(block, sides, width):
    for axis, dim in sides:
        count = lax.axis_size(axis)
        forward = [(i, i + 1) for i in range(count - 1)]
        backward = [(target, source) for source, target in forward]
        low = lax.ppermute(
            lax.slice_in_dim(block, block.shape[dim] - width, None, axis=dim), axis, forward
        )
        high = lax.ppermute(lax.slice_in_dim(block, 0, width, axis=dim), axis, backward)
        block = jnp.concatenate([low, block, high], axis=dim)
    return block


def coarsen(x):
    a, b, c = x.shape
    return x.reshape(a // 2, 2, b // 2, 2, c // 2, 2).sum(axis=(1, 3, 5))


def refine(x):
    return jnp.repeat(jnp.repeat(jnp.repeat(x, 2, 0), 2, 1), 2, 2)


def extended(field):
    return with_halo(field, (("gx", 0), ("gy", 1), ("gz", 2)), 1)


def shifted(padded):
    return [
        padded[2:, 1:-1, 1:-1],
        padded[:-2, 1:-1, 1:-1],
        padded[1:-1, 2:, 1:-1],
        padded[1:-1, :-2, 1:-1],
        padded[1:-1, 1:-1, 2:],
        padded[1:-1, 1:-1, :-2],
    ]


def neighbours(field):
    return shifted(extended(field))


def harmonic(fluid, near, factor):
    total = fluid + near
    return jnp.where(total > 0, factor * 2.0 * fluid * near / jnp.where(total > 0, total, 1.0), 0.0)


def couplings(fluid, factor):
    return [harmonic(fluid, near, factor) for near in neighbours(fluid)]


def apply_op(field, weights, diag):
    total = diag * field
    for weight, near in zip(weights, neighbours(field)):
        total = total - weight * near
    return total


def presmooth(rhs, weights, diag):
    corr = OMEGA * rhs / diag
    for sweep in range(NU - 1):
        corr = corr + OMEGA * (rhs - apply_op(corr, weights, diag)) / diag
    return corr


def postsmooth(corr, rhs, weights, diag):
    for sweep in range(NU):
        corr = corr + OMEGA * (rhs - apply_op(corr, weights, diag)) / diag
    return corr


def tridiag(coeffs, rhs):
    solved = lax.linalg.tridiagonal_solve(coeffs[0], coeffs[1], coeffs[2], rhs[..., None])[..., 0]
    last = rhs.ndim - 1
    shift_col = jnp.sum(rhs, axis=last, keepdims=True) / jnp.sum(
        coeffs[3], axis=last, keepdims=True
    )
    return solved + shift_col


def prepare_columns(weights, diag):
    lower = -weights[5]
    upper = -weights[4]
    across = diag + lower + upper
    return (
        lax.all_gather(lower, "gz", axis=2, tiled=True),
        lax.all_gather(diag, "gz", axis=2, tiled=True),
        lax.all_gather(upper, "gz", axis=2, tiled=True),
        lax.all_gather(across, "gz", axis=2, tiled=True),
    )


def column_solve(rhs, coeffs):
    depth = rhs.shape[2]
    whole = lax.all_gather(rhs, "gz", axis=2, tiled=True)
    solved = tridiag(coeffs, whole)
    return lax.dynamic_slice_in_dim(solved, lax.axis_index("gz") * depth, depth, 2)


def per_device(residual_q2, viscosity, pinned):
    fluid1 = 1.0 / viscosity
    pin1 = 4.0 * pinned.astype(jnp.float32) * fluid1
    rhs1 = coarsen(residual_q2.astype(jnp.float32))
    fluid2 = coarsen(fluid1) / 8.0
    pin2 = coarsen(pin1) / 4.0
    fluid3 = coarsen(fluid2) / 8.0
    pin3 = coarsen(pin2) / 4.0
    weights1 = couplings(fluid1, 1.0)
    weights2 = couplings(fluid2, 2.0)
    weights3 = couplings(fluid3, 4.0)
    diag1 = sum(weights1) + pin1
    diag2 = sum(weights2) + pin2
    diag3 = sum(weights3) + pin3
    coeffs = prepare_columns(weights3, diag3)
    corr1 = presmooth(rhs1, weights1, diag1)
    rhs2 = coarsen(rhs1 - apply_op(corr1, weights1, diag1))
    corr2 = presmooth(rhs2, weights2, diag2)
    rhs3 = coarsen(rhs2 - apply_op(corr2, weights2, diag2))
    corr3 = column_solve(rhs3, coeffs)
    corr3 = corr3 + column_solve(rhs3 - apply_op(corr3, weights3, diag3), coeffs)
    corr2 = postsmooth(corr2 + refine(corr3), rhs2, weights2, diag2)
    corr1 = postsmooth(corr1 + refine(corr2), rhs1, weights1, diag1)
    return diag1 * corr1


PLANE = (32, 32)
SPLIT = (2, 4)
ROWS = 8
LANES = 128
HALO = 16
NEAR = 8
PIECE = 8
TINY = 1e-30
F32 = jnp.float32


def iota(shape, dim):
    return lax.broadcasted_iota(jnp.int32, shape, dim)


def dot01(field, chosen, parts=3):
    total = None
    rest = field
    for part in range(parts):
        piece = rest.astype(jnp.bfloat16)
        term = jnp.dot(piece, chosen, preferred_element_type=F32)
        total = term if total is None else total + term
        if part < parts - 1:
            rest = rest - piece.astype(F32)
    return total


def dot10(chosen, field):
    total = None
    rest = field
    for part in range(3):
        piece = rest.astype(jnp.bfloat16)
        term = lax.dot_general(
            chosen, piece, (((1,), (1,)), ((), ())), preferred_element_type=F32
        )
        total = term if total is None else total + term
        if part < 2:
            rest = rest - piece.astype(F32)
    return total


def where01(condition):
    return jnp.where(condition, 1.0, 0.0).astype(jnp.bfloat16)


def loop(low, high, size, body):
    for plane in range(low, high, size):
        body(plane, min(size, high - plane))


def inverse_of(field):
    first = pl.reciprocal(field, approx=True)
    return first * (2.0 - field * first)


class Level:
    def __init__(self, level):
        self.ny = PLANE[1] >> level
        self.xs = 4 >> level
        self.factor = float(2**level)

    def masks(self, shape):
        lane = iota(shape, 2)
        row = iota(shape, 1)
        within = (lane // self.ny) % self.xs
        y = lane % self.ny
        last_x = (row == ROWS - 1) & (within == self.xs - 1)
        return within, y == self.ny - 1, last_x

    def next_x(self, field):
        within = (iota(field.shape, 2) // self.ny) % self.xs
        moved = pltpu.roll(field, LANES - self.ny, 2)
        return jnp.where(within == self.xs - 1, pltpu.roll(moved, ROWS - 1, 1), moved)

    def last_x(self, field):
        within = (iota(field.shape, 2) // self.ny) % self.xs
        moved = pltpu.roll(field, self.ny, 2)
        return jnp.where(within == 0, pltpu.roll(moved, 1, 1), moved)

    def next_y(self, field):
        return pltpu.roll(field, LANES - 1, 2)

    def last_y(self, field):
        return pltpu.roll(field, 1, 2)

    def spread(self, field, scaled, plane, count):
        mid = field[1:-1]
        near = (
            self.next_x(mid), self.last_x(mid), self.next_y(mid), self.last_y(mid),
            field[2:], field[:-2],
        )
        terms = [weight[pl.ds(plane, count)] * value for weight, value in zip(scaled, near)]
        return mid, ((terms[0] + terms[1]) + (terms[2] + terms[3])) + (terms[4] + terms[5])


def mean_of(fluid, near, factor):
    return ((factor * 2.0) * fluid * near) * inverse_of(jnp.maximum(fluid + near, TINY))


def set_level(level, low, high, fluid, pin, rhs, fields):
    scaled, start, diag = fields

    def body(plane, count):
        wide = fluid[pl.ds(plane - 1, count + 2)]
        mid = wide[1:-1]
        within, end_y, end_x = level.masks(mid.shape)
        to_x = jnp.where(end_x, 0.0, mean_of(mid, level.next_x(mid), level.factor))
        to_y = jnp.where(end_y, 0.0, mean_of(mid, level.next_y(mid), level.factor))
        to_z = mean_of(wide[:-1], wide[1:], level.factor)
        weights = (to_x, level.last_x(to_x), to_y, level.last_y(to_y), to_z[1:], to_z[:-1])
        total = (
            (weights[0] + weights[1])
            + (weights[2] + weights[3])
            + (weights[4] + weights[5])
            + pin[pl.ds(plane, count)]
        )
        gain = OMEGA * inverse_of(jnp.maximum(total, TINY))
        for target, weight in zip(scaled, weights):
            target[pl.ds(plane, count)] = gain * weight
        start[pl.ds(plane, count)] = gain * rhs[pl.ds(plane, count)]
        diag[pl.ds(plane, count)] = total

    loop(low, high, PIECE, body)


def swept(level, plane, count, fields, source, shift=0):
    scaled, start, _ = fields
    mid, total = level.spread(source[pl.ds(plane - 1, count + 2)], scaled, plane - shift, count)
    return (1.0 - OMEGA) * mid + (start[pl.ds(plane - shift, count)] + total)


def sweep(level, low, high, fields, source, target, shift=0):
    def body(plane, count):
        target[pl.ds(plane, count)] = swept(level, plane, count, fields, source, shift)

    loop(low, high, PIECE, body)


def pair_sum(field):
    half = field.reshape((field.shape[0] // 2, 2) + field.shape[1:])
    return half[:, 0] + half[:, 1]


def coarse_residual(level, low, high, fields, corr, target):
    scaled, start, diag = fields

    def body(plane, count):
        mid, total = level.spread(corr[pl.ds(plane - 1, count + 2)], scaled, plane, count)
        rest = (start[pl.ds(plane, count)] + total) - OMEGA * mid
        rest = rest * (diag[pl.ds(plane, count)] * (1.0 / OMEGA))
        target[pl.ds((plane - low) // 2, count // 2)] = pair_sum(rest)

    loop(low, high, PIECE, body)


def lanes_down(level):
    fine = iota((LANES, LANES), 0)
    coarse = iota((LANES, LANES), 1)
    ny, xs = PLANE[1] >> level, 4 >> level
    half = xs // 2
    same_x = ((fine // ny) % xs) // 2 == (coarse // (ny // 2)) % half
    same_y = (fine % ny) // 2 == coarse % (ny // 2)
    return where01((fine < ny * xs) & same_x & same_y)


def in_lanes(field, chosen, parts=3):
    flat = field.reshape(field.shape[0] * ROWS, LANES)
    return dot01(flat, chosen, parts).reshape(field.shape)


def path_of(group):
    nx, ny = SPLIT
    row, column = 0, 0
    for index in range(group + 1):
        columns = list(range(ny)) if column == 0 else list(range(ny))[::-1]
        if index % 2:
            path = [(row, at) for at in columns] + [(1 - row, at) for at in columns[::-1]]
        else:
            path = []
            for at in columns:
                path += [(row, at), (1 - row, at)]
                row = 1 - row
        row, column = path[-1]
    return [row * ny + column for row, column in path]


def lookup(table, index):
    found = table[0]
    for at, value in enumerate(table[1:], 1):
        found = jnp.where(index == at, value, found)
    return found


def own_peer_of(rank):
    return lookup([path_of(group)[rank] for group in range(lax.axis_size("gz"))], lax.axis_index("gz"))


def slabs_of(groups):
    peers = SPLIT[0] * SPLIT[1]
    return [
        group * peers + path_of(group).index(peer) for peer in range(peers) for group in range(groups)
    ]


def own_slab():
    nx, ny = SPLIT
    groups = lax.axis_size("gz")
    device = (lax.axis_index("gx") * ny + lax.axis_index("gy")) * groups + lax.axis_index("gz")
    return lookup(slabs_of(groups), device)


def devices_of(groups):
    slabs = slabs_of(groups)
    return [slabs.index(slab) for slab in range(len(slabs))]


def prepare_kernel(share, res_ref, fluid_ref, pin_ref, out_ref):
    bx, by, depth = fluid_ref.shape
    cells = bx * by
    groups = bx // 4
    order = [x for low in range(4) for x in range(low, bx, 4)]
    fine = iota((cells, 4 * cells), 1)
    x, y = fine // (4 * by), (fine % (2 * by)) // 2
    chosen = where01((x % 4) * (groups * by) + (x // 4) * by + y == iota((cells, 4 * cells), 0))
    wide = lax.dot_general(
        chosen, res_ref[...], (((1,), (0,)), ((), ())), preferred_element_type=F32
    )
    rhs = dot10(where01(iota((depth, 2 * depth), 1) // 2 == iota((depth, 2 * depth), 0)), wide)

    def turned(field_ref):
        field = jnp.concatenate([field_ref[x : x + 1] for x in order], axis=0)
        return field.reshape(cells, depth).T

    fluid, pin = turned(fluid_ref), turned(pin_ref)
    for rank in range(depth // share):
        peer, begin = own_peer_of(rank), rank * share
        for index, field in enumerate((fluid, rhs, pin)):
            out_ref[peer, index * share : (index + 1) * share] = field[begin : begin + share]


def spread_kernel(groups, by, gathered, own, straight):
    for start in range(0, own.shape[0], ROWS):
        place(gathered, start, straight, start, groups, by)
    share = own.shape[0] // 3
    odd = own_slab() % 2 == 1
    for index in range(3):
        for plane in range(share):
            at = jnp.where(odd, share - 1 - plane, plane)
            own[index * share + plane] = straight[index * share + at]


def place(gathered, row, target, plane, groups, by):
    group = (iota((ROWS, LANES), 1) // by) % groups
    nx, ny = SPLIT
    for ix in range(nx):
        found = [gathered[ix * ny + iy, pl.ds(row, ROWS), :] for iy in range(ny)]
        for part in range(groups):
            total = found[part]
            for iy in range(ny):
                if iy != part:
                    moved = pltpu.roll(found[iy], (by * (iy - part)) % LANES, 1)
                    total = jnp.where(group == iy, moved, total)
            target[pl.ds(plane, ROWS), ix * groups + part, :] = total


def near_kernel(
    depth,
    own, inner,
    saved1, saved2, fluid2, pin2, fluid3, pin3,
    fluid1, rhs1, pin1, other1, rhs2, sums,
):
    for index, target in enumerate((fluid1, rhs1, pin1)):
        target[0:depth] = own[index * depth : (index + 1) * depth]
        for plane in range(HALO):
            target[depth + plane] = inner[(index + 1) * depth - 1 - plane]
    fine, coarse = Level(0), Level(1)
    down1, down2 = lanes_down(0), lanes_down(1)
    fields1, corr1 = (saved1[0:6], saved1[6], saved1[7]), saved1[8]
    fields2 = (saved2[0:6], saved2[6], saved2[7])
    planes = depth + HALO
    set_level(fine, 1, planes - 1, fluid1, pin1, rhs1, fields1)
    sweep(fine, 2, planes - 2, fields1, fields1[1], other1)
    sweep(fine, 3, planes - 3, fields1, other1, corr1)
    coarse_residual(fine, 4, planes - 4, fields1, corr1, sums)
    count2 = planes // 2
    for source, target, share in ((fluid1, fluid2, 8.0), (pin1, pin2, 4.0)):
        target[NEAR : NEAR + count2] = in_lanes(pair_sum(source[...]), down1) * (1.0 / share)
    low2, high2 = NEAR + 2, NEAR + count2 - 2
    rhs2[low2:high2] = in_lanes(sums[0 : high2 - low2], down1)
    set_level(coarse, low2, high2, fluid2, pin2, rhs2, fields2)
    for source, target, scale in ((fluid2, fluid3, 0.125), (pin2, pin3, 0.25)):
        target[...] = in_lanes(pair_sum(source[NEAR : NEAR + depth // 2]), down2) * scale


def down_kernel(
    depth,
    own, outer, near2, near_fluid2, near_pin2, fluid3, pin3,
    saved1, saved2,
    packed,
    fluid1, rhs1, pin1, other1, fluid2, rhs2, pin2, other2, sums,
):
    planes = fluid1.shape[0]
    for index, target in enumerate((fluid1, rhs1, pin1)):
        for plane in range(HALO):
            target[plane] = outer[index * depth + HALO - 1 - plane]
        target[HALO:planes] = own[index * depth : index * depth + planes - HALO]

    fine, coarse = Level(0), Level(1)
    down1, down2 = lanes_down(0), lanes_down(1)
    fields1, corr1 = (saved1[0:6], saved1[6], saved1[7]), saved1[8]
    fields2, corr2 = (saved2[0:6], saved2[6], saved2[7]), saved2[8]
    set_level(fine, 1, planes - 1, fluid1, pin1, rhs1, fields1)
    sweep(fine, 2, planes - 2, fields1, fields1[1], other1)
    sweep(fine, 3, planes - 3, fields1, other1, corr1)
    count2 = depth // 2 + 2 * NEAR
    low2, done, high2 = 2, NEAR + 2, count2 - 2
    coarse_residual(fine, 2 * low2, 2 * done, fields1, corr1, sums)
    for source, ready, target, share in (
        (fluid1, near_fluid2, fluid2, 8.0), (pin1, near_pin2, pin2, 4.0)
    ):
        target[0:NEAR] = in_lanes(pair_sum(source[0:HALO]), down1) * (1.0 / share)
        target[NEAR : done + 1] = ready[NEAR : done + 1]
    rhs2[low2:done] = in_lanes(sums[0 : done - low2], down1)
    set_level(coarse, low2, done, fluid2, pin2, rhs2, fields2)
    for source, target in zip(near2, saved2[0:8]):
        target[done:high2] = source[done:high2]
    sweep(coarse, low2 + 1, high2 - 1, fields2, fields2[1], other2)
    sweep(coarse, low2 + 2, high2 - 2, fields2, other2, corr2)
    coarse_residual(coarse, NEAR, NEAR + depth // 2, fields2, corr2, sums)
    count3 = depth // 4
    rhs3 = in_lanes(sums[0:count3], down2)
    lane = iota((count3, LANES), 1) // ROWS
    first = jnp.zeros((count3, LANES), F32)
    second = jnp.zeros((count3, LANES), F32)
    for row in range(ROWS):
        first = jnp.where(lane == row, rhs3[:, row, :], first)
        first = jnp.where(lane == ROWS + row, fluid3[:, row, :], first)
        second = jnp.where(lane % ROWS == row, pin3[:, row, :], second)
    packed[0] = first[0:2]
    packed[1] = first[2:4]
    packed[2] = jnp.where(lane[0:2] < ROWS, second[0:2], second[2:4])
    lane = iota((1, LANES), 1) // (LANES // 4)
    for index, plane in enumerate((NEAR + depth // 2 - 5, NEAR + 4)):
        for half in range(2):
            row = jnp.zeros((1, LANES), F32)
            for quarter in range(4):
                at = half * 4 + quarter
                row = jnp.where(lane == quarter, corr2[plane, at : at + 1, :], row)
            packed[3 + index, half : half + 1, :] = row


def rolled(field, shift):
    count = field.shape[0]
    shift %= count
    if shift % ROWS:
        return pltpu.roll(field, shift, 0)
    return jnp.concatenate([field[count - shift :], field[: count - shift]], axis=0)


def columns(rhs, fluid, pin):
    depth = fluid.shape[0]
    z, lane = iota(fluid.shape, 0), iota(fluid.shape, 1)
    y, x = lane % ROWS, (lane // ROWS) % ROWS

    def next_x(field):
        return pltpu.roll(field, LANES - ROWS, 1)

    def next_y(field):
        return pltpu.roll(field, LANES - 1, 1)

    wz = jnp.where(z == depth - 1, 0.0, mean_of(fluid, rolled(fluid, -1), 4.0))
    wy = jnp.where(y == ROWS - 1, 0.0, mean_of(fluid, next_y(fluid), 4.0))
    wx = jnp.where(x == ROWS - 1, 0.0, mean_of(fluid, next_x(fluid), 4.0))
    across = (wx + pltpu.roll(wx, ROWS, 1)) + (wy + pltpu.roll(wy, 1, 1)) + pin
    share = 1.0 / jnp.sum(across, axis=0, keepdims=True)

    above, below, own = rolled(wz, 1), wz, across
    steps = []
    stride = 1
    while stride < depth:
        inverse = inverse_of(above + below + own)
        up = above * rolled(inverse, stride)
        down = below * rolled(inverse, -stride)
        own = own + up * rolled(own, stride) + down * rolled(own, -stride)
        above = up * rolled(above, stride)
        below = down * rolled(below, -stride)
        steps.append((stride, up, down))
        stride *= 2
    inverse = inverse_of(above + below + own)

    def solve(right):
        mean = jnp.sum(right, axis=0, keepdims=True) * share
        for stride, up, down in steps:
            right = right + up * rolled(right, stride) + down * rolled(right, -stride)
        return right * inverse + mean

    corr = solve(rhs)
    flow_x = wx * (next_x(corr) - corr)
    flow_y = wy * (next_y(corr) - corr)
    flow_z = wz * (rolled(corr, -1) - corr)
    rest = (
        (rhs - pin * corr)
        + (flow_x - pltpu.roll(flow_x, ROWS, 1))
        + (flow_y - pltpu.roll(flow_y, 1, 1))
        + (flow_z - rolled(flow_z, 1))
    )
    return corr + solve(rest)


def up_kernel(
    groups, by, depth,
    packed, near1, far1, far2,
    out_ref,
    one1, two1, one2, two2, lifted, first, second, solved, final,
):
    count3 = depth // 4
    shares = packed.shape[0]
    peers = SPLIT[0] * SPLIT[1]
    devices = devices_of(shares // peers)
    for slab, index in enumerate(devices):
        row = slab * count3
        low, high, both = packed[index, 0], packed[index, 1], packed[index, 2]
        rest = pltpu.roll(both, LANES // 2, 1)
        if slab % 2:
            for at, (level3, pin) in enumerate(((high, rest), (low, both))):
                begin = row + 2 * at
                first[begin : begin + 1] = level3[1:2]
                first[begin + 1 : begin + 2] = level3[0:1]
                second[begin : begin + 1] = pin[1:2]
                second[begin + 1 : begin + 2] = pin[0:1]
        else:
            first[row : row + 2] = low
            first[row + 2 : row + 4] = high
            second[row : row + 2] = both
            second[row + 2 : row + 4] = rest
    half = iota((shares * count3, LANES), 1) < LANES // 2

    def low_half(field):
        return jnp.where(half, field, pltpu.roll(field, LANES // 2, 1))

    def high_half(field):
        return jnp.where(half, pltpu.roll(field, LANES // 2, 1), field)

    solved[NEAR : NEAR + shares * count3] = columns(
        low_half(first[...]), high_half(first[...]), low_half(second[...])
    )
    solved[0:NEAR] = jnp.zeros((NEAR, LANES), F32)
    solved[NEAR + shares * count3 :] = jnp.zeros((2 * NEAR, LANES), F32)

    nx, ny = SPLIT
    part = own_slab()
    count = count3 + 2 * NEAR
    tall = solved[pl.ds(part * count3, count + count3), :]
    fine, coarse = Level(0), Level(1)
    cell = iota((LANES, LANES), 0)
    lane = iota((LANES, LANES), 1)
    spread = where01((cell < ROWS) & (cell == (lane % coarse.ny) // 2))
    rows = tall.shape[0]
    turned = [tall] + [pltpu.roll(tall, LANES - ROWS * row, 1) for row in range(1, ROWS)]
    wide = dot01(jnp.concatenate(turned, axis=0), spread, 2)
    for row in range(ROWS):
        lifted[0:rows, row, :] = wide[row * rows : (row + 1) * rows]

    odd = part % 2 == 1

    def lifted_to(plane):
        parent = plane // 2 + NEAR // 2
        return lifted[jnp.where(odd, count - 1 - parent, parent)]

    near_fields, near_corr1 = (near1[0:6], near1[6], near1[7]), near1[8]
    far_fields, far_corr1 = (far1[0:6], far1[6], far1[7]), far1[8]
    fields2, corr2 = (far2[0:6], far2[6], far2[7]), far2[8]
    low, high = NEAR - 4, NEAR + depth // 2 + 4
    reach = depth // 2 + NEAR
    quarter = iota((ROWS, LANES), 1) // (LANES // 4)
    row = iota((ROWS, LANES), 0)

    def unpacked(index, which):
        pair = packed[lookup(devices, jnp.clip(index, 0, shares - 1)), which]
        total = None
        for shift in range(4):
            moved = pltpu.roll(pair, shift * (LANES // 4), 1)
            wide = jnp.where(row < 4, moved[0:1, :], moved[1:2, :])
            kept = jnp.where((quarter - shift) % 4 == row % 4, wide, 0.0)
            total = kept if total is None else total + kept
        return total

    one2[low - 1] = unpacked(jnp.where(odd, part + 1, part - 1), 4) + lifted_to(low - 1)
    for plane in range(low, high):
        one2[plane] = corr2[plane] + lifted_to(plane)
    one2[high] = unpacked(jnp.where(odd, part - 1, part + 1), 3) + lifted_to(high)
    sweep(coarse, NEAR - 4, reach + 4, fields2, one2, two2)
    sweep(coarse, NEAR - 3, reach + 3, fields2, two2, one2)
    sweep(coarse, NEAR - 2, reach + 2, fields2, one2, two2)

    fine_lane, coarse_lane = iota((LANES, LANES), 1), iota((LANES, LANES), 0)
    x_of = (fine_lane // fine.ny) // 2
    y_of = (fine_lane % fine.ny) // 2
    up = where01(coarse_lane == x_of * coarse.ny + y_of)
    lifted[0 : depth // 2 + 4] = in_lanes(two2[NEAR - 2 : reach + 2], up, 2)
    parents = lifted[0 : depth // 2 + 4]
    twice = jnp.broadcast_to(parents[:, None], (parents.shape[0], 2, ROWS, LANES))
    low, high = HALO - 4, HALO + depth + 4
    turn = HALO + 3
    for plane in range(low, high):
        corr = far_corr1[plane] if plane < turn else near_corr1[plane - HALO]
        one1[plane] = corr + lifted[(plane - low) // 2]
    reach = depth + HALO
    for more, source, target in ((2, one1, two1), (1, two1, one1)):
        sweep(fine, HALO - more, turn, far_fields, source, target)
        sweep(fine, turn, reach + more, near_fields, source, target, HALO)

    def last(fields, shift):
        def body(plane, count):
            value = swept(fine, plane, count, fields, one1, shift)
            value = value * fields[2][pl.ds(plane - shift, count)]
            for index in range(count):
                at = plane - HALO + index
                final[jnp.where(odd, depth - 1 - at, at)] = value[index]

        return body

    loop(HALO, turn, PIECE, last(far_fields, 0))
    loop(turn, reach, PIECE, last(near_fields, HALO))

    group = (iota((depth, LANES), 1) // by) % groups
    for ix in range(nx):
        scaled = [final[:, ix * groups + part, :] for part in range(groups)]
        for iy in range(ny):
            total = scaled[iy]
            for part in range(groups):
                if part != iy:
                    moved = pltpu.roll(scaled[part], (by * (part - iy)) % LANES, 1)
                    total = jnp.where(group == part, moved, total)
            out_ref[ix * ny + iy] = total


def finish_kernel(blocks, out_ref):
    bx, by, depth = out_ref.shape
    peers = blocks.shape[0]
    ordered = jnp.concatenate([blocks[own_peer_of(rank)] for rank in range(peers)], axis=0)
    turned = ordered.T
    for x in range(bx):
        row = ((x % 4) * (bx // 4) + x // 4) * by
        out_ref[x] = turned[row : row + by]


def whole_planes(residual_q2, viscosity, pinned):
    bx, by, depth = viscosity.shape
    groups = bx // 4
    peers = SPLIT[0] * SPLIT[1]
    share = depth // peers
    planes = share + 2 * HALO
    count2 = share // 2 + 2 * NEAR
    limit = pltpu.CompilerParams(vmem_limit_bytes=32 * 2**20)

    def flat(rows):
        return jax.ShapeDtypeStruct((rows, LANES), F32)

    def blocks(count, rows):
        return jax.ShapeDtypeStruct((count, rows, LANES), F32)

    def room(count):
        return pltpu.VMEM((count, ROWS, LANES), F32)

    fluid = 1.0 / viscosity
    pin = 4.0 * pinned.astype(F32) * fluid
    parcels = pl.pallas_call(
        functools.partial(prepare_kernel, share),
        out_shape=blocks(peers, 3 * share),
        compiler_params=limit,
        name="prepare",
    )(residual_q2.reshape(4 * bx * by, 2 * depth), fluid, pin)
    own = pl.pallas_call(
        functools.partial(spread_kernel, groups, by),
        out_shape=blocks(3 * share, ROWS),
        scratch_shapes=[room(3 * share)],
        compiler_params=limit,
        name="spread",
    )(lax.all_to_all(parcels, ("gx", "gy"), 0, 0, tiled=True))
    length = lax.axis_size("gz")
    parts = length * peers

    device = devices_of(length)

    def swap(field, first):
        pairs = [(device[i], device[i + 1]) for i in range(first, parts - 1, 2)]
        return lax.ppermute(field, ("gx", "gy", "gz"), pairs + [pair[::-1] for pair in pairs])

    outer, inner = swap(own, 1), swap(own, 0)
    count3 = share // 4
    near1, near2, far1, far2 = (
        (blocks(count, ROWS),) * fields
        for count, fields in ((share + HALO, 9), (count2, 8), (HALO + 8, 9), (count2, 9))
    )
    near1, near2, fluid2, pin2, fluid3, pin3 = pl.pallas_call(
        functools.partial(near_kernel, share),
        out_shape=(near1, near2) + (blocks(count2, ROWS),) * 2 + (blocks(count3, ROWS),) * 2,
        scratch_shapes=[room(share + HALO)] * 4 + [room(count2)] * 2,
        compiler_params=limit,
        name="near",
    )(own, inner)
    far1, far2, parcel = pl.pallas_call(
        functools.partial(down_kernel, share),
        out_shape=(far1, far2, blocks(5, 2)),
        scratch_shapes=[room(HALO + 8)] * 4 + [room(count2)] * 5,
        compiler_params=limit,
        name="down",
    )(own, outer, near2, fluid2, pin2, fluid3, pin3)
    copies = jnp.broadcast_to(parcel, (parts,) + parcel.shape)
    packed = lax.all_to_all(copies, ("gx", "gy", "gz"), 0, 0, tiled=True)
    depth3 = parts * count3
    mine = pl.pallas_call(
        functools.partial(up_kernel, groups, by, share),
        out_shape=blocks(peers, share),
        scratch_shapes=[room(planes), room(planes), room(count2), room(count2), room(count2)]
        + [pltpu.VMEM((rows, LANES), F32) for rows in (depth3, depth3, depth3 + 3 * NEAR)]
        + [room(share)],
        compiler_params=limit,
        name="up",
    )(packed, near1, far1, far2)
    return pl.pallas_call(
        finish_kernel,
        out_shape=jax.ShapeDtypeStruct((bx, by, depth), F32),
        compiler_params=limit,
        name="finish",
    )(lax.all_to_all(mine, ("gx", "gy"), 0, 0, tiled=True))


def one_tile_planes(mesh, viscosity):
    split = (mesh.shape["gx"], mesh.shape["gy"])
    depth = viscosity.shape[2]
    fits = viscosity.shape[:2] == PLANE and split == SPLIT
    return fits and depth == 4 * LANES and depth // mesh.shape["gz"] == LANES


def solution(mesh):
    placed = (P("gx", "gy", "gz"), P("gx", "gy", "gz"), P("gx", "gy", "gz"))

    def cycle(residual_q2, viscosity, pinned):
        chosen = whole_planes if one_tile_planes(mesh, viscosity) else per_device
        return jax.shard_map(
            chosen, mesh=mesh, in_specs=placed, out_specs=P("gx", "gy", "gz"), check_vma=False
        )(residual_q2, viscosity, pinned)

    return cycle
```

```python
import functools

import jax
import jax.numpy as jnp
from jax import lax
from jax.experimental import pallas as pl
from jax.experimental.pallas import tpu as pltpu
from jax.sharding import PartitionSpec as P

NU = 3


OMEGA = 0.6


def with_halo(block, sides, width):
    for axis, dim in sides:
        count = lax.axis_size(axis)
        forward = [(i, i + 1) for i in range(count - 1)]
        backward = [(target, source) for source, target in forward]
        low = lax.ppermute(
            lax.slice_in_dim(block, block.shape[dim] - width, None, axis=dim), axis, forward
        )
        high = lax.ppermute(lax.slice_in_dim(block, 0, width, axis=dim), axis, backward)
        block = jnp.concatenate([low, block, high], axis=dim)
    return block


def coarsen(x):
    a, b, c = x.shape
    return x.reshape(a // 2, 2, b // 2, 2, c // 2, 2).sum(axis=(1, 3, 5))


def refine(x):
    return jnp.repeat(jnp.repeat(jnp.repeat(x, 2, 0), 2, 1), 2, 2)


def extended(field):
    return with_halo(field, (("gx", 0), ("gy", 1), ("gz", 2)), 1)


def shifted(padded):
    return [
        padded[2:, 1:-1, 1:-1],
        padded[:-2, 1:-1, 1:-1],
        padded[1:-1, 2:, 1:-1],
        padded[1:-1, :-2, 1:-1],
        padded[1:-1, 1:-1, 2:],
        padded[1:-1, 1:-1, :-2],
    ]


def neighbours(field):
    return shifted(extended(field))


def harmonic(fluid, near, factor):
    total = fluid + near
    return jnp.where(total > 0, factor * 2.0 * fluid * near / jnp.where(total > 0, total, 1.0), 0.0)


def couplings(fluid, factor):
    return [harmonic(fluid, near, factor) for near in neighbours(fluid)]


def apply_op(field, weights, diag):
    total = diag * field
    for weight, near in zip(weights, neighbours(field)):
        total = total - weight * near
    return total


def presmooth(rhs, weights, diag):
    corr = OMEGA * rhs / diag
    for sweep in range(NU - 1):
        corr = corr + OMEGA * (rhs - apply_op(corr, weights, diag)) / diag
    return corr


def postsmooth(corr, rhs, weights, diag):
    for sweep in range(NU):
        corr = corr + OMEGA * (rhs - apply_op(corr, weights, diag)) / diag
    return corr


def tridiag(coeffs, rhs):
    solved = lax.linalg.tridiagonal_solve(coeffs[0], coeffs[1], coeffs[2], rhs[..., None])[..., 0]
    last = rhs.ndim - 1
    shift_col = jnp.sum(rhs, axis=last, keepdims=True) / jnp.sum(
        coeffs[3], axis=last, keepdims=True
    )
    return solved + shift_col


def prepare_columns(weights, diag):
    lower = -weights[5]
    upper = -weights[4]
    across = diag + lower + upper
    return (
        lax.all_gather(lower, "gz", axis=2, tiled=True),
        lax.all_gather(diag, "gz", axis=2, tiled=True),
        lax.all_gather(upper, "gz", axis=2, tiled=True),
        lax.all_gather(across, "gz", axis=2, tiled=True),
    )


def column_solve(rhs, coeffs):
    depth = rhs.shape[2]
    whole = lax.all_gather(rhs, "gz", axis=2, tiled=True)
    solved = tridiag(coeffs, whole)
    return lax.dynamic_slice_in_dim(solved, lax.axis_index("gz") * depth, depth, 2)


def per_device(residual_q2, viscosity, pinned):
    fluid1 = 1.0 / viscosity
    pin1 = 4.0 * pinned.astype(jnp.float32) * fluid1
    rhs1 = coarsen(residual_q2.astype(jnp.float32))
    fluid2 = coarsen(fluid1) / 8.0
    pin2 = coarsen(pin1) / 4.0
    fluid3 = coarsen(fluid2) / 8.0
    pin3 = coarsen(pin2) / 4.0
    weights1 = couplings(fluid1, 1.0)
    weights2 = couplings(fluid2, 2.0)
    weights3 = couplings(fluid3, 4.0)
    diag1 = sum(weights1) + pin1
    diag2 = sum(weights2) + pin2
    diag3 = sum(weights3) + pin3
    coeffs = prepare_columns(weights3, diag3)
    corr1 = presmooth(rhs1, weights1, diag1)
    rhs2 = coarsen(rhs1 - apply_op(corr1, weights1, diag1))
    corr2 = presmooth(rhs2, weights2, diag2)
    rhs3 = coarsen(rhs2 - apply_op(corr2, weights2, diag2))
    corr3 = column_solve(rhs3, coeffs)
    corr3 = corr3 + column_solve(rhs3 - apply_op(corr3, weights3, diag3), coeffs)
    corr2 = postsmooth(corr2 + refine(corr3), rhs2, weights2, diag2)
    corr1 = postsmooth(corr1 + refine(corr2), rhs1, weights1, diag1)
    return diag1 * corr1


PLANE = (32, 32)
SPLIT = (2, 4)
ROWS = 8
LANES = 128
HALO = 16
NEAR = 8
PIECE = 8
TINY = 1e-30
F32 = jnp.float32


def iota(shape, dim):
    return lax.broadcasted_iota(jnp.int32, shape, dim)


def dot01(field, chosen, parts=3):
    total = None
    rest = field
    for part in range(parts):
        piece = rest.astype(jnp.bfloat16)
        term = jnp.dot(piece, chosen, preferred_element_type=F32)
        total = term if total is None else total + term
        if part < parts - 1:
            rest = rest - piece.astype(F32)
    return total


def dot10(chosen, field):
    total = None
    rest = field
    for part in range(3):
        piece = rest.astype(jnp.bfloat16)
        term = lax.dot_general(
            chosen, piece, (((1,), (1,)), ((), ())), preferred_element_type=F32
        )
        total = term if total is None else total + term
        if part < 2:
            rest = rest - piece.astype(F32)
    return total


def where01(condition):
    return jnp.where(condition, 1.0, 0.0).astype(jnp.bfloat16)


def loop(low, high, size, body):
    for plane in range(low, high, size):
        body(plane, min(size, high - plane))


def inverse_of(field):
    first = pl.reciprocal(field, approx=True)
    return first * (2.0 - field * first)


class Level:
    def __init__(self, level):
        self.ny = PLANE[1] >> level
        self.xs = 4 >> level
        self.factor = float(2**level)

    def masks(self, shape):
        lane = iota(shape, 2)
        row = iota(shape, 1)
        within = (lane // self.ny) % self.xs
        y = lane % self.ny
        last_x = (row == ROWS - 1) & (within == self.xs - 1)
        return within, y == self.ny - 1, last_x

    def next_x(self, field):
        within = (iota(field.shape, 2) // self.ny) % self.xs
        moved = pltpu.roll(field, LANES - self.ny, 2)
        return jnp.where(within == self.xs - 1, pltpu.roll(moved, ROWS - 1, 1), moved)

    def last_x(self, field):
        within = (iota(field.shape, 2) // self.ny) % self.xs
        moved = pltpu.roll(field, self.ny, 2)
        return jnp.where(within == 0, pltpu.roll(moved, 1, 1), moved)

    def next_y(self, field):
        return pltpu.roll(field, LANES - 1, 2)

    def last_y(self, field):
        return pltpu.roll(field, 1, 2)

    def spread(self, field, scaled, plane, count):
        mid = field[1:-1]
        near = (
            self.next_x(mid), self.last_x(mid), self.next_y(mid), self.last_y(mid),
            field[2:], field[:-2],
        )
        terms = [weight[pl.ds(plane, count)] * value for weight, value in zip(scaled, near)]
        return mid, ((terms[0] + terms[1]) + (terms[2] + terms[3])) + (terms[4] + terms[5])


def mean_of(fluid, near, factor):
    return ((factor * 2.0) * fluid * near) * inverse_of(jnp.maximum(fluid + near, TINY))


def set_level(level, low, high, fluid, pin, rhs, fields):
    scaled, start, diag = fields

    def body(plane, count):
        wide = fluid[pl.ds(plane - 1, count + 2)]
        mid = wide[1:-1]
        within, end_y, end_x = level.masks(mid.shape)
        to_x = jnp.where(end_x, 0.0, mean_of(mid, level.next_x(mid), level.factor))
        to_y = jnp.where(end_y, 0.0, mean_of(mid, level.next_y(mid), level.factor))
        to_z = mean_of(wide[:-1], wide[1:], level.factor)
        weights = (to_x, level.last_x(to_x), to_y, level.last_y(to_y), to_z[1:], to_z[:-1])
        total = (
            (weights[0] + weights[1])
            + (weights[2] + weights[3])
            + (weights[4] + weights[5])
            + pin[pl.ds(plane, count)]
        )
        gain = OMEGA * inverse_of(jnp.maximum(total, TINY))
        for target, weight in zip(scaled, weights):
            target[pl.ds(plane, count)] = gain * weight
        start[pl.ds(plane, count)] = gain * rhs[pl.ds(plane, count)]
        diag[pl.ds(plane, count)] = total

    loop(low, high, PIECE, body)


def swept(level, plane, count, fields, source, shift=0):
    scaled, start, _ = fields
    mid, total = level.spread(source[pl.ds(plane - 1, count + 2)], scaled, plane - shift, count)
    return (1.0 - OMEGA) * mid + (start[pl.ds(plane - shift, count)] + total)


def sweep(level, low, high, fields, source, target, shift=0):
    def body(plane, count):
        target[pl.ds(plane, count)] = swept(level, plane, count, fields, source, shift)

    loop(low, high, PIECE, body)


def pair_sum(field):
    half = field.reshape((field.shape[0] // 2, 2) + field.shape[1:])
    return half[:, 0] + half[:, 1]


def coarse_residual(level, low, high, fields, corr, target):
    scaled, start, diag = fields

    def body(plane, count):
        mid, total = level.spread(corr[pl.ds(plane - 1, count + 2)], scaled, plane, count)
        rest = (start[pl.ds(plane, count)] + total) - OMEGA * mid
        rest = rest * (diag[pl.ds(plane, count)] * (1.0 / OMEGA))
        target[pl.ds((plane - low) // 2, count // 2)] = pair_sum(rest)

    loop(low, high, PIECE, body)


def lanes_down(level):
    fine = iota((LANES, LANES), 0)
    coarse = iota((LANES, LANES), 1)
    ny, xs = PLANE[1] >> level, 4 >> level
    half = xs // 2
    same_x = ((fine // ny) % xs) // 2 == (coarse // (ny // 2)) % half
    same_y = (fine % ny) // 2 == coarse % (ny // 2)
    return where01((fine < ny * xs) & same_x & same_y)


def in_lanes(field, chosen, parts=3):
    flat = field.reshape(field.shape[0] * ROWS, LANES)
    return dot01(flat, chosen, parts).reshape(field.shape)


def path_of(group):
    nx, ny = SPLIT
    row, column = 0, 0
    for index in range(group + 1):
        columns = list(range(ny)) if column == 0 else list(range(ny))[::-1]
        if index % 2:
            path = [(row, at) for at in columns] + [(1 - row, at) for at in columns[::-1]]
        else:
            path = []
            for at in columns:
                path += [(row, at), (1 - row, at)]
                row = 1 - row
        row, column = path[-1]
    return [row * ny + column for row, column in path]


def lookup(table, index):
    found = table[0]
    for at, value in enumerate(table[1:], 1):
        found = jnp.where(index == at, value, found)
    return found


def slot_of(peer):
    return SPLIT[0] * SPLIT[1] - 1 - peer


def own_slot_of(rank):
    groups = range(lax.axis_size("gz"))
    return lookup([slot_of(path_of(group)[rank]) for group in groups], lax.axis_index("gz"))


def exchange(field):
    peers, groups = SPLIT[0] * SPLIT[1], lax.axis_size("gz")
    order = sorted(range(peers), key=slot_of)
    members = [[peer * groups + group for peer in order] for group in range(groups)]
    axes = ("gx", "gy", "gz")
    return lax.all_to_all(field, axes, 0, 0, axis_index_groups=members, tiled=True)


def slabs_of(groups):
    peers = SPLIT[0] * SPLIT[1]
    return [
        group * peers + path_of(group).index(peer) for peer in range(peers) for group in range(groups)
    ]


def own_slab():
    nx, ny = SPLIT
    groups = lax.axis_size("gz")
    device = (lax.axis_index("gx") * ny + lax.axis_index("gy")) * groups + lax.axis_index("gz")
    return lookup(slabs_of(groups), device)


def devices_of(groups):
    slabs = slabs_of(groups)
    return [slabs.index(slab) for slab in range(len(slabs))]


def prepare_kernel(share, res_ref, fluid_ref, pin_ref, out_ref):
    bx, by, depth = fluid_ref.shape
    cells = bx * by
    groups = bx // 4
    order = [x for low in range(4) for x in range(low, bx, 4)]
    fine = iota((cells, 4 * cells), 1)
    x, y = fine // (4 * by), (fine % (2 * by)) // 2
    chosen = where01((x % 4) * (groups * by) + (x // 4) * by + y == iota((cells, 4 * cells), 0))
    wide = lax.dot_general(
        chosen, res_ref[...], (((1,), (0,)), ((), ())), preferred_element_type=F32
    )
    rhs = dot10(where01(iota((depth, 2 * depth), 1) // 2 == iota((depth, 2 * depth), 0)), wide)

    def turned(field_ref):
        field = jnp.concatenate([field_ref[x : x + 1] for x in order], axis=0)
        return field.reshape(cells, depth).T

    fluid, pin = turned(fluid_ref), turned(pin_ref)
    for rank in range(depth // share):
        peer, begin = own_slot_of(rank), rank * share
        for index, field in enumerate((fluid, rhs, pin)):
            out_ref[peer, index * share : (index + 1) * share] = field[begin : begin + share]


def spread_kernel(groups, by, gathered, own, straight):
    for start in range(0, own.shape[0], ROWS):
        place(gathered, start, straight, start, groups, by)
    share = own.shape[0] // 3
    odd = own_slab() % 2 == 1
    for index in range(3):
        for plane in range(share):
            at = jnp.where(odd, share - 1 - plane, plane)
            own[index * share + plane] = straight[index * share + at]


def place(gathered, row, target, plane, groups, by):
    group = (iota((ROWS, LANES), 1) // by) % groups
    nx, ny = SPLIT
    for ix in range(nx):
        found = [gathered[slot_of(ix * ny + iy), pl.ds(row, ROWS), :] for iy in range(ny)]
        for part in range(groups):
            total = found[part]
            for iy in range(ny):
                if iy != part:
                    moved = pltpu.roll(found[iy], (by * (iy - part)) % LANES, 1)
                    total = jnp.where(group == iy, moved, total)
            target[pl.ds(plane, ROWS), ix * groups + part, :] = total


def near_kernel(
    depth,
    own, inner,
    saved1, saved2, fluid2, pin2, fluid3, pin3,
    fluid1, rhs1, pin1, other1, rhs2, sums,
):
    for index, target in enumerate((fluid1, rhs1, pin1)):
        target[0:depth] = own[index * depth : (index + 1) * depth]
        for plane in range(HALO):
            target[depth + plane] = inner[(index + 1) * depth - 1 - plane]
    fine, coarse = Level(0), Level(1)
    down1, down2 = lanes_down(0), lanes_down(1)
    fields1, corr1 = (saved1[0:6], saved1[6], saved1[7]), saved1[8]
    fields2 = (saved2[0:6], saved2[6], saved2[7])
    planes = depth + HALO
    set_level(fine, 1, planes - 1, fluid1, pin1, rhs1, fields1)
    sweep(fine, 2, planes - 2, fields1, fields1[1], other1)
    sweep(fine, 3, planes - 3, fields1, other1, corr1)
    coarse_residual(fine, 4, planes - 4, fields1, corr1, sums)
    count2 = planes // 2
    for source, target, share in ((fluid1, fluid2, 8.0), (pin1, pin2, 4.0)):
        target[NEAR : NEAR + count2] = in_lanes(pair_sum(source[...]), down1) * (1.0 / share)
    low2, high2 = NEAR + 2, NEAR + count2 - 2
    rhs2[low2:high2] = in_lanes(sums[0 : high2 - low2], down1)
    set_level(coarse, low2, high2, fluid2, pin2, rhs2, fields2)
    for source, target, scale in ((fluid2, fluid3, 0.125), (pin2, pin3, 0.25)):
        target[...] = in_lanes(pair_sum(source[NEAR : NEAR + depth // 2]), down2) * scale


def down_kernel(
    depth,
    own, outer, near2, near_fluid2, near_pin2, fluid3, pin3,
    saved1, saved2,
    packed,
    fluid1, rhs1, pin1, other1, fluid2, rhs2, pin2, other2, sums,
):
    planes = fluid1.shape[0]
    for index, target in enumerate((fluid1, rhs1, pin1)):
        for plane in range(HALO):
            target[plane] = outer[index * depth + HALO - 1 - plane]
        target[HALO:planes] = own[index * depth : index * depth + planes - HALO]

    fine, coarse = Level(0), Level(1)
    down1, down2 = lanes_down(0), lanes_down(1)
    fields1, corr1 = (saved1[0:6], saved1[6], saved1[7]), saved1[8]
    fields2, corr2 = (saved2[0:6], saved2[6], saved2[7]), saved2[8]
    set_level(fine, 1, planes - 1, fluid1, pin1, rhs1, fields1)
    sweep(fine, 2, planes - 2, fields1, fields1[1], other1)
    sweep(fine, 3, planes - 3, fields1, other1, corr1)
    count2 = depth // 2 + 2 * NEAR
    low2, done, high2 = 2, NEAR + 2, count2 - 2
    coarse_residual(fine, 2 * low2, 2 * done, fields1, corr1, sums)
    for source, ready, target, share in (
        (fluid1, near_fluid2, fluid2, 8.0), (pin1, near_pin2, pin2, 4.0)
    ):
        target[0:NEAR] = in_lanes(pair_sum(source[0:HALO]), down1) * (1.0 / share)
        target[NEAR : done + 1] = ready[NEAR : done + 1]
    rhs2[low2:done] = in_lanes(sums[0 : done - low2], down1)
    set_level(coarse, low2, done, fluid2, pin2, rhs2, fields2)
    for source, target in zip(near2, saved2[0:8]):
        target[done:high2] = source[done:high2]
    sweep(coarse, low2 + 1, high2 - 1, fields2, fields2[1], other2)
    sweep(coarse, low2 + 2, high2 - 2, fields2, other2, corr2)
    coarse_residual(coarse, NEAR, NEAR + depth // 2, fields2, corr2, sums)
    count3 = depth // 4
    rhs3 = in_lanes(sums[0:count3], down2)
    lane = iota((count3, LANES), 1) // ROWS
    first = jnp.zeros((count3, LANES), F32)
    second = jnp.zeros((count3, LANES), F32)
    for row in range(ROWS):
        first = jnp.where(lane == row, rhs3[:, row, :], first)
        first = jnp.where(lane == ROWS + row, fluid3[:, row, :], first)
        second = jnp.where(lane % ROWS == row, pin3[:, row, :], second)
    packed[0] = first[0:2]
    packed[1] = first[2:4]
    packed[2] = jnp.where(lane[0:2] < ROWS, second[0:2], second[2:4])
    lane = iota((1, LANES), 1) // (LANES // 4)
    for index, plane in enumerate((NEAR + depth // 2 - 5, NEAR + 4)):
        for half in range(2):
            row = jnp.zeros((1, LANES), F32)
            for quarter in range(4):
                at = half * 4 + quarter
                row = jnp.where(lane == quarter, corr2[plane, at : at + 1, :], row)
            packed[3 + index, half : half + 1, :] = row


def rolled(field, shift):
    count = field.shape[0]
    shift %= count
    if shift % ROWS:
        return pltpu.roll(field, shift, 0)
    return jnp.concatenate([field[count - shift :], field[: count - shift]], axis=0)


def columns(rhs, fluid, pin):
    depth = fluid.shape[0]
    z, lane = iota(fluid.shape, 0), iota(fluid.shape, 1)
    y, x = lane % ROWS, (lane // ROWS) % ROWS

    def next_x(field):
        return pltpu.roll(field, LANES - ROWS, 1)

    def next_y(field):
        return pltpu.roll(field, LANES - 1, 1)

    wz = jnp.where(z == depth - 1, 0.0, mean_of(fluid, rolled(fluid, -1), 4.0))
    wy = jnp.where(y == ROWS - 1, 0.0, mean_of(fluid, next_y(fluid), 4.0))
    wx = jnp.where(x == ROWS - 1, 0.0, mean_of(fluid, next_x(fluid), 4.0))
    across = (wx + pltpu.roll(wx, ROWS, 1)) + (wy + pltpu.roll(wy, 1, 1)) + pin
    share = 1.0 / jnp.sum(across, axis=0, keepdims=True)

    above, below, own = rolled(wz, 1), wz, across
    steps = []
    stride = 1
    while stride < depth:
        inverse = inverse_of(above + below + own)
        up = above * rolled(inverse, stride)
        down = below * rolled(inverse, -stride)
        own = own + up * rolled(own, stride) + down * rolled(own, -stride)
        above = up * rolled(above, stride)
        below = down * rolled(below, -stride)
        steps.append((stride, up, down))
        stride *= 2
    inverse = inverse_of(above + below + own)

    def solve(right):
        mean = jnp.sum(right, axis=0, keepdims=True) * share
        for stride, up, down in steps:
            right = right + up * rolled(right, stride) + down * rolled(right, -stride)
        return right * inverse + mean

    corr = solve(rhs)
    flow_x = wx * (next_x(corr) - corr)
    flow_y = wy * (next_y(corr) - corr)
    flow_z = wz * (rolled(corr, -1) - corr)
    rest = (
        (rhs - pin * corr)
        + (flow_x - pltpu.roll(flow_x, ROWS, 1))
        + (flow_y - pltpu.roll(flow_y, 1, 1))
        + (flow_z - rolled(flow_z, 1))
    )
    return corr + solve(rest)


def up_kernel(
    groups, by, depth,
    packed, near1, far1, far2,
    out_ref,
    one1, two1, one2, two2, lifted, first, second, solved, final,
):
    count3 = depth // 4
    shares = packed.shape[0]
    peers = SPLIT[0] * SPLIT[1]
    devices = devices_of(shares // peers)
    for slab, index in enumerate(devices):
        row = slab * count3
        low, high, both = packed[index, 0], packed[index, 1], packed[index, 2]
        rest = pltpu.roll(both, LANES // 2, 1)
        if slab % 2:
            for at, (level3, pin) in enumerate(((high, rest), (low, both))):
                begin = row + 2 * at
                first[begin : begin + 1] = level3[1:2]
                first[begin + 1 : begin + 2] = level3[0:1]
                second[begin : begin + 1] = pin[1:2]
                second[begin + 1 : begin + 2] = pin[0:1]
        else:
            first[row : row + 2] = low
            first[row + 2 : row + 4] = high
            second[row : row + 2] = both
            second[row + 2 : row + 4] = rest
    half = iota((shares * count3, LANES), 1) < LANES // 2

    def low_half(field):
        return jnp.where(half, field, pltpu.roll(field, LANES // 2, 1))

    def high_half(field):
        return jnp.where(half, pltpu.roll(field, LANES // 2, 1), field)

    solved[NEAR : NEAR + shares * count3] = columns(
        low_half(first[...]), high_half(first[...]), low_half(second[...])
    )
    solved[0:NEAR] = jnp.zeros((NEAR, LANES), F32)
    solved[NEAR + shares * count3 :] = jnp.zeros((2 * NEAR, LANES), F32)

    nx, ny = SPLIT
    part = own_slab()
    count = count3 + 2 * NEAR
    tall = solved[pl.ds(part * count3, count + count3), :]
    fine, coarse = Level(0), Level(1)
    cell = iota((LANES, LANES), 0)
    lane = iota((LANES, LANES), 1)
    spread = where01((cell < ROWS) & (cell == (lane % coarse.ny) // 2))
    rows = tall.shape[0]
    turned = [tall] + [pltpu.roll(tall, LANES - ROWS * row, 1) for row in range(1, ROWS)]
    wide = dot01(jnp.concatenate(turned, axis=0), spread, 2)
    for row in range(ROWS):
        lifted[0:rows, row, :] = wide[row * rows : (row + 1) * rows]

    odd = part % 2 == 1

    def lifted_to(plane):
        parent = plane // 2 + NEAR // 2
        return lifted[jnp.where(odd, count - 1 - parent, parent)]

    near_fields, near_corr1 = (near1[0:6], near1[6], near1[7]), near1[8]
    far_fields, far_corr1 = (far1[0:6], far1[6], far1[7]), far1[8]
    fields2, corr2 = (far2[0:6], far2[6], far2[7]), far2[8]
    low, high = NEAR - 4, NEAR + depth // 2 + 4
    reach = depth // 2 + NEAR
    quarter = iota((ROWS, LANES), 1) // (LANES // 4)
    row = iota((ROWS, LANES), 0)

    def unpacked(index, which):
        pair = packed[lookup(devices, jnp.clip(index, 0, shares - 1)), which]
        total = None
        for shift in range(4):
            moved = pltpu.roll(pair, shift * (LANES // 4), 1)
            wide = jnp.where(row < 4, moved[0:1, :], moved[1:2, :])
            kept = jnp.where((quarter - shift) % 4 == row % 4, wide, 0.0)
            total = kept if total is None else total + kept
        return total

    one2[low - 1] = unpacked(jnp.where(odd, part + 1, part - 1), 4) + lifted_to(low - 1)
    for plane in range(low, high):
        one2[plane] = corr2[plane] + lifted_to(plane)
    one2[high] = unpacked(jnp.where(odd, part - 1, part + 1), 3) + lifted_to(high)
    sweep(coarse, NEAR - 4, reach + 4, fields2, one2, two2)
    sweep(coarse, NEAR - 3, reach + 3, fields2, two2, one2)
    sweep(coarse, NEAR - 2, reach + 2, fields2, one2, two2)

    fine_lane, coarse_lane = iota((LANES, LANES), 1), iota((LANES, LANES), 0)
    x_of = (fine_lane // fine.ny) // 2
    y_of = (fine_lane % fine.ny) // 2
    up = where01(coarse_lane == x_of * coarse.ny + y_of)
    lifted[0 : depth // 2 + 4] = in_lanes(two2[NEAR - 2 : reach + 2], up, 2)
    parents = lifted[0 : depth // 2 + 4]
    twice = jnp.broadcast_to(parents[:, None], (parents.shape[0], 2, ROWS, LANES))
    low, high = HALO - 4, HALO + depth + 4
    turn = HALO + 3
    for plane in range(low, high):
        corr = far_corr1[plane] if plane < turn else near_corr1[plane - HALO]
        one1[plane] = corr + lifted[(plane - low) // 2]
    reach = depth + HALO
    for more, source, target in ((2, one1, two1), (1, two1, one1)):
        sweep(fine, HALO - more, turn, far_fields, source, target)
        sweep(fine, turn, reach + more, near_fields, source, target, HALO)

    def last(fields, shift):
        def body(plane, count):
            value = swept(fine, plane, count, fields, one1, shift)
            value = value * fields[2][pl.ds(plane - shift, count)]
            for index in range(count):
                at = plane - HALO + index
                final[jnp.where(odd, depth - 1 - at, at)] = value[index]

        return body

    loop(HALO, turn, PIECE, last(far_fields, 0))
    loop(turn, reach, PIECE, last(near_fields, HALO))

    group = (iota((depth, LANES), 1) // by) % groups
    for ix in range(nx):
        scaled = [final[:, ix * groups + part, :] for part in range(groups)]
        for iy in range(ny):
            total = scaled[iy]
            for part in range(groups):
                if part != iy:
                    moved = pltpu.roll(scaled[part], (by * (part - iy)) % LANES, 1)
                    total = jnp.where(group == part, moved, total)
            out_ref[slot_of(ix * ny + iy)] = total


def finish_kernel(blocks, out_ref):
    bx, by, depth = out_ref.shape
    peers = blocks.shape[0]
    ordered = jnp.concatenate([blocks[own_slot_of(rank)] for rank in range(peers)], axis=0)
    turned = ordered.T
    for x in range(bx):
        row = ((x % 4) * (bx // 4) + x // 4) * by
        out_ref[x] = turned[row : row + by]


def whole_planes(residual_q2, viscosity, pinned):
    bx, by, depth = viscosity.shape
    groups = bx // 4
    peers = SPLIT[0] * SPLIT[1]
    share = depth // peers
    planes = share + 2 * HALO
    count2 = share // 2 + 2 * NEAR
    limit = pltpu.CompilerParams(vmem_limit_bytes=32 * 2**20)

    def flat(rows):
        return jax.ShapeDtypeStruct((rows, LANES), F32)

    def blocks(count, rows):
        return jax.ShapeDtypeStruct((count, rows, LANES), F32)

    def room(count):
        return pltpu.VMEM((count, ROWS, LANES), F32)

    fluid = 1.0 / viscosity
    pin = 4.0 * pinned.astype(F32) * fluid
    parcels = pl.pallas_call(
        functools.partial(prepare_kernel, share),
        out_shape=blocks(peers, 3 * share),
        compiler_params=limit,
        name="prepare",
    )(residual_q2.reshape(4 * bx * by, 2 * depth), fluid, pin)
    own = pl.pallas_call(
        functools.partial(spread_kernel, groups, by),
        out_shape=blocks(3 * share, ROWS),
        scratch_shapes=[room(3 * share)],
        compiler_params=limit,
        name="spread",
    )(exchange(parcels))
    length = lax.axis_size("gz")
    parts = length * peers

    device = devices_of(length)

    def swap(field, first):
        pairs = [(device[i], device[i + 1]) for i in range(first, parts - 1, 2)]
        return lax.ppermute(field, ("gx", "gy", "gz"), pairs + [pair[::-1] for pair in pairs])

    outer, inner = swap(own, 1), swap(own, 0)
    count3 = share // 4
    near1, near2, far1, far2 = (
        (blocks(count, ROWS),) * fields
        for count, fields in ((share + HALO, 9), (count2, 8), (HALO + 8, 9), (count2, 9))
    )
    near1, near2, fluid2, pin2, fluid3, pin3 = pl.pallas_call(
        functools.partial(near_kernel, share),
        out_shape=(near1, near2) + (blocks(count2, ROWS),) * 2 + (blocks(count3, ROWS),) * 2,
        scratch_shapes=[room(share + HALO)] * 4 + [room(count2)] * 2,
        compiler_params=limit,
        name="near",
    )(own, inner)
    far1, far2, parcel = pl.pallas_call(
        functools.partial(down_kernel, share),
        out_shape=(far1, far2, blocks(5, 2)),
        scratch_shapes=[room(HALO + 8)] * 4 + [room(count2)] * 5,
        compiler_params=limit,
        name="down",
    )(own, outer, near2, fluid2, pin2, fluid3, pin3)
    copies = jnp.broadcast_to(parcel, (parts,) + parcel.shape)
    packed = lax.all_to_all(copies, ("gx", "gy", "gz"), 0, 0, tiled=True)
    depth3 = parts * count3
    mine = pl.pallas_call(
        functools.partial(up_kernel, groups, by, share),
        out_shape=blocks(peers, share),
        scratch_shapes=[room(planes), room(planes), room(count2), room(count2), room(count2)]
        + [pltpu.VMEM((rows, LANES), F32) for rows in (depth3, depth3, depth3 + 3 * NEAR)]
        + [room(share)],
        compiler_params=limit,
        name="up",
    )(packed, near1, far1, far2)
    return pl.pallas_call(
        finish_kernel,
        out_shape=jax.ShapeDtypeStruct((bx, by, depth), F32),
        compiler_params=limit,
        name="finish",
    )(exchange(mine))


def one_tile_planes(mesh, viscosity):
    split = (mesh.shape["gx"], mesh.shape["gy"])
    depth = viscosity.shape[2]
    fits = viscosity.shape[:2] == PLANE and split == SPLIT
    return fits and depth == 4 * LANES and depth // mesh.shape["gz"] == LANES


def solution(mesh):
    placed = (P("gx", "gy", "gz"), P("gx", "gy", "gz"), P("gx", "gy", "gz"))

    def cycle(residual_q2, viscosity, pinned):
        chosen = whole_planes if one_tile_planes(mesh, viscosity) else per_device
        return jax.shard_map(
            chosen, mesh=mesh, in_specs=placed, out_specs=P("gx", "gy", "gz"), check_vma=False
        )(residual_q2, viscosity, pinned)

    return cycle
```

```python
import functools

import jax
import jax.numpy as jnp
from jax import lax
from jax.experimental import pallas as pl
from jax.experimental.pallas import tpu as pltpu
from jax.sharding import PartitionSpec as P

NU = 3


OMEGA = 0.6


def with_halo(block, sides, width):
    for axis, dim in sides:
        count = lax.axis_size(axis)
        forward = [(i, i + 1) for i in range(count - 1)]
        backward = [(target, source) for source, target in forward]
        low = lax.ppermute(
            lax.slice_in_dim(block, block.shape[dim] - width, None, axis=dim), axis, forward
        )
        high = lax.ppermute(lax.slice_in_dim(block, 0, width, axis=dim), axis, backward)
        block = jnp.concatenate([low, block, high], axis=dim)
    return block


def coarsen(x):
    a, b, c = x.shape
    return x.reshape(a // 2, 2, b // 2, 2, c // 2, 2).sum(axis=(1, 3, 5))


def refine(x):
    return jnp.repeat(jnp.repeat(jnp.repeat(x, 2, 0), 2, 1), 2, 2)


def extended(field):
    return with_halo(field, (("gx", 0), ("gy", 1), ("gz", 2)), 1)


def shifted(padded):
    return [
        padded[2:, 1:-1, 1:-1],
        padded[:-2, 1:-1, 1:-1],
        padded[1:-1, 2:, 1:-1],
        padded[1:-1, :-2, 1:-1],
        padded[1:-1, 1:-1, 2:],
        padded[1:-1, 1:-1, :-2],
    ]


def neighbours(field):
    return shifted(extended(field))


def harmonic(fluid, near, factor):
    total = fluid + near
    return jnp.where(total > 0, factor * 2.0 * fluid * near / jnp.where(total > 0, total, 1.0), 0.0)


def couplings(fluid, factor):
    return [harmonic(fluid, near, factor) for near in neighbours(fluid)]


def apply_op(field, weights, diag):
    total = diag * field
    for weight, near in zip(weights, neighbours(field)):
        total = total - weight * near
    return total


def presmooth(rhs, weights, diag):
    corr = OMEGA * rhs / diag
    for sweep in range(NU - 1):
        corr = corr + OMEGA * (rhs - apply_op(corr, weights, diag)) / diag
    return corr


def postsmooth(corr, rhs, weights, diag):
    for sweep in range(NU):
        corr = corr + OMEGA * (rhs - apply_op(corr, weights, diag)) / diag
    return corr


def tridiag(coeffs, rhs):
    solved = lax.linalg.tridiagonal_solve(coeffs[0], coeffs[1], coeffs[2], rhs[..., None])[..., 0]
    last = rhs.ndim - 1
    shift_col = jnp.sum(rhs, axis=last, keepdims=True) / jnp.sum(
        coeffs[3], axis=last, keepdims=True
    )
    return solved + shift_col


def prepare_columns(weights, diag):
    lower = -weights[5]
    upper = -weights[4]
    across = diag + lower + upper
    return (
        lax.all_gather(lower, "gz", axis=2, tiled=True),
        lax.all_gather(diag, "gz", axis=2, tiled=True),
        lax.all_gather(upper, "gz", axis=2, tiled=True),
        lax.all_gather(across, "gz", axis=2, tiled=True),
    )


def column_solve(rhs, coeffs):
    depth = rhs.shape[2]
    whole = lax.all_gather(rhs, "gz", axis=2, tiled=True)
    solved = tridiag(coeffs, whole)
    return lax.dynamic_slice_in_dim(solved, lax.axis_index("gz") * depth, depth, 2)


def per_device(residual_q2, viscosity, pinned):
    fluid1 = 1.0 / viscosity
    pin1 = 4.0 * pinned.astype(jnp.float32) * fluid1
    rhs1 = coarsen(residual_q2.astype(jnp.float32))
    fluid2 = coarsen(fluid1) / 8.0
    pin2 = coarsen(pin1) / 4.0
    fluid3 = coarsen(fluid2) / 8.0
    pin3 = coarsen(pin2) / 4.0
    weights1 = couplings(fluid1, 1.0)
    weights2 = couplings(fluid2, 2.0)
    weights3 = couplings(fluid3, 4.0)
    diag1 = sum(weights1) + pin1
    diag2 = sum(weights2) + pin2
    diag3 = sum(weights3) + pin3
    coeffs = prepare_columns(weights3, diag3)
    corr1 = presmooth(rhs1, weights1, diag1)
    rhs2 = coarsen(rhs1 - apply_op(corr1, weights1, diag1))
    corr2 = presmooth(rhs2, weights2, diag2)
    rhs3 = coarsen(rhs2 - apply_op(corr2, weights2, diag2))
    corr3 = column_solve(rhs3, coeffs)
    corr3 = corr3 + column_solve(rhs3 - apply_op(corr3, weights3, diag3), coeffs)
    corr2 = postsmooth(corr2 + refine(corr3), rhs2, weights2, diag2)
    corr1 = postsmooth(corr1 + refine(corr2), rhs1, weights1, diag1)
    return diag1 * corr1


PLANE = (32, 32)
SPLIT = (2, 4)
ROWS = 8
LANES = 128
HALO = 16
NEAR = 8
PIECE = 8
TINY = 1e-30
F32 = jnp.float32


def iota(shape, dim):
    return lax.broadcasted_iota(jnp.int32, shape, dim)


def dot01(field, chosen, parts=3):
    total = None
    rest = field
    for part in range(parts):
        piece = rest.astype(jnp.bfloat16)
        term = jnp.dot(piece, chosen, preferred_element_type=F32)
        total = term if total is None else total + term
        if part < parts - 1:
            rest = rest - piece.astype(F32)
    return total


def dot10(chosen, field):
    total = None
    rest = field
    for part in range(3):
        piece = rest.astype(jnp.bfloat16)
        term = lax.dot_general(
            chosen, piece, (((1,), (1,)), ((), ())), preferred_element_type=F32
        )
        total = term if total is None else total + term
        if part < 2:
            rest = rest - piece.astype(F32)
    return total


def where01(condition):
    return jnp.where(condition, 1.0, 0.0).astype(jnp.bfloat16)


def loop(low, high, size, body):
    for plane in range(low, high, size):
        body(plane, min(size, high - plane))


def inverse_of(field):
    first = pl.reciprocal(field, approx=True)
    return first * (2.0 - field * first)


class Level:
    def __init__(self, level):
        self.ny = PLANE[1] >> level
        self.xs = 4 >> level
        self.factor = float(2**level)

    def masks(self, shape):
        lane = iota(shape, 2)
        row = iota(shape, 1)
        within = (lane // self.ny) % self.xs
        y = lane % self.ny
        last_x = (row == ROWS - 1) & (within == self.xs - 1)
        return within, y == self.ny - 1, last_x

    def next_x(self, field):
        within = (iota(field.shape, 2) // self.ny) % self.xs
        moved = pltpu.roll(field, LANES - self.ny, 2)
        return jnp.where(within == self.xs - 1, pltpu.roll(moved, ROWS - 1, 1), moved)

    def last_x(self, field):
        within = (iota(field.shape, 2) // self.ny) % self.xs
        moved = pltpu.roll(field, self.ny, 2)
        return jnp.where(within == 0, pltpu.roll(moved, 1, 1), moved)

    def next_y(self, field):
        return pltpu.roll(field, LANES - 1, 2)

    def last_y(self, field):
        return pltpu.roll(field, 1, 2)

    def spread(self, field, scaled, plane, count):
        mid = field[1:-1]
        near = (
            self.next_x(mid), self.last_x(mid), self.next_y(mid), self.last_y(mid),
            field[2:], field[:-2],
        )
        terms = [weight[pl.ds(plane, count)] * value for weight, value in zip(scaled, near)]
        return mid, ((terms[0] + terms[1]) + (terms[2] + terms[3])) + (terms[4] + terms[5])


def mean_of(fluid, near, factor):
    return ((factor * 2.0) * fluid * near) * inverse_of(jnp.maximum(fluid + near, TINY))


def set_level(level, low, high, fluid, pin, rhs, fields):
    scaled, start, diag = fields

    def body(plane, count):
        wide = fluid[pl.ds(plane - 1, count + 2)]
        mid = wide[1:-1]
        within, end_y, end_x = level.masks(mid.shape)
        to_x = jnp.where(end_x, 0.0, mean_of(mid, level.next_x(mid), level.factor))
        to_y = jnp.where(end_y, 0.0, mean_of(mid, level.next_y(mid), level.factor))
        to_z = mean_of(wide[:-1], wide[1:], level.factor)
        weights = (to_x, level.last_x(to_x), to_y, level.last_y(to_y), to_z[1:], to_z[:-1])
        total = (
            (weights[0] + weights[1])
            + (weights[2] + weights[3])
            + (weights[4] + weights[5])
            + pin[pl.ds(plane, count)]
        )
        gain = OMEGA * inverse_of(jnp.maximum(total, TINY))
        for target, weight in zip(scaled, weights):
            target[pl.ds(plane, count)] = gain * weight
        start[pl.ds(plane, count)] = gain * rhs[pl.ds(plane, count)]
        diag[pl.ds(plane, count)] = total

    loop(low, high, PIECE, body)


def swept(level, plane, count, fields, source, shift=0):
    scaled, start, _ = fields
    mid, total = level.spread(source[pl.ds(plane - 1, count + 2)], scaled, plane - shift, count)
    return (1.0 - OMEGA) * mid + (start[pl.ds(plane - shift, count)] + total)


def sweep(level, low, high, fields, source, target, shift=0):
    def body(plane, count):
        target[pl.ds(plane, count)] = swept(level, plane, count, fields, source, shift)

    loop(low, high, PIECE, body)


def pair_sum(field):
    half = field.reshape((field.shape[0] // 2, 2) + field.shape[1:])
    return half[:, 0] + half[:, 1]


def coarse_residual(level, low, high, fields, corr, target):
    scaled, start, diag = fields

    def body(plane, count):
        mid, total = level.spread(corr[pl.ds(plane - 1, count + 2)], scaled, plane, count)
        rest = (start[pl.ds(plane, count)] + total) - OMEGA * mid
        rest = rest * (diag[pl.ds(plane, count)] * (1.0 / OMEGA))
        target[pl.ds((plane - low) // 2, count // 2)] = pair_sum(rest)

    loop(low, high, PIECE, body)


def lanes_down(level):
    fine = iota((LANES, LANES), 0)
    coarse = iota((LANES, LANES), 1)
    ny, xs = PLANE[1] >> level, 4 >> level
    half = xs // 2
    same_x = ((fine // ny) % xs) // 2 == (coarse // (ny // 2)) % half
    same_y = (fine % ny) // 2 == coarse % (ny // 2)
    return where01((fine < ny * xs) & same_x & same_y)


def in_lanes(field, chosen, parts=3):
    flat = field.reshape(field.shape[0] * ROWS, LANES)
    return dot01(flat, chosen, parts).reshape(field.shape)


def path_of(group):
    nx, ny = SPLIT
    row, column = 0, 0
    for index in range(group + 1):
        columns = list(range(ny)) if column == 0 else list(range(ny))[::-1]
        if index % 2:
            path = [(row, at) for at in columns] + [(1 - row, at) for at in columns[::-1]]
        else:
            path = []
            for at in columns:
                path += [(row, at), (1 - row, at)]
                row = 1 - row
        row, column = path[-1]
    return [row * ny + column for row, column in path]


def lookup(table, index):
    found = table[0]
    for at, value in enumerate(table[1:], 1):
        found = jnp.where(index == at, value, found)
    return found


def slot_of(peer):
    return SPLIT[0] * SPLIT[1] - 1 - peer


def own_slot_of(rank):
    groups = range(lax.axis_size("gz"))
    return lookup([slot_of(path_of(group)[rank]) for group in groups], lax.axis_index("gz"))


def exchange(field):
    peers, groups = SPLIT[0] * SPLIT[1], lax.axis_size("gz")
    order = sorted(range(peers), key=slot_of)
    members = [[peer * groups + group for peer in order] for group in range(groups)]
    axes = ("gx", "gy", "gz")
    return lax.all_to_all(field, axes, 0, 0, axis_index_groups=members, tiled=True)


def slabs_of(groups):
    peers = SPLIT[0] * SPLIT[1]
    return [
        group * peers + path_of(group).index(peer) for peer in range(peers) for group in range(groups)
    ]


def own_slab():
    nx, ny = SPLIT
    groups = lax.axis_size("gz")
    device = (lax.axis_index("gx") * ny + lax.axis_index("gy")) * groups + lax.axis_index("gz")
    return lookup(slabs_of(groups), device)


def slots_of(groups):
    peers = SPLIT[0] * SPLIT[1]
    return [
        (groups - 1 - group) * peers + slot_of(peer)
        for group in range(groups)
        for peer in path_of(group)
    ]


def exchange_all(field):
    groups = lax.axis_size("gz")
    members = [device for _, device in sorted(zip(slots_of(groups), devices_of(groups)))]
    axes = ("gx", "gy", "gz")
    return lax.all_to_all(field, axes, 0, 0, axis_index_groups=[members], tiled=True)


def devices_of(groups):
    slabs = slabs_of(groups)
    return [slabs.index(slab) for slab in range(len(slabs))]


def prepare_kernel(share, res_ref, fluid_ref, pin_ref, out_ref):
    bx, by, depth = fluid_ref.shape
    cells = bx * by
    groups = bx // 4
    order = [x for low in range(4) for x in range(low, bx, 4)]
    fine = iota((cells, 4 * cells), 1)
    x, y = fine // (4 * by), (fine % (2 * by)) // 2
    chosen = where01((x % 4) * (groups * by) + (x // 4) * by + y == iota((cells, 4 * cells), 0))
    wide = lax.dot_general(
        chosen, res_ref[...], (((1,), (0,)), ((), ())), preferred_element_type=F32
    )
    rhs = dot10(where01(iota((depth, 2 * depth), 1) // 2 == iota((depth, 2 * depth), 0)), wide)

    def turned(field_ref):
        field = jnp.concatenate([field_ref[x : x + 1] for x in order], axis=0)
        return field.reshape(cells, depth).T

    fluid, pin = turned(fluid_ref), turned(pin_ref)
    for rank in range(depth // share):
        peer, begin = own_slot_of(rank), rank * share
        for index, field in enumerate((fluid, rhs, pin)):
            out_ref[peer, index * share : (index + 1) * share] = field[begin : begin + share]


def spread_kernel(groups, by, gathered, own, straight):
    for start in range(0, own.shape[0], ROWS):
        place(gathered, start, straight, start, groups, by)
    share = own.shape[0] // 3
    odd = own_slab() % 2 == 1
    for index in range(3):
        for plane in range(share):
            at = jnp.where(odd, share - 1 - plane, plane)
            own[index * share + plane] = straight[index * share + at]


def place(gathered, row, target, plane, groups, by):
    group = (iota((ROWS, LANES), 1) // by) % groups
    nx, ny = SPLIT
    for ix in range(nx):
        found = [gathered[slot_of(ix * ny + iy), pl.ds(row, ROWS), :] for iy in range(ny)]
        for part in range(groups):
            total = found[part]
            for iy in range(ny):
                if iy != part:
                    moved = pltpu.roll(found[iy], (by * (iy - part)) % LANES, 1)
                    total = jnp.where(group == iy, moved, total)
            target[pl.ds(plane, ROWS), ix * groups + part, :] = total


def near_kernel(
    depth,
    own, inner,
    saved1, saved2, fluid2, pin2, fluid3, pin3,
    fluid1, rhs1, pin1, other1, rhs2, sums,
):
    for index, target in enumerate((fluid1, rhs1, pin1)):
        target[0:depth] = own[index * depth : (index + 1) * depth]
        for plane in range(HALO):
            target[depth + plane] = inner[(index + 1) * depth - 1 - plane]
    fine, coarse = Level(0), Level(1)
    down1, down2 = lanes_down(0), lanes_down(1)
    fields1, corr1 = (saved1[0:6], saved1[6], saved1[7]), saved1[8]
    fields2 = (saved2[0:6], saved2[6], saved2[7])
    planes = depth + HALO
    set_level(fine, 1, planes - 1, fluid1, pin1, rhs1, fields1)
    sweep(fine, 2, planes - 2, fields1, fields1[1], other1)
    sweep(fine, 3, planes - 3, fields1, other1, corr1)
    coarse_residual(fine, 4, planes - 4, fields1, corr1, sums)
    count2 = planes // 2
    for source, target, share in ((fluid1, fluid2, 8.0), (pin1, pin2, 4.0)):
        target[NEAR : NEAR + count2] = in_lanes(pair_sum(source[...]), down1) * (1.0 / share)
    low2, high2 = NEAR + 2, NEAR + count2 - 2
    rhs2[low2:high2] = in_lanes(sums[0 : high2 - low2], down1)
    set_level(coarse, low2, high2, fluid2, pin2, rhs2, fields2)
    for source, target, scale in ((fluid2, fluid3, 0.125), (pin2, pin3, 0.25)):
        target[...] = in_lanes(pair_sum(source[NEAR : NEAR + depth // 2]), down2) * scale


def down_kernel(
    depth,
    own, outer, near2, near_fluid2, near_pin2, fluid3, pin3,
    saved1, saved2,
    packed,
    fluid1, rhs1, pin1, other1, fluid2, rhs2, pin2, other2, sums,
):
    planes = fluid1.shape[0]
    for index, target in enumerate((fluid1, rhs1, pin1)):
        for plane in range(HALO):
            target[plane] = outer[index * depth + HALO - 1 - plane]
        target[HALO:planes] = own[index * depth : index * depth + planes - HALO]

    fine, coarse = Level(0), Level(1)
    down1, down2 = lanes_down(0), lanes_down(1)
    fields1, corr1 = (saved1[0:6], saved1[6], saved1[7]), saved1[8]
    fields2, corr2 = (saved2[0:6], saved2[6], saved2[7]), saved2[8]
    set_level(fine, 1, planes - 1, fluid1, pin1, rhs1, fields1)
    sweep(fine, 2, planes - 2, fields1, fields1[1], other1)
    sweep(fine, 3, planes - 3, fields1, other1, corr1)
    count2 = depth // 2 + 2 * NEAR
    low2, done, high2 = 2, NEAR + 2, count2 - 2
    coarse_residual(fine, 2 * low2, 2 * done, fields1, corr1, sums)
    for source, ready, target, share in (
        (fluid1, near_fluid2, fluid2, 8.0), (pin1, near_pin2, pin2, 4.0)
    ):
        target[0:NEAR] = in_lanes(pair_sum(source[0:HALO]), down1) * (1.0 / share)
        target[NEAR : done + 1] = ready[NEAR : done + 1]
    rhs2[low2:done] = in_lanes(sums[0 : done - low2], down1)
    set_level(coarse, low2, done, fluid2, pin2, rhs2, fields2)
    for source, target in zip(near2, saved2[0:8]):
        target[done:high2] = source[done:high2]
    sweep(coarse, low2 + 1, high2 - 1, fields2, fields2[1], other2)
    sweep(coarse, low2 + 2, high2 - 2, fields2, other2, corr2)
    coarse_residual(coarse, NEAR, NEAR + depth // 2, fields2, corr2, sums)
    count3 = depth // 4
    rhs3 = in_lanes(sums[0:count3], down2)
    lane = iota((count3, LANES), 1) // ROWS
    first = jnp.zeros((count3, LANES), F32)
    second = jnp.zeros((count3, LANES), F32)
    for row in range(ROWS):
        first = jnp.where(lane == row, rhs3[:, row, :], first)
        first = jnp.where(lane == ROWS + row, fluid3[:, row, :], first)
        second = jnp.where(lane % ROWS == row, pin3[:, row, :], second)
    packed[0] = first[0:2]
    packed[1] = first[2:4]
    packed[2] = jnp.where(lane[0:2] < ROWS, second[0:2], second[2:4])
    lane = iota((1, LANES), 1) // (LANES // 4)
    for index, plane in enumerate((NEAR + depth // 2 - 5, NEAR + 4)):
        for half in range(2):
            row = jnp.zeros((1, LANES), F32)
            for quarter in range(4):
                at = half * 4 + quarter
                row = jnp.where(lane == quarter, corr2[plane, at : at + 1, :], row)
            packed[3 + index, half : half + 1, :] = row


def rolled(field, shift):
    count = field.shape[0]
    shift %= count
    if shift % ROWS:
        return pltpu.roll(field, shift, 0)
    return jnp.concatenate([field[count - shift :], field[: count - shift]], axis=0)


def columns(rhs, fluid, pin):
    depth = fluid.shape[0]
    z, lane = iota(fluid.shape, 0), iota(fluid.shape, 1)
    y, x = lane % ROWS, (lane // ROWS) % ROWS

    def next_x(field):
        return pltpu.roll(field, LANES - ROWS, 1)

    def next_y(field):
        return pltpu.roll(field, LANES - 1, 1)

    wz = jnp.where(z == depth - 1, 0.0, mean_of(fluid, rolled(fluid, -1), 4.0))
    wy = jnp.where(y == ROWS - 1, 0.0, mean_of(fluid, next_y(fluid), 4.0))
    wx = jnp.where(x == ROWS - 1, 0.0, mean_of(fluid, next_x(fluid), 4.0))
    across = (wx + pltpu.roll(wx, ROWS, 1)) + (wy + pltpu.roll(wy, 1, 1)) + pin
    share = 1.0 / jnp.sum(across, axis=0, keepdims=True)

    above, below, own = rolled(wz, 1), wz, across
    steps = []
    stride = 1
    while stride < depth:
        inverse = inverse_of(above + below + own)
        up = above * rolled(inverse, stride)
        down = below * rolled(inverse, -stride)
        own = own + up * rolled(own, stride) + down * rolled(own, -stride)
        above = up * rolled(above, stride)
        below = down * rolled(below, -stride)
        steps.append((stride, up, down))
        stride *= 2
    inverse = inverse_of(above + below + own)

    def solve(right):
        mean = jnp.sum(right, axis=0, keepdims=True) * share
        for stride, up, down in steps:
            right = right + up * rolled(right, stride) + down * rolled(right, -stride)
        return right * inverse + mean

    corr = solve(rhs)
    flow_x = wx * (next_x(corr) - corr)
    flow_y = wy * (next_y(corr) - corr)
    flow_z = wz * (rolled(corr, -1) - corr)
    rest = (
        (rhs - pin * corr)
        + (flow_x - pltpu.roll(flow_x, ROWS, 1))
        + (flow_y - pltpu.roll(flow_y, 1, 1))
        + (flow_z - rolled(flow_z, 1))
    )
    return corr + solve(rest)


def up_kernel(
    groups, by, depth,
    packed, near1, far1, far2,
    out_ref,
    one1, two1, one2, two2, lifted, first, second, solved, final,
):
    count3 = depth // 4
    shares = packed.shape[0]
    peers = SPLIT[0] * SPLIT[1]
    slots = slots_of(shares // peers)
    for slab, index in enumerate(slots):
        row = slab * count3
        low, high, both = packed[index, 0], packed[index, 1], packed[index, 2]
        rest = pltpu.roll(both, LANES // 2, 1)
        if slab % 2:
            for at, (level3, pin) in enumerate(((high, rest), (low, both))):
                begin = row + 2 * at
                first[begin : begin + 1] = level3[1:2]
                first[begin + 1 : begin + 2] = level3[0:1]
                second[begin : begin + 1] = pin[1:2]
                second[begin + 1 : begin + 2] = pin[0:1]
        else:
            first[row : row + 2] = low
            first[row + 2 : row + 4] = high
            second[row : row + 2] = both
            second[row + 2 : row + 4] = rest
    half = iota((shares * count3, LANES), 1) < LANES // 2

    def low_half(field):
        return jnp.where(half, field, pltpu.roll(field, LANES // 2, 1))

    def high_half(field):
        return jnp.where(half, pltpu.roll(field, LANES // 2, 1), field)

    solved[NEAR : NEAR + shares * count3] = columns(
        low_half(first[...]), high_half(first[...]), low_half(second[...])
    )
    solved[0:NEAR] = jnp.zeros((NEAR, LANES), F32)
    solved[NEAR + shares * count3 :] = jnp.zeros((2 * NEAR, LANES), F32)

    nx, ny = SPLIT
    part = own_slab()
    count = count3 + 2 * NEAR
    tall = solved[pl.ds(part * count3, count + count3), :]
    fine, coarse = Level(0), Level(1)
    cell = iota((LANES, LANES), 0)
    lane = iota((LANES, LANES), 1)
    spread = where01((cell < ROWS) & (cell == (lane % coarse.ny) // 2))
    rows = tall.shape[0]
    turned = [tall] + [pltpu.roll(tall, LANES - ROWS * row, 1) for row in range(1, ROWS)]
    wide = dot01(jnp.concatenate(turned, axis=0), spread, 2)
    for row in range(ROWS):
        lifted[0:rows, row, :] = wide[row * rows : (row + 1) * rows]

    odd = part % 2 == 1

    def lifted_to(plane):
        parent = plane // 2 + NEAR // 2
        return lifted[jnp.where(odd, count - 1 - parent, parent)]

    near_fields, near_corr1 = (near1[0:6], near1[6], near1[7]), near1[8]
    far_fields, far_corr1 = (far1[0:6], far1[6], far1[7]), far1[8]
    fields2, corr2 = (far2[0:6], far2[6], far2[7]), far2[8]
    low, high = NEAR - 4, NEAR + depth // 2 + 4
    reach = depth // 2 + NEAR
    quarter = iota((ROWS, LANES), 1) // (LANES // 4)
    row = iota((ROWS, LANES), 0)

    def unpacked(index, which):
        pair = packed[lookup(slots, jnp.clip(index, 0, shares - 1)), which]
        total = None
        for shift in range(4):
            moved = pltpu.roll(pair, shift * (LANES // 4), 1)
            wide = jnp.where(row < 4, moved[0:1, :], moved[1:2, :])
            kept = jnp.where((quarter - shift) % 4 == row % 4, wide, 0.0)
            total = kept if total is None else total + kept
        return total

    one2[low - 1] = unpacked(jnp.where(odd, part + 1, part - 1), 4) + lifted_to(low - 1)
    for plane in range(low, high):
        one2[plane] = corr2[plane] + lifted_to(plane)
    one2[high] = unpacked(jnp.where(odd, part - 1, part + 1), 3) + lifted_to(high)
    sweep(coarse, NEAR - 4, reach + 4, fields2, one2, two2)
    sweep(coarse, NEAR - 3, reach + 3, fields2, two2, one2)
    sweep(coarse, NEAR - 2, reach + 2, fields2, one2, two2)

    fine_lane, coarse_lane = iota((LANES, LANES), 1), iota((LANES, LANES), 0)
    x_of = (fine_lane // fine.ny) // 2
    y_of = (fine_lane % fine.ny) // 2
    up = where01(coarse_lane == x_of * coarse.ny + y_of)
    lifted[0 : depth // 2 + 4] = in_lanes(two2[NEAR - 2 : reach + 2], up, 2)
    parents = lifted[0 : depth // 2 + 4]
    twice = jnp.broadcast_to(parents[:, None], (parents.shape[0], 2, ROWS, LANES))
    low, high = HALO - 4, HALO + depth + 4
    turn = HALO + 3
    for plane in range(low, high):
        corr = far_corr1[plane] if plane < turn else near_corr1[plane - HALO]
        one1[plane] = corr + lifted[(plane - low) // 2]
    reach = depth + HALO
    for more, source, target in ((2, one1, two1), (1, two1, one1)):
        sweep(fine, HALO - more, turn, far_fields, source, target)
        sweep(fine, turn, reach + more, near_fields, source, target, HALO)

    def last(fields, shift):
        def body(plane, count):
            value = swept(fine, plane, count, fields, one1, shift)
            value = value * fields[2][pl.ds(plane - shift, count)]
            for index in range(count):
                at = plane - HALO + index
                final[jnp.where(odd, depth - 1 - at, at)] = value[index]

        return body

    loop(HALO, turn, PIECE, last(far_fields, 0))
    loop(turn, reach, PIECE, last(near_fields, HALO))

    group = (iota((depth, LANES), 1) // by) % groups
    for ix in range(nx):
        scaled = [final[:, ix * groups + part, :] for part in range(groups)]
        for iy in range(ny):
            total = scaled[iy]
            for part in range(groups):
                if part != iy:
                    moved = pltpu.roll(scaled[part], (by * (part - iy)) % LANES, 1)
                    total = jnp.where(group == part, moved, total)
            out_ref[slot_of(ix * ny + iy)] = total


def finish_kernel(blocks, out_ref):
    bx, by, depth = out_ref.shape
    peers = blocks.shape[0]
    ordered = jnp.concatenate([blocks[own_slot_of(rank)] for rank in range(peers)], axis=0)
    turned = ordered.T
    for x in range(bx):
        row = ((x % 4) * (bx // 4) + x // 4) * by
        out_ref[x] = turned[row : row + by]


def whole_planes(residual_q2, viscosity, pinned):
    bx, by, depth = viscosity.shape
    groups = bx // 4
    peers = SPLIT[0] * SPLIT[1]
    share = depth // peers
    planes = share + 2 * HALO
    count2 = share // 2 + 2 * NEAR
    limit = pltpu.CompilerParams(vmem_limit_bytes=32 * 2**20)

    def flat(rows):
        return jax.ShapeDtypeStruct((rows, LANES), F32)

    def blocks(count, rows):
        return jax.ShapeDtypeStruct((count, rows, LANES), F32)

    def room(count):
        return pltpu.VMEM((count, ROWS, LANES), F32)

    fluid = 1.0 / viscosity
    pin = 4.0 * pinned.astype(F32) * fluid
    parcels = pl.pallas_call(
        functools.partial(prepare_kernel, share),
        out_shape=blocks(peers, 3 * share),
        compiler_params=limit,
        name="prepare",
    )(residual_q2.reshape(4 * bx * by, 2 * depth), fluid, pin)
    own = pl.pallas_call(
        functools.partial(spread_kernel, groups, by),
        out_shape=blocks(3 * share, ROWS),
        scratch_shapes=[room(3 * share)],
        compiler_params=limit,
        name="spread",
    )(exchange(parcels))
    length = lax.axis_size("gz")
    parts = length * peers

    device = devices_of(length)

    def swap(field, first):
        pairs = [(device[i], device[i + 1]) for i in range(first, parts - 1, 2)]
        return lax.ppermute(field, ("gx", "gy", "gz"), pairs + [pair[::-1] for pair in pairs])

    outer, inner = swap(own, 1), swap(own, 0)
    count3 = share // 4
    near1, near2, far1, far2 = (
        (blocks(count, ROWS),) * fields
        for count, fields in ((share + HALO, 9), (count2, 8), (HALO + 8, 9), (count2, 9))
    )
    near1, near2, fluid2, pin2, fluid3, pin3 = pl.pallas_call(
        functools.partial(near_kernel, share),
        out_shape=(near1, near2) + (blocks(count2, ROWS),) * 2 + (blocks(count3, ROWS),) * 2,
        scratch_shapes=[room(share + HALO)] * 4 + [room(count2)] * 2,
        compiler_params=limit,
        name="near",
    )(own, inner)
    far1, far2, parcel = pl.pallas_call(
        functools.partial(down_kernel, share),
        out_shape=(far1, far2, blocks(5, 2)),
        scratch_shapes=[room(HALO + 8)] * 4 + [room(count2)] * 5,
        compiler_params=limit,
        name="down",
    )(own, outer, near2, fluid2, pin2, fluid3, pin3)
    copies = jnp.broadcast_to(parcel, (parts,) + parcel.shape)
    packed = exchange_all(copies)
    depth3 = parts * count3
    mine = pl.pallas_call(
        functools.partial(up_kernel, groups, by, share),
        out_shape=blocks(peers, share),
        scratch_shapes=[room(planes), room(planes), room(count2), room(count2), room(count2)]
        + [pltpu.VMEM((rows, LANES), F32) for rows in (depth3, depth3, depth3 + 3 * NEAR)]
        + [room(share)],
        compiler_params=limit,
        name="up",
    )(packed, near1, far1, far2)
    return pl.pallas_call(
        finish_kernel,
        out_shape=jax.ShapeDtypeStruct((bx, by, depth), F32),
        compiler_params=limit,
        name="finish",
    )(exchange(mine))


def one_tile_planes(mesh, viscosity):
    split = (mesh.shape["gx"], mesh.shape["gy"])
    depth = viscosity.shape[2]
    fits = viscosity.shape[:2] == PLANE and split == SPLIT
    return fits and depth == 4 * LANES and depth // mesh.shape["gz"] == LANES


def solution(mesh):
    placed = (P("gx", "gy", "gz"), P("gx", "gy", "gz"), P("gx", "gy", "gz"))

    def cycle(residual_q2, viscosity, pinned):
        chosen = whole_planes if one_tile_planes(mesh, viscosity) else per_device
        return jax.shard_map(
            chosen, mesh=mesh, in_specs=placed, out_specs=P("gx", "gy", "gz"), check_vma=False
        )(residual_q2, viscosity, pinned)

    return cycle
```

```python
import functools

import jax
import jax.numpy as jnp
from jax import lax
from jax.experimental import pallas as pl
from jax.experimental.pallas import tpu as pltpu
from jax.sharding import PartitionSpec as P

NU = 3


OMEGA = 0.6


def with_halo(block, sides, width):
    for axis, dim in sides:
        count = lax.axis_size(axis)
        forward = [(i, i + 1) for i in range(count - 1)]
        backward = [(target, source) for source, target in forward]
        low = lax.ppermute(
            lax.slice_in_dim(block, block.shape[dim] - width, None, axis=dim), axis, forward
        )
        high = lax.ppermute(lax.slice_in_dim(block, 0, width, axis=dim), axis, backward)
        block = jnp.concatenate([low, block, high], axis=dim)
    return block


def coarsen(x):
    a, b, c = x.shape
    return x.reshape(a // 2, 2, b // 2, 2, c // 2, 2).sum(axis=(1, 3, 5))


def refine(x):
    return jnp.repeat(jnp.repeat(jnp.repeat(x, 2, 0), 2, 1), 2, 2)


def extended(field):
    return with_halo(field, (("gx", 0), ("gy", 1), ("gz", 2)), 1)


def shifted(padded):
    return [
        padded[2:, 1:-1, 1:-1],
        padded[:-2, 1:-1, 1:-1],
        padded[1:-1, 2:, 1:-1],
        padded[1:-1, :-2, 1:-1],
        padded[1:-1, 1:-1, 2:],
        padded[1:-1, 1:-1, :-2],
    ]


def neighbours(field):
    return shifted(extended(field))


def harmonic(fluid, near, factor):
    total = fluid + near
    return jnp.where(total > 0, factor * 2.0 * fluid * near / jnp.where(total > 0, total, 1.0), 0.0)


def couplings(fluid, factor):
    return [harmonic(fluid, near, factor) for near in neighbours(fluid)]


def apply_op(field, weights, diag):
    total = diag * field
    for weight, near in zip(weights, neighbours(field)):
        total = total - weight * near
    return total


def presmooth(rhs, weights, diag):
    corr = OMEGA * rhs / diag
    for sweep in range(NU - 1):
        corr = corr + OMEGA * (rhs - apply_op(corr, weights, diag)) / diag
    return corr


def postsmooth(corr, rhs, weights, diag):
    for sweep in range(NU):
        corr = corr + OMEGA * (rhs - apply_op(corr, weights, diag)) / diag
    return corr


def tridiag(coeffs, rhs):
    solved = lax.linalg.tridiagonal_solve(coeffs[0], coeffs[1], coeffs[2], rhs[..., None])[..., 0]
    last = rhs.ndim - 1
    shift_col = jnp.sum(rhs, axis=last, keepdims=True) / jnp.sum(
        coeffs[3], axis=last, keepdims=True
    )
    return solved + shift_col


def prepare_columns(weights, diag):
    lower = -weights[5]
    upper = -weights[4]
    across = diag + lower + upper
    return (
        lax.all_gather(lower, "gz", axis=2, tiled=True),
        lax.all_gather(diag, "gz", axis=2, tiled=True),
        lax.all_gather(upper, "gz", axis=2, tiled=True),
        lax.all_gather(across, "gz", axis=2, tiled=True),
    )


def column_solve(rhs, coeffs):
    depth = rhs.shape[2]
    whole = lax.all_gather(rhs, "gz", axis=2, tiled=True)
    solved = tridiag(coeffs, whole)
    return lax.dynamic_slice_in_dim(solved, lax.axis_index("gz") * depth, depth, 2)


def per_device(residual_q2, viscosity, pinned):
    fluid1 = 1.0 / viscosity
    pin1 = 4.0 * pinned.astype(jnp.float32) * fluid1
    rhs1 = coarsen(residual_q2.astype(jnp.float32))
    fluid2 = coarsen(fluid1) / 8.0
    pin2 = coarsen(pin1) / 4.0
    fluid3 = coarsen(fluid2) / 8.0
    pin3 = coarsen(pin2) / 4.0
    weights1 = couplings(fluid1, 1.0)
    weights2 = couplings(fluid2, 2.0)
    weights3 = couplings(fluid3, 4.0)
    diag1 = sum(weights1) + pin1
    diag2 = sum(weights2) + pin2
    diag3 = sum(weights3) + pin3
    coeffs = prepare_columns(weights3, diag3)
    corr1 = presmooth(rhs1, weights1, diag1)
    rhs2 = coarsen(rhs1 - apply_op(corr1, weights1, diag1))
    corr2 = presmooth(rhs2, weights2, diag2)
    rhs3 = coarsen(rhs2 - apply_op(corr2, weights2, diag2))
    corr3 = column_solve(rhs3, coeffs)
    corr3 = corr3 + column_solve(rhs3 - apply_op(corr3, weights3, diag3), coeffs)
    corr2 = postsmooth(corr2 + refine(corr3), rhs2, weights2, diag2)
    corr1 = postsmooth(corr1 + refine(corr2), rhs1, weights1, diag1)
    return diag1 * corr1


PLANE = (32, 32)
SPLIT = (2, 4)
ROWS = 8
LANES = 128
HALO = 16
NEAR = 8
PIECE = 8
TINY = 1e-30
F32 = jnp.float32


def iota(shape, dim):
    return lax.broadcasted_iota(jnp.int32, shape, dim)


def dot01(field, chosen):
    total = None
    rest = field
    for part in range(3):
        piece = rest.astype(jnp.bfloat16)
        term = jnp.dot(piece, chosen, preferred_element_type=F32)
        total = term if total is None else total + term
        if part < 2:
            rest = rest - piece.astype(F32)
    return total


def dot10(chosen, field):
    total = None
    rest = field
    for part in range(3):
        piece = rest.astype(jnp.bfloat16)
        term = lax.dot_general(
            chosen, piece, (((1,), (1,)), ((), ())), preferred_element_type=F32
        )
        total = term if total is None else total + term
        if part < 2:
            rest = rest - piece.astype(F32)
    return total


def where01(condition):
    return jnp.where(condition, 1.0, 0.0).astype(jnp.bfloat16)


def loop(low, high, size, body):
    for plane in range(low, high, size):
        body(plane, min(size, high - plane))


def inverse_of(field):
    first = pl.reciprocal(field, approx=True)
    return first * (2.0 - field * first)


class Level:
    def __init__(self, level):
        self.ny = PLANE[1] >> level
        self.xs = 4 >> level
        self.factor = float(2**level)

    def masks(self, shape):
        lane = iota(shape, 2)
        row = iota(shape, 1)
        within = (lane // self.ny) % self.xs
        y = lane % self.ny
        last_x = (row == ROWS - 1) & (within == self.xs - 1)
        return within, y == self.ny - 1, last_x

    def next_x(self, field):
        within = (iota(field.shape, 2) // self.ny) % self.xs
        moved = pltpu.roll(field, LANES - self.ny, 2)
        return jnp.where(within == self.xs - 1, pltpu.roll(moved, ROWS - 1, 1), moved)

    def last_x(self, field):
        within = (iota(field.shape, 2) // self.ny) % self.xs
        moved = pltpu.roll(field, self.ny, 2)
        return jnp.where(within == 0, pltpu.roll(moved, 1, 1), moved)

    def next_y(self, field):
        return pltpu.roll(field, LANES - 1, 2)

    def last_y(self, field):
        return pltpu.roll(field, 1, 2)

    def spread(self, field, scaled, plane, count):
        mid = field[1:-1]
        near = (
            self.next_x(mid), self.last_x(mid), self.next_y(mid), self.last_y(mid),
            field[2:], field[:-2],
        )
        terms = [weight[pl.ds(plane, count)] * value for weight, value in zip(scaled, near)]
        return mid, ((terms[0] + terms[1]) + (terms[2] + terms[3])) + (terms[4] + terms[5])


def mean_of(fluid, near, factor):
    return ((factor * 2.0) * fluid * near) * inverse_of(jnp.maximum(fluid + near, TINY))


def set_level(level, low, high, fluid, pin, rhs, fields):
    scaled, start, diag = fields

    def body(plane, count):
        wide = fluid[pl.ds(plane - 1, count + 2)]
        mid = wide[1:-1]
        within, end_y, end_x = level.masks(mid.shape)
        to_x = jnp.where(end_x, 0.0, mean_of(mid, level.next_x(mid), level.factor))
        to_y = jnp.where(end_y, 0.0, mean_of(mid, level.next_y(mid), level.factor))
        to_z = mean_of(wide[:-1], wide[1:], level.factor)
        weights = (to_x, level.last_x(to_x), to_y, level.last_y(to_y), to_z[1:], to_z[:-1])
        total = (
            (weights[0] + weights[1])
            + (weights[2] + weights[3])
            + (weights[4] + weights[5])
            + pin[pl.ds(plane, count)]
        )
        gain = OMEGA * inverse_of(jnp.maximum(total, TINY))
        for target, weight in zip(scaled, weights):
            target[pl.ds(plane, count)] = gain * weight
        start[pl.ds(plane, count)] = gain * rhs[pl.ds(plane, count)]
        diag[pl.ds(plane, count)] = total

    loop(low, high, PIECE, body)


def swept(level, plane, count, fields, source, shift=0):
    scaled, start, _ = fields
    mid, total = level.spread(source[pl.ds(plane - 1, count + 2)], scaled, plane - shift, count)
    return (1.0 - OMEGA) * mid + (start[pl.ds(plane - shift, count)] + total)


def sweep(level, low, high, fields, source, target, shift=0):
    def body(plane, count):
        target[pl.ds(plane, count)] = swept(level, plane, count, fields, source, shift)

    loop(low, high, PIECE, body)


def pair_sum(field):
    half = field.reshape((field.shape[0] // 2, 2) + field.shape[1:])
    return half[:, 0] + half[:, 1]


def coarse_residual(level, low, high, fields, corr, target):
    scaled, start, diag = fields

    def body(plane, count):
        mid, total = level.spread(corr[pl.ds(plane - 1, count + 2)], scaled, plane, count)
        rest = (start[pl.ds(plane, count)] + total) - OMEGA * mid
        rest = rest * (diag[pl.ds(plane, count)] * (1.0 / OMEGA))
        target[pl.ds((plane - low) // 2, count // 2)] = pair_sum(rest)

    loop(low, high, PIECE, body)


def lanes_down(level):
    fine = iota((LANES, LANES), 0)
    coarse = iota((LANES, LANES), 1)
    ny, xs = PLANE[1] >> level, 4 >> level
    half = xs // 2
    same_x = ((fine // ny) % xs) // 2 == (coarse // (ny // 2)) % half
    same_y = (fine % ny) // 2 == coarse % (ny // 2)
    return where01((fine < ny * xs) & same_x & same_y)


def in_lanes(field, chosen):
    flat = field.reshape(field.shape[0] * ROWS, LANES)
    return dot01(flat, chosen).reshape(field.shape)


def path_of(group):
    nx, ny = SPLIT
    row, column = 0, 0
    for index in range(group + 1):
        columns = list(range(ny)) if column == 0 else list(range(ny))[::-1]
        if index % 2:
            path = [(row, at) for at in columns] + [(1 - row, at) for at in columns[::-1]]
        else:
            path = []
            for at in columns:
                path += [(row, at), (1 - row, at)]
                row = 1 - row
        row, column = path[-1]
    return [row * ny + column for row, column in path]


def lookup(table, index):
    found = table[0]
    for at, value in enumerate(table[1:], 1):
        found = jnp.where(index == at, value, found)
    return found


def slot_of(peer):
    return SPLIT[0] * SPLIT[1] - 1 - peer


def own_slot_of(rank):
    groups = range(lax.axis_size("gz"))
    return lookup([slot_of(path_of(group)[rank]) for group in groups], lax.axis_index("gz"))


def exchange(field):
    peers, groups = SPLIT[0] * SPLIT[1], lax.axis_size("gz")
    order = sorted(range(peers), key=slot_of)
    members = [[peer * groups + group for peer in order] for group in range(groups)]
    axes = ("gx", "gy", "gz")
    return lax.all_to_all(field, axes, 0, 0, axis_index_groups=members, tiled=True)


def slabs_of(groups):
    peers = SPLIT[0] * SPLIT[1]
    return [
        group * peers + path_of(group).index(peer) for peer in range(peers) for group in range(groups)
    ]


def own_slab():
    nx, ny = SPLIT
    groups = lax.axis_size("gz")
    device = (lax.axis_index("gx") * ny + lax.axis_index("gy")) * groups + lax.axis_index("gz")
    return lookup(slabs_of(groups), device)


def devices_of(groups):
    slabs = slabs_of(groups)
    return [slabs.index(slab) for slab in range(len(slabs))]


def prepare_kernel(share, res_ref, fluid_ref, pin_ref, out_ref):
    bx, by, depth = fluid_ref.shape
    cells = bx * by
    groups = bx // 4
    order = [x for low in range(4) for x in range(low, bx, 4)]
    fine = iota((cells, 4 * cells), 1)
    x, y = fine // (4 * by), (fine % (2 * by)) // 2
    chosen = where01((x % 4) * (groups * by) + (x // 4) * by + y == iota((cells, 4 * cells), 0))
    wide = lax.dot_general(
        chosen, res_ref[...], (((1,), (0,)), ((), ())), preferred_element_type=F32
    )
    rhs = dot10(where01(iota((depth, 2 * depth), 1) // 2 == iota((depth, 2 * depth), 0)), wide)

    def turned(field_ref):
        field = jnp.concatenate([field_ref[x : x + 1] for x in order], axis=0)
        return field.reshape(cells, depth).T

    fluid, pin = turned(fluid_ref), turned(pin_ref)
    for rank in range(depth // share):
        peer, begin = own_slot_of(rank), rank * share
        for index, field in enumerate((fluid, rhs, pin)):
            out_ref[peer, index * share : (index + 1) * share] = field[begin : begin + share]


def spread_kernel(groups, by, gathered, own, inner, outer, straight):
    for start in range(0, own.shape[0], ROWS):
        place(gathered, start, straight, start, groups, by)
    share = own.shape[0] // 3
    odd = own_slab() % 2 == 1
    for index in range(3):
        for plane in range(share):
            at = jnp.where(odd, share - 1 - plane, plane)
            own[index * share + plane] = straight[index * share + at]
    for target, drop in ((inner, 0), (outer, share - 1)):
        row = 0
        for index in range(3):
            for plane in range(share):
                if index == 0 or plane != drop:
                    target[row] = own[index * share + plane]
                    row += 1


def place(gathered, row, target, plane, groups, by):
    group = (iota((ROWS, LANES), 1) // by) % groups
    nx, ny = SPLIT
    for ix in range(nx):
        found = [gathered[slot_of(ix * ny + iy), pl.ds(row, ROWS), :] for iy in range(ny)]
        for part in range(groups):
            total = found[part]
            for iy in range(ny):
                if iy != part:
                    moved = pltpu.roll(found[iy], (by * (iy - part)) % LANES, 1)
                    total = jnp.where(group == iy, moved, total)
            target[pl.ds(plane, ROWS), ix * groups + part, :] = total


def near_kernel(
    depth,
    own, inner,
    saved1, saved2, fluid2, pin2, fluid3, pin3,
    fluid1, rhs1, pin1, other1, rhs2, sums,
):
    row = 0
    for index, target in enumerate((fluid1, rhs1, pin1)):
        target[0:depth] = own[index * depth : (index + 1) * depth]
        count = HALO if index == 0 else HALO - 1
        for plane in range(count):
            target[depth + plane] = inner[row + count - 1 - plane]
        if count < HALO:
            target[depth + count] = jnp.zeros((ROWS, LANES), F32)
        row += count
    fine, coarse = Level(0), Level(1)
    down1, down2 = lanes_down(0), lanes_down(1)
    fields1, corr1 = (saved1[0:6], saved1[6], saved1[7]), saved1[8]
    fields2 = (saved2[0:6], saved2[6], saved2[7])
    planes = depth + HALO
    set_level(fine, 1, planes - 1, fluid1, pin1, rhs1, fields1)
    sweep(fine, 2, planes - 2, fields1, fields1[1], other1)
    sweep(fine, 3, planes - 3, fields1, other1, corr1)
    coarse_residual(fine, 4, planes - 4, fields1, corr1, sums)
    count2 = planes // 2
    for source, target, share in ((fluid1, fluid2, 8.0), (pin1, pin2, 4.0)):
        target[NEAR : NEAR + count2] = in_lanes(pair_sum(source[...]), down1) * (1.0 / share)
    low2, high2 = NEAR + 2, NEAR + count2 - 2
    rhs2[low2:high2] = in_lanes(sums[0 : high2 - low2], down1)
    set_level(coarse, low2, high2, fluid2, pin2, rhs2, fields2)
    for source, target, scale in ((fluid2, fluid3, 0.125), (pin2, pin3, 0.25)):
        target[...] = in_lanes(pair_sum(source[NEAR : NEAR + depth // 2]), down2) * scale


def down_kernel(
    depth,
    own, outer, near2, near_fluid2, near_pin2, fluid3, pin3,
    saved1, saved2,
    packed,
    fluid1, rhs1, pin1, other1, fluid2, rhs2, pin2, other2, sums,
):
    planes = fluid1.shape[0]
    row = 0
    for index, target in enumerate((fluid1, rhs1, pin1)):
        count = HALO if index == 0 else HALO - 1
        if count < HALO:
            target[0] = jnp.zeros((ROWS, LANES), F32)
        for plane in range(count):
            target[HALO - count + plane] = outer[row + count - 1 - plane]
        row += count
        target[HALO:planes] = own[index * depth : index * depth + planes - HALO]

    fine, coarse = Level(0), Level(1)
    down1, down2 = lanes_down(0), lanes_down(1)
    fields1, corr1 = (saved1[0:6], saved1[6], saved1[7]), saved1[8]
    fields2, corr2 = (saved2[0:6], saved2[6], saved2[7]), saved2[8]
    set_level(fine, 1, planes - 1, fluid1, pin1, rhs1, fields1)
    sweep(fine, 2, planes - 2, fields1, fields1[1], other1)
    sweep(fine, 3, planes - 3, fields1, other1, corr1)
    count2 = depth // 2 + 2 * NEAR
    low2, done, high2 = 2, NEAR + 2, count2 - 2
    coarse_residual(fine, 2 * low2, 2 * done, fields1, corr1, sums)
    for source, ready, target, share in (
        (fluid1, near_fluid2, fluid2, 8.0), (pin1, near_pin2, pin2, 4.0)
    ):
        target[0:NEAR] = in_lanes(pair_sum(source[0:HALO]), down1) * (1.0 / share)
        target[NEAR : done + 1] = ready[NEAR : done + 1]
    rhs2[low2:done] = in_lanes(sums[0 : done - low2], down1)
    set_level(coarse, low2, done, fluid2, pin2, rhs2, fields2)
    for source, target in zip(near2, saved2[0:8]):
        target[done:high2] = source[done:high2]
    sweep(coarse, low2 + 1, high2 - 1, fields2, fields2[1], other2)
    sweep(coarse, low2 + 2, high2 - 2, fields2, other2, corr2)
    coarse_residual(coarse, NEAR, NEAR + depth // 2, fields2, corr2, sums)
    count3 = depth // 4
    rhs3 = in_lanes(sums[0:count3], down2)
    lane = iota((count3, LANES), 1) // ROWS
    first = jnp.zeros((count3, LANES), F32)
    second = jnp.zeros((count3, LANES), F32)
    for row in range(ROWS):
        first = jnp.where(lane == row, rhs3[:, row, :], first)
        first = jnp.where(lane == ROWS + row, fluid3[:, row, :], first)
        second = jnp.where(lane % ROWS == row, pin3[:, row, :], second)
    odd = own_slab() % 2 == 1

    def ordered(field):
        back = [field[row : row + 1] for row in reversed(range(count3))]
        return jnp.where(odd, jnp.concatenate(back, axis=0), field)

    first, second = ordered(first), ordered(second)
    packed[0] = first[0:2]
    packed[1] = first[2:4]
    packed[2] = jnp.where(lane[0:2] < ROWS, second[0:2], second[2:4])
    lane = iota((1, LANES), 1) // (LANES // 4)
    for index, plane in enumerate((NEAR + depth // 2 - 5, NEAR + 4)):
        for half in range(2):
            row = jnp.zeros((1, LANES), F32)
            for quarter in range(4):
                at = half * 4 + quarter
                row = jnp.where(lane == quarter, corr2[plane, at : at + 1, :], row)
            packed[3 + index, half : half + 1, :] = row


def rolled(field, shift):
    count = field.shape[0]
    shift %= count
    if shift % ROWS:
        return pltpu.roll(field, shift, 0)
    return jnp.concatenate([field[count - shift :], field[: count - shift]], axis=0)


def columns(rhs, fluid, pin):
    depth = fluid.shape[0]
    z, lane = iota(fluid.shape, 0), iota(fluid.shape, 1)
    y, x = lane % ROWS, (lane // ROWS) % ROWS

    def next_x(field):
        return pltpu.roll(field, LANES - ROWS, 1)

    def next_y(field):
        return pltpu.roll(field, LANES - 1, 1)

    wz = jnp.where(z == depth - 1, 0.0, mean_of(fluid, rolled(fluid, -1), 4.0))
    wy = jnp.where(y == ROWS - 1, 0.0, mean_of(fluid, next_y(fluid), 4.0))
    wx = jnp.where(x == ROWS - 1, 0.0, mean_of(fluid, next_x(fluid), 4.0))
    across = (wx + pltpu.roll(wx, ROWS, 1)) + (wy + pltpu.roll(wy, 1, 1)) + pin
    share = 1.0 / jnp.sum(across, axis=0, keepdims=True)

    above, below, own = rolled(wz, 1), wz, across
    steps = []
    stride, right = 1, rhs
    while stride < depth:
        inverse = inverse_of(above + below + own)
        up = above * rolled(inverse, stride)
        down = below * rolled(inverse, -stride)
        own = own + up * rolled(own, stride) + down * rolled(own, -stride)
        above = up * rolled(above, stride)
        below = down * rolled(below, -stride)
        right = right + up * rolled(right, stride) + down * rolled(right, -stride)
        steps.append((stride, up, down))
        stride *= 2
    inverse = inverse_of(above + below + own)

    def mean(right):
        return jnp.sum(right, axis=0, keepdims=True) * share

    corr = right * inverse + mean(rhs)
    flow_x = wx * (next_x(corr) - corr)
    flow_y = wy * (next_y(corr) - corr)
    flow_z = wz * (rolled(corr, -1) - corr)
    rest = (
        (rhs - pin * corr)
        + (flow_x - pltpu.roll(flow_x, ROWS, 1))
        + (flow_y - pltpu.roll(flow_y, 1, 1))
        + (flow_z - rolled(flow_z, 1))
    )
    right = rest
    for stride, up, down in steps:
        right = right + up * rolled(right, stride) + down * rolled(right, -stride)
    return (corr + mean(rest)) + right * inverse


def up_kernel(
    groups, by, depth,
    packed, near1, far1, far2,
    out_ref,
    one1, two1, one2, two2, lifted, first, second, solved, final,
):
    count3 = depth // 4
    shares = packed.shape[0]
    peers = SPLIT[0] * SPLIT[1]
    devices = devices_of(shares // peers)
    for slab, index in enumerate(devices):
        row = slab * count3
        first[row : row + 2] = packed[index, 0]
        first[row + 2 : row + 4] = packed[index, 1]
        both = packed[index, 2]
        second[row : row + 2] = both
        second[row + 2 : row + 4] = pltpu.roll(both, LANES // 2, 1)
    half = iota((shares * count3, LANES), 1) < LANES // 2

    def low_half(field):
        return jnp.where(half, field, pltpu.roll(field, LANES // 2, 1))

    def high_half(field):
        return jnp.where(half, pltpu.roll(field, LANES // 2, 1), field)

    solved[NEAR : NEAR + shares * count3] = columns(
        low_half(first[...]), high_half(first[...]), low_half(second[...])
    )
    solved[0:NEAR] = jnp.zeros((NEAR, LANES), F32)
    solved[NEAR + shares * count3 :] = jnp.zeros((2 * NEAR, LANES), F32)

    nx, ny = SPLIT
    part = own_slab()
    count = count3 + 2 * NEAR
    tall = solved[pl.ds(part * count3, count + count3), :]
    fine, coarse = Level(0), Level(1)
    cell = iota((LANES, LANES), 0)
    lane = iota((LANES, LANES), 1)
    spread = where01((cell < ROWS) & (cell == (lane % coarse.ny) // 2))
    rows = tall.shape[0]
    turned = [tall] + [pltpu.roll(tall, LANES - ROWS * row, 1) for row in range(1, ROWS)]
    wide = dot01(jnp.concatenate(turned, axis=0), spread)
    for row in range(ROWS):
        lifted[0:rows, row, :] = wide[row * rows : (row + 1) * rows]

    odd = part % 2 == 1

    def lifted_to(plane):
        parent = plane // 2 + NEAR // 2
        return lifted[jnp.where(odd, count - 1 - parent, parent)]

    near_fields, near_corr1 = (near1[0:6], near1[6], near1[7]), near1[8]
    far_fields, far_corr1 = (far1[0:6], far1[6], far1[7]), far1[8]
    fields2, corr2 = (far2[0:6], far2[6], far2[7]), far2[8]
    low, high = NEAR - 4, NEAR + depth // 2 + 4
    reach = depth // 2 + NEAR
    quarter = iota((ROWS, LANES), 1) // (LANES // 4)
    row = iota((ROWS, LANES), 0)

    def unpacked(index, which):
        pair = packed[lookup(devices, jnp.clip(index, 0, shares - 1)), which]
        total = None
        for shift in range(4):
            moved = pltpu.roll(pair, shift * (LANES // 4), 1)
            wide = jnp.where(row < 4, moved[0:1, :], moved[1:2, :])
            kept = jnp.where((quarter - shift) % 4 == row % 4, wide, 0.0)
            total = kept if total is None else total + kept
        return total

    one2[low - 1] = unpacked(jnp.where(odd, part + 1, part - 1), 4) + lifted_to(low - 1)
    for plane in range(low, high):
        one2[plane] = corr2[plane] + lifted_to(plane)
    one2[high] = unpacked(jnp.where(odd, part - 1, part + 1), 3) + lifted_to(high)
    sweep(coarse, NEAR - 4, reach + 4, fields2, one2, two2)
    sweep(coarse, NEAR - 3, reach + 3, fields2, two2, one2)
    sweep(coarse, NEAR - 2, reach + 2, fields2, one2, two2)

    fine_lane, coarse_lane = iota((LANES, LANES), 1), iota((LANES, LANES), 0)
    x_of = (fine_lane // fine.ny) // 2
    y_of = (fine_lane % fine.ny) // 2
    up = where01(coarse_lane == x_of * coarse.ny + y_of)
    lifted[0 : depth // 2 + 4] = in_lanes(two2[NEAR - 2 : reach + 2], up)
    parents = lifted[0 : depth // 2 + 4]
    twice = jnp.broadcast_to(parents[:, None], (parents.shape[0], 2, ROWS, LANES))
    low, high = HALO - 4, HALO + depth + 4
    turn = HALO + 3
    for plane in range(low, high):
        corr = far_corr1[plane] if plane < turn else near_corr1[plane - HALO]
        one1[plane] = corr + lifted[(plane - low) // 2]
    reach = depth + HALO
    for more, source, target in ((2, one1, two1), (1, two1, one1)):
        sweep(fine, HALO - more, turn, far_fields, source, target)
        sweep(fine, turn, reach + more, near_fields, source, target, HALO)

    def last(fields, shift):
        def body(plane, count):
            value = swept(fine, plane, count, fields, one1, shift)
            value = value * fields[2][pl.ds(plane - shift, count)]
            for index in range(count):
                at = plane - HALO + index
                final[jnp.where(odd, depth - 1 - at, at)] = value[index]

        return body

    loop(HALO, turn, PIECE, last(far_fields, 0))
    loop(turn, reach, PIECE, last(near_fields, HALO))

    group = (iota((depth, LANES), 1) // by) % groups
    for ix in range(nx):
        scaled = [final[:, ix * groups + part, :] for part in range(groups)]
        for iy in range(ny):
            total = scaled[iy]
            for part in range(groups):
                if part != iy:
                    moved = pltpu.roll(scaled[part], (by * (part - iy)) % LANES, 1)
                    total = jnp.where(group == part, moved, total)
            out_ref[slot_of(ix * ny + iy)] = total


def finish_kernel(blocks, out_ref):
    bx, by, depth = out_ref.shape
    peers = blocks.shape[0]
    ordered = jnp.concatenate([blocks[own_slot_of(rank)] for rank in range(peers)], axis=0)
    turned = ordered.T
    for x in range(bx):
        row = ((x % 4) * (bx // 4) + x // 4) * by
        out_ref[x] = turned[row : row + by]


def whole_planes(residual_q2, viscosity, pinned):
    bx, by, depth = viscosity.shape
    groups = bx // 4
    peers = SPLIT[0] * SPLIT[1]
    share = depth // peers
    planes = share + 2 * HALO
    count2 = share // 2 + 2 * NEAR
    limit = pltpu.CompilerParams(vmem_limit_bytes=32 * 2**20)

    def flat(rows):
        return jax.ShapeDtypeStruct((rows, LANES), F32)

    def blocks(count, rows):
        return jax.ShapeDtypeStruct((count, rows, LANES), F32)

    def room(count):
        return pltpu.VMEM((count, ROWS, LANES), F32)

    fluid = 1.0 / viscosity
    pin = 4.0 * pinned.astype(F32) * fluid
    parcels = pl.pallas_call(
        functools.partial(prepare_kernel, share),
        out_shape=blocks(peers, 3 * share),
        compiler_params=limit,
        name="prepare",
    )(residual_q2.reshape(4 * bx * by, 2 * depth), fluid, pin)
    own, inner, outer = pl.pallas_call(
        functools.partial(spread_kernel, groups, by),
        out_shape=(blocks(3 * share, ROWS),) + (blocks(3 * HALO - 2, ROWS),) * 2,
        scratch_shapes=[room(3 * share)],
        compiler_params=limit,
        name="spread",
    )(exchange(parcels))
    length = lax.axis_size("gz")
    parts = length * peers

    device = devices_of(length)

    def swap(field, first):
        pairs = [(device[i], device[i + 1]) for i in range(first, parts - 1, 2)]
        return lax.ppermute(field, ("gx", "gy", "gz"), pairs + [pair[::-1] for pair in pairs])

    outer, inner = swap(outer, 1), swap(inner, 0)
    count3 = share // 4
    near1, near2, far1, far2 = (
        (blocks(count, ROWS),) * fields
        for count, fields in ((share + HALO, 9), (count2, 8), (HALO + 8, 9), (count2, 9))
    )
    near1, near2, fluid2, pin2, fluid3, pin3 = pl.pallas_call(
        functools.partial(near_kernel, share),
        out_shape=(near1, near2) + (blocks(count2, ROWS),) * 2 + (blocks(count3, ROWS),) * 2,
        scratch_shapes=[room(share + HALO)] * 4 + [room(count2)] * 2,
        compiler_params=limit,
        name="near",
    )(own, inner)
    far1, far2, parcel = pl.pallas_call(
        functools.partial(down_kernel, share),
        out_shape=(far1, far2, blocks(5, 2)),
        scratch_shapes=[room(HALO + 8)] * 4 + [room(count2)] * 5,
        compiler_params=limit,
        name="down",
    )(own, outer, near2, fluid2, pin2, fluid3, pin3)
    copies = jnp.broadcast_to(parcel, (parts,) + parcel.shape)
    packed = lax.all_to_all(copies, ("gx", "gy", "gz"), 0, 0, tiled=True)
    depth3 = parts * count3
    mine = pl.pallas_call(
        functools.partial(up_kernel, groups, by, share),
        out_shape=blocks(peers, share),
        scratch_shapes=[room(planes), room(planes), room(count2), room(count2), room(count2)]
        + [pltpu.VMEM((rows, LANES), F32) for rows in (depth3, depth3, depth3 + 3 * NEAR)]
        + [room(share)],
        compiler_params=limit,
        name="up",
    )(packed, near1, far1, far2)
    return pl.pallas_call(
        finish_kernel,
        out_shape=jax.ShapeDtypeStruct((bx, by, depth), F32),
        compiler_params=limit,
        name="finish",
    )(exchange(mine))


def one_tile_planes(mesh, viscosity):
    split = (mesh.shape["gx"], mesh.shape["gy"])
    depth = viscosity.shape[2]
    fits = viscosity.shape[:2] == PLANE and split == SPLIT
    return fits and depth == 4 * LANES and depth // mesh.shape["gz"] == LANES


def solution(mesh):
    placed = (P("gx", "gy", "gz"), P("gx", "gy", "gz"), P("gx", "gy", "gz"))

    def cycle(residual_q2, viscosity, pinned):
        chosen = whole_planes if one_tile_planes(mesh, viscosity) else per_device
        return jax.shard_map(
            chosen, mesh=mesh, in_specs=placed, out_specs=P("gx", "gy", "gz"), check_vma=False
        )(residual_q2, viscosity, pinned)

    return cycle
```

```python
import functools

import jax
import jax.numpy as jnp
from jax import lax
from jax.experimental import pallas as pl
from jax.experimental.pallas import tpu as pltpu
from jax.sharding import PartitionSpec as P

NU = 3


OMEGA = 0.6


def with_halo(block, sides, width):
    for axis, dim in sides:
        count = lax.axis_size(axis)
        forward = [(i, i + 1) for i in range(count - 1)]
        backward = [(target, source) for source, target in forward]
        low = lax.ppermute(
            lax.slice_in_dim(block, block.shape[dim] - width, None, axis=dim), axis, forward
        )
        high = lax.ppermute(lax.slice_in_dim(block, 0, width, axis=dim), axis, backward)
        block = jnp.concatenate([low, block, high], axis=dim)
    return block


def coarsen(x):
    a, b, c = x.shape
    return x.reshape(a // 2, 2, b // 2, 2, c // 2, 2).sum(axis=(1, 3, 5))


def refine(x):
    return jnp.repeat(jnp.repeat(jnp.repeat(x, 2, 0), 2, 1), 2, 2)


def extended(field):
    return with_halo(field, (("gx", 0), ("gy", 1), ("gz", 2)), 1)


def shifted(padded):
    return [
        padded[2:, 1:-1, 1:-1],
        padded[:-2, 1:-1, 1:-1],
        padded[1:-1, 2:, 1:-1],
        padded[1:-1, :-2, 1:-1],
        padded[1:-1, 1:-1, 2:],
        padded[1:-1, 1:-1, :-2],
    ]


def neighbours(field):
    return shifted(extended(field))


def harmonic(fluid, near, factor):
    total = fluid + near
    return jnp.where(total > 0, factor * 2.0 * fluid * near / jnp.where(total > 0, total, 1.0), 0.0)


def couplings(fluid, factor):
    return [harmonic(fluid, near, factor) for near in neighbours(fluid)]


def apply_op(field, weights, diag):
    total = diag * field
    for weight, near in zip(weights, neighbours(field)):
        total = total - weight * near
    return total


def presmooth(rhs, weights, diag):
    corr = OMEGA * rhs / diag
    for sweep in range(NU - 1):
        corr = corr + OMEGA * (rhs - apply_op(corr, weights, diag)) / diag
    return corr


def postsmooth(corr, rhs, weights, diag):
    for sweep in range(NU):
        corr = corr + OMEGA * (rhs - apply_op(corr, weights, diag)) / diag
    return corr


def tridiag(coeffs, rhs):
    solved = lax.linalg.tridiagonal_solve(coeffs[0], coeffs[1], coeffs[2], rhs[..., None])[..., 0]
    last = rhs.ndim - 1
    shift_col = jnp.sum(rhs, axis=last, keepdims=True) / jnp.sum(
        coeffs[3], axis=last, keepdims=True
    )
    return solved + shift_col


def prepare_columns(weights, diag):
    lower = -weights[5]
    upper = -weights[4]
    across = diag + lower + upper
    return (
        lax.all_gather(lower, "gz", axis=2, tiled=True),
        lax.all_gather(diag, "gz", axis=2, tiled=True),
        lax.all_gather(upper, "gz", axis=2, tiled=True),
        lax.all_gather(across, "gz", axis=2, tiled=True),
    )


def column_solve(rhs, coeffs):
    depth = rhs.shape[2]
    whole = lax.all_gather(rhs, "gz", axis=2, tiled=True)
    solved = tridiag(coeffs, whole)
    return lax.dynamic_slice_in_dim(solved, lax.axis_index("gz") * depth, depth, 2)


def per_device(residual_q2, viscosity, pinned):
    fluid1 = 1.0 / viscosity
    pin1 = 4.0 * pinned.astype(jnp.float32) * fluid1
    rhs1 = coarsen(residual_q2.astype(jnp.float32))
    fluid2 = coarsen(fluid1) / 8.0
    pin2 = coarsen(pin1) / 4.0
    fluid3 = coarsen(fluid2) / 8.0
    pin3 = coarsen(pin2) / 4.0
    weights1 = couplings(fluid1, 1.0)
    weights2 = couplings(fluid2, 2.0)
    weights3 = couplings(fluid3, 4.0)
    diag1 = sum(weights1) + pin1
    diag2 = sum(weights2) + pin2
    diag3 = sum(weights3) + pin3
    coeffs = prepare_columns(weights3, diag3)
    corr1 = presmooth(rhs1, weights1, diag1)
    rhs2 = coarsen(rhs1 - apply_op(corr1, weights1, diag1))
    corr2 = presmooth(rhs2, weights2, diag2)
    rhs3 = coarsen(rhs2 - apply_op(corr2, weights2, diag2))
    corr3 = column_solve(rhs3, coeffs)
    corr3 = corr3 + column_solve(rhs3 - apply_op(corr3, weights3, diag3), coeffs)
    corr2 = postsmooth(corr2 + refine(corr3), rhs2, weights2, diag2)
    corr1 = postsmooth(corr1 + refine(corr2), rhs1, weights1, diag1)
    return diag1 * corr1


PLANE = (32, 32)
SPLIT = (2, 4)
ROWS = 8
LANES = 128
HALO = 16
NEAR = 8
PIECE = 8
TINY = 1e-30
F32 = jnp.float32


def iota(shape, dim):
    return lax.broadcasted_iota(jnp.int32, shape, dim)


def dot01(field, chosen):
    total = None
    rest = field
    for part in range(3):
        piece = rest.astype(jnp.bfloat16)
        term = jnp.dot(piece, chosen, preferred_element_type=F32)
        total = term if total is None else total + term
        if part < 2:
            rest = rest - piece.astype(F32)
    return total


def dot10(chosen, field):
    total = None
    rest = field
    for part in range(3):
        piece = rest.astype(jnp.bfloat16)
        term = lax.dot_general(
            chosen, piece, (((1,), (1,)), ((), ())), preferred_element_type=F32
        )
        total = term if total is None else total + term
        if part < 2:
            rest = rest - piece.astype(F32)
    return total


def where01(condition):
    return jnp.where(condition, 1.0, 0.0).astype(jnp.bfloat16)


def loop(low, high, size, body):
    for plane in range(low, high, size):
        body(plane, min(size, high - plane))


def inverse_of(field):
    first = pl.reciprocal(field, approx=True)
    return first * (2.0 - field * first)


class Level:
    def __init__(self, level):
        self.ny = PLANE[1] >> level
        self.xs = 4 >> level
        self.factor = float(2**level)

    def masks(self, shape):
        lane = iota(shape, 2)
        row = iota(shape, 1)
        within = (lane // self.ny) % self.xs
        y = lane % self.ny
        last_x = (row == ROWS - 1) & (within == self.xs - 1)
        return within, y == self.ny - 1, last_x

    def next_x(self, field):
        within = (iota(field.shape, 2) // self.ny) % self.xs
        moved = pltpu.roll(field, LANES - self.ny, 2)
        return jnp.where(within == self.xs - 1, pltpu.roll(moved, ROWS - 1, 1), moved)

    def last_x(self, field):
        within = (iota(field.shape, 2) // self.ny) % self.xs
        moved = pltpu.roll(field, self.ny, 2)
        return jnp.where(within == 0, pltpu.roll(moved, 1, 1), moved)

    def next_y(self, field):
        return pltpu.roll(field, LANES - 1, 2)

    def last_y(self, field):
        return pltpu.roll(field, 1, 2)

    def spread(self, field, scaled, plane, count):
        mid = field[1:-1]
        near = (
            self.next_x(mid), self.last_x(mid), self.next_y(mid), self.last_y(mid),
            field[2:], field[:-2],
        )
        terms = [weight[pl.ds(plane, count)] * value for weight, value in zip(scaled, near)]
        return mid, ((terms[0] + terms[1]) + (terms[2] + terms[3])) + (terms[4] + terms[5])


def mean_of(fluid, near, factor):
    return ((factor * 2.0) * fluid * near) * inverse_of(jnp.maximum(fluid + near, TINY))


def set_level(level, low, high, fluid, pin, rhs, fields):
    scaled, start, diag = fields

    def body(plane, count):
        wide = fluid[pl.ds(plane - 1, count + 2)]
        mid = wide[1:-1]
        within, end_y, end_x = level.masks(mid.shape)
        to_x = jnp.where(end_x, 0.0, mean_of(mid, level.next_x(mid), level.factor))
        to_y = jnp.where(end_y, 0.0, mean_of(mid, level.next_y(mid), level.factor))
        to_z = mean_of(wide[:-1], wide[1:], level.factor)
        weights = (to_x, level.last_x(to_x), to_y, level.last_y(to_y), to_z[1:], to_z[:-1])
        total = (
            (weights[0] + weights[1])
            + (weights[2] + weights[3])
            + (weights[4] + weights[5])
            + pin[pl.ds(plane, count)]
        )
        gain = OMEGA * inverse_of(jnp.maximum(total, TINY))
        for target, weight in zip(scaled, weights):
            target[pl.ds(plane, count)] = gain * weight
        start[pl.ds(plane, count)] = gain * rhs[pl.ds(plane, count)]
        diag[pl.ds(plane, count)] = total

    loop(low, high, PIECE, body)


def swept(level, plane, count, fields, source, shift=0):
    scaled, start, _ = fields
    mid, total = level.spread(source[pl.ds(plane - 1, count + 2)], scaled, plane - shift, count)
    return (1.0 - OMEGA) * mid + (start[pl.ds(plane - shift, count)] + total)


def sweep(level, low, high, fields, source, target, shift=0):
    def body(plane, count):
        target[pl.ds(plane, count)] = swept(level, plane, count, fields, source, shift)

    loop(low, high, PIECE, body)


def pair_sum(field):
    half = field.reshape((field.shape[0] // 2, 2) + field.shape[1:])
    return half[:, 0] + half[:, 1]


def coarse_residual(level, low, high, fields, corr, target):
    scaled, start, diag = fields

    def body(plane, count):
        mid, total = level.spread(corr[pl.ds(plane - 1, count + 2)], scaled, plane, count)
        rest = (start[pl.ds(plane, count)] + total) - OMEGA * mid
        rest = rest * (diag[pl.ds(plane, count)] * (1.0 / OMEGA))
        target[pl.ds((plane - low) // 2, count // 2)] = pair_sum(rest)

    loop(low, high, PIECE, body)


def lanes_down(level):
    fine = iota((LANES, LANES), 0)
    coarse = iota((LANES, LANES), 1)
    ny, xs = PLANE[1] >> level, 4 >> level
    half = xs // 2
    same_x = ((fine // ny) % xs) // 2 == (coarse // (ny // 2)) % half
    same_y = (fine % ny) // 2 == coarse % (ny // 2)
    return where01((fine < ny * xs) & same_x & same_y)


def in_lanes(field, chosen):
    flat = field.reshape(field.shape[0] * ROWS, LANES)
    return dot01(flat, chosen).reshape(field.shape)


def path_of(group):
    nx, ny = SPLIT
    row, column = 0, 0
    for index in range(group + 1):
        columns = list(range(ny)) if column == 0 else list(range(ny))[::-1]
        if index % 2 == 0:
            path = [(row, at) for at in columns] + [(1 - row, at) for at in columns[::-1]]
        else:
            path = []
            for at in columns:
                path += [(row, at), (1 - row, at)]
                row = 1 - row
        row, column = path[-1]
    return [row * ny + column for row, column in path]


def lookup(table, index):
    found = table[0]
    for at, value in enumerate(table[1:], 1):
        found = jnp.where(index == at, value, found)
    return found


def slot_of(peer):
    return SPLIT[0] * SPLIT[1] - 1 - peer


def own_slot_of(rank):
    groups = range(lax.axis_size("gz"))
    return lookup([slot_of(path_of(group)[rank]) for group in groups], lax.axis_index("gz"))


def exchange(field):
    peers, groups = SPLIT[0] * SPLIT[1], lax.axis_size("gz")
    order = sorted(range(peers), key=slot_of)
    members = [[peer * groups + group for peer in order] for group in range(groups)]
    axes = ("gx", "gy", "gz")
    return lax.all_to_all(field, axes, 0, 0, axis_index_groups=members, tiled=True)


def slabs_of(groups):
    peers = SPLIT[0] * SPLIT[1]
    return [
        group * peers + path_of(group).index(peer) for peer in range(peers) for group in range(groups)
    ]


def own_slab():
    nx, ny = SPLIT
    groups = lax.axis_size("gz")
    device = (lax.axis_index("gx") * ny + lax.axis_index("gy")) * groups + lax.axis_index("gz")
    return lookup(slabs_of(groups), device)


def devices_of(groups):
    slabs = slabs_of(groups)
    return [slabs.index(slab) for slab in range(len(slabs))]


def prepare_kernel(share, res_ref, fluid_ref, pin_ref, out_ref):
    bx, by, depth = fluid_ref.shape
    cells = bx * by
    groups = bx // 4
    order = [x for low in range(4) for x in range(low, bx, 4)]
    fine = iota((cells, 4 * cells), 1)
    x, y = fine // (4 * by), (fine % (2 * by)) // 2
    chosen = where01((x % 4) * (groups * by) + (x // 4) * by + y == iota((cells, 4 * cells), 0))
    wide = lax.dot_general(
        chosen, res_ref[...], (((1,), (0,)), ((), ())), preferred_element_type=F32
    )
    rhs = dot10(where01(iota((depth, 2 * depth), 1) // 2 == iota((depth, 2 * depth), 0)), wide)

    def turned(field_ref):
        field = jnp.concatenate([field_ref[x : x + 1] for x in order], axis=0)
        return field.reshape(cells, depth).T

    fluid, pin = turned(fluid_ref), turned(pin_ref)
    for rank in range(depth // share):
        peer, begin = own_slot_of(rank), rank * share
        for index, field in enumerate((fluid, rhs, pin)):
            out_ref[peer, index * share : (index + 1) * share] = field[begin : begin + share]


def spread_kernel(groups, by, gathered, own, inner, outer, straight):
    for start in range(0, own.shape[0], ROWS):
        place(gathered, start, straight, start, groups, by)
    share = own.shape[0] // 3
    odd = own_slab() % 2 == 1
    for index in range(3):
        for plane in range(share):
            at = jnp.where(odd, share - 1 - plane, plane)
            own[index * share + plane] = straight[index * share + at]
    for target, drop in ((inner, 0), (outer, share - 1)):
        row = 0
        for index in range(3):
            for plane in range(share):
                if index == 0 or plane != drop:
                    target[row] = own[index * share + plane]
                    row += 1


def place(gathered, row, target, plane, groups, by):
    group = (iota((ROWS, LANES), 1) // by) % groups
    nx, ny = SPLIT
    for ix in range(nx):
        found = [gathered[slot_of(ix * ny + iy), pl.ds(row, ROWS), :] for iy in range(ny)]
        for part in range(groups):
            total = found[part]
            for iy in range(ny):
                if iy != part:
                    moved = pltpu.roll(found[iy], (by * (iy - part)) % LANES, 1)
                    total = jnp.where(group == iy, moved, total)
            target[pl.ds(plane, ROWS), ix * groups + part, :] = total


def near_kernel(
    depth,
    own, inner,
    saved1, saved2, fluid2, pin2, fluid3, pin3,
    fluid1, rhs1, pin1, other1, rhs2, sums,
):
    row = 0
    for index, target in enumerate((fluid1, rhs1, pin1)):
        target[0:depth] = own[index * depth : (index + 1) * depth]
        count = HALO if index == 0 else HALO - 1
        for plane in range(count):
            target[depth + plane] = inner[row + count - 1 - plane]
        if count < HALO:
            target[depth + count] = jnp.zeros((ROWS, LANES), F32)
        row += count
    fine, coarse = Level(0), Level(1)
    down1, down2 = lanes_down(0), lanes_down(1)
    fields1, corr1 = (saved1[0:6], saved1[6], saved1[7]), saved1[8]
    fields2 = (saved2[0:6], saved2[6], saved2[7])
    planes = depth + HALO
    set_level(fine, 1, planes - 1, fluid1, pin1, rhs1, fields1)
    sweep(fine, 2, planes - 2, fields1, fields1[1], other1)
    sweep(fine, 3, planes - 3, fields1, other1, corr1)
    coarse_residual(fine, 4, planes - 4, fields1, corr1, sums)
    count2 = planes // 2
    for source, target, share in ((fluid1, fluid2, 8.0), (pin1, pin2, 4.0)):
        target[NEAR : NEAR + count2] = in_lanes(pair_sum(source[...]), down1) * (1.0 / share)
    low2, high2 = NEAR + 2, NEAR + count2 - 2
    rhs2[low2:high2] = in_lanes(sums[0 : high2 - low2], down1)
    set_level(coarse, low2, high2, fluid2, pin2, rhs2, fields2)
    for source, target, scale in ((fluid2, fluid3, 0.125), (pin2, pin3, 0.25)):
        target[...] = in_lanes(pair_sum(source[NEAR : NEAR + depth // 2]), down2) * scale


def down_kernel(
    depth,
    own, outer, near2, near_fluid2, near_pin2, fluid3, pin3,
    saved1, saved2,
    packed,
    fluid1, rhs1, pin1, other1, fluid2, rhs2, pin2, other2, sums,
):
    planes = fluid1.shape[0]
    row = 0
    for index, target in enumerate((fluid1, rhs1, pin1)):
        count = HALO if index == 0 else HALO - 1
        if count < HALO:
            target[0] = jnp.zeros((ROWS, LANES), F32)
        for plane in range(count):
            target[HALO - count + plane] = outer[row + count - 1 - plane]
        row += count
        target[HALO:planes] = own[index * depth : index * depth + planes - HALO]

    fine, coarse = Level(0), Level(1)
    down1, down2 = lanes_down(0), lanes_down(1)
    fields1, corr1 = (saved1[0:6], saved1[6], saved1[7]), saved1[8]
    fields2, corr2 = (saved2[0:6], saved2[6], saved2[7]), saved2[8]
    set_level(fine, 1, planes - 1, fluid1, pin1, rhs1, fields1)
    sweep(fine, 2, planes - 2, fields1, fields1[1], other1)
    sweep(fine, 3, planes - 3, fields1, other1, corr1)
    count2 = depth // 2 + 2 * NEAR
    low2, done, high2 = 2, NEAR + 2, count2 - 2
    coarse_residual(fine, 2 * low2, 2 * done, fields1, corr1, sums)
    for source, ready, target, share in (
        (fluid1, near_fluid2, fluid2, 8.0), (pin1, near_pin2, pin2, 4.0)
    ):
        target[0:NEAR] = in_lanes(pair_sum(source[0:HALO]), down1) * (1.0 / share)
        target[NEAR : done + 1] = ready[NEAR : done + 1]
    rhs2[low2:done] = in_lanes(sums[0 : done - low2], down1)
    set_level(coarse, low2, done, fluid2, pin2, rhs2, fields2)
    for source, target in zip(near2, saved2[0:8]):
        target[done:high2] = source[done:high2]
    sweep(coarse, low2 + 1, high2 - 1, fields2, fields2[1], other2)
    sweep(coarse, low2 + 2, high2 - 2, fields2, other2, corr2)
    coarse_residual(coarse, NEAR, NEAR + depth // 2, fields2, corr2, sums)
    count3 = depth // 4
    rhs3 = in_lanes(sums[0:count3], down2)
    lane = iota((count3, LANES), 1) // ROWS
    first = jnp.zeros((count3, LANES), F32)
    second = jnp.zeros((count3, LANES), F32)
    for row in range(ROWS):
        first = jnp.where(lane == row, rhs3[:, row, :], first)
        first = jnp.where(lane == ROWS + row, fluid3[:, row, :], first)
        second = jnp.where(lane % ROWS == row, pin3[:, row, :], second)
    odd = own_slab() % 2 == 1

    def ordered(field):
        back = [field[row : row + 1] for row in reversed(range(count3))]
        return jnp.where(odd, jnp.concatenate(back, axis=0), field)

    first, second = ordered(first), ordered(second)
    packed[0] = first[0:2]
    packed[1] = first[2:4]
    packed[2] = jnp.where(lane[0:2] < ROWS, second[0:2], second[2:4])
    lane = iota((1, LANES), 1) // (LANES // 4)
    for index, plane in enumerate((NEAR + depth // 2 - 5, NEAR + 4)):
        for half in range(2):
            row = jnp.zeros((1, LANES), F32)
            for quarter in range(4):
                at = half * 4 + quarter
                row = jnp.where(lane == quarter, corr2[plane, at : at + 1, :], row)
            packed[3 + index, half : half + 1, :] = row


def rolled(field, shift):
    count = field.shape[0]
    shift %= count
    if shift % ROWS:
        return pltpu.roll(field, shift, 0)
    return jnp.concatenate([field[count - shift :], field[: count - shift]], axis=0)


def columns(rhs, fluid, pin):
    depth = fluid.shape[0]
    z, lane = iota(fluid.shape, 0), iota(fluid.shape, 1)
    y, x = lane % ROWS, (lane // ROWS) % ROWS

    def next_x(field):
        return pltpu.roll(field, LANES - ROWS, 1)

    def next_y(field):
        return pltpu.roll(field, LANES - 1, 1)

    wz = jnp.where(z == depth - 1, 0.0, mean_of(fluid, rolled(fluid, -1), 4.0))
    wy = jnp.where(y == ROWS - 1, 0.0, mean_of(fluid, next_y(fluid), 4.0))
    wx = jnp.where(x == ROWS - 1, 0.0, mean_of(fluid, next_x(fluid), 4.0))
    across = (wx + pltpu.roll(wx, ROWS, 1)) + (wy + pltpu.roll(wy, 1, 1)) + pin
    share = 1.0 / jnp.sum(across, axis=0, keepdims=True)

    above, below, own = rolled(wz, 1), wz, across
    steps = []
    stride, right = 1, rhs
    while stride < depth:
        inverse = inverse_of(above + below + own)
        up = above * rolled(inverse, stride)
        down = below * rolled(inverse, -stride)
        own = own + up * rolled(own, stride) + down * rolled(own, -stride)
        above = up * rolled(above, stride)
        below = down * rolled(below, -stride)
        right = right + up * rolled(right, stride) + down * rolled(right, -stride)
        steps.append((stride, up, down))
        stride *= 2
    inverse = inverse_of(above + below + own)

    def mean(right):
        return jnp.sum(right, axis=0, keepdims=True) * share

    corr = right * inverse + mean(rhs)
    flow_x = wx * (next_x(corr) - corr)
    flow_y = wy * (next_y(corr) - corr)
    flow_z = wz * (rolled(corr, -1) - corr)
    rest = (
        (rhs - pin * corr)
        + (flow_x - pltpu.roll(flow_x, ROWS, 1))
        + (flow_y - pltpu.roll(flow_y, 1, 1))
        + (flow_z - rolled(flow_z, 1))
    )
    right = rest
    for stride, up, down in steps:
        right = right + up * rolled(right, stride) + down * rolled(right, -stride)
    return (corr + mean(rest)) + right * inverse


def up_kernel(
    groups, by, depth,
    packed, near1, far1, far2,
    out_ref,
    one1, two1, one2, two2, lifted, first, second, solved, final,
):
    count3 = depth // 4
    shares = packed.shape[0]
    peers = SPLIT[0] * SPLIT[1]
    devices = devices_of(shares // peers)
    for slab, index in enumerate(devices):
        row = slab * count3
        first[row : row + 2] = packed[index, 0]
        first[row + 2 : row + 4] = packed[index, 1]
        both = packed[index, 2]
        second[row : row + 2] = both
        second[row + 2 : row + 4] = pltpu.roll(both, LANES // 2, 1)
    half = iota((shares * count3, LANES), 1) < LANES // 2

    def low_half(field):
        return jnp.where(half, field, pltpu.roll(field, LANES // 2, 1))

    def high_half(field):
        return jnp.where(half, pltpu.roll(field, LANES // 2, 1), field)

    solved[NEAR : NEAR + shares * count3] = columns(
        low_half(first[...]), high_half(first[...]), low_half(second[...])
    )
    solved[0:NEAR] = jnp.zeros((NEAR, LANES), F32)
    solved[NEAR + shares * count3 :] = jnp.zeros((2 * NEAR, LANES), F32)

    nx, ny = SPLIT
    part = own_slab()
    count = count3 + 2 * NEAR
    tall = solved[pl.ds(part * count3, count + count3), :]
    fine, coarse = Level(0), Level(1)
    cell = iota((LANES, LANES), 0)
    lane = iota((LANES, LANES), 1)
    spread = where01((cell < ROWS) & (cell == (lane % coarse.ny) // 2))
    rows = tall.shape[0]
    turned = [tall] + [pltpu.roll(tall, LANES - ROWS * row, 1) for row in range(1, ROWS)]
    wide = dot01(jnp.concatenate(turned, axis=0), spread)
    for row in range(ROWS):
        lifted[0:rows, row, :] = wide[row * rows : (row + 1) * rows]

    odd = part % 2 == 1

    def lifted_to(plane):
        parent = plane // 2 + NEAR // 2
        return lifted[jnp.where(odd, count - 1 - parent, parent)]

    near_fields, near_corr1 = (near1[0:6], near1[6], near1[7]), near1[8]
    far_fields, far_corr1 = (far1[0:6], far1[6], far1[7]), far1[8]
    fields2, corr2 = (far2[0:6], far2[6], far2[7]), far2[8]
    low, high = NEAR - 4, NEAR + depth // 2 + 4
    reach = depth // 2 + NEAR
    quarter = iota((ROWS, LANES), 1) // (LANES // 4)
    row = iota((ROWS, LANES), 0)

    def unpacked(index, which):
        pair = packed[lookup(devices, jnp.clip(index, 0, shares - 1)), which]
        total = None
        for shift in range(4):
            moved = pltpu.roll(pair, shift * (LANES // 4), 1)
            wide = jnp.where(row < 4, moved[0:1, :], moved[1:2, :])
            kept = jnp.where((quarter - shift) % 4 == row % 4, wide, 0.0)
            total = kept if total is None else total + kept
        return total

    one2[low - 1] = unpacked(jnp.where(odd, part + 1, part - 1), 4) + lifted_to(low - 1)
    for plane in range(low, high):
        one2[plane] = corr2[plane] + lifted_to(plane)
    one2[high] = unpacked(jnp.where(odd, part - 1, part + 1), 3) + lifted_to(high)
    sweep(coarse, NEAR - 4, reach + 4, fields2, one2, two2)
    sweep(coarse, NEAR - 3, reach + 3, fields2, two2, one2)
    sweep(coarse, NEAR - 2, reach + 2, fields2, one2, two2)

    fine_lane, coarse_lane = iota((LANES, LANES), 1), iota((LANES, LANES), 0)
    x_of = (fine_lane // fine.ny) // 2
    y_of = (fine_lane % fine.ny) // 2
    up = where01(coarse_lane == x_of * coarse.ny + y_of)
    lifted[0 : depth // 2 + 4] = in_lanes(two2[NEAR - 2 : reach + 2], up)
    parents = lifted[0 : depth // 2 + 4]
    twice = jnp.broadcast_to(parents[:, None], (parents.shape[0], 2, ROWS, LANES))
    low, high = HALO - 4, HALO + depth + 4
    turn = HALO + 3
    for plane in range(low, high):
        corr = far_corr1[plane] if plane < turn else near_corr1[plane - HALO]
        one1[plane] = corr + lifted[(plane - low) // 2]
    reach = depth + HALO
    for more, source, target in ((2, one1, two1), (1, two1, one1)):
        sweep(fine, HALO - more, turn, far_fields, source, target)
        sweep(fine, turn, reach + more, near_fields, source, target, HALO)

    def last(fields, shift):
        def body(plane, count):
            value = swept(fine, plane, count, fields, one1, shift)
            value = value * fields[2][pl.ds(plane - shift, count)]
            for index in range(count):
                at = plane - HALO + index
                final[jnp.where(odd, depth - 1 - at, at)] = value[index]

        return body

    loop(HALO, turn, PIECE, last(far_fields, 0))
    loop(turn, reach, PIECE, last(near_fields, HALO))

    group = (iota((depth, LANES), 1) // by) % groups
    for ix in range(nx):
        scaled = [final[:, ix * groups + part, :] for part in range(groups)]
        for iy in range(ny):
            total = scaled[iy]
            for part in range(groups):
                if part != iy:
                    moved = pltpu.roll(scaled[part], (by * (part - iy)) % LANES, 1)
                    total = jnp.where(group == part, moved, total)
            out_ref[slot_of(ix * ny + iy)] = total


def finish_kernel(blocks, out_ref):
    bx, by, depth = out_ref.shape
    peers = blocks.shape[0]
    ordered = jnp.concatenate([blocks[own_slot_of(rank)] for rank in range(peers)], axis=0)
    turned = ordered.T
    for x in range(bx):
        row = ((x % 4) * (bx // 4) + x // 4) * by
        out_ref[x] = turned[row : row + by]


def whole_planes(residual_q2, viscosity, pinned):
    bx, by, depth = viscosity.shape
    groups = bx // 4
    peers = SPLIT[0] * SPLIT[1]
    share = depth // peers
    planes = share + 2 * HALO
    count2 = share // 2 + 2 * NEAR
    limit = pltpu.CompilerParams(vmem_limit_bytes=32 * 2**20)

    def flat(rows):
        return jax.ShapeDtypeStruct((rows, LANES), F32)

    def blocks(count, rows):
        return jax.ShapeDtypeStruct((count, rows, LANES), F32)

    def room(count):
        return pltpu.VMEM((count, ROWS, LANES), F32)

    fluid = 1.0 / viscosity
    pin = 4.0 * pinned.astype(F32) * fluid
    parcels = pl.pallas_call(
        functools.partial(prepare_kernel, share),
        out_shape=blocks(peers, 3 * share),
        compiler_params=limit,
        name="prepare",
    )(residual_q2.reshape(4 * bx * by, 2 * depth), fluid, pin)
    own, inner, outer = pl.pallas_call(
        functools.partial(spread_kernel, groups, by),
        out_shape=(blocks(3 * share, ROWS),) + (blocks(3 * HALO - 2, ROWS),) * 2,
        scratch_shapes=[room(3 * share)],
        compiler_params=limit,
        name="spread",
    )(exchange(parcels))
    length = lax.axis_size("gz")
    parts = length * peers

    device = devices_of(length)

    def swap(field, first):
        pairs = [(device[i], device[i + 1]) for i in range(first, parts - 1, 2)]
        return lax.ppermute(field, ("gx", "gy", "gz"), pairs + [pair[::-1] for pair in pairs])

    outer, inner = swap(outer, 1), swap(inner, 0)
    count3 = share // 4
    near1, near2, far1, far2 = (
        (blocks(count, ROWS),) * fields
        for count, fields in ((share + HALO, 9), (count2, 8), (HALO + 8, 9), (count2, 9))
    )
    near1, near2, fluid2, pin2, fluid3, pin3 = pl.pallas_call(
        functools.partial(near_kernel, share),
        out_shape=(near1, near2) + (blocks(count2, ROWS),) * 2 + (blocks(count3, ROWS),) * 2,
        scratch_shapes=[room(share + HALO)] * 4 + [room(count2)] * 2,
        compiler_params=limit,
        name="near",
    )(own, inner)
    far1, far2, parcel = pl.pallas_call(
        functools.partial(down_kernel, share),
        out_shape=(far1, far2, blocks(5, 2)),
        scratch_shapes=[room(HALO + 8)] * 4 + [room(count2)] * 5,
        compiler_params=limit,
        name="down",
    )(own, outer, near2, fluid2, pin2, fluid3, pin3)
    copies = jnp.broadcast_to(parcel, (parts,) + parcel.shape)
    packed = lax.all_to_all(copies, ("gx", "gy", "gz"), 0, 0, tiled=True)
    depth3 = parts * count3
    mine = pl.pallas_call(
        functools.partial(up_kernel, groups, by, share),
        out_shape=blocks(peers, share),
        scratch_shapes=[room(planes), room(planes), room(count2), room(count2), room(count2)]
        + [pltpu.VMEM((rows, LANES), F32) for rows in (depth3, depth3, depth3 + 3 * NEAR)]
        + [room(share)],
        compiler_params=limit,
        name="up",
    )(packed, near1, far1, far2)
    return pl.pallas_call(
        finish_kernel,
        out_shape=jax.ShapeDtypeStruct((bx, by, depth), F32),
        compiler_params=limit,
        name="finish",
    )(exchange(mine))


def one_tile_planes(mesh, viscosity):
    split = (mesh.shape["gx"], mesh.shape["gy"])
    depth = viscosity.shape[2]
    fits = viscosity.shape[:2] == PLANE and split == SPLIT
    return fits and depth == 4 * LANES and depth // mesh.shape["gz"] == LANES


def solution(mesh):
    placed = (P("gx", "gy", "gz"), P("gx", "gy", "gz"), P("gx", "gy", "gz"))

    def cycle(residual_q2, viscosity, pinned):
        chosen = whole_planes if one_tile_planes(mesh, viscosity) else per_device
        return jax.shard_map(
            chosen, mesh=mesh, in_specs=placed, out_specs=P("gx", "gy", "gz"), check_vma=False
        )(residual_q2, viscosity, pinned)

    return cycle
```

```python
import functools

import jax
import jax.numpy as jnp
from jax import lax
from jax.experimental import pallas as pl
from jax.experimental.pallas import tpu as pltpu
from jax.sharding import PartitionSpec as P

NU = 3


OMEGA = 0.6


def with_halo(block, sides, width):
    for axis, dim in sides:
        count = lax.axis_size(axis)
        forward = [(i, i + 1) for i in range(count - 1)]
        backward = [(target, source) for source, target in forward]
        low = lax.ppermute(
            lax.slice_in_dim(block, block.shape[dim] - width, None, axis=dim), axis, forward
        )
        high = lax.ppermute(lax.slice_in_dim(block, 0, width, axis=dim), axis, backward)
        block = jnp.concatenate([low, block, high], axis=dim)
    return block


def coarsen(x):
    a, b, c = x.shape
    return x.reshape(a // 2, 2, b // 2, 2, c // 2, 2).sum(axis=(1, 3, 5))


def refine(x):
    return jnp.repeat(jnp.repeat(jnp.repeat(x, 2, 0), 2, 1), 2, 2)


def extended(field):
    return with_halo(field, (("gx", 0), ("gy", 1), ("gz", 2)), 1)


def shifted(padded):
    return [
        padded[2:, 1:-1, 1:-1],
        padded[:-2, 1:-1, 1:-1],
        padded[1:-1, 2:, 1:-1],
        padded[1:-1, :-2, 1:-1],
        padded[1:-1, 1:-1, 2:],
        padded[1:-1, 1:-1, :-2],
    ]


def neighbours(field):
    return shifted(extended(field))


def harmonic(fluid, near, factor):
    total = fluid + near
    return jnp.where(total > 0, factor * 2.0 * fluid * near / jnp.where(total > 0, total, 1.0), 0.0)


def couplings(fluid, factor):
    return [harmonic(fluid, near, factor) for near in neighbours(fluid)]


def apply_op(field, weights, diag):
    total = diag * field
    for weight, near in zip(weights, neighbours(field)):
        total = total - weight * near
    return total


def presmooth(rhs, weights, diag):
    corr = OMEGA * rhs / diag
    for sweep in range(NU - 1):
        corr = corr + OMEGA * (rhs - apply_op(corr, weights, diag)) / diag
    return corr


def postsmooth(corr, rhs, weights, diag):
    for sweep in range(NU):
        corr = corr + OMEGA * (rhs - apply_op(corr, weights, diag)) / diag
    return corr


def tridiag(coeffs, rhs):
    solved = lax.linalg.tridiagonal_solve(coeffs[0], coeffs[1], coeffs[2], rhs[..., None])[..., 0]
    last = rhs.ndim - 1
    shift_col = jnp.sum(rhs, axis=last, keepdims=True) / jnp.sum(
        coeffs[3], axis=last, keepdims=True
    )
    return solved + shift_col


def prepare_columns(weights, diag):
    lower = -weights[5]
    upper = -weights[4]
    across = diag + lower + upper
    return (
        lax.all_gather(lower, "gz", axis=2, tiled=True),
        lax.all_gather(diag, "gz", axis=2, tiled=True),
        lax.all_gather(upper, "gz", axis=2, tiled=True),
        lax.all_gather(across, "gz", axis=2, tiled=True),
    )


def column_solve(rhs, coeffs):
    depth = rhs.shape[2]
    whole = lax.all_gather(rhs, "gz", axis=2, tiled=True)
    solved = tridiag(coeffs, whole)
    return lax.dynamic_slice_in_dim(solved, lax.axis_index("gz") * depth, depth, 2)


def per_device(residual_q2, viscosity, pinned):
    fluid1 = 1.0 / viscosity
    pin1 = 4.0 * pinned.astype(jnp.float32) * fluid1
    rhs1 = coarsen(residual_q2.astype(jnp.float32))
    fluid2 = coarsen(fluid1) / 8.0
    pin2 = coarsen(pin1) / 4.0
    fluid3 = coarsen(fluid2) / 8.0
    pin3 = coarsen(pin2) / 4.0
    weights1 = couplings(fluid1, 1.0)
    weights2 = couplings(fluid2, 2.0)
    weights3 = couplings(fluid3, 4.0)
    diag1 = sum(weights1) + pin1
    diag2 = sum(weights2) + pin2
    diag3 = sum(weights3) + pin3
    coeffs = prepare_columns(weights3, diag3)
    corr1 = presmooth(rhs1, weights1, diag1)
    rhs2 = coarsen(rhs1 - apply_op(corr1, weights1, diag1))
    corr2 = presmooth(rhs2, weights2, diag2)
    rhs3 = coarsen(rhs2 - apply_op(corr2, weights2, diag2))
    corr3 = column_solve(rhs3, coeffs)
    corr3 = corr3 + column_solve(rhs3 - apply_op(corr3, weights3, diag3), coeffs)
    corr2 = postsmooth(corr2 + refine(corr3), rhs2, weights2, diag2)
    corr1 = postsmooth(corr1 + refine(corr2), rhs1, weights1, diag1)
    return diag1 * corr1


PLANE = (32, 32)
SPLIT = (2, 4)
ROWS = 8
LANES = 128
HALO = 16
NEAR = 8
PIECE = 8
TINY = 1e-30
F32 = jnp.float32


def iota(shape, dim):
    return lax.broadcasted_iota(jnp.int32, shape, dim)


def dot01(field, chosen):
    total = None
    rest = field
    for part in range(3):
        piece = rest.astype(jnp.bfloat16)
        term = jnp.dot(piece, chosen, preferred_element_type=F32)
        total = term if total is None else total + term
        if part < 2:
            rest = rest - piece.astype(F32)
    return total


def dot10(chosen, field):
    total = None
    rest = field
    for part in range(3):
        piece = rest.astype(jnp.bfloat16)
        term = lax.dot_general(
            chosen, piece, (((1,), (1,)), ((), ())), preferred_element_type=F32
        )
        total = term if total is None else total + term
        if part < 2:
            rest = rest - piece.astype(F32)
    return total


def where01(condition):
    return jnp.where(condition, 1.0, 0.0).astype(jnp.bfloat16)


def loop(low, high, size, body):
    for plane in range(low, high, size):
        body(plane, min(size, high - plane))


def inverse_of(field):
    first = pl.reciprocal(field, approx=True)
    return first * (2.0 - field * first)


class Level:
    def __init__(self, level):
        self.ny = PLANE[1] >> level
        self.xs = 4 >> level
        self.factor = float(2**level)

    def masks(self, shape):
        lane = iota(shape, 2)
        row = iota(shape, 1)
        within = (lane // self.ny) % self.xs
        y = lane % self.ny
        last_x = (row == ROWS - 1) & (within == self.xs - 1)
        return within, y == self.ny - 1, last_x

    def next_x(self, field):
        within = (iota(field.shape, 2) // self.ny) % self.xs
        moved = pltpu.roll(field, LANES - self.ny, 2)
        return jnp.where(within == self.xs - 1, pltpu.roll(moved, ROWS - 1, 1), moved)

    def last_x(self, field):
        within = (iota(field.shape, 2) // self.ny) % self.xs
        moved = pltpu.roll(field, self.ny, 2)
        return jnp.where(within == 0, pltpu.roll(moved, 1, 1), moved)

    def next_y(self, field):
        return pltpu.roll(field, LANES - 1, 2)

    def last_y(self, field):
        return pltpu.roll(field, 1, 2)

    def spread(self, source, scaled, plane, shift, count):
        field = source[pl.ds(plane - 1, count + 2)]
        mid = field[1:-1]
        rows = source.reshape(source.shape[0] * ROWS, LANES)
        ahead = rows[pl.ds(plane * ROWS + 1, count * ROWS)].reshape(mid.shape)
        behind = rows[pl.ds(plane * ROWS - 1, count * ROWS)].reshape(mid.shape)
        within = (iota(mid.shape, 2) // self.ny) % self.xs
        near = (
            pltpu.roll(jnp.where(within == 0, ahead, mid), LANES - self.ny, 2),
            pltpu.roll(jnp.where(within == self.xs - 1, behind, mid), self.ny, 2),
            self.next_y(mid),
            self.last_y(mid),
            field[2:],
            field[:-2],
        )
        terms = [weight[pl.ds(plane - shift, count)] * value for weight, value in zip(scaled, near)]
        return mid, ((terms[0] + terms[1]) + (terms[2] + terms[3])) + (terms[4] + terms[5])


def mean_of(fluid, near, factor):
    return ((factor * 2.0) * fluid * near) * inverse_of(jnp.maximum(fluid + near, TINY))


def set_level(level, low, high, fluid, pin, rhs, fields):
    scaled, start, diag = fields

    def body(plane, count):
        wide = fluid[pl.ds(plane - 1, count + 2)]
        mid = wide[1:-1]
        within, end_y, end_x = level.masks(mid.shape)
        to_x = jnp.where(end_x, 0.0, mean_of(mid, level.next_x(mid), level.factor))
        to_y = jnp.where(end_y, 0.0, mean_of(mid, level.next_y(mid), level.factor))
        to_z = mean_of(wide[:-1], wide[1:], level.factor)
        weights = (to_x, level.last_x(to_x), to_y, level.last_y(to_y), to_z[1:], to_z[:-1])
        total = (
            (weights[0] + weights[1])
            + (weights[2] + weights[3])
            + (weights[4] + weights[5])
            + pin[pl.ds(plane, count)]
        )
        gain = OMEGA * inverse_of(jnp.maximum(total, TINY))
        for target, weight in zip(scaled, weights):
            target[pl.ds(plane, count)] = gain * weight
        start[pl.ds(plane, count)] = gain * rhs[pl.ds(plane, count)]
        diag[pl.ds(plane, count)] = total

    loop(low, high, PIECE, body)


def swept(level, plane, count, fields, source, shift=0):
    scaled, start, _ = fields
    mid, total = level.spread(source, scaled, plane, shift, count)
    return (1.0 - OMEGA) * mid + (start[pl.ds(plane - shift, count)] + total)


def sweep(level, low, high, fields, source, target, shift=0):
    def body(plane, count):
        target[pl.ds(plane, count)] = swept(level, plane, count, fields, source, shift)

    loop(low, high, PIECE, body)


def pair_sum(field):
    half = field.reshape((field.shape[0] // 2, 2) + field.shape[1:])
    return half[:, 0] + half[:, 1]


def coarse_residual(level, low, high, fields, corr, target):
    scaled, start, diag = fields

    def body(plane, count):
        mid, total = level.spread(corr, scaled, plane, 0, count)
        rest = (start[pl.ds(plane, count)] + total) - OMEGA * mid
        rest = rest * (diag[pl.ds(plane, count)] * (1.0 / OMEGA))
        target[pl.ds((plane - low) // 2, count // 2)] = pair_sum(rest)

    loop(low, high, PIECE, body)


def lanes_down(level):
    fine = iota((LANES, LANES), 0)
    coarse = iota((LANES, LANES), 1)
    ny, xs = PLANE[1] >> level, 4 >> level
    half = xs // 2
    same_x = ((fine // ny) % xs) // 2 == (coarse // (ny // 2)) % half
    same_y = (fine % ny) // 2 == coarse % (ny // 2)
    return where01((fine < ny * xs) & same_x & same_y)


def in_lanes(field, chosen):
    flat = field.reshape(field.shape[0] * ROWS, LANES)
    return dot01(flat, chosen).reshape(field.shape)


def path_of(group):
    nx, ny = SPLIT
    row, column = 0, 0
    for index in range(group + 1):
        columns = list(range(ny)) if column == 0 else list(range(ny))[::-1]
        if index % 2:
            path = [(row, at) for at in columns] + [(1 - row, at) for at in columns[::-1]]
        else:
            path = []
            for at in columns:
                path += [(row, at), (1 - row, at)]
                row = 1 - row
        row, column = path[-1]
    return [row * ny + column for row, column in path]


def lookup(table, index):
    found = table[0]
    for at, value in enumerate(table[1:], 1):
        found = jnp.where(index == at, value, found)
    return found


def slot_of(peer):
    return SPLIT[0] * SPLIT[1] - 1 - peer


def own_slot_of(rank):
    groups = range(lax.axis_size("gz"))
    return lookup([slot_of(path_of(group)[rank]) for group in groups], lax.axis_index("gz"))


def exchange(field):
    peers, groups = SPLIT[0] * SPLIT[1], lax.axis_size("gz")
    order = sorted(range(peers), key=slot_of)
    members = [[peer * groups + group for peer in order] for group in range(groups)]
    axes = ("gx", "gy", "gz")
    return lax.all_to_all(field, axes, 0, 0, axis_index_groups=members, tiled=True)


def slabs_of(groups):
    peers = SPLIT[0] * SPLIT[1]
    return [
        group * peers + path_of(group).index(peer) for peer in range(peers) for group in range(groups)
    ]


def own_slab():
    nx, ny = SPLIT
    groups = lax.axis_size("gz")
    device = (lax.axis_index("gx") * ny + lax.axis_index("gy")) * groups + lax.axis_index("gz")
    return lookup(slabs_of(groups), device)


def devices_of(groups):
    slabs = slabs_of(groups)
    return [slabs.index(slab) for slab in range(len(slabs))]


def prepare_kernel(share, res_ref, fluid_ref, pin_ref, out_ref):
    bx, by, depth = fluid_ref.shape
    cells = bx * by
    groups = bx // 4
    order = [x for low in range(4) for x in range(low, bx, 4)]
    fine = iota((cells, 4 * cells), 1)
    x, y = fine // (4 * by), (fine % (2 * by)) // 2
    chosen = where01((x % 4) * (groups * by) + (x // 4) * by + y == iota((cells, 4 * cells), 0))
    wide = lax.dot_general(
        chosen, res_ref[...], (((1,), (0,)), ((), ())), preferred_element_type=F32
    )
    rhs = dot10(where01(iota((depth, 2 * depth), 1) // 2 == iota((depth, 2 * depth), 0)), wide)

    def turned(field_ref):
        field = jnp.concatenate([field_ref[x : x + 1] for x in order], axis=0)
        return field.reshape(cells, depth).T

    fluid, pin = turned(fluid_ref), turned(pin_ref)
    for rank in range(depth // share):
        peer, begin = own_slot_of(rank), rank * share
        for index, field in enumerate((fluid, rhs, pin)):
            out_ref[peer, index * share : (index + 1) * share] = field[begin : begin + share]


def spread_kernel(groups, by, gathered, own, inner, outer, straight):
    for start in range(0, own.shape[0], ROWS):
        place(gathered, start, straight, start, groups, by)
    share = own.shape[0] // 3
    odd = own_slab() % 2 == 1
    for index in range(3):
        for plane in range(share):
            at = jnp.where(odd, share - 1 - plane, plane)
            own[index * share + plane] = straight[index * share + at]
    for target, drop in ((inner, 0), (outer, share - 1)):
        row = 0
        for index in range(3):
            for plane in range(share):
                if index == 0 or plane != drop:
                    target[row] = own[index * share + plane]
                    row += 1


def place(gathered, row, target, plane, groups, by):
    group = (iota((ROWS, LANES), 1) // by) % groups
    nx, ny = SPLIT
    for ix in range(nx):
        found = [gathered[slot_of(ix * ny + iy), pl.ds(row, ROWS), :] for iy in range(ny)]
        for part in range(groups):
            total = found[part]
            for iy in range(ny):
                if iy != part:
                    moved = pltpu.roll(found[iy], (by * (iy - part)) % LANES, 1)
                    total = jnp.where(group == iy, moved, total)
            target[pl.ds(plane, ROWS), ix * groups + part, :] = total


def near_kernel(
    depth,
    own, inner,
    saved1, saved2, fluid2, pin2, fluid3, pin3,
    fluid1, rhs1, pin1, other1, rhs2, sums,
):
    row = 0
    for index, target in enumerate((fluid1, rhs1, pin1)):
        target[0:depth] = own[index * depth : (index + 1) * depth]
        count = HALO if index == 0 else HALO - 1
        for plane in range(count):
            target[depth + plane] = inner[row + count - 1 - plane]
        if count < HALO:
            target[depth + count] = jnp.zeros((ROWS, LANES), F32)
        row += count
    fine, coarse = Level(0), Level(1)
    down1, down2 = lanes_down(0), lanes_down(1)
    fields1, corr1 = (saved1[0:6], saved1[6], saved1[7]), saved1[8]
    fields2 = (saved2[0:6], saved2[6], saved2[7])
    planes = depth + HALO
    set_level(fine, 1, planes - 1, fluid1, pin1, rhs1, fields1)
    sweep(fine, 2, planes - 2, fields1, fields1[1], other1)
    sweep(fine, 3, planes - 3, fields1, other1, corr1)
    coarse_residual(fine, 4, planes - 4, fields1, corr1, sums)
    count2 = planes // 2
    for source, target, share in ((fluid1, fluid2, 8.0), (pin1, pin2, 4.0)):
        target[NEAR : NEAR + count2] = in_lanes(pair_sum(source[...]), down1) * (1.0 / share)
    low2, high2 = NEAR + 2, NEAR + count2 - 2
    rhs2[low2:high2] = in_lanes(sums[0 : high2 - low2], down1)
    set_level(coarse, low2, high2, fluid2, pin2, rhs2, fields2)
    for source, target, scale in ((fluid2, fluid3, 0.125), (pin2, pin3, 0.25)):
        target[...] = in_lanes(pair_sum(source[NEAR : NEAR + depth // 2]), down2) * scale


def down_kernel(
    depth,
    own, outer, near2, near_fluid2, near_pin2, fluid3, pin3,
    saved1, saved2,
    packed,
    fluid1, rhs1, pin1, other1, fluid2, rhs2, pin2, other2, sums,
):
    planes = fluid1.shape[0]
    row = 0
    for index, target in enumerate((fluid1, rhs1, pin1)):
        count = HALO if index == 0 else HALO - 1
        if count < HALO:
            target[0] = jnp.zeros((ROWS, LANES), F32)
        for plane in range(count):
            target[HALO - count + plane] = outer[row + count - 1 - plane]
        row += count
        target[HALO:planes] = own[index * depth : index * depth + planes - HALO]

    fine, coarse = Level(0), Level(1)
    down1, down2 = lanes_down(0), lanes_down(1)
    fields1, corr1 = (saved1[0:6], saved1[6], saved1[7]), saved1[8]
    fields2, corr2 = (saved2[0:6], saved2[6], saved2[7]), saved2[8]
    set_level(fine, 1, planes - 1, fluid1, pin1, rhs1, fields1)
    sweep(fine, 2, planes - 2, fields1, fields1[1], other1)
    sweep(fine, 3, planes - 3, fields1, other1, corr1)
    count2 = depth // 2 + 2 * NEAR
    low2, done, high2 = 2, NEAR + 2, count2 - 2
    coarse_residual(fine, 2 * low2, 2 * done, fields1, corr1, sums)
    for source, ready, target, share in (
        (fluid1, near_fluid2, fluid2, 8.0), (pin1, near_pin2, pin2, 4.0)
    ):
        target[0:NEAR] = in_lanes(pair_sum(source[0:HALO]), down1) * (1.0 / share)
        target[NEAR : done + 1] = ready[NEAR : done + 1]
    rhs2[low2:done] = in_lanes(sums[0 : done - low2], down1)
    set_level(coarse, low2, done, fluid2, pin2, rhs2, fields2)
    for source, target in zip(near2, saved2[0:8]):
        target[done:high2] = source[done:high2]
    sweep(coarse, low2 + 1, high2 - 1, fields2, fields2[1], other2)
    sweep(coarse, low2 + 2, high2 - 2, fields2, other2, corr2)
    coarse_residual(coarse, NEAR, NEAR + depth // 2, fields2, corr2, sums)
    count3 = depth // 4
    rhs3 = in_lanes(sums[0:count3], down2)
    lane = iota((count3, LANES), 1) // ROWS
    first = jnp.zeros((count3, LANES), F32)
    second = jnp.zeros((count3, LANES), F32)
    for row in range(ROWS):
        first = jnp.where(lane == row, rhs3[:, row, :], first)
        first = jnp.where(lane == ROWS + row, fluid3[:, row, :], first)
        second = jnp.where(lane % ROWS == row, pin3[:, row, :], second)
    odd = own_slab() % 2 == 1

    def ordered(field):
        back = [field[row : row + 1] for row in reversed(range(count3))]
        return jnp.where(odd, jnp.concatenate(back, axis=0), field)

    first, second = ordered(first), ordered(second)
    packed[0] = first[0:2]
    packed[1] = first[2:4]
    packed[2] = jnp.where(lane[0:2] < ROWS, second[0:2], second[2:4])
    lane = iota((1, LANES), 1) // (LANES // 4)
    for index, plane in enumerate((NEAR + depth // 2 - 5, NEAR + 4)):
        for half in range(2):
            row = jnp.zeros((1, LANES), F32)
            for quarter in range(4):
                at = half * 4 + quarter
                row = jnp.where(lane == quarter, corr2[plane, at : at + 1, :], row)
            packed[3 + index, half : half + 1, :] = row


def rolled(field, shift):
    count = field.shape[0]
    shift %= count
    if shift % ROWS:
        return pltpu.roll(field, shift, 0)
    return jnp.concatenate([field[count - shift :], field[: count - shift]], axis=0)


def columns(rhs, fluid, pin):
    depth = fluid.shape[0]
    z, lane = iota(fluid.shape, 0), iota(fluid.shape, 1)
    y, x = lane % ROWS, (lane // ROWS) % ROWS

    def next_x(field):
        return pltpu.roll(field, LANES - ROWS, 1)

    def next_y(field):
        return pltpu.roll(field, LANES - 1, 1)

    wz = jnp.where(z == depth - 1, 0.0, mean_of(fluid, rolled(fluid, -1), 4.0))
    wy = jnp.where(y == ROWS - 1, 0.0, mean_of(fluid, next_y(fluid), 4.0))
    wx = jnp.where(x == ROWS - 1, 0.0, mean_of(fluid, next_x(fluid), 4.0))
    across = (wx + pltpu.roll(wx, ROWS, 1)) + (wy + pltpu.roll(wy, 1, 1)) + pin
    share = 1.0 / jnp.sum(across, axis=0, keepdims=True)

    above, below, own = rolled(wz, 1), wz, across
    steps = []
    stride, right = 1, rhs
    while stride < depth:
        inverse = inverse_of(above + below + own)
        up = above * rolled(inverse, stride)
        down = below * rolled(inverse, -stride)
        own = own + up * rolled(own, stride) + down * rolled(own, -stride)
        above = up * rolled(above, stride)
        below = down * rolled(below, -stride)
        right = right + up * rolled(right, stride) + down * rolled(right, -stride)
        steps.append((stride, up, down))
        stride *= 2
    inverse = inverse_of(above + below + own)

    def mean(right):
        return jnp.sum(right, axis=0, keepdims=True) * share

    corr = right * inverse + mean(rhs)
    flow_x = wx * (next_x(corr) - corr)
    flow_y = wy * (next_y(corr) - corr)
    flow_z = wz * (rolled(corr, -1) - corr)
    rest = (
        (rhs - pin * corr)
        + (flow_x - pltpu.roll(flow_x, ROWS, 1))
        + (flow_y - pltpu.roll(flow_y, 1, 1))
        + (flow_z - rolled(flow_z, 1))
    )
    right = rest
    for stride, up, down in steps:
        right = right + up * rolled(right, stride) + down * rolled(right, -stride)
    return (corr + mean(rest)) + right * inverse


def up_kernel(
    groups, by, depth,
    packed, near1, far1, far2,
    out_ref,
    one1, two1, one2, two2, lifted, first, second, solved, final,
):
    count3 = depth // 4
    shares = packed.shape[0]
    peers = SPLIT[0] * SPLIT[1]
    devices = devices_of(shares // peers)
    for slab, index in enumerate(devices):
        row = slab * count3
        first[row : row + 2] = packed[index, 0]
        first[row + 2 : row + 4] = packed[index, 1]
        both = packed[index, 2]
        second[row : row + 2] = both
        second[row + 2 : row + 4] = pltpu.roll(both, LANES // 2, 1)
    half = iota((shares * count3, LANES), 1) < LANES // 2

    def low_half(field):
        return jnp.where(half, field, pltpu.roll(field, LANES // 2, 1))

    def high_half(field):
        return jnp.where(half, pltpu.roll(field, LANES // 2, 1), field)

    solved[NEAR : NEAR + shares * count3] = columns(
        low_half(first[...]), high_half(first[...]), low_half(second[...])
    )
    solved[0:NEAR] = jnp.zeros((NEAR, LANES), F32)
    solved[NEAR + shares * count3 :] = jnp.zeros((2 * NEAR, LANES), F32)

    nx, ny = SPLIT
    part = own_slab()
    count = count3 + 2 * NEAR
    tall = solved[pl.ds(part * count3, count + count3), :]
    fine, coarse = Level(0), Level(1)
    cell = iota((LANES, LANES), 0)
    lane = iota((LANES, LANES), 1)
    spread = where01((cell < ROWS) & (cell == (lane % coarse.ny) // 2))
    rows = tall.shape[0]
    turned = [tall] + [pltpu.roll(tall, LANES - ROWS * row, 1) for row in range(1, ROWS)]
    wide = dot01(jnp.concatenate(turned, axis=0), spread)
    for row in range(ROWS):
        lifted[0:rows, row, :] = wide[row * rows : (row + 1) * rows]

    odd = part % 2 == 1

    def lifted_to(plane):
        parent = plane // 2 + NEAR // 2
        return lifted[jnp.where(odd, count - 1 - parent, parent)]

    near_fields, near_corr1 = (near1[0:6], near1[6], near1[7]), near1[8]
    far_fields, far_corr1 = (far1[0:6], far1[6], far1[7]), far1[8]
    fields2, corr2 = (far2[0:6], far2[6], far2[7]), far2[8]
    low, high = NEAR - 4, NEAR + depth // 2 + 4
    reach = depth // 2 + NEAR
    quarter = iota((ROWS, LANES), 1) // (LANES // 4)
    row = iota((ROWS, LANES), 0)

    def unpacked(index, which):
        pair = packed[lookup(devices, jnp.clip(index, 0, shares - 1)), which]
        total = None
        for shift in range(4):
            moved = pltpu.roll(pair, shift * (LANES // 4), 1)
            wide = jnp.where(row < 4, moved[0:1, :], moved[1:2, :])
            kept = jnp.where((quarter - shift) % 4 == row % 4, wide, 0.0)
            total = kept if total is None else total + kept
        return total

    one2[low - 1] = unpacked(jnp.where(odd, part + 1, part - 1), 4) + lifted_to(low - 1)
    for plane in range(low, high):
        one2[plane] = corr2[plane] + lifted_to(plane)
    one2[high] = unpacked(jnp.where(odd, part - 1, part + 1), 3) + lifted_to(high)
    sweep(coarse, NEAR - 4, reach + 4, fields2, one2, two2)
    sweep(coarse, NEAR - 3, reach + 3, fields2, two2, one2)
    sweep(coarse, NEAR - 2, reach + 2, fields2, one2, two2)

    fine_lane, coarse_lane = iota((LANES, LANES), 1), iota((LANES, LANES), 0)
    x_of = (fine_lane // fine.ny) // 2
    y_of = (fine_lane % fine.ny) // 2
    up = where01(coarse_lane == x_of * coarse.ny + y_of)
    lifted[0 : depth // 2 + 4] = in_lanes(two2[NEAR - 2 : reach + 2], up)
    parents = lifted[0 : depth // 2 + 4]
    twice = jnp.broadcast_to(parents[:, None], (parents.shape[0], 2, ROWS, LANES))
    low, high = HALO - 4, HALO + depth + 4
    turn = HALO + 3
    for plane in range(low, high):
        corr = far_corr1[plane] if plane < turn else near_corr1[plane - HALO]
        one1[plane] = corr + lifted[(plane - low) // 2]
    reach = depth + HALO
    for more, source, target in ((2, one1, two1), (1, two1, one1)):
        sweep(fine, HALO - more, turn, far_fields, source, target)
        sweep(fine, turn, reach + more, near_fields, source, target, HALO)

    def last(fields, shift):
        def body(plane, count):
            value = swept(fine, plane, count, fields, one1, shift)
            value = value * fields[2][pl.ds(plane - shift, count)]
            for index in range(count):
                at = plane - HALO + index
                final[jnp.where(odd, depth - 1 - at, at)] = value[index]

        return body

    loop(HALO, turn, PIECE, last(far_fields, 0))
    loop(turn, reach, PIECE, last(near_fields, HALO))

    group = (iota((depth, LANES), 1) // by) % groups
    for ix in range(nx):
        scaled = [final[:, ix * groups + part, :] for part in range(groups)]
        for iy in range(ny):
            total = scaled[iy]
            for part in range(groups):
                if part != iy:
                    moved = pltpu.roll(scaled[part], (by * (part - iy)) % LANES, 1)
                    total = jnp.where(group == part, moved, total)
            out_ref[slot_of(ix * ny + iy)] = total


def finish_kernel(blocks, out_ref):
    bx, by, depth = out_ref.shape
    peers = blocks.shape[0]
    ordered = jnp.concatenate([blocks[own_slot_of(rank)] for rank in range(peers)], axis=0)
    turned = ordered.T
    for x in range(bx):
        row = ((x % 4) * (bx // 4) + x // 4) * by
        out_ref[x] = turned[row : row + by]


def whole_planes(residual_q2, viscosity, pinned):
    bx, by, depth = viscosity.shape
    groups = bx // 4
    peers = SPLIT[0] * SPLIT[1]
    share = depth // peers
    planes = share + 2 * HALO
    count2 = share // 2 + 2 * NEAR
    limit = pltpu.CompilerParams(vmem_limit_bytes=32 * 2**20)

    def flat(rows):
        return jax.ShapeDtypeStruct((rows, LANES), F32)

    def blocks(count, rows):
        return jax.ShapeDtypeStruct((count, rows, LANES), F32)

    def room(count):
        return pltpu.VMEM((count, ROWS, LANES), F32)

    fluid = 1.0 / viscosity
    pin = 4.0 * pinned.astype(F32) * fluid
    parcels = pl.pallas_call(
        functools.partial(prepare_kernel, share),
        out_shape=blocks(peers, 3 * share),
        compiler_params=limit,
        name="prepare",
    )(residual_q2.reshape(4 * bx * by, 2 * depth), fluid, pin)
    own, inner, outer = pl.pallas_call(
        functools.partial(spread_kernel, groups, by),
        out_shape=(blocks(3 * share, ROWS),) + (blocks(3 * HALO - 2, ROWS),) * 2,
        scratch_shapes=[room(3 * share)],
        compiler_params=limit,
        name="spread",
    )(exchange(parcels))
    length = lax.axis_size("gz")
    parts = length * peers

    device = devices_of(length)

    def swap(field, first):
        pairs = [(device[i], device[i + 1]) for i in range(first, parts - 1, 2)]
        return lax.ppermute(field, ("gx", "gy", "gz"), pairs + [pair[::-1] for pair in pairs])

    outer, inner = swap(outer, 1), swap(inner, 0)
    count3 = share // 4
    near1, near2, far1, far2 = (
        (blocks(count, ROWS),) * fields
        for count, fields in ((share + HALO, 9), (count2, 8), (HALO + 8, 9), (count2, 9))
    )
    near1, near2, fluid2, pin2, fluid3, pin3 = pl.pallas_call(
        functools.partial(near_kernel, share),
        out_shape=(near1, near2) + (blocks(count2, ROWS),) * 2 + (blocks(count3, ROWS),) * 2,
        scratch_shapes=[room(share + HALO)] * 4 + [room(count2)] * 2,
        compiler_params=limit,
        name="near",
    )(own, inner)
    far1, far2, parcel = pl.pallas_call(
        functools.partial(down_kernel, share),
        out_shape=(far1, far2, blocks(5, 2)),
        scratch_shapes=[room(HALO + 8)] * 4 + [room(count2)] * 5,
        compiler_params=limit,
        name="down",
    )(own, outer, near2, fluid2, pin2, fluid3, pin3)
    copies = jnp.broadcast_to(parcel, (parts,) + parcel.shape)
    packed = lax.all_to_all(copies, ("gx", "gy", "gz"), 0, 0, tiled=True)
    depth3 = parts * count3
    mine = pl.pallas_call(
        functools.partial(up_kernel, groups, by, share),
        out_shape=blocks(peers, share),
        scratch_shapes=[room(planes), room(planes), room(count2), room(count2), room(count2)]
        + [pltpu.VMEM((rows, LANES), F32) for rows in (depth3, depth3, depth3 + 3 * NEAR)]
        + [room(share)],
        compiler_params=limit,
        name="up",
    )(packed, near1, far1, far2)
    return pl.pallas_call(
        finish_kernel,
        out_shape=jax.ShapeDtypeStruct((bx, by, depth), F32),
        compiler_params=limit,
        name="finish",
    )(exchange(mine))


def one_tile_planes(mesh, viscosity):
    split = (mesh.shape["gx"], mesh.shape["gy"])
    depth = viscosity.shape[2]
    fits = viscosity.shape[:2] == PLANE and split == SPLIT
    return fits and depth == 4 * LANES and depth // mesh.shape["gz"] == LANES


def solution(mesh):
    placed = (P("gx", "gy", "gz"), P("gx", "gy", "gz"), P("gx", "gy", "gz"))

    def cycle(residual_q2, viscosity, pinned):
        chosen = whole_planes if one_tile_planes(mesh, viscosity) else per_device
        return jax.shard_map(
            chosen, mesh=mesh, in_specs=placed, out_specs=P("gx", "gy", "gz"), check_vma=False
        )(residual_q2, viscosity, pinned)

    return cycle
```

```python
import functools

import jax
import jax.numpy as jnp
from jax import lax
from jax.experimental import pallas as pl
from jax.experimental.pallas import tpu as pltpu
from jax.sharding import PartitionSpec as P

NU = 3


OMEGA = 0.6


def with_halo(block, sides, width):
    for axis, dim in sides:
        count = lax.axis_size(axis)
        forward = [(i, i + 1) for i in range(count - 1)]
        backward = [(target, source) for source, target in forward]
        low = lax.ppermute(
            lax.slice_in_dim(block, block.shape[dim] - width, None, axis=dim), axis, forward
        )
        high = lax.ppermute(lax.slice_in_dim(block, 0, width, axis=dim), axis, backward)
        block = jnp.concatenate([low, block, high], axis=dim)
    return block


def coarsen(x):
    a, b, c = x.shape
    return x.reshape(a // 2, 2, b // 2, 2, c // 2, 2).sum(axis=(1, 3, 5))


def refine(x):
    return jnp.repeat(jnp.repeat(jnp.repeat(x, 2, 0), 2, 1), 2, 2)


def extended(field):
    return with_halo(field, (("gx", 0), ("gy", 1), ("gz", 2)), 1)


def shifted(padded):
    return [
        padded[2:, 1:-1, 1:-1],
        padded[:-2, 1:-1, 1:-1],
        padded[1:-1, 2:, 1:-1],
        padded[1:-1, :-2, 1:-1],
        padded[1:-1, 1:-1, 2:],
        padded[1:-1, 1:-1, :-2],
    ]


def neighbours(field):
    return shifted(extended(field))


def harmonic(fluid, near, factor):
    total = fluid + near
    return jnp.where(total > 0, factor * 2.0 * fluid * near / jnp.where(total > 0, total, 1.0), 0.0)


def couplings(fluid, factor):
    return [harmonic(fluid, near, factor) for near in neighbours(fluid)]


def apply_op(field, weights, diag):
    total = diag * field
    for weight, near in zip(weights, neighbours(field)):
        total = total - weight * near
    return total


def presmooth(rhs, weights, diag):
    corr = OMEGA * rhs / diag
    for sweep in range(NU - 1):
        corr = corr + OMEGA * (rhs - apply_op(corr, weights, diag)) / diag
    return corr


def postsmooth(corr, rhs, weights, diag):
    for sweep in range(NU):
        corr = corr + OMEGA * (rhs - apply_op(corr, weights, diag)) / diag
    return corr


def tridiag(coeffs, rhs):
    solved = lax.linalg.tridiagonal_solve(coeffs[0], coeffs[1], coeffs[2], rhs[..., None])[..., 0]
    last = rhs.ndim - 1
    shift_col = jnp.sum(rhs, axis=last, keepdims=True) / jnp.sum(
        coeffs[3], axis=last, keepdims=True
    )
    return solved + shift_col


def prepare_columns(weights, diag):
    lower = -weights[5]
    upper = -weights[4]
    across = diag + lower + upper
    return (
        lax.all_gather(lower, "gz", axis=2, tiled=True),
        lax.all_gather(diag, "gz", axis=2, tiled=True),
        lax.all_gather(upper, "gz", axis=2, tiled=True),
        lax.all_gather(across, "gz", axis=2, tiled=True),
    )


def column_solve(rhs, coeffs):
    depth = rhs.shape[2]
    whole = lax.all_gather(rhs, "gz", axis=2, tiled=True)
    solved = tridiag(coeffs, whole)
    return lax.dynamic_slice_in_dim(solved, lax.axis_index("gz") * depth, depth, 2)


def per_device(residual_q2, viscosity, pinned):
    fluid1 = 1.0 / viscosity
    pin1 = 4.0 * pinned.astype(jnp.float32) * fluid1
    rhs1 = coarsen(residual_q2.astype(jnp.float32))
    fluid2 = coarsen(fluid1) / 8.0
    pin2 = coarsen(pin1) / 4.0
    fluid3 = coarsen(fluid2) / 8.0
    pin3 = coarsen(pin2) / 4.0
    weights1 = couplings(fluid1, 1.0)
    weights2 = couplings(fluid2, 2.0)
    weights3 = couplings(fluid3, 4.0)
    diag1 = sum(weights1) + pin1
    diag2 = sum(weights2) + pin2
    diag3 = sum(weights3) + pin3
    coeffs = prepare_columns(weights3, diag3)
    corr1 = presmooth(rhs1, weights1, diag1)
    rhs2 = coarsen(rhs1 - apply_op(corr1, weights1, diag1))
    corr2 = presmooth(rhs2, weights2, diag2)
    rhs3 = coarsen(rhs2 - apply_op(corr2, weights2, diag2))
    corr3 = column_solve(rhs3, coeffs)
    corr3 = corr3 + column_solve(rhs3 - apply_op(corr3, weights3, diag3), coeffs)
    corr2 = postsmooth(corr2 + refine(corr3), rhs2, weights2, diag2)
    corr1 = postsmooth(corr1 + refine(corr2), rhs1, weights1, diag1)
    return diag1 * corr1


PLANE = (32, 32)
SPLIT = (2, 4)
ROWS = 8
LANES = 128
HALO = 16
NEAR = 8
PIECE = 4
TINY = 1e-30
F32 = jnp.float32


def iota(shape, dim):
    return lax.broadcasted_iota(jnp.int32, shape, dim)


def dot01(field, chosen):
    total = None
    rest = field
    for part in range(3):
        piece = rest.astype(jnp.bfloat16)
        term = jnp.dot(piece, chosen, preferred_element_type=F32)
        total = term if total is None else total + term
        if part < 2:
            rest = rest - piece.astype(F32)
    return total


def dot10(chosen, field):
    total = None
    rest = field
    for part in range(3):
        piece = rest.astype(jnp.bfloat16)
        term = lax.dot_general(
            chosen, piece, (((1,), (1,)), ((), ())), preferred_element_type=F32
        )
        total = term if total is None else total + term
        if part < 2:
            rest = rest - piece.astype(F32)
    return total


def where01(condition):
    return jnp.where(condition, 1.0, 0.0).astype(jnp.bfloat16)


def loop(low, high, size, body):
    for plane in range(low, high, size):
        body(plane, min(size, high - plane))


def inverse_of(field):
    first = pl.reciprocal(field, approx=True)
    return first * (2.0 - field * first)


class Level:
    def __init__(self, level):
        self.ny = PLANE[1] >> level
        self.xs = 4 >> level
        self.factor = float(2**level)

    def masks(self, shape):
        lane = iota(shape, 2)
        row = iota(shape, 1)
        within = (lane // self.ny) % self.xs
        y = lane % self.ny
        last_x = (row == ROWS - 1) & (within == self.xs - 1)
        return within, y == self.ny - 1, last_x

    def next_x(self, field):
        within = (iota(field.shape, 2) // self.ny) % self.xs
        moved = pltpu.roll(field, LANES - self.ny, 2)
        return jnp.where(within == self.xs - 1, pltpu.roll(moved, ROWS - 1, 1), moved)

    def last_x(self, field):
        within = (iota(field.shape, 2) // self.ny) % self.xs
        moved = pltpu.roll(field, self.ny, 2)
        return jnp.where(within == 0, pltpu.roll(moved, 1, 1), moved)

    def next_y(self, field):
        return pltpu.roll(field, LANES - 1, 2)

    def last_y(self, field):
        return pltpu.roll(field, 1, 2)

    def spread(self, field, scaled, plane, count):
        mid = field[1:-1]
        near = (
            self.next_x(mid), self.last_x(mid), self.next_y(mid), self.last_y(mid),
            field[2:], field[:-2],
        )
        terms = [weight[pl.ds(plane, count)] * value for weight, value in zip(scaled, near)]
        return mid, ((terms[0] + terms[1]) + (terms[2] + terms[3])) + (terms[4] + terms[5])


def mean_of(fluid, near, factor):
    return ((factor * 2.0) * fluid * near) * inverse_of(jnp.maximum(fluid + near, TINY))


def set_level(level, low, high, fluid, pin, rhs, fields):
    scaled, start, diag = fields

    def body(plane, count):
        wide = fluid[pl.ds(plane - 1, count + 2)]
        mid = wide[1:-1]
        within, end_y, end_x = level.masks(mid.shape)
        to_x = jnp.where(end_x, 0.0, mean_of(mid, level.next_x(mid), level.factor))
        to_y = jnp.where(end_y, 0.0, mean_of(mid, level.next_y(mid), level.factor))
        to_z = mean_of(wide[:-1], wide[1:], level.factor)
        weights = (to_x, level.last_x(to_x), to_y, level.last_y(to_y), to_z[1:], to_z[:-1])
        total = (
            (weights[0] + weights[1])
            + (weights[2] + weights[3])
            + (weights[4] + weights[5])
            + pin[pl.ds(plane, count)]
        )
        gain = OMEGA * inverse_of(jnp.maximum(total, TINY))
        for target, weight in zip(scaled, weights):
            target[pl.ds(plane, count)] = gain * weight
        start[pl.ds(plane, count)] = gain * rhs[pl.ds(plane, count)]
        diag[pl.ds(plane, count)] = total

    loop(low, high, PIECE, body)


def swept(level, plane, count, fields, source, shift=0):
    scaled, start, _ = fields
    mid, total = level.spread(source[pl.ds(plane - 1, count + 2)], scaled, plane - shift, count)
    return (1.0 - OMEGA) * mid + (start[pl.ds(plane - shift, count)] + total)


def sweep(level, low, high, fields, source, target, shift=0):
    def body(plane, count):
        target[pl.ds(plane, count)] = swept(level, plane, count, fields, source, shift)

    loop(low, high, PIECE, body)


def pair_sum(field):
    half = field.reshape((field.shape[0] // 2, 2) + field.shape[1:])
    return half[:, 0] + half[:, 1]


def coarse_residual(level, low, high, fields, corr, target):
    scaled, start, diag = fields

    def body(plane, count):
        mid, total = level.spread(corr[pl.ds(plane - 1, count + 2)], scaled, plane, count)
        rest = (start[pl.ds(plane, count)] + total) - OMEGA * mid
        rest = rest * (diag[pl.ds(plane, count)] * (1.0 / OMEGA))
        target[pl.ds((plane - low) // 2, count // 2)] = pair_sum(rest)

    loop(low, high, PIECE, body)


def lanes_down(level):
    fine = iota((LANES, LANES), 0)
    coarse = iota((LANES, LANES), 1)
    ny, xs = PLANE[1] >> level, 4 >> level
    half = xs // 2
    same_x = ((fine // ny) % xs) // 2 == (coarse // (ny // 2)) % half
    same_y = (fine % ny) // 2 == coarse % (ny // 2)
    return where01((fine < ny * xs) & same_x & same_y)


def in_lanes(field, chosen):
    flat = field.reshape(field.shape[0] * ROWS, LANES)
    return dot01(flat, chosen).reshape(field.shape)


def path_of(group):
    nx, ny = SPLIT
    row, column = 0, 0
    for index in range(group + 1):
        columns = list(range(ny)) if column == 0 else list(range(ny))[::-1]
        if index % 2:
            path = [(row, at) for at in columns] + [(1 - row, at) for at in columns[::-1]]
        else:
            path = []
            for at in columns:
                path += [(row, at), (1 - row, at)]
                row = 1 - row
        row, column = path[-1]
    return [row * ny + column for row, column in path]


def lookup(table, index):
    found = table[0]
    for at, value in enumerate(table[1:], 1):
        found = jnp.where(index == at, value, found)
    return found


def slot_of(peer):
    return SPLIT[0] * SPLIT[1] - 1 - peer


def own_slot_of(rank):
    groups = range(lax.axis_size("gz"))
    return lookup([slot_of(path_of(group)[rank]) for group in groups], lax.axis_index("gz"))


def exchange(field):
    peers, groups = SPLIT[0] * SPLIT[1], lax.axis_size("gz")
    order = sorted(range(peers), key=slot_of)
    members = [[peer * groups + group for peer in order] for group in range(groups)]
    axes = ("gx", "gy", "gz")
    return lax.all_to_all(field, axes, 0, 0, axis_index_groups=members, tiled=True)


def slabs_of(groups):
    peers = SPLIT[0] * SPLIT[1]
    return [
        group * peers + path_of(group).index(peer) for peer in range(peers) for group in range(groups)
    ]


def own_slab():
    nx, ny = SPLIT
    groups = lax.axis_size("gz")
    device = (lax.axis_index("gx") * ny + lax.axis_index("gy")) * groups + lax.axis_index("gz")
    return lookup(slabs_of(groups), device)


def devices_of(groups):
    slabs = slabs_of(groups)
    return [slabs.index(slab) for slab in range(len(slabs))]


def prepare_kernel(share, res_ref, fluid_ref, pin_ref, out_ref):
    bx, by, depth = fluid_ref.shape
    cells = bx * by
    groups = bx // 4
    order = [x for low in range(4) for x in range(low, bx, 4)]
    fine = iota((cells, 4 * cells), 1)
    x, y = fine // (4 * by), (fine % (2 * by)) // 2
    chosen = where01((x % 4) * (groups * by) + (x // 4) * by + y == iota((cells, 4 * cells), 0))
    wide = lax.dot_general(
        chosen, res_ref[...], (((1,), (0,)), ((), ())), preferred_element_type=F32
    )
    rhs = dot10(where01(iota((depth, 2 * depth), 1) // 2 == iota((depth, 2 * depth), 0)), wide)

    def turned(field_ref):
        field = jnp.concatenate([field_ref[x : x + 1] for x in order], axis=0)
        return field.reshape(cells, depth).T

    fluid, pin = turned(fluid_ref), turned(pin_ref)
    for rank in range(depth // share):
        peer, begin = own_slot_of(rank), rank * share
        for index, field in enumerate((fluid, rhs, pin)):
            out_ref[peer, index * share : (index + 1) * share] = field[begin : begin + share]


def spread_kernel(groups, by, gathered, own, inner, outer, straight):
    for start in range(0, own.shape[0], ROWS):
        place(gathered, start, straight, start, groups, by)
    share = own.shape[0] // 3
    odd = own_slab() % 2 == 1
    for index in range(3):
        for plane in range(share):
            at = jnp.where(odd, share - 1 - plane, plane)
            own[index * share + plane] = straight[index * share + at]
    for target, drop in ((inner, 0), (outer, share - 1)):
        row = 0
        for index in range(3):
            for plane in range(share):
                if index == 0 or plane != drop:
                    target[row] = own[index * share + plane]
                    row += 1


def place(gathered, row, target, plane, groups, by):
    group = (iota((ROWS, LANES), 1) // by) % groups
    nx, ny = SPLIT
    for ix in range(nx):
        found = [gathered[slot_of(ix * ny + iy), pl.ds(row, ROWS), :] for iy in range(ny)]
        for part in range(groups):
            total = found[part]
            for iy in range(ny):
                if iy != part:
                    moved = pltpu.roll(found[iy], (by * (iy - part)) % LANES, 1)
                    total = jnp.where(group == iy, moved, total)
            target[pl.ds(plane, ROWS), ix * groups + part, :] = total


def near_kernel(
    depth,
    own, inner,
    saved1, saved2, fluid2, pin2, fluid3, pin3,
    fluid1, rhs1, pin1, other1, rhs2, sums,
):
    row = 0
    for index, target in enumerate((fluid1, rhs1, pin1)):
        target[0:depth] = own[index * depth : (index + 1) * depth]
        count = HALO if index == 0 else HALO - 1
        for plane in range(count):
            target[depth + plane] = inner[row + count - 1 - plane]
        if count < HALO:
            target[depth + count] = jnp.zeros((ROWS, LANES), F32)
        row += count
    fine, coarse = Level(0), Level(1)
    down1, down2 = lanes_down(0), lanes_down(1)
    fields1, corr1 = (saved1[0:6], saved1[6], saved1[7]), saved1[8]
    fields2 = (saved2[0:6], saved2[6], saved2[7])
    planes = depth + HALO
    set_level(fine, 1, planes - 1, fluid1, pin1, rhs1, fields1)
    sweep(fine, 2, planes - 2, fields1, fields1[1], other1)
    sweep(fine, 3, planes - 3, fields1, other1, corr1)
    coarse_residual(fine, 4, planes - 4, fields1, corr1, sums)
    count2 = planes // 2
    for source, target, share in ((fluid1, fluid2, 8.0), (pin1, pin2, 4.0)):
        target[NEAR : NEAR + count2] = in_lanes(pair_sum(source[...]), down1) * (1.0 / share)
    low2, high2 = NEAR + 2, NEAR + count2 - 2
    rhs2[low2:high2] = in_lanes(sums[0 : high2 - low2], down1)
    set_level(coarse, low2, high2, fluid2, pin2, rhs2, fields2)
    for source, target, scale in ((fluid2, fluid3, 0.125), (pin2, pin3, 0.25)):
        target[...] = in_lanes(pair_sum(source[NEAR : NEAR + depth // 2]), down2) * scale


def down_kernel(
    depth,
    own, outer, near2, near_fluid2, near_pin2, fluid3, pin3,
    saved1, saved2,
    packed,
    fluid1, rhs1, pin1, other1, fluid2, rhs2, pin2, other2, sums,
):
    planes = fluid1.shape[0]
    row = 0
    for index, target in enumerate((fluid1, rhs1, pin1)):
        count = HALO if index == 0 else HALO - 1
        if count < HALO:
            target[0] = jnp.zeros((ROWS, LANES), F32)
        for plane in range(count):
            target[HALO - count + plane] = outer[row + count - 1 - plane]
        row += count
        target[HALO:planes] = own[index * depth : index * depth + planes - HALO]

    fine, coarse = Level(0), Level(1)
    down1, down2 = lanes_down(0), lanes_down(1)
    fields1, corr1 = (saved1[0:6], saved1[6], saved1[7]), saved1[8]
    fields2, corr2 = (saved2[0:6], saved2[6], saved2[7]), saved2[8]
    set_level(fine, 1, planes - 1, fluid1, pin1, rhs1, fields1)
    sweep(fine, 2, planes - 2, fields1, fields1[1], other1)
    sweep(fine, 3, planes - 3, fields1, other1, corr1)
    count2 = depth // 2 + 2 * NEAR
    low2, done, high2 = 2, NEAR + 2, count2 - 2
    coarse_residual(fine, 2 * low2, 2 * done, fields1, corr1, sums)
    for source, ready, target, share in (
        (fluid1, near_fluid2, fluid2, 8.0), (pin1, near_pin2, pin2, 4.0)
    ):
        target[0:NEAR] = in_lanes(pair_sum(source[0:HALO]), down1) * (1.0 / share)
        target[NEAR : done + 1] = ready[NEAR : done + 1]
    rhs2[low2:done] = in_lanes(sums[0 : done - low2], down1)
    set_level(coarse, low2, done, fluid2, pin2, rhs2, fields2)
    for source, target in zip(near2, saved2[0:8]):
        target[done:high2] = source[done:high2]
    sweep(coarse, low2 + 1, high2 - 1, fields2, fields2[1], other2)
    sweep(coarse, low2 + 2, high2 - 2, fields2, other2, corr2)
    coarse_residual(coarse, NEAR, NEAR + depth // 2, fields2, corr2, sums)
    count3 = depth // 4
    rhs3 = in_lanes(sums[0:count3], down2)
    lane = iota((count3, LANES), 1) // ROWS
    first = jnp.zeros((count3, LANES), F32)
    second = jnp.zeros((count3, LANES), F32)
    for row in range(ROWS):
        first = jnp.where(lane == row, rhs3[:, row, :], first)
        first = jnp.where(lane == ROWS + row, fluid3[:, row, :], first)
        second = jnp.where(lane % ROWS == row, pin3[:, row, :], second)
    odd = own_slab() % 2 == 1

    def ordered(field):
        back = [field[row : row + 1] for row in reversed(range(count3))]
        return jnp.where(odd, jnp.concatenate(back, axis=0), field)

    first, second = ordered(first), ordered(second)
    packed[0] = first[0:2]
    packed[1] = first[2:4]
    packed[2] = jnp.where(lane[0:2] < ROWS, second[0:2], second[2:4])
    lane = iota((1, LANES), 1) // (LANES // 4)
    for index, plane in enumerate((NEAR + depth // 2 - 5, NEAR + 4)):
        for half in range(2):
            row = jnp.zeros((1, LANES), F32)
            for quarter in range(4):
                at = half * 4 + quarter
                row = jnp.where(lane == quarter, corr2[plane, at : at + 1, :], row)
            packed[3 + index, half : half + 1, :] = row


def rolled(field, shift):
    count = field.shape[0]
    shift %= count
    if shift % ROWS:
        return pltpu.roll(field, shift, 0)
    return jnp.concatenate([field[count - shift :], field[: count - shift]], axis=0)


def columns(rhs, fluid, pin):
    depth = fluid.shape[0]
    z, lane = iota(fluid.shape, 0), iota(fluid.shape, 1)
    y, x = lane % ROWS, (lane // ROWS) % ROWS

    def next_x(field):
        return pltpu.roll(field, LANES - ROWS, 1)

    def next_y(field):
        return pltpu.roll(field, LANES - 1, 1)

    wz = jnp.where(z == depth - 1, 0.0, mean_of(fluid, rolled(fluid, -1), 4.0))
    wy = jnp.where(y == ROWS - 1, 0.0, mean_of(fluid, next_y(fluid), 4.0))
    wx = jnp.where(x == ROWS - 1, 0.0, mean_of(fluid, next_x(fluid), 4.0))
    across = (wx + pltpu.roll(wx, ROWS, 1)) + (wy + pltpu.roll(wy, 1, 1)) + pin
    share = 1.0 / jnp.sum(across, axis=0, keepdims=True)

    above, below, own = rolled(wz, 1), wz, across
    steps = []
    stride, right = 1, rhs
    while stride < depth:
        inverse = inverse_of(above + below + own)
        up = above * rolled(inverse, stride)
        down = below * rolled(inverse, -stride)
        own = own + up * rolled(own, stride) + down * rolled(own, -stride)
        above = up * rolled(above, stride)
        below = down * rolled(below, -stride)
        right = right + up * rolled(right, stride) + down * rolled(right, -stride)
        steps.append((stride, up, down))
        stride *= 2
    inverse = inverse_of(above + below + own)

    def mean(right):
        return jnp.sum(right, axis=0, keepdims=True) * share

    corr = right * inverse + mean(rhs)
    flow_x = wx * (next_x(corr) - corr)
    flow_y = wy * (next_y(corr) - corr)
    flow_z = wz * (rolled(corr, -1) - corr)
    rest = (
        (rhs - pin * corr)
        + (flow_x - pltpu.roll(flow_x, ROWS, 1))
        + (flow_y - pltpu.roll(flow_y, 1, 1))
        + (flow_z - rolled(flow_z, 1))
    )
    right = rest
    for stride, up, down in steps:
        right = right + up * rolled(right, stride) + down * rolled(right, -stride)
    return (corr + mean(rest)) + right * inverse


def up_kernel(
    groups, by, depth,
    packed, near1, far1, far2,
    out_ref,
    one1, two1, one2, two2, lifted, first, second, solved, final,
):
    count3 = depth // 4
    shares = packed.shape[0]
    peers = SPLIT[0] * SPLIT[1]
    devices = devices_of(shares // peers)
    for slab, index in enumerate(devices):
        row = slab * count3
        first[row : row + 2] = packed[index, 0]
        first[row + 2 : row + 4] = packed[index, 1]
        both = packed[index, 2]
        second[row : row + 2] = both
        second[row + 2 : row + 4] = pltpu.roll(both, LANES // 2, 1)
    half = iota((shares * count3, LANES), 1) < LANES // 2

    def low_half(field):
        return jnp.where(half, field, pltpu.roll(field, LANES // 2, 1))

    def high_half(field):
        return jnp.where(half, pltpu.roll(field, LANES // 2, 1), field)

    solved[NEAR : NEAR + shares * count3] = columns(
        low_half(first[...]), high_half(first[...]), low_half(second[...])
    )
    solved[0:NEAR] = jnp.zeros((NEAR, LANES), F32)
    solved[NEAR + shares * count3 :] = jnp.zeros((2 * NEAR, LANES), F32)

    nx, ny = SPLIT
    part = own_slab()
    count = count3 + 2 * NEAR
    tall = solved[pl.ds(part * count3, count + count3), :]
    fine, coarse = Level(0), Level(1)
    cell = iota((LANES, LANES), 0)
    lane = iota((LANES, LANES), 1)
    spread = where01((cell < ROWS) & (cell == (lane % coarse.ny) // 2))
    rows = tall.shape[0]
    turned = [tall] + [pltpu.roll(tall, LANES - ROWS * row, 1) for row in range(1, ROWS)]
    wide = dot01(jnp.concatenate(turned, axis=0), spread)
    for row in range(ROWS):
        lifted[0:rows, row, :] = wide[row * rows : (row + 1) * rows]

    odd = part % 2 == 1

    def lifted_to(plane):
        parent = plane // 2 + NEAR // 2
        return lifted[jnp.where(odd, count - 1 - parent, parent)]

    near_fields, near_corr1 = (near1[0:6], near1[6], near1[7]), near1[8]
    far_fields, far_corr1 = (far1[0:6], far1[6], far1[7]), far1[8]
    fields2, corr2 = (far2[0:6], far2[6], far2[7]), far2[8]
    low, high = NEAR - 4, NEAR + depth // 2 + 4
    reach = depth // 2 + NEAR
    quarter = iota((ROWS, LANES), 1) // (LANES // 4)
    row = iota((ROWS, LANES), 0)

    def unpacked(index, which):
        pair = packed[lookup(devices, jnp.clip(index, 0, shares - 1)), which]
        total = None
        for shift in range(4):
            moved = pltpu.roll(pair, shift * (LANES // 4), 1)
            wide = jnp.where(row < 4, moved[0:1, :], moved[1:2, :])
            kept = jnp.where((quarter - shift) % 4 == row % 4, wide, 0.0)
            total = kept if total is None else total + kept
        return total

    one2[low - 1] = unpacked(jnp.where(odd, part + 1, part - 1), 4) + lifted_to(low - 1)
    for plane in range(low, high):
        one2[plane] = corr2[plane] + lifted_to(plane)
    one2[high] = unpacked(jnp.where(odd, part - 1, part + 1), 3) + lifted_to(high)
    sweep(coarse, NEAR - 4, reach + 4, fields2, one2, two2)
    sweep(coarse, NEAR - 3, reach + 3, fields2, two2, one2)
    sweep(coarse, NEAR - 2, reach + 2, fields2, one2, two2)

    fine_lane, coarse_lane = iota((LANES, LANES), 1), iota((LANES, LANES), 0)
    x_of = (fine_lane // fine.ny) // 2
    y_of = (fine_lane % fine.ny) // 2
    up = where01(coarse_lane == x_of * coarse.ny + y_of)
    lifted[0 : depth // 2 + 4] = in_lanes(two2[NEAR - 2 : reach + 2], up)
    parents = lifted[0 : depth // 2 + 4]
    twice = jnp.broadcast_to(parents[:, None], (parents.shape[0], 2, ROWS, LANES))
    low, high = HALO - 4, HALO + depth + 4
    turn = HALO + 3
    for plane in range(low, high):
        corr = far_corr1[plane] if plane < turn else near_corr1[plane - HALO]
        one1[plane] = corr + lifted[(plane - low) // 2]
    reach = depth + HALO
    for more, source, target in ((2, one1, two1), (1, two1, one1)):
        sweep(fine, HALO - more, turn, far_fields, source, target)
        sweep(fine, turn, reach + more, near_fields, source, target, HALO)

    def last(fields, shift):
        def body(plane, count):
            value = swept(fine, plane, count, fields, one1, shift)
            value = value * fields[2][pl.ds(plane - shift, count)]
            for index in range(count):
                at = plane - HALO + index
                final[jnp.where(odd, depth - 1 - at, at)] = value[index]

        return body

    loop(HALO, turn, PIECE, last(far_fields, 0))
    loop(turn, reach, PIECE, last(near_fields, HALO))

    group = (iota((depth, LANES), 1) // by) % groups
    for ix in range(nx):
        scaled = [final[:, ix * groups + part, :] for part in range(groups)]
        for iy in range(ny):
            total = scaled[iy]
            for part in range(groups):
                if part != iy:
                    moved = pltpu.roll(scaled[part], (by * (part - iy)) % LANES, 1)
                    total = jnp.where(group == part, moved, total)
            out_ref[slot_of(ix * ny + iy)] = total


def finish_kernel(blocks, out_ref):
    bx, by, depth = out_ref.shape
    peers = blocks.shape[0]
    ordered = jnp.concatenate([blocks[own_slot_of(rank)] for rank in range(peers)], axis=0)
    turned = ordered.T
    for x in range(bx):
        row = ((x % 4) * (bx // 4) + x // 4) * by
        out_ref[x] = turned[row : row + by]


def whole_planes(residual_q2, viscosity, pinned):
    bx, by, depth = viscosity.shape
    groups = bx // 4
    peers = SPLIT[0] * SPLIT[1]
    share = depth // peers
    planes = share + 2 * HALO
    count2 = share // 2 + 2 * NEAR
    limit = pltpu.CompilerParams(vmem_limit_bytes=32 * 2**20)

    def flat(rows):
        return jax.ShapeDtypeStruct((rows, LANES), F32)

    def blocks(count, rows):
        return jax.ShapeDtypeStruct((count, rows, LANES), F32)

    def room(count):
        return pltpu.VMEM((count, ROWS, LANES), F32)

    fluid = 1.0 / viscosity
    pin = 4.0 * pinned.astype(F32) * fluid
    parcels = pl.pallas_call(
        functools.partial(prepare_kernel, share),
        out_shape=blocks(peers, 3 * share),
        compiler_params=limit,
        name="prepare",
    )(residual_q2.reshape(4 * bx * by, 2 * depth), fluid, pin)
    own, inner, outer = pl.pallas_call(
        functools.partial(spread_kernel, groups, by),
        out_shape=(blocks(3 * share, ROWS),) + (blocks(3 * HALO - 2, ROWS),) * 2,
        scratch_shapes=[room(3 * share)],
        compiler_params=limit,
        name="spread",
    )(exchange(parcels))
    length = lax.axis_size("gz")
    parts = length * peers

    device = devices_of(length)

    def swap(field, first):
        pairs = [(device[i], device[i + 1]) for i in range(first, parts - 1, 2)]
        return lax.ppermute(field, ("gx", "gy", "gz"), pairs + [pair[::-1] for pair in pairs])

    outer, inner = swap(outer, 1), swap(inner, 0)
    count3 = share // 4
    near1, near2, far1, far2 = (
        (blocks(count, ROWS),) * fields
        for count, fields in ((share + HALO, 9), (count2, 8), (HALO + 8, 9), (count2, 9))
    )
    near1, near2, fluid2, pin2, fluid3, pin3 = pl.pallas_call(
        functools.partial(near_kernel, share),
        out_shape=(near1, near2) + (blocks(count2, ROWS),) * 2 + (blocks(count3, ROWS),) * 2,
        scratch_shapes=[room(share + HALO)] * 4 + [room(count2)] * 2,
        compiler_params=limit,
        name="near",
    )(own, inner)
    far1, far2, parcel = pl.pallas_call(
        functools.partial(down_kernel, share),
        out_shape=(far1, far2, blocks(5, 2)),
        scratch_shapes=[room(HALO + 8)] * 4 + [room(count2)] * 5,
        compiler_params=limit,
        name="down",
    )(own, outer, near2, fluid2, pin2, fluid3, pin3)
    copies = jnp.broadcast_to(parcel, (parts,) + parcel.shape)
    packed = lax.all_to_all(copies, ("gx", "gy", "gz"), 0, 0, tiled=True)
    depth3 = parts * count3
    mine = pl.pallas_call(
        functools.partial(up_kernel, groups, by, share),
        out_shape=blocks(peers, share),
        scratch_shapes=[room(planes), room(planes), room(count2), room(count2), room(count2)]
        + [pltpu.VMEM((rows, LANES), F32) for rows in (depth3, depth3, depth3 + 3 * NEAR)]
        + [room(share)],
        compiler_params=limit,
        name="up",
    )(packed, near1, far1, far2)
    return pl.pallas_call(
        finish_kernel,
        out_shape=jax.ShapeDtypeStruct((bx, by, depth), F32),
        compiler_params=limit,
        name="finish",
    )(exchange(mine))


def one_tile_planes(mesh, viscosity):
    split = (mesh.shape["gx"], mesh.shape["gy"])
    depth = viscosity.shape[2]
    fits = viscosity.shape[:2] == PLANE and split == SPLIT
    return fits and depth == 4 * LANES and depth // mesh.shape["gz"] == LANES


def solution(mesh):
    placed = (P("gx", "gy", "gz"), P("gx", "gy", "gz"), P("gx", "gy", "gz"))

    def cycle(residual_q2, viscosity, pinned):
        chosen = whole_planes if one_tile_planes(mesh, viscosity) else per_device
        return jax.shard_map(
            chosen, mesh=mesh, in_specs=placed, out_specs=P("gx", "gy", "gz"), check_vma=False
        )(residual_q2, viscosity, pinned)

    return cycle
```

```python
import functools

import jax
import jax.numpy as jnp
from jax import lax
from jax.experimental import pallas as pl
from jax.experimental.pallas import tpu as pltpu
from jax.sharding import PartitionSpec as P

NU = 3


OMEGA = 0.6


def with_halo(block, sides, width):
    for axis, dim in sides:
        count = lax.axis_size(axis)
        forward = [(i, i + 1) for i in range(count - 1)]
        backward = [(target, source) for source, target in forward]
        low = lax.ppermute(
            lax.slice_in_dim(block, block.shape[dim] - width, None, axis=dim), axis, forward
        )
        high = lax.ppermute(lax.slice_in_dim(block, 0, width, axis=dim), axis, backward)
        block = jnp.concatenate([low, block, high], axis=dim)
    return block


def coarsen(x):
    a, b, c = x.shape
    return x.reshape(a // 2, 2, b // 2, 2, c // 2, 2).sum(axis=(1, 3, 5))


def refine(x):
    return jnp.repeat(jnp.repeat(jnp.repeat(x, 2, 0), 2, 1), 2, 2)


def extended(field):
    return with_halo(field, (("gx", 0), ("gy", 1), ("gz", 2)), 1)


def shifted(padded):
    return [
        padded[2:, 1:-1, 1:-1],
        padded[:-2, 1:-1, 1:-1],
        padded[1:-1, 2:, 1:-1],
        padded[1:-1, :-2, 1:-1],
        padded[1:-1, 1:-1, 2:],
        padded[1:-1, 1:-1, :-2],
    ]


def neighbours(field):
    return shifted(extended(field))


def harmonic(fluid, near, factor):
    total = fluid + near
    return jnp.where(total > 0, factor * 2.0 * fluid * near / jnp.where(total > 0, total, 1.0), 0.0)


def couplings(fluid, factor):
    return [harmonic(fluid, near, factor) for near in neighbours(fluid)]


def apply_op(field, weights, diag):
    total = diag * field
    for weight, near in zip(weights, neighbours(field)):
        total = total - weight * near
    return total


def presmooth(rhs, weights, diag):
    corr = OMEGA * rhs / diag
    for sweep in range(NU - 1):
        corr = corr + OMEGA * (rhs - apply_op(corr, weights, diag)) / diag
    return corr


def postsmooth(corr, rhs, weights, diag):
    for sweep in range(NU):
        corr = corr + OMEGA * (rhs - apply_op(corr, weights, diag)) / diag
    return corr


def tridiag(coeffs, rhs):
    solved = lax.linalg.tridiagonal_solve(coeffs[0], coeffs[1], coeffs[2], rhs[..., None])[..., 0]
    last = rhs.ndim - 1
    shift_col = jnp.sum(rhs, axis=last, keepdims=True) / jnp.sum(
        coeffs[3], axis=last, keepdims=True
    )
    return solved + shift_col


def prepare_columns(weights, diag):
    lower = -weights[5]
    upper = -weights[4]
    across = diag + lower + upper
    return (
        lax.all_gather(lower, "gz", axis=2, tiled=True),
        lax.all_gather(diag, "gz", axis=2, tiled=True),
        lax.all_gather(upper, "gz", axis=2, tiled=True),
        lax.all_gather(across, "gz", axis=2, tiled=True),
    )


def column_solve(rhs, coeffs):
    depth = rhs.shape[2]
    whole = lax.all_gather(rhs, "gz", axis=2, tiled=True)
    solved = tridiag(coeffs, whole)
    return lax.dynamic_slice_in_dim(solved, lax.axis_index("gz") * depth, depth, 2)


def per_device(residual_q2, viscosity, pinned):
    fluid1 = 1.0 / viscosity
    pin1 = 4.0 * pinned.astype(jnp.float32) * fluid1
    rhs1 = coarsen(residual_q2.astype(jnp.float32))
    fluid2 = coarsen(fluid1) / 8.0
    pin2 = coarsen(pin1) / 4.0
    fluid3 = coarsen(fluid2) / 8.0
    pin3 = coarsen(pin2) / 4.0
    weights1 = couplings(fluid1, 1.0)
    weights2 = couplings(fluid2, 2.0)
    weights3 = couplings(fluid3, 4.0)
    diag1 = sum(weights1) + pin1
    diag2 = sum(weights2) + pin2
    diag3 = sum(weights3) + pin3
    coeffs = prepare_columns(weights3, diag3)
    corr1 = presmooth(rhs1, weights1, diag1)
    rhs2 = coarsen(rhs1 - apply_op(corr1, weights1, diag1))
    corr2 = presmooth(rhs2, weights2, diag2)
    rhs3 = coarsen(rhs2 - apply_op(corr2, weights2, diag2))
    corr3 = column_solve(rhs3, coeffs)
    corr3 = corr3 + column_solve(rhs3 - apply_op(corr3, weights3, diag3), coeffs)
    corr2 = postsmooth(corr2 + refine(corr3), rhs2, weights2, diag2)
    corr1 = postsmooth(corr1 + refine(corr2), rhs1, weights1, diag1)
    return diag1 * corr1


PLANE = (32, 32)
SPLIT = (2, 4)
ROWS = 8
LANES = 128
HALO = 16
NEAR = 8
PIECE = 8
TINY = 1e-30
F32 = jnp.float32


def iota(shape, dim):
    return lax.broadcasted_iota(jnp.int32, shape, dim)


def dot01(field, chosen):
    total = None
    rest = field
    for part in range(3):
        piece = rest.astype(jnp.bfloat16)
        term = jnp.dot(piece, chosen, preferred_element_type=F32)
        total = term if total is None else total + term
        if part < 2:
            rest = rest - piece.astype(F32)
    return total


def dot10(chosen, field):
    total = None
    rest = field
    for part in range(3):
        piece = rest.astype(jnp.bfloat16)
        term = lax.dot_general(
            chosen, piece, (((1,), (1,)), ((), ())), preferred_element_type=F32
        )
        total = term if total is None else total + term
        if part < 2:
            rest = rest - piece.astype(F32)
    return total


def where01(condition):
    return jnp.where(condition, 1.0, 0.0).astype(jnp.bfloat16)


def loop(low, high, size, body):
    for plane in range(low, high, size):
        body(plane, min(size, high - plane))


def inverse_of(field):
    first = pl.reciprocal(field, approx=True)
    return first * (2.0 - field * first)


class Level:
    def __init__(self, level):
        self.ny = PLANE[1] >> level
        self.xs = 4 >> level
        self.factor = float(2**level)

    def masks(self, shape):
        lane = iota(shape, 2)
        row = iota(shape, 1)
        within = (lane // self.ny) % self.xs
        y = lane % self.ny
        last_x = (row == ROWS - 1) & (within == self.xs - 1)
        return within, y == self.ny - 1, last_x

    def next_x(self, field):
        within = (iota(field.shape, 2) // self.ny) % self.xs
        moved = pltpu.roll(field, LANES - self.ny, 2)
        return jnp.where(within == self.xs - 1, pltpu.roll(moved, ROWS - 1, 1), moved)

    def last_x(self, field):
        within = (iota(field.shape, 2) // self.ny) % self.xs
        moved = pltpu.roll(field, self.ny, 2)
        return jnp.where(within == 0, pltpu.roll(moved, 1, 1), moved)

    def next_y(self, field):
        return pltpu.roll(field, LANES - 1, 2)

    def last_y(self, field):
        return pltpu.roll(field, 1, 2)

    def spread(self, field, scaled, plane, count):
        mid = field[1:-1]
        near = (
            self.next_x(mid), self.last_x(mid), self.next_y(mid), self.last_y(mid),
            field[2:], field[:-2],
        )
        terms = [weight[pl.ds(plane, count)] * value for weight, value in zip(scaled, near)]
        return mid, ((terms[0] + terms[1]) + (terms[2] + terms[3])) + (terms[4] + terms[5])


def mean_of(fluid, near, factor):
    return ((factor * 2.0) * fluid * near) * inverse_of(jnp.maximum(fluid + near, TINY))


def set_level(level, low, high, fluid, pin, rhs, fields):
    scaled, start, diag = fields

    def body(plane, count):
        wide = fluid[pl.ds(plane - 1, count + 2)]
        mid = wide[1:-1]
        within, end_y, end_x = level.masks(mid.shape)
        to_x = jnp.where(end_x, 0.0, mean_of(mid, level.next_x(mid), level.factor))
        to_y = jnp.where(end_y, 0.0, mean_of(mid, level.next_y(mid), level.factor))
        to_z = mean_of(wide[:-1], wide[1:], level.factor)
        weights = (to_x, level.last_x(to_x), to_y, level.last_y(to_y), to_z[1:], to_z[:-1])
        total = (
            (weights[0] + weights[1])
            + (weights[2] + weights[3])
            + (weights[4] + weights[5])
            + pin[pl.ds(plane, count)]
        )
        gain = OMEGA * inverse_of(jnp.maximum(total, TINY))
        for target, weight in zip(scaled, weights):
            target[pl.ds(plane, count)] = gain * weight
        start[pl.ds(plane, count)] = gain * rhs[pl.ds(plane, count)]
        diag[pl.ds(plane, count)] = total

    loop(low, high, PIECE, body)


def swept(level, plane, count, fields, source, shift=0):
    scaled, start, _ = fields
    mid, total = level.spread(source[pl.ds(plane - 1, count + 2)], scaled, plane - shift, count)
    return (1.0 - OMEGA) * mid + (start[pl.ds(plane - shift, count)] + total)


def sweep(level, low, high, fields, source, target, shift=0):
    def body(plane, count):
        target[pl.ds(plane, count)] = swept(level, plane, count, fields, source, shift)

    loop(low, high, PIECE, body)


def pair_sum(field):
    half = field.reshape((field.shape[0] // 2, 2) + field.shape[1:])
    return half[:, 0] + half[:, 1]


def coarse_residual(level, low, high, fields, corr, target):
    scaled, start, diag = fields

    def body(plane, count):
        mid, total = level.spread(corr[pl.ds(plane - 1, count + 2)], scaled, plane, count)
        rest = (start[pl.ds(plane, count)] + total) - OMEGA * mid
        rest = rest * (diag[pl.ds(plane, count)] * (1.0 / OMEGA))
        target[pl.ds((plane - low) // 2, count // 2)] = pair_sum(rest)

    loop(low, high, PIECE, body)


def lanes_down(level):
    fine = iota((LANES, LANES), 0)
    coarse = iota((LANES, LANES), 1)
    ny, xs = PLANE[1] >> level, 4 >> level
    half = xs // 2
    same_x = ((fine // ny) % xs) // 2 == (coarse // (ny // 2)) % half
    same_y = (fine % ny) // 2 == coarse % (ny // 2)
    return where01((fine < ny * xs) & same_x & same_y)


def in_lanes(field, chosen):
    flat = field.reshape(field.shape[0] * ROWS, LANES)
    return dot01(flat, chosen).reshape(field.shape)


def path_of(group):
    nx, ny = SPLIT
    row, column = 0, 0
    for index in range(group + 1):
        columns = list(range(ny)) if column == 0 else list(range(ny))[::-1]
        if index % 2:
            path = [(row, at) for at in columns] + [(1 - row, at) for at in columns[::-1]]
        else:
            path = []
            for at in columns:
                path += [(row, at), (1 - row, at)]
                row = 1 - row
        row, column = path[-1]
    return [row * ny + column for row, column in path]


def lookup(table, index):
    found = table[0]
    for at, value in enumerate(table[1:], 1):
        found = jnp.where(index == at, value, found)
    return found


def slot_of(peer):
    nx, ny = SPLIT
    return nx * ny - 1 - (peer % ny * nx + peer // ny)


def own_slot_of(rank):
    groups = range(lax.axis_size("gz"))
    return lookup([slot_of(path_of(group)[rank]) for group in groups], lax.axis_index("gz"))


def exchange(field):
    peers, groups = SPLIT[0] * SPLIT[1], lax.axis_size("gz")
    order = sorted(range(peers), key=slot_of)
    members = [[peer * groups + group for peer in order] for group in range(groups)]
    axes = ("gx", "gy", "gz")
    return lax.all_to_all(field, axes, 0, 0, axis_index_groups=members, tiled=True)


def slabs_of(groups):
    peers = SPLIT[0] * SPLIT[1]
    return [
        group * peers + path_of(group).index(peer) for peer in range(peers) for group in range(groups)
    ]


def own_slab():
    nx, ny = SPLIT
    groups = lax.axis_size("gz")
    device = (lax.axis_index("gx") * ny + lax.axis_index("gy")) * groups + lax.axis_index("gz")
    return lookup(slabs_of(groups), device)


def devices_of(groups):
    slabs = slabs_of(groups)
    return [slabs.index(slab) for slab in range(len(slabs))]


def prepare_kernel(share, res_ref, fluid_ref, pin_ref, out_ref):
    bx, by, depth = fluid_ref.shape
    cells = bx * by
    groups = bx // 4
    order = [x for low in range(4) for x in range(low, bx, 4)]
    fine = iota((cells, 4 * cells), 1)
    x, y = fine // (4 * by), (fine % (2 * by)) // 2
    chosen = where01((x % 4) * (groups * by) + (x // 4) * by + y == iota((cells, 4 * cells), 0))
    wide = lax.dot_general(
        chosen, res_ref[...], (((1,), (0,)), ((), ())), preferred_element_type=F32
    )
    rhs = dot10(where01(iota((depth, 2 * depth), 1) // 2 == iota((depth, 2 * depth), 0)), wide)

    def turned(field_ref):
        field = jnp.concatenate([field_ref[x : x + 1] for x in order], axis=0)
        return field.reshape(cells, depth).T

    fluid, pin = turned(fluid_ref), turned(pin_ref)
    for rank in range(depth // share):
        peer, begin = own_slot_of(rank), rank * share
        for index, field in enumerate((fluid, rhs, pin)):
            out_ref[peer, index * share : (index + 1) * share] = field[begin : begin + share]


def spread_kernel(groups, by, gathered, own, inner, outer, straight):
    for start in range(0, own.shape[0], ROWS):
        place(gathered, start, straight, start, groups, by)
    share = own.shape[0] // 3
    odd = own_slab() % 2 == 1
    for index in range(3):
        for plane in range(share):
            at = jnp.where(odd, share - 1 - plane, plane)
            own[index * share + plane] = straight[index * share + at]
    for target, drop in ((inner, 0), (outer, share - 1)):
        row = 0
        for index in range(3):
            for plane in range(share):
                if index == 0 or plane != drop:
                    target[row] = own[index * share + plane]
                    row += 1


def place(gathered, row, target, plane, groups, by):
    group = (iota((ROWS, LANES), 1) // by) % groups
    nx, ny = SPLIT
    for ix in range(nx):
        found = [gathered[slot_of(ix * ny + iy), pl.ds(row, ROWS), :] for iy in range(ny)]
        for part in range(groups):
            total = found[part]
            for iy in range(ny):
                if iy != part:
                    moved = pltpu.roll(found[iy], (by * (iy - part)) % LANES, 1)
                    total = jnp.where(group == iy, moved, total)
            target[pl.ds(plane, ROWS), ix * groups + part, :] = total


def near_kernel(
    depth,
    own, inner,
    saved1, saved2, fluid2, pin2, fluid3, pin3,
    fluid1, rhs1, pin1, other1, rhs2, sums,
):
    row = 0
    for index, target in enumerate((fluid1, rhs1, pin1)):
        target[0:depth] = own[index * depth : (index + 1) * depth]
        count = HALO if index == 0 else HALO - 1
        for plane in range(count):
            target[depth + plane] = inner[row + count - 1 - plane]
        if count < HALO:
            target[depth + count] = jnp.zeros((ROWS, LANES), F32)
        row += count
    fine, coarse = Level(0), Level(1)
    down1, down2 = lanes_down(0), lanes_down(1)
    fields1, corr1 = (saved1[0:6], saved1[6], saved1[7]), saved1[8]
    fields2 = (saved2[0:6], saved2[6], saved2[7])
    planes = depth + HALO
    set_level(fine, 1, planes - 1, fluid1, pin1, rhs1, fields1)
    sweep(fine, 2, planes - 2, fields1, fields1[1], other1)
    sweep(fine, 3, planes - 3, fields1, other1, corr1)
    coarse_residual(fine, 4, planes - 4, fields1, corr1, sums)
    count2 = planes // 2
    for source, target, share in ((fluid1, fluid2, 8.0), (pin1, pin2, 4.0)):
        target[NEAR : NEAR + count2] = in_lanes(pair_sum(source[...]), down1) * (1.0 / share)
    low2, high2 = NEAR + 2, NEAR + count2 - 2
    rhs2[low2:high2] = in_lanes(sums[0 : high2 - low2], down1)
    set_level(coarse, low2, high2, fluid2, pin2, rhs2, fields2)
    for source, target, scale in ((fluid2, fluid3, 0.125), (pin2, pin3, 0.25)):
        target[...] = in_lanes(pair_sum(source[NEAR : NEAR + depth // 2]), down2) * scale


def down_kernel(
    depth,
    own, outer, near2, near_fluid2, near_pin2, fluid3, pin3,
    saved1, saved2,
    packed,
    fluid1, rhs1, pin1, other1, fluid2, rhs2, pin2, other2, sums,
):
    planes = fluid1.shape[0]
    row = 0
    for index, target in enumerate((fluid1, rhs1, pin1)):
        count = HALO if index == 0 else HALO - 1
        if count < HALO:
            target[0] = jnp.zeros((ROWS, LANES), F32)
        for plane in range(count):
            target[HALO - count + plane] = outer[row + count - 1 - plane]
        row += count
        target[HALO:planes] = own[index * depth : index * depth + planes - HALO]

    fine, coarse = Level(0), Level(1)
    down1, down2 = lanes_down(0), lanes_down(1)
    fields1, corr1 = (saved1[0:6], saved1[6], saved1[7]), saved1[8]
    fields2, corr2 = (saved2[0:6], saved2[6], saved2[7]), saved2[8]
    set_level(fine, 1, planes - 1, fluid1, pin1, rhs1, fields1)
    sweep(fine, 2, planes - 2, fields1, fields1[1], other1)
    sweep(fine, 3, planes - 3, fields1, other1, corr1)
    count2 = depth // 2 + 2 * NEAR
    low2, done, high2 = 2, NEAR + 2, count2 - 2
    coarse_residual(fine, 2 * low2, 2 * done, fields1, corr1, sums)
    for source, ready, target, share in (
        (fluid1, near_fluid2, fluid2, 8.0), (pin1, near_pin2, pin2, 4.0)
    ):
        target[0:NEAR] = in_lanes(pair_sum(source[0:HALO]), down1) * (1.0 / share)
        target[NEAR : done + 1] = ready[NEAR : done + 1]
    rhs2[low2:done] = in_lanes(sums[0 : done - low2], down1)
    set_level(coarse, low2, done, fluid2, pin2, rhs2, fields2)
    for source, target in zip(near2, saved2[0:8]):
        target[done:high2] = source[done:high2]
    sweep(coarse, low2 + 1, high2 - 1, fields2, fields2[1], other2)
    sweep(coarse, low2 + 2, high2 - 2, fields2, other2, corr2)
    coarse_residual(coarse, NEAR, NEAR + depth // 2, fields2, corr2, sums)
    count3 = depth // 4
    rhs3 = in_lanes(sums[0:count3], down2)
    lane = iota((count3, LANES), 1) // ROWS
    first = jnp.zeros((count3, LANES), F32)
    second = jnp.zeros((count3, LANES), F32)
    for row in range(ROWS):
        first = jnp.where(lane == row, rhs3[:, row, :], first)
        first = jnp.where(lane == ROWS + row, fluid3[:, row, :], first)
        second = jnp.where(lane % ROWS == row, pin3[:, row, :], second)
    odd = own_slab() % 2 == 1

    def ordered(field):
        back = [field[row : row + 1] for row in reversed(range(count3))]
        return jnp.where(odd, jnp.concatenate(back, axis=0), field)

    first, second = ordered(first), ordered(second)
    packed[0] = first[0:2]
    packed[1] = first[2:4]
    packed[2] = jnp.where(lane[0:2] < ROWS, second[0:2], second[2:4])
    lane = iota((1, LANES), 1) // (LANES // 4)
    for index, plane in enumerate((NEAR + depth // 2 - 5, NEAR + 4)):
        for half in range(2):
            row = jnp.zeros((1, LANES), F32)
            for quarter in range(4):
                at = half * 4 + quarter
                row = jnp.where(lane == quarter, corr2[plane, at : at + 1, :], row)
            packed[3 + index, half : half + 1, :] = row


def rolled(field, shift):
    count = field.shape[0]
    shift %= count
    if shift % ROWS:
        return pltpu.roll(field, shift, 0)
    return jnp.concatenate([field[count - shift :], field[: count - shift]], axis=0)


def columns(rhs, fluid, pin):
    depth = fluid.shape[0]
    z, lane = iota(fluid.shape, 0), iota(fluid.shape, 1)
    y, x = lane % ROWS, (lane // ROWS) % ROWS

    def next_x(field):
        return pltpu.roll(field, LANES - ROWS, 1)

    def next_y(field):
        return pltpu.roll(field, LANES - 1, 1)

    wz = jnp.where(z == depth - 1, 0.0, mean_of(fluid, rolled(fluid, -1), 4.0))
    wy = jnp.where(y == ROWS - 1, 0.0, mean_of(fluid, next_y(fluid), 4.0))
    wx = jnp.where(x == ROWS - 1, 0.0, mean_of(fluid, next_x(fluid), 4.0))
    across = (wx + pltpu.roll(wx, ROWS, 1)) + (wy + pltpu.roll(wy, 1, 1)) + pin
    share = 1.0 / jnp.sum(across, axis=0, keepdims=True)

    above, below, own = rolled(wz, 1), wz, across
    steps = []
    stride, right = 1, rhs
    while stride < depth:
        inverse = inverse_of(above + below + own)
        up = above * rolled(inverse, stride)
        down = below * rolled(inverse, -stride)
        own = own + up * rolled(own, stride) + down * rolled(own, -stride)
        above = up * rolled(above, stride)
        below = down * rolled(below, -stride)
        right = right + up * rolled(right, stride) + down * rolled(right, -stride)
        steps.append((stride, up, down))
        stride *= 2
    inverse = inverse_of(above + below + own)

    def mean(right):
        return jnp.sum(right, axis=0, keepdims=True) * share

    corr = right * inverse + mean(rhs)
    flow_x = wx * (next_x(corr) - corr)
    flow_y = wy * (next_y(corr) - corr)
    flow_z = wz * (rolled(corr, -1) - corr)
    rest = (
        (rhs - pin * corr)
        + (flow_x - pltpu.roll(flow_x, ROWS, 1))
        + (flow_y - pltpu.roll(flow_y, 1, 1))
        + (flow_z - rolled(flow_z, 1))
    )
    right = rest
    for stride, up, down in steps:
        right = right + up * rolled(right, stride) + down * rolled(right, -stride)
    return (corr + mean(rest)) + right * inverse


def up_kernel(
    groups, by, depth,
    packed, near1, far1, far2,
    out_ref,
    one1, two1, one2, two2, lifted, first, second, solved, final,
):
    count3 = depth // 4
    shares = packed.shape[0]
    peers = SPLIT[0] * SPLIT[1]
    devices = devices_of(shares // peers)
    for slab, index in enumerate(devices):
        row = slab * count3
        first[row : row + 2] = packed[index, 0]
        first[row + 2 : row + 4] = packed[index, 1]
        both = packed[index, 2]
        second[row : row + 2] = both
        second[row + 2 : row + 4] = pltpu.roll(both, LANES // 2, 1)
    half = iota((shares * count3, LANES), 1) < LANES // 2

    def low_half(field):
        return jnp.where(half, field, pltpu.roll(field, LANES // 2, 1))

    def high_half(field):
        return jnp.where(half, pltpu.roll(field, LANES // 2, 1), field)

    solved[NEAR : NEAR + shares * count3] = columns(
        low_half(first[...]), high_half(first[...]), low_half(second[...])
    )
    solved[0:NEAR] = jnp.zeros((NEAR, LANES), F32)
    solved[NEAR + shares * count3 :] = jnp.zeros((2 * NEAR, LANES), F32)

    nx, ny = SPLIT
    part = own_slab()
    count = count3 + 2 * NEAR
    tall = solved[pl.ds(part * count3, count + count3), :]
    fine, coarse = Level(0), Level(1)
    cell = iota((LANES, LANES), 0)
    lane = iota((LANES, LANES), 1)
    spread = where01((cell < ROWS) & (cell == (lane % coarse.ny) // 2))
    rows = tall.shape[0]
    turned = [tall] + [pltpu.roll(tall, LANES - ROWS * row, 1) for row in range(1, ROWS)]
    wide = dot01(jnp.concatenate(turned, axis=0), spread)
    for row in range(ROWS):
        lifted[0:rows, row, :] = wide[row * rows : (row + 1) * rows]

    odd = part % 2 == 1

    def lifted_to(plane):
        parent = plane // 2 + NEAR // 2
        return lifted[jnp.where(odd, count - 1 - parent, parent)]

    near_fields, near_corr1 = (near1[0:6], near1[6], near1[7]), near1[8]
    far_fields, far_corr1 = (far1[0:6], far1[6], far1[7]), far1[8]
    fields2, corr2 = (far2[0:6], far2[6], far2[7]), far2[8]
    low, high = NEAR - 4, NEAR + depth // 2 + 4
    reach = depth // 2 + NEAR
    quarter = iota((ROWS, LANES), 1) // (LANES // 4)
    row = iota((ROWS, LANES), 0)

    def unpacked(index, which):
        pair = packed[lookup(devices, jnp.clip(index, 0, shares - 1)), which]
        total = None
        for shift in range(4):
            moved = pltpu.roll(pair, shift * (LANES // 4), 1)
            wide = jnp.where(row < 4, moved[0:1, :], moved[1:2, :])
            kept = jnp.where((quarter - shift) % 4 == row % 4, wide, 0.0)
            total = kept if total is None else total + kept
        return total

    one2[low - 1] = unpacked(jnp.where(odd, part + 1, part - 1), 4) + lifted_to(low - 1)
    for plane in range(low, high):
        one2[plane] = corr2[plane] + lifted_to(plane)
    one2[high] = unpacked(jnp.where(odd, part - 1, part + 1), 3) + lifted_to(high)
    sweep(coarse, NEAR - 4, reach + 4, fields2, one2, two2)
    sweep(coarse, NEAR - 3, reach + 3, fields2, two2, one2)
    sweep(coarse, NEAR - 2, reach + 2, fields2, one2, two2)

    fine_lane, coarse_lane = iota((LANES, LANES), 1), iota((LANES, LANES), 0)
    x_of = (fine_lane // fine.ny) // 2
    y_of = (fine_lane % fine.ny) // 2
    up = where01(coarse_lane == x_of * coarse.ny + y_of)
    lifted[0 : depth // 2 + 4] = in_lanes(two2[NEAR - 2 : reach + 2], up)
    parents = lifted[0 : depth // 2 + 4]
    twice = jnp.broadcast_to(parents[:, None], (parents.shape[0], 2, ROWS, LANES))
    low, high = HALO - 4, HALO + depth + 4
    turn = HALO + 3
    for plane in range(low, high):
        corr = far_corr1[plane] if plane < turn else near_corr1[plane - HALO]
        one1[plane] = corr + lifted[(plane - low) // 2]
    reach = depth + HALO
    for more, source, target in ((2, one1, two1), (1, two1, one1)):
        sweep(fine, HALO - more, turn, far_fields, source, target)
        sweep(fine, turn, reach + more, near_fields, source, target, HALO)

    def last(fields, shift):
        def body(plane, count):
            value = swept(fine, plane, count, fields, one1, shift)
            value = value * fields[2][pl.ds(plane - shift, count)]
            for index in range(count):
                at = plane - HALO + index
                final[jnp.where(odd, depth - 1 - at, at)] = value[index]

        return body

    loop(HALO, turn, PIECE, last(far_fields, 0))
    loop(turn, reach, PIECE, last(near_fields, HALO))

    group = (iota((depth, LANES), 1) // by) % groups
    for ix in range(nx):
        scaled = [final[:, ix * groups + part, :] for part in range(groups)]
        for iy in range(ny):
            total = scaled[iy]
            for part in range(groups):
                if part != iy:
                    moved = pltpu.roll(scaled[part], (by * (part - iy)) % LANES, 1)
                    total = jnp.where(group == part, moved, total)
            out_ref[slot_of(ix * ny + iy)] = total


def finish_kernel(blocks, out_ref):
    bx, by, depth = out_ref.shape
    peers = blocks.shape[0]
    ordered = jnp.concatenate([blocks[own_slot_of(rank)] for rank in range(peers)], axis=0)
    turned = ordered.T
    for x in range(bx):
        row = ((x % 4) * (bx // 4) + x // 4) * by
        out_ref[x] = turned[row : row + by]


def whole_planes(residual_q2, viscosity, pinned):
    bx, by, depth = viscosity.shape
    groups = bx // 4
    peers = SPLIT[0] * SPLIT[1]
    share = depth // peers
    planes = share + 2 * HALO
    count2 = share // 2 + 2 * NEAR
    limit = pltpu.CompilerParams(vmem_limit_bytes=32 * 2**20)

    def flat(rows):
        return jax.ShapeDtypeStruct((rows, LANES), F32)

    def blocks(count, rows):
        return jax.ShapeDtypeStruct((count, rows, LANES), F32)

    def room(count):
        return pltpu.VMEM((count, ROWS, LANES), F32)

    fluid = 1.0 / viscosity
    pin = 4.0 * pinned.astype(F32) * fluid
    parcels = pl.pallas_call(
        functools.partial(prepare_kernel, share),
        out_shape=blocks(peers, 3 * share),
        compiler_params=limit,
        name="prepare",
    )(residual_q2.reshape(4 * bx * by, 2 * depth), fluid, pin)
    own, inner, outer = pl.pallas_call(
        functools.partial(spread_kernel, groups, by),
        out_shape=(blocks(3 * share, ROWS),) + (blocks(3 * HALO - 2, ROWS),) * 2,
        scratch_shapes=[room(3 * share)],
        compiler_params=limit,
        name="spread",
    )(exchange(parcels))
    length = lax.axis_size("gz")
    parts = length * peers

    device = devices_of(length)

    def swap(field, first):
        pairs = [(device[i], device[i + 1]) for i in range(first, parts - 1, 2)]
        return lax.ppermute(field, ("gx", "gy", "gz"), pairs + [pair[::-1] for pair in pairs])

    outer, inner = swap(outer, 1), swap(inner, 0)
    count3 = share // 4
    near1, near2, far1, far2 = (
        (blocks(count, ROWS),) * fields
        for count, fields in ((share + HALO, 9), (count2, 8), (HALO + 8, 9), (count2, 9))
    )
    near1, near2, fluid2, pin2, fluid3, pin3 = pl.pallas_call(
        functools.partial(near_kernel, share),
        out_shape=(near1, near2) + (blocks(count2, ROWS),) * 2 + (blocks(count3, ROWS),) * 2,
        scratch_shapes=[room(share + HALO)] * 4 + [room(count2)] * 2,
        compiler_params=limit,
        name="near",
    )(own, inner)
    far1, far2, parcel = pl.pallas_call(
        functools.partial(down_kernel, share),
        out_shape=(far1, far2, blocks(5, 2)),
        scratch_shapes=[room(HALO + 8)] * 4 + [room(count2)] * 5,
        compiler_params=limit,
        name="down",
    )(own, outer, near2, fluid2, pin2, fluid3, pin3)
    copies = jnp.broadcast_to(parcel, (parts,) + parcel.shape)
    packed = lax.all_to_all(copies, ("gx", "gy", "gz"), 0, 0, tiled=True)
    depth3 = parts * count3
    mine = pl.pallas_call(
        functools.partial(up_kernel, groups, by, share),
        out_shape=blocks(peers, share),
        scratch_shapes=[room(planes), room(planes), room(count2), room(count2), room(count2)]
        + [pltpu.VMEM((rows, LANES), F32) for rows in (depth3, depth3, depth3 + 3 * NEAR)]
        + [room(share)],
        compiler_params=limit,
        name="up",
    )(packed, near1, far1, far2)
    return pl.pallas_call(
        finish_kernel,
        out_shape=jax.ShapeDtypeStruct((bx, by, depth), F32),
        compiler_params=limit,
        name="finish",
    )(exchange(mine))


def one_tile_planes(mesh, viscosity):
    split = (mesh.shape["gx"], mesh.shape["gy"])
    depth = viscosity.shape[2]
    fits = viscosity.shape[:2] == PLANE and split == SPLIT
    return fits and depth == 4 * LANES and depth // mesh.shape["gz"] == LANES


def solution(mesh):
    placed = (P("gx", "gy", "gz"), P("gx", "gy", "gz"), P("gx", "gy", "gz"))

    def cycle(residual_q2, viscosity, pinned):
        chosen = whole_planes if one_tile_planes(mesh, viscosity) else per_device
        return jax.shard_map(
            chosen, mesh=mesh, in_specs=placed, out_specs=P("gx", "gy", "gz"), check_vma=False
        )(residual_q2, viscosity, pinned)

    return cycle
```

```python
import functools

import jax
import jax.numpy as jnp
from jax import lax
from jax.experimental import pallas as pl
from jax.experimental.pallas import tpu as pltpu
from jax.sharding import PartitionSpec as P

NU = 3


OMEGA = 0.6


def with_halo(block, sides, width):
    for axis, dim in sides:
        count = lax.axis_size(axis)
        forward = [(i, i + 1) for i in range(count - 1)]
        backward = [(target, source) for source, target in forward]
        low = lax.ppermute(
            lax.slice_in_dim(block, block.shape[dim] - width, None, axis=dim), axis, forward
        )
        high = lax.ppermute(lax.slice_in_dim(block, 0, width, axis=dim), axis, backward)
        block = jnp.concatenate([low, block, high], axis=dim)
    return block


def coarsen(x):
    a, b, c = x.shape
    return x.reshape(a // 2, 2, b // 2, 2, c // 2, 2).sum(axis=(1, 3, 5))


def refine(x):
    return jnp.repeat(jnp.repeat(jnp.repeat(x, 2, 0), 2, 1), 2, 2)


def extended(field):
    return with_halo(field, (("gx", 0), ("gy", 1), ("gz", 2)), 1)


def shifted(padded):
    return [
        padded[2:, 1:-1, 1:-1],
        padded[:-2, 1:-1, 1:-1],
        padded[1:-1, 2:, 1:-1],
        padded[1:-1, :-2, 1:-1],
        padded[1:-1, 1:-1, 2:],
        padded[1:-1, 1:-1, :-2],
    ]


def neighbours(field):
    return shifted(extended(field))


def harmonic(fluid, near, factor):
    total = fluid + near
    return jnp.where(total > 0, factor * 2.0 * fluid * near / jnp.where(total > 0, total, 1.0), 0.0)


def couplings(fluid, factor):
    return [harmonic(fluid, near, factor) for near in neighbours(fluid)]


def apply_op(field, weights, diag):
    total = diag * field
    for weight, near in zip(weights, neighbours(field)):
        total = total - weight * near
    return total


def presmooth(rhs, weights, diag):
    corr = OMEGA * rhs / diag
    for sweep in range(NU - 1):
        corr = corr + OMEGA * (rhs - apply_op(corr, weights, diag)) / diag
    return corr


def postsmooth(corr, rhs, weights, diag):
    for sweep in range(NU):
        corr = corr + OMEGA * (rhs - apply_op(corr, weights, diag)) / diag
    return corr


def tridiag(coeffs, rhs):
    solved = lax.linalg.tridiagonal_solve(coeffs[0], coeffs[1], coeffs[2], rhs[..., None])[..., 0]
    last = rhs.ndim - 1
    shift_col = jnp.sum(rhs, axis=last, keepdims=True) / jnp.sum(
        coeffs[3], axis=last, keepdims=True
    )
    return solved + shift_col


def prepare_columns(weights, diag):
    lower = -weights[5]
    upper = -weights[4]
    across = diag + lower + upper
    return (
        lax.all_gather(lower, "gz", axis=2, tiled=True),
        lax.all_gather(diag, "gz", axis=2, tiled=True),
        lax.all_gather(upper, "gz", axis=2, tiled=True),
        lax.all_gather(across, "gz", axis=2, tiled=True),
    )


def column_solve(rhs, coeffs):
    depth = rhs.shape[2]
    whole = lax.all_gather(rhs, "gz", axis=2, tiled=True)
    solved = tridiag(coeffs, whole)
    return lax.dynamic_slice_in_dim(solved, lax.axis_index("gz") * depth, depth, 2)


def per_device(residual_q2, viscosity, pinned):
    fluid1 = 1.0 / viscosity
    pin1 = 4.0 * pinned.astype(jnp.float32) * fluid1
    rhs1 = coarsen(residual_q2.astype(jnp.float32))
    fluid2 = coarsen(fluid1) / 8.0
    pin2 = coarsen(pin1) / 4.0
    fluid3 = coarsen(fluid2) / 8.0
    pin3 = coarsen(pin2) / 4.0
    weights1 = couplings(fluid1, 1.0)
    weights2 = couplings(fluid2, 2.0)
    weights3 = couplings(fluid3, 4.0)
    diag1 = sum(weights1) + pin1
    diag2 = sum(weights2) + pin2
    diag3 = sum(weights3) + pin3
    coeffs = prepare_columns(weights3, diag3)
    corr1 = presmooth(rhs1, weights1, diag1)
    rhs2 = coarsen(rhs1 - apply_op(corr1, weights1, diag1))
    corr2 = presmooth(rhs2, weights2, diag2)
    rhs3 = coarsen(rhs2 - apply_op(corr2, weights2, diag2))
    corr3 = column_solve(rhs3, coeffs)
    corr3 = corr3 + column_solve(rhs3 - apply_op(corr3, weights3, diag3), coeffs)
    corr2 = postsmooth(corr2 + refine(corr3), rhs2, weights2, diag2)
    corr1 = postsmooth(corr1 + refine(corr2), rhs1, weights1, diag1)
    return diag1 * corr1


PLANE = (32, 32)
SPLIT = (2, 4)
ROWS = 8
LANES = 128
HALO = 16
NEAR = 8
PIECE = 8
TINY = 1e-30
F32 = jnp.float32


def iota(shape, dim):
    return lax.broadcasted_iota(jnp.int32, shape, dim)


def dot01(field, chosen):
    total = None
    rest = field
    for part in range(3):
        piece = rest.astype(jnp.bfloat16)
        term = jnp.dot(piece, chosen, preferred_element_type=F32)
        total = term if total is None else total + term
        if part < 2:
            rest = rest - piece.astype(F32)
    return total


def dot10(chosen, field):
    total = None
    rest = field
    for part in range(3):
        piece = rest.astype(jnp.bfloat16)
        term = lax.dot_general(
            chosen, piece, (((1,), (1,)), ((), ())), preferred_element_type=F32
        )
        total = term if total is None else total + term
        if part < 2:
            rest = rest - piece.astype(F32)
    return total


def where01(condition):
    return jnp.where(condition, 1.0, 0.0).astype(jnp.bfloat16)


def loop(low, high, size, body):
    for plane in range(low, high, size):
        body(plane, min(size, high - plane))


def inverse_of(field):
    first = pl.reciprocal(field, approx=True)
    return first * (2.0 - field * first)


class Level:
    def __init__(self, level):
        self.ny = PLANE[1] >> level
        self.xs = 4 >> level
        self.factor = float(2**level)

    def masks(self, shape):
        lane = iota(shape, 2)
        row = iota(shape, 1)
        within = (lane // self.ny) % self.xs
        y = lane % self.ny
        last_x = (row == ROWS - 1) & (within == self.xs - 1)
        return within, y == self.ny - 1, last_x

    def next_x(self, field):
        within = (iota(field.shape, 2) // self.ny) % self.xs
        moved = pltpu.roll(field, LANES - self.ny, 2)
        return jnp.where(within == self.xs - 1, pltpu.roll(moved, ROWS - 1, 1), moved)

    def last_x(self, field):
        within = (iota(field.shape, 2) // self.ny) % self.xs
        moved = pltpu.roll(field, self.ny, 2)
        return jnp.where(within == 0, pltpu.roll(moved, 1, 1), moved)

    def next_y(self, field):
        return pltpu.roll(field, LANES - 1, 2)

    def last_y(self, field):
        return pltpu.roll(field, 1, 2)

    def spread(self, field, scaled, plane, count):
        mid = field[1:-1]
        near = (
            self.next_x(mid), self.last_x(mid), self.next_y(mid), self.last_y(mid),
            field[2:], field[:-2],
        )
        terms = [weight[pl.ds(plane, count)] * value for weight, value in zip(scaled, near)]
        return mid, ((terms[0] + terms[1]) + (terms[2] + terms[3])) + (terms[4] + terms[5])


def mean_of(fluid, near, factor):
    return ((factor * 2.0) * fluid * near) * inverse_of(jnp.maximum(fluid + near, TINY))


def set_level(level, low, high, fluid, pin, rhs, fields):
    scaled, start, diag = fields

    def body(plane, count):
        wide = fluid[pl.ds(plane - 1, count + 2)]
        mid = wide[1:-1]
        within, end_y, end_x = level.masks(mid.shape)
        to_x = jnp.where(end_x, 0.0, mean_of(mid, level.next_x(mid), level.factor))
        to_y = jnp.where(end_y, 0.0, mean_of(mid, level.next_y(mid), level.factor))
        to_z = mean_of(wide[:-1], wide[1:], level.factor)
        weights = (to_x, level.last_x(to_x), to_y, level.last_y(to_y), to_z[1:], to_z[:-1])
        total = (
            (weights[0] + weights[1])
            + (weights[2] + weights[3])
            + (weights[4] + weights[5])
            + pin[pl.ds(plane, count)]
        )
        gain = OMEGA * inverse_of(jnp.maximum(total, TINY))
        for target, weight in zip(scaled, weights):
            target[pl.ds(plane, count)] = gain * weight
        start[pl.ds(plane, count)] = gain * rhs[pl.ds(plane, count)]
        diag[pl.ds(plane, count)] = total

    loop(low, high, PIECE, body)


def swept(level, plane, count, fields, source, shift=0):
    scaled, start, _ = fields
    mid, total = level.spread(source[pl.ds(plane - 1, count + 2)], scaled, plane - shift, count)
    return (1.0 - OMEGA) * mid + (start[pl.ds(plane - shift, count)] + total)


def sweep(level, low, high, fields, source, target, shift=0):
    def body(plane, count):
        target[pl.ds(plane, count)] = swept(level, plane, count, fields, source, shift)

    loop(low, high, PIECE, body)


def pair_sum(field):
    half = field.reshape((field.shape[0] // 2, 2) + field.shape[1:])
    return half[:, 0] + half[:, 1]


def coarse_residual(level, low, high, fields, corr, target):
    scaled, start, diag = fields

    def body(plane, count):
        mid, total = level.spread(corr[pl.ds(plane - 1, count + 2)], scaled, plane, count)
        rest = (start[pl.ds(plane, count)] + total) - OMEGA * mid
        rest = rest * (diag[pl.ds(plane, count)] * (1.0 / OMEGA))
        target[pl.ds((plane - low) // 2, count // 2)] = pair_sum(rest)

    loop(low, high, PIECE, body)


def lanes_down(level):
    fine = iota((LANES, LANES), 0)
    coarse = iota((LANES, LANES), 1)
    ny, xs = PLANE[1] >> level, 4 >> level
    half = xs // 2
    same_x = ((fine // ny) % xs) // 2 == (coarse // (ny // 2)) % half
    same_y = (fine % ny) // 2 == coarse % (ny // 2)
    return where01((fine < ny * xs) & same_x & same_y)


def in_lanes(field, chosen):
    flat = field.reshape(field.shape[0] * ROWS, LANES)
    return dot01(flat, chosen).reshape(field.shape)


def path_of(group):
    nx, ny = SPLIT
    row, column = 0, 0
    for index in range(group + 1):
        columns = list(range(ny)) if column == 0 else list(range(ny))[::-1]
        if index % 2:
            path = [(row, at) for at in columns] + [(1 - row, at) for at in columns[::-1]]
        else:
            path = []
            for at in columns:
                path += [(row, at), (1 - row, at)]
                row = 1 - row
        row, column = path[-1]
    return [row * ny + column for row, column in path]


def lookup(table, index):
    found = table[0]
    for at, value in enumerate(table[1:], 1):
        found = jnp.where(index == at, value, found)
    return found


def slot_of(peer):
    nx, ny = SPLIT
    return nx * ny - 1 - (peer % ny * nx + peer // ny)


def own_slot_of(rank):
    groups = range(lax.axis_size("gz"))
    return lookup([slot_of(path_of(group)[rank]) for group in groups], lax.axis_index("gz"))


def exchange(field):
    peers, groups = SPLIT[0] * SPLIT[1], lax.axis_size("gz")
    order = sorted(range(peers), key=slot_of)
    members = [[peer * groups + group for peer in order] for group in range(groups)]
    axes = ("gx", "gy", "gz")
    return lax.all_to_all(field, axes, 0, 0, axis_index_groups=members, tiled=True)


def slabs_of(groups):
    peers = SPLIT[0] * SPLIT[1]
    return [
        group * peers + path_of(group).index(peer) for peer in range(peers) for group in range(groups)
    ]


def own_slab():
    nx, ny = SPLIT
    groups = lax.axis_size("gz")
    device = (lax.axis_index("gx") * ny + lax.axis_index("gy")) * groups + lax.axis_index("gz")
    return lookup(slabs_of(groups), device)


def slots_of(groups):
    peers = SPLIT[0] * SPLIT[1]
    return [
        slot_of(peer) * groups + groups - 1 - group for group in range(groups) for peer in path_of(group)
    ]


def exchange_all(field):
    groups = lax.axis_size("gz")
    members = [device for _, device in sorted(zip(slots_of(groups), devices_of(groups)))]
    axes = ("gx", "gy", "gz")
    return lax.all_to_all(field, axes, 0, 0, axis_index_groups=[members], tiled=True)


def devices_of(groups):
    slabs = slabs_of(groups)
    return [slabs.index(slab) for slab in range(len(slabs))]


def prepare_kernel(share, res_ref, fluid_ref, pin_ref, out_ref):
    bx, by, depth = fluid_ref.shape
    cells = bx * by
    groups = bx // 4
    order = [x for low in range(4) for x in range(low, bx, 4)]
    fine = iota((cells, 4 * cells), 1)
    x, y = fine // (4 * by), (fine % (2 * by)) // 2
    chosen = where01((x % 4) * (groups * by) + (x // 4) * by + y == iota((cells, 4 * cells), 0))
    wide = lax.dot_general(
        chosen, res_ref[...], (((1,), (0,)), ((), ())), preferred_element_type=F32
    )
    rhs = dot10(where01(iota((depth, 2 * depth), 1) // 2 == iota((depth, 2 * depth), 0)), wide)

    def turned(field_ref):
        field = jnp.concatenate([field_ref[x : x + 1] for x in order], axis=0)
        return field.reshape(cells, depth).T

    fluid, pin = turned(fluid_ref), turned(pin_ref)
    for rank in range(depth // share):
        peer, begin = own_slot_of(rank), rank * share
        for index, field in enumerate((fluid, rhs, pin)):
            out_ref[peer, index * share : (index + 1) * share] = field[begin : begin + share]


def spread_kernel(groups, by, gathered, own, inner, outer, straight):
    for start in range(0, own.shape[0], ROWS):
        place(gathered, start, straight, start, groups, by)
    share = own.shape[0] // 3
    odd = own_slab() % 2 == 1
    for index in range(3):
        for plane in range(share):
            at = jnp.where(odd, share - 1 - plane, plane)
            own[index * share + plane] = straight[index * share + at]
    for target, drop in ((inner, 0), (outer, share - 1)):
        row = 0
        for index in range(3):
            for plane in range(share):
                if index == 0 or plane != drop:
                    target[row] = own[index * share + plane]
                    row += 1


def place(gathered, row, target, plane, groups, by):
    group = (iota((ROWS, LANES), 1) // by) % groups
    nx, ny = SPLIT
    for ix in range(nx):
        found = [gathered[slot_of(ix * ny + iy), pl.ds(row, ROWS), :] for iy in range(ny)]
        for part in range(groups):
            total = found[part]
            for iy in range(ny):
                if iy != part:
                    moved = pltpu.roll(found[iy], (by * (iy - part)) % LANES, 1)
                    total = jnp.where(group == iy, moved, total)
            target[pl.ds(plane, ROWS), ix * groups + part, :] = total


def near_kernel(
    depth,
    own, inner,
    saved1, saved2, fluid2, pin2, fluid3, pin3,
    fluid1, rhs1, pin1, other1, rhs2, sums,
):
    row = 0
    for index, target in enumerate((fluid1, rhs1, pin1)):
        target[0:depth] = own[index * depth : (index + 1) * depth]
        count = HALO if index == 0 else HALO - 1
        for plane in range(count):
            target[depth + plane] = inner[row + count - 1 - plane]
        if count < HALO:
            target[depth + count] = jnp.zeros((ROWS, LANES), F32)
        row += count
    fine, coarse = Level(0), Level(1)
    down1, down2 = lanes_down(0), lanes_down(1)
    fields1, corr1 = (saved1[0:6], saved1[6], saved1[7]), saved1[8]
    fields2 = (saved2[0:6], saved2[6], saved2[7])
    planes = depth + HALO
    set_level(fine, 1, planes - 1, fluid1, pin1, rhs1, fields1)
    sweep(fine, 2, planes - 2, fields1, fields1[1], other1)
    sweep(fine, 3, planes - 3, fields1, other1, corr1)
    coarse_residual(fine, 4, planes - 4, fields1, corr1, sums)
    count2 = planes // 2
    for source, target, share in ((fluid1, fluid2, 8.0), (pin1, pin2, 4.0)):
        target[NEAR : NEAR + count2] = in_lanes(pair_sum(source[...]), down1) * (1.0 / share)
    low2, high2 = NEAR + 2, NEAR + count2 - 2
    rhs2[low2:high2] = in_lanes(sums[0 : high2 - low2], down1)
    set_level(coarse, low2, high2, fluid2, pin2, rhs2, fields2)
    for source, target, scale in ((fluid2, fluid3, 0.125), (pin2, pin3, 0.25)):
        target[...] = in_lanes(pair_sum(source[NEAR : NEAR + depth // 2]), down2) * scale


def down_kernel(
    depth,
    own, outer, near2, near_fluid2, near_pin2, fluid3, pin3,
    saved1, saved2,
    packed,
    fluid1, rhs1, pin1, other1, fluid2, rhs2, pin2, other2, sums,
):
    planes = fluid1.shape[0]
    row = 0
    for index, target in enumerate((fluid1, rhs1, pin1)):
        count = HALO if index == 0 else HALO - 1
        if count < HALO:
            target[0] = jnp.zeros((ROWS, LANES), F32)
        for plane in range(count):
            target[HALO - count + plane] = outer[row + count - 1 - plane]
        row += count
        target[HALO:planes] = own[index * depth : index * depth + planes - HALO]

    fine, coarse = Level(0), Level(1)
    down1, down2 = lanes_down(0), lanes_down(1)
    fields1, corr1 = (saved1[0:6], saved1[6], saved1[7]), saved1[8]
    fields2, corr2 = (saved2[0:6], saved2[6], saved2[7]), saved2[8]
    set_level(fine, 1, planes - 1, fluid1, pin1, rhs1, fields1)
    sweep(fine, 2, planes - 2, fields1, fields1[1], other1)
    sweep(fine, 3, planes - 3, fields1, other1, corr1)
    count2 = depth // 2 + 2 * NEAR
    low2, done, high2 = 2, NEAR + 2, count2 - 2
    coarse_residual(fine, 2 * low2, 2 * done, fields1, corr1, sums)
    for source, ready, target, share in (
        (fluid1, near_fluid2, fluid2, 8.0), (pin1, near_pin2, pin2, 4.0)
    ):
        target[0:NEAR] = in_lanes(pair_sum(source[0:HALO]), down1) * (1.0 / share)
        target[NEAR : done + 1] = ready[NEAR : done + 1]
    rhs2[low2:done] = in_lanes(sums[0 : done - low2], down1)
    set_level(coarse, low2, done, fluid2, pin2, rhs2, fields2)
    for source, target in zip(near2, saved2[0:8]):
        target[done:high2] = source[done:high2]
    sweep(coarse, low2 + 1, high2 - 1, fields2, fields2[1], other2)
    sweep(coarse, low2 + 2, high2 - 2, fields2, other2, corr2)
    coarse_residual(coarse, NEAR, NEAR + depth // 2, fields2, corr2, sums)
    count3 = depth // 4
    rhs3 = in_lanes(sums[0:count3], down2)
    lane = iota((count3, LANES), 1) // ROWS
    first = jnp.zeros((count3, LANES), F32)
    second = jnp.zeros((count3, LANES), F32)
    for row in range(ROWS):
        first = jnp.where(lane == row, rhs3[:, row, :], first)
        first = jnp.where(lane == ROWS + row, fluid3[:, row, :], first)
        second = jnp.where(lane % ROWS == row, pin3[:, row, :], second)
    odd = own_slab() % 2 == 1

    def ordered(field):
        back = [field[row : row + 1] for row in reversed(range(count3))]
        return jnp.where(odd, jnp.concatenate(back, axis=0), field)

    first, second = ordered(first), ordered(second)
    packed[0] = first[0:2]
    packed[1] = first[2:4]
    packed[2] = jnp.where(lane[0:2] < ROWS, second[0:2], second[2:4])
    lane = iota((1, LANES), 1) // (LANES // 4)
    for index, plane in enumerate((NEAR + depth // 2 - 5, NEAR + 4)):
        for half in range(2):
            row = jnp.zeros((1, LANES), F32)
            for quarter in range(4):
                at = half * 4 + quarter
                row = jnp.where(lane == quarter, corr2[plane, at : at + 1, :], row)
            packed[3 + index, half : half + 1, :] = row


def rolled(field, shift):
    count = field.shape[0]
    shift %= count
    if shift % ROWS:
        return pltpu.roll(field, shift, 0)
    return jnp.concatenate([field[count - shift :], field[: count - shift]], axis=0)


def columns(rhs, fluid, pin):
    depth = fluid.shape[0]
    z, lane = iota(fluid.shape, 0), iota(fluid.shape, 1)
    y, x = lane % ROWS, (lane // ROWS) % ROWS

    def next_x(field):
        return pltpu.roll(field, LANES - ROWS, 1)

    def next_y(field):
        return pltpu.roll(field, LANES - 1, 1)

    wz = jnp.where(z == depth - 1, 0.0, mean_of(fluid, rolled(fluid, -1), 4.0))
    wy = jnp.where(y == ROWS - 1, 0.0, mean_of(fluid, next_y(fluid), 4.0))
    wx = jnp.where(x == ROWS - 1, 0.0, mean_of(fluid, next_x(fluid), 4.0))
    across = (wx + pltpu.roll(wx, ROWS, 1)) + (wy + pltpu.roll(wy, 1, 1)) + pin
    share = 1.0 / jnp.sum(across, axis=0, keepdims=True)

    above, below, own = rolled(wz, 1), wz, across
    steps = []
    stride, right = 1, rhs
    while stride < depth:
        inverse = inverse_of(above + below + own)
        up = above * rolled(inverse, stride)
        down = below * rolled(inverse, -stride)
        own = own + up * rolled(own, stride) + down * rolled(own, -stride)
        above = up * rolled(above, stride)
        below = down * rolled(below, -stride)
        right = right + up * rolled(right, stride) + down * rolled(right, -stride)
        steps.append((stride, up, down))
        stride *= 2
    inverse = inverse_of(above + below + own)

    def mean(right):
        return jnp.sum(right, axis=0, keepdims=True) * share

    corr = right * inverse + mean(rhs)
    flow_x = wx * (next_x(corr) - corr)
    flow_y = wy * (next_y(corr) - corr)
    flow_z = wz * (rolled(corr, -1) - corr)
    rest = (
        (rhs - pin * corr)
        + (flow_x - pltpu.roll(flow_x, ROWS, 1))
        + (flow_y - pltpu.roll(flow_y, 1, 1))
        + (flow_z - rolled(flow_z, 1))
    )
    right = rest
    for stride, up, down in steps:
        right = right + up * rolled(right, stride) + down * rolled(right, -stride)
    return (corr + mean(rest)) + right * inverse


def up_kernel(
    groups, by, depth,
    packed, near1, far1, far2,
    out_ref,
    one1, two1, one2, two2, lifted, first, second, solved, final,
):
    count3 = depth // 4
    shares = packed.shape[0]
    peers = SPLIT[0] * SPLIT[1]
    slots = slots_of(shares // peers)
    for slab, index in enumerate(slots):
        row = slab * count3
        first[row : row + 2] = packed[index, 0]
        first[row + 2 : row + 4] = packed[index, 1]
        both = packed[index, 2]
        second[row : row + 2] = both
        second[row + 2 : row + 4] = pltpu.roll(both, LANES // 2, 1)
    half = iota((shares * count3, LANES), 1) < LANES // 2

    def low_half(field):
        return jnp.where(half, field, pltpu.roll(field, LANES // 2, 1))

    def high_half(field):
        return jnp.where(half, pltpu.roll(field, LANES // 2, 1), field)

    solved[NEAR : NEAR + shares * count3] = columns(
        low_half(first[...]), high_half(first[...]), low_half(second[...])
    )
    solved[0:NEAR] = jnp.zeros((NEAR, LANES), F32)
    solved[NEAR + shares * count3 :] = jnp.zeros((2 * NEAR, LANES), F32)

    nx, ny = SPLIT
    part = own_slab()
    count = count3 + 2 * NEAR
    tall = solved[pl.ds(part * count3, count + count3), :]
    fine, coarse = Level(0), Level(1)
    cell = iota((LANES, LANES), 0)
    lane = iota((LANES, LANES), 1)
    spread = where01((cell < ROWS) & (cell == (lane % coarse.ny) // 2))
    rows = tall.shape[0]
    turned = [tall] + [pltpu.roll(tall, LANES - ROWS * row, 1) for row in range(1, ROWS)]
    wide = dot01(jnp.concatenate(turned, axis=0), spread)
    for row in range(ROWS):
        lifted[0:rows, row, :] = wide[row * rows : (row + 1) * rows]

    odd = part % 2 == 1

    def lifted_to(plane):
        parent = plane // 2 + NEAR // 2
        return lifted[jnp.where(odd, count - 1 - parent, parent)]

    near_fields, near_corr1 = (near1[0:6], near1[6], near1[7]), near1[8]
    far_fields, far_corr1 = (far1[0:6], far1[6], far1[7]), far1[8]
    fields2, corr2 = (far2[0:6], far2[6], far2[7]), far2[8]
    low, high = NEAR - 4, NEAR + depth // 2 + 4
    reach = depth // 2 + NEAR
    quarter = iota((ROWS, LANES), 1) // (LANES // 4)
    row = iota((ROWS, LANES), 0)

    def unpacked(index, which):
        pair = packed[lookup(slots, jnp.clip(index, 0, shares - 1)), which]
        total = None
        for shift in range(4):
            moved = pltpu.roll(pair, shift * (LANES // 4), 1)
            wide = jnp.where(row < 4, moved[0:1, :], moved[1:2, :])
            kept = jnp.where((quarter - shift) % 4 == row % 4, wide, 0.0)
            total = kept if total is None else total + kept
        return total

    one2[low - 1] = unpacked(jnp.where(odd, part + 1, part - 1), 4) + lifted_to(low - 1)
    for plane in range(low, high):
        one2[plane] = corr2[plane] + lifted_to(plane)
    one2[high] = unpacked(jnp.where(odd, part - 1, part + 1), 3) + lifted_to(high)
    sweep(coarse, NEAR - 4, reach + 4, fields2, one2, two2)
    sweep(coarse, NEAR - 3, reach + 3, fields2, two2, one2)
    sweep(coarse, NEAR - 2, reach + 2, fields2, one2, two2)

    fine_lane, coarse_lane = iota((LANES, LANES), 1), iota((LANES, LANES), 0)
    x_of = (fine_lane // fine.ny) // 2
    y_of = (fine_lane % fine.ny) // 2
    up = where01(coarse_lane == x_of * coarse.ny + y_of)
    lifted[0 : depth // 2 + 4] = in_lanes(two2[NEAR - 2 : reach + 2], up)
    parents = lifted[0 : depth // 2 + 4]
    twice = jnp.broadcast_to(parents[:, None], (parents.shape[0], 2, ROWS, LANES))
    low, high = HALO - 4, HALO + depth + 4
    turn = HALO + 3
    for plane in range(low, high):
        corr = far_corr1[plane] if plane < turn else near_corr1[plane - HALO]
        one1[plane] = corr + lifted[(plane - low) // 2]
    reach = depth + HALO
    for more, source, target in ((2, one1, two1), (1, two1, one1)):
        sweep(fine, HALO - more, turn, far_fields, source, target)
        sweep(fine, turn, reach + more, near_fields, source, target, HALO)

    def last(fields, shift):
        def body(plane, count):
            value = swept(fine, plane, count, fields, one1, shift)
            value = value * fields[2][pl.ds(plane - shift, count)]
            for index in range(count):
                at = plane - HALO + index
                final[jnp.where(odd, depth - 1 - at, at)] = value[index]

        return body

    loop(HALO, turn, PIECE, last(far_fields, 0))
    loop(turn, reach, PIECE, last(near_fields, HALO))

    group = (iota((depth, LANES), 1) // by) % groups
    for ix in range(nx):
        scaled = [final[:, ix * groups + part, :] for part in range(groups)]
        for iy in range(ny):
            total = scaled[iy]
            for part in range(groups):
                if part != iy:
                    moved = pltpu.roll(scaled[part], (by * (part - iy)) % LANES, 1)
                    total = jnp.where(group == part, moved, total)
            out_ref[slot_of(ix * ny + iy)] = total


def finish_kernel(blocks, out_ref):
    bx, by, depth = out_ref.shape
    peers = blocks.shape[0]
    ordered = jnp.concatenate([blocks[own_slot_of(rank)] for rank in range(peers)], axis=0)
    turned = ordered.T
    for x in range(bx):
        row = ((x % 4) * (bx // 4) + x // 4) * by
        out_ref[x] = turned[row : row + by]


def whole_planes(residual_q2, viscosity, pinned):
    bx, by, depth = viscosity.shape
    groups = bx // 4
    peers = SPLIT[0] * SPLIT[1]
    share = depth // peers
    planes = share + 2 * HALO
    count2 = share // 2 + 2 * NEAR
    limit = pltpu.CompilerParams(vmem_limit_bytes=32 * 2**20)

    def flat(rows):
        return jax.ShapeDtypeStruct((rows, LANES), F32)

    def blocks(count, rows):
        return jax.ShapeDtypeStruct((count, rows, LANES), F32)

    def room(count):
        return pltpu.VMEM((count, ROWS, LANES), F32)

    fluid = 1.0 / viscosity
    pin = 4.0 * pinned.astype(F32) * fluid
    parcels = pl.pallas_call(
        functools.partial(prepare_kernel, share),
        out_shape=blocks(peers, 3 * share),
        compiler_params=limit,
        name="prepare",
    )(residual_q2.reshape(4 * bx * by, 2 * depth), fluid, pin)
    own, inner, outer = pl.pallas_call(
        functools.partial(spread_kernel, groups, by),
        out_shape=(blocks(3 * share, ROWS),) + (blocks(3 * HALO - 2, ROWS),) * 2,
        scratch_shapes=[room(3 * share)],
        compiler_params=limit,
        name="spread",
    )(exchange(parcels))
    length = lax.axis_size("gz")
    parts = length * peers

    device = devices_of(length)

    def swap(field, first):
        pairs = [(device[i], device[i + 1]) for i in range(first, parts - 1, 2)]
        return lax.ppermute(field, ("gx", "gy", "gz"), pairs + [pair[::-1] for pair in pairs])

    outer, inner = swap(outer, 1), swap(inner, 0)
    count3 = share // 4
    near1, near2, far1, far2 = (
        (blocks(count, ROWS),) * fields
        for count, fields in ((share + HALO, 9), (count2, 8), (HALO + 8, 9), (count2, 9))
    )
    near1, near2, fluid2, pin2, fluid3, pin3 = pl.pallas_call(
        functools.partial(near_kernel, share),
        out_shape=(near1, near2) + (blocks(count2, ROWS),) * 2 + (blocks(count3, ROWS),) * 2,
        scratch_shapes=[room(share + HALO)] * 4 + [room(count2)] * 2,
        compiler_params=limit,
        name="near",
    )(own, inner)
    far1, far2, parcel = pl.pallas_call(
        functools.partial(down_kernel, share),
        out_shape=(far1, far2, blocks(5, 2)),
        scratch_shapes=[room(HALO + 8)] * 4 + [room(count2)] * 5,
        compiler_params=limit,
        name="down",
    )(own, outer, near2, fluid2, pin2, fluid3, pin3)
    copies = jnp.broadcast_to(parcel, (parts,) + parcel.shape)
    packed = exchange_all(copies)
    depth3 = parts * count3
    mine = pl.pallas_call(
        functools.partial(up_kernel, groups, by, share),
        out_shape=blocks(peers, share),
        scratch_shapes=[room(planes), room(planes), room(count2), room(count2), room(count2)]
        + [pltpu.VMEM((rows, LANES), F32) for rows in (depth3, depth3, depth3 + 3 * NEAR)]
        + [room(share)],
        compiler_params=limit,
        name="up",
    )(packed, near1, far1, far2)
    return pl.pallas_call(
        finish_kernel,
        out_shape=jax.ShapeDtypeStruct((bx, by, depth), F32),
        compiler_params=limit,
        name="finish",
    )(exchange(mine))


def one_tile_planes(mesh, viscosity):
    split = (mesh.shape["gx"], mesh.shape["gy"])
    depth = viscosity.shape[2]
    fits = viscosity.shape[:2] == PLANE and split == SPLIT
    return fits and depth == 4 * LANES and depth // mesh.shape["gz"] == LANES


def solution(mesh):
    placed = (P("gx", "gy", "gz"), P("gx", "gy", "gz"), P("gx", "gy", "gz"))

    def cycle(residual_q2, viscosity, pinned):
        chosen = whole_planes if one_tile_planes(mesh, viscosity) else per_device
        return jax.shard_map(
            chosen, mesh=mesh, in_specs=placed, out_specs=P("gx", "gy", "gz"), check_vma=False
        )(residual_q2, viscosity, pinned)

    return cycle
```

```python
import functools

import jax
import jax.numpy as jnp
from jax import lax
from jax.experimental import pallas as pl
from jax.experimental.pallas import tpu as pltpu
from jax.sharding import PartitionSpec as P

NU = 3


OMEGA = 0.6


def with_halo(block, sides, width):
    for axis, dim in sides:
        count = lax.axis_size(axis)
        forward = [(i, i + 1) for i in range(count - 1)]
        backward = [(target, source) for source, target in forward]
        low = lax.ppermute(
            lax.slice_in_dim(block, block.shape[dim] - width, None, axis=dim), axis, forward
        )
        high = lax.ppermute(lax.slice_in_dim(block, 0, width, axis=dim), axis, backward)
        block = jnp.concatenate([low, block, high], axis=dim)
    return block


def coarsen(x):
    a, b, c = x.shape
    return x.reshape(a // 2, 2, b // 2, 2, c // 2, 2).sum(axis=(1, 3, 5))


def refine(x):
    return jnp.repeat(jnp.repeat(jnp.repeat(x, 2, 0), 2, 1), 2, 2)


def extended(field):
    return with_halo(field, (("gx", 0), ("gy", 1), ("gz", 2)), 1)


def shifted(padded):
    return [
        padded[2:, 1:-1, 1:-1],
        padded[:-2, 1:-1, 1:-1],
        padded[1:-1, 2:, 1:-1],
        padded[1:-1, :-2, 1:-1],
        padded[1:-1, 1:-1, 2:],
        padded[1:-1, 1:-1, :-2],
    ]


def neighbours(field):
    return shifted(extended(field))


def harmonic(fluid, near, factor):
    total = fluid + near
    return jnp.where(total > 0, factor * 2.0 * fluid * near / jnp.where(total > 0, total, 1.0), 0.0)


def couplings(fluid, factor):
    return [harmonic(fluid, near, factor) for near in neighbours(fluid)]


def apply_op(field, weights, diag):
    total = diag * field
    for weight, near in zip(weights, neighbours(field)):
        total = total - weight * near
    return total


def presmooth(rhs, weights, diag):
    corr = OMEGA * rhs / diag
    for sweep in range(NU - 1):
        corr = corr + OMEGA * (rhs - apply_op(corr, weights, diag)) / diag
    return corr


def postsmooth(corr, rhs, weights, diag):
    for sweep in range(NU):
        corr = corr + OMEGA * (rhs - apply_op(corr, weights, diag)) / diag
    return corr


def tridiag(coeffs, rhs):
    solved = lax.linalg.tridiagonal_solve(coeffs[0], coeffs[1], coeffs[2], rhs[..., None])[..., 0]
    last = rhs.ndim - 1
    shift_col = jnp.sum(rhs, axis=last, keepdims=True) / jnp.sum(
        coeffs[3], axis=last, keepdims=True
    )
    return solved + shift_col


def prepare_columns(weights, diag):
    lower = -weights[5]
    upper = -weights[4]
    across = diag + lower + upper
    return (
        lax.all_gather(lower, "gz", axis=2, tiled=True),
        lax.all_gather(diag, "gz", axis=2, tiled=True),
        lax.all_gather(upper, "gz", axis=2, tiled=True),
        lax.all_gather(across, "gz", axis=2, tiled=True),
    )


def column_solve(rhs, coeffs):
    depth = rhs.shape[2]
    whole = lax.all_gather(rhs, "gz", axis=2, tiled=True)
    solved = tridiag(coeffs, whole)
    return lax.dynamic_slice_in_dim(solved, lax.axis_index("gz") * depth, depth, 2)


def per_device(residual_q2, viscosity, pinned):
    fluid1 = 1.0 / viscosity
    pin1 = 4.0 * pinned.astype(jnp.float32) * fluid1
    rhs1 = coarsen(residual_q2.astype(jnp.float32))
    fluid2 = coarsen(fluid1) / 8.0
    pin2 = coarsen(pin1) / 4.0
    fluid3 = coarsen(fluid2) / 8.0
    pin3 = coarsen(pin2) / 4.0
    weights1 = couplings(fluid1, 1.0)
    weights2 = couplings(fluid2, 2.0)
    weights3 = couplings(fluid3, 4.0)
    diag1 = sum(weights1) + pin1
    diag2 = sum(weights2) + pin2
    diag3 = sum(weights3) + pin3
    coeffs = prepare_columns(weights3, diag3)
    corr1 = presmooth(rhs1, weights1, diag1)
    rhs2 = coarsen(rhs1 - apply_op(corr1, weights1, diag1))
    corr2 = presmooth(rhs2, weights2, diag2)
    rhs3 = coarsen(rhs2 - apply_op(corr2, weights2, diag2))
    corr3 = column_solve(rhs3, coeffs)
    corr3 = corr3 + column_solve(rhs3 - apply_op(corr3, weights3, diag3), coeffs)
    corr2 = postsmooth(corr2 + refine(corr3), rhs2, weights2, diag2)
    corr1 = postsmooth(corr1 + refine(corr2), rhs1, weights1, diag1)
    return diag1 * corr1


PLANE = (32, 32)
SPLIT = (2, 4)
ROWS = 8
LANES = 128
HALO = 16
NEAR = 8
PIECE = 8
TINY = 1e-30
F32 = jnp.float32


def iota(shape, dim):
    return lax.broadcasted_iota(jnp.int32, shape, dim)


def quotient(index, count):
    return index >> (count.bit_length() - 1)


def remainder(index, count):
    return index & (count - 1)


def dot01(field, chosen):
    total = None
    rest = field
    for part in range(3):
        piece = rest.astype(jnp.bfloat16)
        term = jnp.dot(piece, chosen, preferred_element_type=F32)
        total = term if total is None else total + term
        if part < 2:
            rest = rest - piece.astype(F32)
    return total


def dot10(chosen, field):
    total = None
    rest = field
    for part in range(3):
        piece = rest.astype(jnp.bfloat16)
        term = lax.dot_general(
            chosen, piece, (((1,), (1,)), ((), ())), preferred_element_type=F32
        )
        total = term if total is None else total + term
        if part < 2:
            rest = rest - piece.astype(F32)
    return total


def where01(condition):
    return jnp.where(condition, 1.0, 0.0).astype(jnp.bfloat16)


def loop(low, high, size, body):
    for plane in range(low, high, size):
        body(plane, min(size, high - plane))


def inverse_of(field):
    first = pl.reciprocal(field, approx=True)
    return first * (2.0 - field * first)


class Level:
    def __init__(self, level):
        self.ny = PLANE[1] >> level
        self.xs = 4 >> level
        self.factor = float(2**level)

    def within(self, shape):
        lane = iota((1,) + shape[1:], 2)
        return jnp.broadcast_to(remainder(quotient(lane, self.ny), self.xs), shape)

    def ends(self, shape):
        one = (1,) + shape[1:]
        lane = iota(one, 2)
        last_x = (iota(one, 1) == ROWS - 1) & (remainder(quotient(lane, self.ny), self.xs) == self.xs - 1)
        last_y = remainder(lane, self.ny) == self.ny - 1
        code = jnp.where(last_y, 1, 0) + jnp.where(last_x, 2, 0)
        code = jnp.broadcast_to(code, shape)
        return (code & 1) == 1, code >= 2

    def next_x(self, field):
        moved = pltpu.roll(field, LANES - self.ny, 2)
        wrapped = self.within(field.shape) == self.xs - 1
        return jnp.where(wrapped, pltpu.roll(moved, ROWS - 1, 1), moved)

    def last_x(self, field):
        moved = pltpu.roll(field, self.ny, 2)
        return jnp.where(self.within(field.shape) == 0, pltpu.roll(moved, 1, 1), moved)

    def next_y(self, field):
        return pltpu.roll(field, LANES - 1, 2)

    def last_y(self, field):
        return pltpu.roll(field, 1, 2)

    def spread(self, field, scaled, plane, count):
        mid = field[1:-1]
        near = (
            self.next_x(mid), self.last_x(mid), self.next_y(mid), self.last_y(mid),
            field[2:], field[:-2],
        )
        terms = [weight[pl.ds(plane, count)] * value for weight, value in zip(scaled, near)]
        return mid, ((terms[0] + terms[1]) + (terms[2] + terms[3])) + (terms[4] + terms[5])


def mean_of(fluid, near, factor):
    return ((factor * 2.0) * fluid * near) * inverse_of(jnp.maximum(fluid + near, TINY))


def set_level(level, low, high, fluid, pin, rhs, fields):
    scaled, start, diag = fields

    def body(plane, count):
        wide = fluid[pl.ds(plane - 1, count + 2)]
        mid = wide[1:-1]
        end_y, end_x = level.ends(mid.shape)
        to_x = jnp.where(end_x, 0.0, mean_of(mid, level.next_x(mid), level.factor))
        to_y = jnp.where(end_y, 0.0, mean_of(mid, level.next_y(mid), level.factor))
        to_z = mean_of(wide[:-1], wide[1:], level.factor)
        weights = (to_x, level.last_x(to_x), to_y, level.last_y(to_y), to_z[1:], to_z[:-1])
        total = (
            (weights[0] + weights[1])
            + (weights[2] + weights[3])
            + (weights[4] + weights[5])
            + pin[pl.ds(plane, count)]
        )
        gain = OMEGA * inverse_of(jnp.maximum(total, TINY))
        for target, weight in zip(scaled, weights):
            target[pl.ds(plane, count)] = gain * weight
        start[pl.ds(plane, count)] = gain * rhs[pl.ds(plane, count)]
        diag[pl.ds(plane, count)] = total

    loop(low, high, PIECE, body)


def swept(level, plane, count, fields, source, shift=0):
    scaled, start, _ = fields
    mid, total = level.spread(source[pl.ds(plane - 1, count + 2)], scaled, plane - shift, count)
    return (1.0 - OMEGA) * mid + (start[pl.ds(plane - shift, count)] + total)


def sweep(level, low, high, fields, source, target, shift=0):
    def body(plane, count):
        target[pl.ds(plane, count)] = swept(level, plane, count, fields, source, shift)

    loop(low, high, PIECE, body)


def pair_sum(field):
    half = field.reshape((field.shape[0] // 2, 2) + field.shape[1:])
    return half[:, 0] + half[:, 1]


def coarse_residual(level, low, high, fields, corr, target):
    scaled, start, diag = fields

    def body(plane, count):
        mid, total = level.spread(corr[pl.ds(plane - 1, count + 2)], scaled, plane, count)
        rest = (start[pl.ds(plane, count)] + total) - OMEGA * mid
        rest = rest * (diag[pl.ds(plane, count)] * (1.0 / OMEGA))
        target[pl.ds((plane - low) // 2, count // 2)] = pair_sum(rest)

    loop(low, high, PIECE, body)


def lanes_down(level):
    fine = iota((LANES, LANES), 0)
    coarse = iota((LANES, LANES), 1)
    ny, xs = PLANE[1] >> level, 4 >> level
    half = xs // 2
    fine_x, coarse_x = remainder(quotient(fine, ny), xs), quotient(coarse, ny // 2)
    same_x = quotient(fine_x, 2) == remainder(coarse_x, half)
    same_y = quotient(remainder(fine, ny), 2) == remainder(coarse, ny // 2)
    return where01((fine < ny * xs) & same_x & same_y)


def in_lanes(field, chosen):
    flat = field.reshape(field.shape[0] * ROWS, LANES)
    return dot01(flat, chosen).reshape(field.shape)


def path_of(group):
    nx, ny = SPLIT
    row, column = 0, 0
    for index in range(group + 1):
        columns = list(range(ny)) if column == 0 else list(range(ny))[::-1]
        if index % 2:
            path = [(row, at) for at in columns] + [(1 - row, at) for at in columns[::-1]]
        else:
            path = []
            for at in columns:
                path += [(row, at), (1 - row, at)]
                row = 1 - row
        row, column = path[-1]
    return [row * ny + column for row, column in path]


def lookup(table, index):
    found = table[0]
    for at, value in enumerate(table[1:], 1):
        found = jnp.where(index == at, value, found)
    return found


def slot_of(peer):
    nx, ny = SPLIT
    return nx * ny - 1 - (peer % ny * nx + peer // ny)


def own_slot_of(rank):
    groups = range(lax.axis_size("gz"))
    return lookup([slot_of(path_of(group)[rank]) for group in groups], lax.axis_index("gz"))


def exchange(field):
    peers, groups = SPLIT[0] * SPLIT[1], lax.axis_size("gz")
    order = sorted(range(peers), key=slot_of)
    members = [[peer * groups + group for peer in order] for group in range(groups)]
    axes = ("gx", "gy", "gz")
    return lax.all_to_all(field, axes, 0, 0, axis_index_groups=members, tiled=True)


def slabs_of(groups):
    peers = SPLIT[0] * SPLIT[1]
    return [
        group * peers + path_of(group).index(peer) for peer in range(peers) for group in range(groups)
    ]


def own_slab():
    nx, ny = SPLIT
    groups = lax.axis_size("gz")
    device = (lax.axis_index("gx") * ny + lax.axis_index("gy")) * groups + lax.axis_index("gz")
    return lookup(slabs_of(groups), device)


def slots_of(groups):
    peers = SPLIT[0] * SPLIT[1]
    return [
        slot_of(peer) * groups + groups - 1 - group for group in range(groups) for peer in path_of(group)
    ]


def exchange_all(field):
    groups = lax.axis_size("gz")
    members = [device for _, device in sorted(zip(slots_of(groups), devices_of(groups)))]
    axes = ("gx", "gy", "gz")
    return lax.all_to_all(field, axes, 0, 0, axis_index_groups=[members], tiled=True)


def devices_of(groups):
    slabs = slabs_of(groups)
    return [slabs.index(slab) for slab in range(len(slabs))]


def prepare_kernel(share, res_ref, fluid_ref, pin_ref, out_ref):
    bx, by, depth = fluid_ref.shape
    cells = bx * by
    groups = bx // 4
    order = [x for low in range(4) for x in range(low, bx, 4)]
    fine = iota((cells, 4 * cells), 1)
    x, y = quotient(fine, 4 * by), quotient(remainder(fine, 2 * by), 2)
    lane = remainder(x, 4) * (groups * by) + quotient(x, 4) * by + y
    chosen = where01(lane == iota((cells, 4 * cells), 0))
    wide = lax.dot_general(
        chosen, res_ref[...], (((1,), (0,)), ((), ())), preferred_element_type=F32
    )
    rhs = dot10(where01(quotient(iota((depth, 2 * depth), 1), 2) == iota((depth, 2 * depth), 0)), wide)

    def turned(field_ref):
        field = jnp.concatenate([field_ref[x : x + 1] for x in order], axis=0)
        return field.reshape(cells, depth).T

    fluid, pin = turned(fluid_ref), turned(pin_ref)
    for rank in range(depth // share):
        peer, begin = own_slot_of(rank), rank * share
        for index, field in enumerate((fluid, rhs, pin)):
            out_ref[peer, index * share : (index + 1) * share] = field[begin : begin + share]


def spread_kernel(groups, by, gathered, own, inner, outer, straight):
    for start in range(0, own.shape[0], ROWS):
        place(gathered, start, straight, start, groups, by)
    share = own.shape[0] // 3
    odd = own_slab() % 2 == 1
    for index in range(3):
        for plane in range(share):
            at = jnp.where(odd, share - 1 - plane, plane)
            own[index * share + plane] = straight[index * share + at]
    for target, drop in ((inner, 0), (outer, share - 1)):
        row = 0
        for index in range(3):
            for plane in range(share):
                if index == 0 or plane != drop:
                    target[row] = own[index * share + plane]
                    row += 1


def place(gathered, row, target, plane, groups, by):
    group = remainder(quotient(iota((ROWS, LANES), 1), by), groups)
    nx, ny = SPLIT
    for ix in range(nx):
        found = [gathered[slot_of(ix * ny + iy), pl.ds(row, ROWS), :] for iy in range(ny)]
        for part in range(groups):
            total = found[part]
            for iy in range(ny):
                if iy != part:
                    moved = pltpu.roll(found[iy], (by * (iy - part)) % LANES, 1)
                    total = jnp.where(group == iy, moved, total)
            target[pl.ds(plane, ROWS), ix * groups + part, :] = total


def near_kernel(
    depth,
    own, inner,
    saved1, saved2, fluid2, pin2, fluid3, pin3,
    fluid1, rhs1, pin1, other1, rhs2, sums,
):
    row = 0
    for index, target in enumerate((fluid1, rhs1, pin1)):
        target[0:depth] = own[index * depth : (index + 1) * depth]
        count = HALO if index == 0 else HALO - 1
        for plane in range(count):
            target[depth + plane] = inner[row + count - 1 - plane]
        if count < HALO:
            target[depth + count] = jnp.zeros((ROWS, LANES), F32)
        row += count
    fine, coarse = Level(0), Level(1)
    down1, down2 = lanes_down(0), lanes_down(1)
    fields1, corr1 = (saved1[0:6], saved1[6], saved1[7]), saved1[8]
    fields2 = (saved2[0:6], saved2[6], saved2[7])
    planes = depth + HALO
    set_level(fine, 1, planes - 1, fluid1, pin1, rhs1, fields1)
    sweep(fine, 2, planes - 2, fields1, fields1[1], other1)
    sweep(fine, 3, planes - 3, fields1, other1, corr1)
    coarse_residual(fine, 4, planes - 4, fields1, corr1, sums)
    count2 = planes // 2
    for source, target, share in ((fluid1, fluid2, 8.0), (pin1, pin2, 4.0)):
        target[NEAR : NEAR + count2] = in_lanes(pair_sum(source[...]), down1) * (1.0 / share)
    low2, high2 = NEAR + 2, NEAR + count2 - 2
    rhs2[low2:high2] = in_lanes(sums[0 : high2 - low2], down1)
    set_level(coarse, low2, high2, fluid2, pin2, rhs2, fields2)
    for source, target, scale in ((fluid2, fluid3, 0.125), (pin2, pin3, 0.25)):
        target[...] = in_lanes(pair_sum(source[NEAR : NEAR + depth // 2]), down2) * scale


def down_kernel(
    depth,
    own, outer, near2, near_fluid2, near_pin2, fluid3, pin3,
    saved1, saved2,
    packed,
    fluid1, rhs1, pin1, other1, fluid2, rhs2, pin2, other2, sums,
):
    planes = fluid1.shape[0]
    row = 0
    for index, target in enumerate((fluid1, rhs1, pin1)):
        count = HALO if index == 0 else HALO - 1
        if count < HALO:
            target[0] = jnp.zeros((ROWS, LANES), F32)
        for plane in range(count):
            target[HALO - count + plane] = outer[row + count - 1 - plane]
        row += count
        target[HALO:planes] = own[index * depth : index * depth + planes - HALO]

    fine, coarse = Level(0), Level(1)
    down1, down2 = lanes_down(0), lanes_down(1)
    fields1, corr1 = (saved1[0:6], saved1[6], saved1[7]), saved1[8]
    fields2, corr2 = (saved2[0:6], saved2[6], saved2[7]), saved2[8]
    set_level(fine, 1, planes - 1, fluid1, pin1, rhs1, fields1)
    sweep(fine, 2, planes - 2, fields1, fields1[1], other1)
    sweep(fine, 3, planes - 3, fields1, other1, corr1)
    count2 = depth // 2 + 2 * NEAR
    low2, done, high2 = 2, NEAR + 2, count2 - 2
    coarse_residual(fine, 2 * low2, 2 * done, fields1, corr1, sums)
    for source, ready, target, share in (
        (fluid1, near_fluid2, fluid2, 8.0), (pin1, near_pin2, pin2, 4.0)
    ):
        target[0:NEAR] = in_lanes(pair_sum(source[0:HALO]), down1) * (1.0 / share)
        target[NEAR : done + 1] = ready[NEAR : done + 1]
    rhs2[low2:done] = in_lanes(sums[0 : done - low2], down1)
    set_level(coarse, low2, done, fluid2, pin2, rhs2, fields2)
    for source, target in zip(near2, saved2[0:8]):
        target[done:high2] = source[done:high2]
    sweep(coarse, low2 + 1, high2 - 1, fields2, fields2[1], other2)
    sweep(coarse, low2 + 2, high2 - 2, fields2, other2, corr2)
    coarse_residual(coarse, NEAR, NEAR + depth // 2, fields2, corr2, sums)
    count3 = depth // 4
    rhs3 = in_lanes(sums[0:count3], down2)
    lane = quotient(iota((count3, LANES), 1), ROWS)
    first = jnp.zeros((count3, LANES), F32)
    second = jnp.zeros((count3, LANES), F32)
    for row in range(ROWS):
        first = jnp.where(lane == row, rhs3[:, row, :], first)
        first = jnp.where(lane == ROWS + row, fluid3[:, row, :], first)
        second = jnp.where(remainder(lane, ROWS) == row, pin3[:, row, :], second)
    odd = own_slab() % 2 == 1

    def ordered(field):
        back = [field[row : row + 1] for row in reversed(range(count3))]
        return jnp.where(odd, jnp.concatenate(back, axis=0), field)

    first, second = ordered(first), ordered(second)
    packed[0] = first[0:2]
    packed[1] = first[2:4]
    packed[2] = jnp.where(lane[0:2] < ROWS, second[0:2], second[2:4])
    lane = quotient(iota((1, LANES), 1), LANES // 4)
    for index, plane in enumerate((NEAR + depth // 2 - 5, NEAR + 4)):
        for half in range(2):
            row = jnp.zeros((1, LANES), F32)
            for quarter in range(4):
                at = half * 4 + quarter
                row = jnp.where(lane == quarter, corr2[plane, at : at + 1, :], row)
            packed[3 + index, half : half + 1, :] = row


def rolled(field, shift):
    count = field.shape[0]
    shift %= count
    if shift % ROWS:
        return pltpu.roll(field, shift, 0)
    return jnp.concatenate([field[count - shift :], field[: count - shift]], axis=0)


def columns(rhs, fluid, pin):
    depth = fluid.shape[0]
    z, lane = iota(fluid.shape, 0), iota(fluid.shape, 1)
    y, x = remainder(lane, ROWS), remainder(quotient(lane, ROWS), ROWS)

    def next_x(field):
        return pltpu.roll(field, LANES - ROWS, 1)

    def next_y(field):
        return pltpu.roll(field, LANES - 1, 1)

    wz = jnp.where(z == depth - 1, 0.0, mean_of(fluid, rolled(fluid, -1), 4.0))
    wy = jnp.where(y == ROWS - 1, 0.0, mean_of(fluid, next_y(fluid), 4.0))
    wx = jnp.where(x == ROWS - 1, 0.0, mean_of(fluid, next_x(fluid), 4.0))
    across = (wx + pltpu.roll(wx, ROWS, 1)) + (wy + pltpu.roll(wy, 1, 1)) + pin
    share = 1.0 / jnp.sum(across, axis=0, keepdims=True)

    above, below, own = rolled(wz, 1), wz, across
    steps = []
    stride, right = 1, rhs
    while stride < depth:
        inverse = inverse_of(above + below + own)
        up = above * rolled(inverse, stride)
        down = below * rolled(inverse, -stride)
        own = own + up * rolled(own, stride) + down * rolled(own, -stride)
        above = up * rolled(above, stride)
        below = down * rolled(below, -stride)
        right = right + up * rolled(right, stride) + down * rolled(right, -stride)
        steps.append((stride, up, down))
        stride *= 2
    inverse = inverse_of(above + below + own)

    def mean(right):
        return jnp.sum(right, axis=0, keepdims=True) * share

    corr = right * inverse + mean(rhs)
    flow_x = wx * (next_x(corr) - corr)
    flow_y = wy * (next_y(corr) - corr)
    flow_z = wz * (rolled(corr, -1) - corr)
    rest = (
        (rhs - pin * corr)
        + (flow_x - pltpu.roll(flow_x, ROWS, 1))
        + (flow_y - pltpu.roll(flow_y, 1, 1))
        + (flow_z - rolled(flow_z, 1))
    )
    right = rest
    for stride, up, down in steps:
        right = right + up * rolled(right, stride) + down * rolled(right, -stride)
    return (corr + mean(rest)) + right * inverse


def up_kernel(
    groups, by, depth,
    packed, near1, far1, far2,
    out_ref,
    one1, two1, one2, two2, lifted, first, second, solved, final,
):
    count3 = depth // 4
    shares = packed.shape[0]
    peers = SPLIT[0] * SPLIT[1]
    slots = slots_of(shares // peers)
    for slab, index in enumerate(slots):
        row = slab * count3
        first[row : row + 2] = packed[index, 0]
        first[row + 2 : row + 4] = packed[index, 1]
        both = packed[index, 2]
        second[row : row + 2] = both
        second[row + 2 : row + 4] = pltpu.roll(both, LANES // 2, 1)
    half = iota((shares * count3, LANES), 1) < LANES // 2

    def low_half(field):
        return jnp.where(half, field, pltpu.roll(field, LANES // 2, 1))

    def high_half(field):
        return jnp.where(half, pltpu.roll(field, LANES // 2, 1), field)

    solved[NEAR : NEAR + shares * count3] = columns(
        low_half(first[...]), high_half(first[...]), low_half(second[...])
    )
    solved[0:NEAR] = jnp.zeros((NEAR, LANES), F32)
    solved[NEAR + shares * count3 :] = jnp.zeros((2 * NEAR, LANES), F32)

    nx, ny = SPLIT
    part = own_slab()
    count = count3 + 2 * NEAR
    tall = solved[pl.ds(part * count3, count + count3), :]
    fine, coarse = Level(0), Level(1)
    cell = iota((LANES, LANES), 0)
    lane = iota((LANES, LANES), 1)
    spread = where01((cell < ROWS) & (cell == quotient(remainder(lane, coarse.ny), 2)))
    rows = tall.shape[0]
    turned = [tall] + [pltpu.roll(tall, LANES - ROWS * row, 1) for row in range(1, ROWS)]
    wide = dot01(jnp.concatenate(turned, axis=0), spread)
    for row in range(ROWS):
        lifted[0:rows, row, :] = wide[row * rows : (row + 1) * rows]

    odd = part % 2 == 1

    def lifted_to(plane):
        parent = plane // 2 + NEAR // 2
        return lifted[jnp.where(odd, count - 1 - parent, parent)]

    near_fields, near_corr1 = (near1[0:6], near1[6], near1[7]), near1[8]
    far_fields, far_corr1 = (far1[0:6], far1[6], far1[7]), far1[8]
    fields2, corr2 = (far2[0:6], far2[6], far2[7]), far2[8]
    low, high = NEAR - 4, NEAR + depth // 2 + 4
    reach = depth // 2 + NEAR
    quarter = quotient(iota((ROWS, LANES), 1), LANES // 4)
    row = iota((ROWS, LANES), 0)

    def unpacked(index, which):
        pair = packed[lookup(slots, jnp.clip(index, 0, shares - 1)), which]
        total = None
        for shift in range(4):
            moved = pltpu.roll(pair, shift * (LANES // 4), 1)
            wide = jnp.where(row < 4, moved[0:1, :], moved[1:2, :])
            kept = jnp.where(remainder(quarter - shift, 4) == remainder(row, 4), wide, 0.0)
            total = kept if total is None else total + kept
        return total

    one2[low - 1] = unpacked(jnp.where(odd, part + 1, part - 1), 4) + lifted_to(low - 1)
    for plane in range(low, high):
        one2[plane] = corr2[plane] + lifted_to(plane)
    one2[high] = unpacked(jnp.where(odd, part - 1, part + 1), 3) + lifted_to(high)
    sweep(coarse, NEAR - 4, reach + 4, fields2, one2, two2)
    sweep(coarse, NEAR - 3, reach + 3, fields2, two2, one2)
    sweep(coarse, NEAR - 2, reach + 2, fields2, one2, two2)

    fine_lane, coarse_lane = iota((LANES, LANES), 1), iota((LANES, LANES), 0)
    x_of = quotient(fine_lane, 2 * fine.ny)
    y_of = quotient(remainder(fine_lane, fine.ny), 2)
    up = where01(coarse_lane == x_of * coarse.ny + y_of)
    lifted[0 : depth // 2 + 4] = in_lanes(two2[NEAR - 2 : reach + 2], up)
    parents = lifted[0 : depth // 2 + 4]
    twice = jnp.broadcast_to(parents[:, None], (parents.shape[0], 2, ROWS, LANES))
    low, high = HALO - 4, HALO + depth + 4
    turn = HALO + 3
    for plane in range(low, high):
        corr = far_corr1[plane] if plane < turn else near_corr1[plane - HALO]
        one1[plane] = corr + lifted[(plane - low) // 2]
    reach = depth + HALO
    for more, source, target in ((2, one1, two1), (1, two1, one1)):
        sweep(fine, HALO - more, turn, far_fields, source, target)
        sweep(fine, turn, reach + more, near_fields, source, target, HALO)

    def last(fields, shift):
        def body(plane, count):
            value = swept(fine, plane, count, fields, one1, shift)
            value = value * fields[2][pl.ds(plane - shift, count)]
            for index in range(count):
                at = plane - HALO + index
                final[jnp.where(odd, depth - 1 - at, at)] = value[index]

        return body

    loop(HALO, turn, PIECE, last(far_fields, 0))
    loop(turn, reach, PIECE, last(near_fields, HALO))

    group = remainder(quotient(iota((depth, LANES), 1), by), groups)
    for ix in range(nx):
        scaled = [final[:, ix * groups + part, :] for part in range(groups)]
        for iy in range(ny):
            total = scaled[iy]
            for part in range(groups):
                if part != iy:
                    moved = pltpu.roll(scaled[part], (by * (part - iy)) % LANES, 1)
                    total = jnp.where(group == part, moved, total)
            out_ref[slot_of(ix * ny + iy)] = total


def finish_kernel(blocks, out_ref):
    bx, by, depth = out_ref.shape
    peers = blocks.shape[0]
    ordered = jnp.concatenate([blocks[own_slot_of(rank)] for rank in range(peers)], axis=0)
    turned = ordered.T
    for x in range(bx):
        row = ((x % 4) * (bx // 4) + x // 4) * by
        out_ref[x] = turned[row : row + by]


def whole_planes(residual_q2, viscosity, pinned):
    bx, by, depth = viscosity.shape
    groups = bx // 4
    peers = SPLIT[0] * SPLIT[1]
    share = depth // peers
    planes = share + 2 * HALO
    count2 = share // 2 + 2 * NEAR
    limit = pltpu.CompilerParams(vmem_limit_bytes=32 * 2**20)

    def flat(rows):
        return jax.ShapeDtypeStruct((rows, LANES), F32)

    def blocks(count, rows):
        return jax.ShapeDtypeStruct((count, rows, LANES), F32)

    def room(count):
        return pltpu.VMEM((count, ROWS, LANES), F32)

    fluid = 1.0 / viscosity
    pin = 4.0 * pinned.astype(F32) * fluid
    parcels = pl.pallas_call(
        functools.partial(prepare_kernel, share),
        out_shape=blocks(peers, 3 * share),
        compiler_params=limit,
        name="prepare",
    )(residual_q2.reshape(4 * bx * by, 2 * depth), fluid, pin)
    own, inner, outer = pl.pallas_call(
        functools.partial(spread_kernel, groups, by),
        out_shape=(blocks(3 * share, ROWS),) + (blocks(3 * HALO - 2, ROWS),) * 2,
        scratch_shapes=[room(3 * share)],
        compiler_params=limit,
        name="spread",
    )(exchange(parcels))
    length = lax.axis_size("gz")
    parts = length * peers

    device = devices_of(length)

    def swap(field, first):
        pairs = [(device[i], device[i + 1]) for i in range(first, parts - 1, 2)]
        return lax.ppermute(field, ("gx", "gy", "gz"), pairs + [pair[::-1] for pair in pairs])

    outer, inner = swap(outer, 1), swap(inner, 0)
    count3 = share // 4
    near1, near2, far1, far2 = (
        (blocks(count, ROWS),) * fields
        for count, fields in ((share + HALO, 9), (count2, 8), (HALO + 8, 9), (count2, 9))
    )
    near1, near2, fluid2, pin2, fluid3, pin3 = pl.pallas_call(
        functools.partial(near_kernel, share),
        out_shape=(near1, near2) + (blocks(count2, ROWS),) * 2 + (blocks(count3, ROWS),) * 2,
        scratch_shapes=[room(share + HALO)] * 4 + [room(count2)] * 2,
        compiler_params=limit,
        name="near",
    )(own, inner)
    far1, far2, parcel = pl.pallas_call(
        functools.partial(down_kernel, share),
        out_shape=(far1, far2, blocks(5, 2)),
        scratch_shapes=[room(HALO + 8)] * 4 + [room(count2)] * 5,
        compiler_params=limit,
        name="down",
    )(own, outer, near2, fluid2, pin2, fluid3, pin3)
    copies = jnp.broadcast_to(parcel, (parts,) + parcel.shape)
    packed = exchange_all(copies)
    depth3 = parts * count3
    mine = pl.pallas_call(
        functools.partial(up_kernel, groups, by, share),
        out_shape=blocks(peers, share),
        scratch_shapes=[room(planes), room(planes), room(count2), room(count2), room(count2)]
        + [pltpu.VMEM((rows, LANES), F32) for rows in (depth3, depth3, depth3 + 3 * NEAR)]
        + [room(share)],
        compiler_params=limit,
        name="up",
    )(packed, near1, far1, far2)
    return pl.pallas_call(
        finish_kernel,
        out_shape=jax.ShapeDtypeStruct((bx, by, depth), F32),
        compiler_params=limit,
        name="finish",
    )(exchange(mine))


def one_tile_planes(mesh, viscosity):
    split = (mesh.shape["gx"], mesh.shape["gy"])
    depth = viscosity.shape[2]
    fits = viscosity.shape[:2] == PLANE and split == SPLIT
    return fits and depth == 4 * LANES and depth // mesh.shape["gz"] == LANES


def solution(mesh):
    placed = (P("gx", "gy", "gz"), P("gx", "gy", "gz"), P("gx", "gy", "gz"))

    def cycle(residual_q2, viscosity, pinned):
        chosen = whole_planes if one_tile_planes(mesh, viscosity) else per_device
        return jax.shard_map(
            chosen, mesh=mesh, in_specs=placed, out_specs=P("gx", "gy", "gz"), check_vma=False
        )(residual_q2, viscosity, pinned)

    return cycle
```

```python
import functools

import jax
import jax.numpy as jnp
from jax import lax
from jax.experimental import pallas as pl
from jax.experimental.pallas import tpu as pltpu
from jax.sharding import PartitionSpec as P

NU = 3


OMEGA = 0.6


def with_halo(block, sides, width):
    for axis, dim in sides:
        count = lax.axis_size(axis)
        forward = [(i, i + 1) for i in range(count - 1)]
        backward = [(target, source) for source, target in forward]
        low = lax.ppermute(
            lax.slice_in_dim(block, block.shape[dim] - width, None, axis=dim), axis, forward
        )
        high = lax.ppermute(lax.slice_in_dim(block, 0, width, axis=dim), axis, backward)
        block = jnp.concatenate([low, block, high], axis=dim)
    return block


def coarsen(x):
    a, b, c = x.shape
    return x.reshape(a // 2, 2, b // 2, 2, c // 2, 2).sum(axis=(1, 3, 5))


def refine(x):
    return jnp.repeat(jnp.repeat(jnp.repeat(x, 2, 0), 2, 1), 2, 2)


def extended(field):
    return with_halo(field, (("gx", 0), ("gy", 1), ("gz", 2)), 1)


def shifted(padded):
    return [
        padded[2:, 1:-1, 1:-1],
        padded[:-2, 1:-1, 1:-1],
        padded[1:-1, 2:, 1:-1],
        padded[1:-1, :-2, 1:-1],
        padded[1:-1, 1:-1, 2:],
        padded[1:-1, 1:-1, :-2],
    ]


def neighbours(field):
    return shifted(extended(field))


def harmonic(fluid, near, factor):
    total = fluid + near
    return jnp.where(total > 0, factor * 2.0 * fluid * near / jnp.where(total > 0, total, 1.0), 0.0)


def couplings(fluid, factor):
    return [harmonic(fluid, near, factor) for near in neighbours(fluid)]


def apply_op(field, weights, diag):
    total = diag * field
    for weight, near in zip(weights, neighbours(field)):
        total = total - weight * near
    return total


def presmooth(rhs, weights, diag):
    corr = OMEGA * rhs / diag
    for sweep in range(NU - 1):
        corr = corr + OMEGA * (rhs - apply_op(corr, weights, diag)) / diag
    return corr


def postsmooth(corr, rhs, weights, diag):
    for sweep in range(NU):
        corr = corr + OMEGA * (rhs - apply_op(corr, weights, diag)) / diag
    return corr


def tridiag(coeffs, rhs):
    solved = lax.linalg.tridiagonal_solve(coeffs[0], coeffs[1], coeffs[2], rhs[..., None])[..., 0]
    last = rhs.ndim - 1
    shift_col = jnp.sum(rhs, axis=last, keepdims=True) / jnp.sum(
        coeffs[3], axis=last, keepdims=True
    )
    return solved + shift_col


def prepare_columns(weights, diag):
    lower = -weights[5]
    upper = -weights[4]
    across = diag + lower + upper
    return (
        lax.all_gather(lower, "gz", axis=2, tiled=True),
        lax.all_gather(diag, "gz", axis=2, tiled=True),
        lax.all_gather(upper, "gz", axis=2, tiled=True),
        lax.all_gather(across, "gz", axis=2, tiled=True),
    )


def column_solve(rhs, coeffs):
    depth = rhs.shape[2]
    whole = lax.all_gather(rhs, "gz", axis=2, tiled=True)
    solved = tridiag(coeffs, whole)
    return lax.dynamic_slice_in_dim(solved, lax.axis_index("gz") * depth, depth, 2)


def per_device(residual_q2, viscosity, pinned):
    fluid1 = 1.0 / viscosity
    pin1 = 4.0 * pinned.astype(jnp.float32) * fluid1
    rhs1 = coarsen(residual_q2.astype(jnp.float32))
    fluid2 = coarsen(fluid1) / 8.0
    pin2 = coarsen(pin1) / 4.0
    fluid3 = coarsen(fluid2) / 8.0
    pin3 = coarsen(pin2) / 4.0
    weights1 = couplings(fluid1, 1.0)
    weights2 = couplings(fluid2, 2.0)
    weights3 = couplings(fluid3, 4.0)
    diag1 = sum(weights1) + pin1
    diag2 = sum(weights2) + pin2
    diag3 = sum(weights3) + pin3
    coeffs = prepare_columns(weights3, diag3)
    corr1 = presmooth(rhs1, weights1, diag1)
    rhs2 = coarsen(rhs1 - apply_op(corr1, weights1, diag1))
    corr2 = presmooth(rhs2, weights2, diag2)
    rhs3 = coarsen(rhs2 - apply_op(corr2, weights2, diag2))
    corr3 = column_solve(rhs3, coeffs)
    corr3 = corr3 + column_solve(rhs3 - apply_op(corr3, weights3, diag3), coeffs)
    corr2 = postsmooth(corr2 + refine(corr3), rhs2, weights2, diag2)
    corr1 = postsmooth(corr1 + refine(corr2), rhs1, weights1, diag1)
    return diag1 * corr1


PLANE = (32, 32)
SPLIT = (2, 4)
ROWS = 8
LANES = 128
HALO = 16
NEAR = 8
PIECE = 8
TINY = 1e-30
F32 = jnp.float32


def iota(shape, dim):
    return lax.broadcasted_iota(jnp.int32, shape, dim)


def quotient(index, count):
    return index >> (count.bit_length() - 1)


def remainder(index, count):
    return index & (count - 1)


def dot01(field, chosen):
    total = None
    rest = field
    for part in range(3):
        piece = rest.astype(jnp.bfloat16)
        term = jnp.dot(piece, chosen, preferred_element_type=F32)
        total = term if total is None else total + term
        if part < 2:
            rest = rest - piece.astype(F32)
    return total


def dot10(chosen, field):
    total = None
    rest = field
    for part in range(3):
        piece = rest.astype(jnp.bfloat16)
        term = lax.dot_general(
            chosen, piece, (((1,), (1,)), ((), ())), preferred_element_type=F32
        )
        total = term if total is None else total + term
        if part < 2:
            rest = rest - piece.astype(F32)
    return total


def where01(condition):
    return jnp.where(condition, 1.0, 0.0).astype(jnp.bfloat16)


def loop(low, high, size, body):
    for plane in range(low, high, size):
        body(plane, min(size, high - plane))


def inverse_of(field):
    first = pl.reciprocal(field, approx=True)
    return first * (2.0 - field * first)


class Level:
    def __init__(self, level):
        self.ny = PLANE[1] >> level
        self.xs = 4 >> level
        self.factor = float(2**level)

    def within(self, shape):
        lane = iota((1,) + shape[1:], 2)
        return jnp.broadcast_to(remainder(quotient(lane, self.ny), self.xs), shape)

    def ends(self, shape):
        one = (1,) + shape[1:]
        lane = iota(one, 2)
        last_x = (iota(one, 1) == ROWS - 1) & (remainder(quotient(lane, self.ny), self.xs) == self.xs - 1)
        last_y = remainder(lane, self.ny) == self.ny - 1
        code = jnp.where(last_y, 1, 0) + jnp.where(last_x, 2, 0)
        code = jnp.broadcast_to(code, shape)
        return (code & 1) == 1, code >= 2

    def next_x(self, field):
        moved = pltpu.roll(field, LANES - self.ny, 2)
        wrapped = self.within(field.shape) == self.xs - 1
        return jnp.where(wrapped, pltpu.roll(moved, ROWS - 1, 1), moved)

    def last_x(self, field):
        moved = pltpu.roll(field, self.ny, 2)
        return jnp.where(self.within(field.shape) == 0, pltpu.roll(moved, 1, 1), moved)

    def next_y(self, field):
        return pltpu.roll(field, LANES - 1, 2)

    def last_y(self, field):
        return pltpu.roll(field, 1, 2)

    def spread(self, field, scaled, plane, count):
        mid = field[1:-1]
        near = (
            self.next_x(mid), self.last_x(mid), self.next_y(mid), self.last_y(mid),
            field[2:], field[:-2],
        )
        terms = [weight[pl.ds(plane, count)] * value for weight, value in zip(scaled, near)]
        return mid, ((terms[0] + terms[1]) + (terms[2] + terms[3])) + (terms[4] + terms[5])


def mean_of(fluid, near, factor):
    return ((factor * 2.0) * fluid * near) * inverse_of(jnp.maximum(fluid + near, TINY))


def set_level(level, low, high, fluid, pin, rhs, fields):
    scaled, start, diag = fields

    def body(plane, count):
        wide = fluid[pl.ds(plane - 1, count + 2)]
        mid = wide[1:-1]
        end_y, end_x = level.ends(mid.shape)
        to_x = jnp.where(end_x, 0.0, mean_of(mid, level.next_x(mid), level.factor))
        to_y = jnp.where(end_y, 0.0, mean_of(mid, level.next_y(mid), level.factor))
        to_z = mean_of(wide[:-1], wide[1:], level.factor)
        weights = (to_x, level.last_x(to_x), to_y, level.last_y(to_y), to_z[1:], to_z[:-1])
        total = (
            (weights[0] + weights[1])
            + (weights[2] + weights[3])
            + (weights[4] + weights[5])
            + pin[pl.ds(plane, count)]
        )
        gain = OMEGA * inverse_of(jnp.maximum(total, TINY))
        for target, weight in zip(scaled, weights):
            target[pl.ds(plane, count)] = gain * weight
        start[pl.ds(plane, count)] = gain * rhs[pl.ds(plane, count)]
        diag[pl.ds(plane, count)] = total

    loop(low, high, PIECE, body)


def swept(level, plane, count, fields, source, shift=0):
    scaled, start, _ = fields
    mid, total = level.spread(source[pl.ds(plane - 1, count + 2)], scaled, plane - shift, count)
    return (1.0 - OMEGA) * mid + (start[pl.ds(plane - shift, count)] + total)


def sweep(level, low, high, fields, source, target, shift=0):
    def body(plane, count):
        target[pl.ds(plane, count)] = swept(level, plane, count, fields, source, shift)

    loop(low, high, PIECE, body)


def pair_sum(field):
    half = field.reshape((field.shape[0] // 2, 2) + field.shape[1:])
    return half[:, 0] + half[:, 1]


def coarse_residual(level, low, high, fields, corr, target):
    scaled, start, diag = fields

    def body(plane, count):
        mid, total = level.spread(corr[pl.ds(plane - 1, count + 2)], scaled, plane, count)
        rest = (start[pl.ds(plane, count)] + total) - OMEGA * mid
        rest = rest * (diag[pl.ds(plane, count)] * (1.0 / OMEGA))
        target[pl.ds((plane - low) // 2, count // 2)] = pair_sum(rest)

    loop(low, high, PIECE, body)


def lanes_down(level):
    fine = iota((LANES, LANES), 0)
    coarse = iota((LANES, LANES), 1)
    ny, xs = PLANE[1] >> level, 4 >> level
    half = xs // 2
    fine_x, coarse_x = remainder(quotient(fine, ny), xs), quotient(coarse, ny // 2)
    same_x = quotient(fine_x, 2) == remainder(coarse_x, half)
    same_y = quotient(remainder(fine, ny), 2) == remainder(coarse, ny // 2)
    return where01((fine < ny * xs) & same_x & same_y)


def in_lanes(field, chosen):
    flat = field.reshape(field.shape[0] * ROWS, LANES)
    return dot01(flat, chosen).reshape(field.shape)


def path_of(group):
    nx, ny = SPLIT
    row, column = 0, 0
    for index in range(group + 1):
        columns = list(range(ny)) if column == 0 else list(range(ny))[::-1]
        if index % 2:
            path = [(row, at) for at in columns] + [(1 - row, at) for at in columns[::-1]]
        else:
            path = []
            for at in columns:
                path += [(row, at), (1 - row, at)]
                row = 1 - row
        row, column = path[-1]
    return [row * ny + column for row, column in path]


def lookup(table, index):
    found = table[0]
    for at, value in enumerate(table[1:], 1):
        found = jnp.where(index == at, value, found)
    return found


def slot_of(peer):
    nx, ny = SPLIT
    return nx * ny - 1 - (peer % ny * nx + peer // ny)


def own_slot_of(rank):
    groups = range(lax.axis_size("gz"))
    return lookup([slot_of(path_of(group)[rank]) for group in groups], lax.axis_index("gz"))


def exchange(field):
    peers, groups = SPLIT[0] * SPLIT[1], lax.axis_size("gz")
    order = sorted(range(peers), key=slot_of)
    members = [[peer * groups + group for peer in order] for group in range(groups)]
    axes = ("gx", "gy", "gz")
    return lax.all_to_all(field, axes, 0, 0, axis_index_groups=members, tiled=True)


def slabs_of(groups):
    peers = SPLIT[0] * SPLIT[1]
    return [
        group * peers + path_of(group).index(peer) for peer in range(peers) for group in range(groups)
    ]


def own_slab():
    nx, ny = SPLIT
    groups = lax.axis_size("gz")
    device = (lax.axis_index("gx") * ny + lax.axis_index("gy")) * groups + lax.axis_index("gz")
    return lookup(slabs_of(groups), device)


def slots_of(groups):
    peers = SPLIT[0] * SPLIT[1]
    return [
        slot_of(peer) * groups + groups - 1 - group for group in range(groups) for peer in path_of(group)
    ]


def exchange_all(field):
    groups = lax.axis_size("gz")
    members = [device for _, device in sorted(zip(slots_of(groups), devices_of(groups)))]
    axes = ("gx", "gy", "gz")
    return lax.all_to_all(field, axes, 0, 0, axis_index_groups=[members], tiled=True)


def devices_of(groups):
    slabs = slabs_of(groups)
    return [slabs.index(slab) for slab in range(len(slabs))]


def prepare_kernel(share, res_ref, fluid_ref, pin_ref, out_ref):
    bx, by, depth = fluid_ref.shape
    cells = bx * by
    groups = bx // 4
    order = [x for low in range(4) for x in range(low, bx, 4)]
    fine = iota((cells, 4 * cells), 1)
    x, y = quotient(fine, 4 * by), quotient(remainder(fine, 2 * by), 2)
    lane = remainder(x, 4) * (groups * by) + quotient(x, 4) * by + y
    chosen = where01(lane == iota((cells, 4 * cells), 0))
    wide = lax.dot_general(
        chosen, res_ref[...], (((1,), (0,)), ((), ())), preferred_element_type=F32
    )
    rhs = dot10(where01(quotient(iota((depth, 2 * depth), 1), 2) == iota((depth, 2 * depth), 0)), wide)

    def turned(field_ref):
        field = jnp.concatenate([field_ref[x : x + 1] for x in order], axis=0)
        return field.reshape(cells, depth).T

    fluid, pin = turned(fluid_ref), turned(pin_ref)
    for rank in range(depth // share):
        peer, begin = own_slot_of(rank), rank * share
        for index, field in enumerate((fluid, rhs, pin)):
            out_ref[peer, index * share : (index + 1) * share] = field[begin : begin + share]


def spread_kernel(groups, by, gathered, own, inner, outer, straight):
    for start in range(0, own.shape[0], ROWS):
        place(gathered, start, straight, start, groups, by)
    share = own.shape[0] // 3
    odd = own_slab() % 2 == 1
    for index in range(3):
        for plane in range(share):
            at = jnp.where(odd, share - 1 - plane, plane)
            own[index * share + plane] = straight[index * share + at]
    for target, drop in ((inner, 0), (outer, share - 1)):
        row = 0
        for index in range(3):
            for plane in range(share):
                if index == 0 or plane != drop:
                    target[row] = own[index * share + plane]
                    row += 1


def place(gathered, row, target, plane, groups, by):
    group = remainder(quotient(iota((ROWS, LANES), 1), by), groups)
    nx, ny = SPLIT
    for ix in range(nx):
        found = [gathered[slot_of(ix * ny + iy), pl.ds(row, ROWS), :] for iy in range(ny)]
        for part in range(groups):
            total = found[part]
            for iy in range(ny):
                if iy != part:
                    moved = pltpu.roll(found[iy], (by * (iy - part)) % LANES, 1)
                    total = jnp.where(group == iy, moved, total)
            target[pl.ds(plane, ROWS), ix * groups + part, :] = total


def ordered(field):
    back = [field[row : row + 1] for row in reversed(range(field.shape[0]))]
    return jnp.where(own_slab() % 2 == 1, jnp.concatenate(back, axis=0), field)


def near_kernel(
    depth,
    own, inner,
    saved1, saved2, fluid2, pin2, fluids, pins,
    fluid1, rhs1, pin1, other1, rhs2, sums,
):
    row = 0
    for index, target in enumerate((fluid1, rhs1, pin1)):
        target[0:depth] = own[index * depth : (index + 1) * depth]
        count = HALO if index == 0 else HALO - 1
        for plane in range(count):
            target[depth + plane] = inner[row + count - 1 - plane]
        if count < HALO:
            target[depth + count] = jnp.zeros((ROWS, LANES), F32)
        row += count
    fine, coarse = Level(0), Level(1)
    down1, down2 = lanes_down(0), lanes_down(1)
    fields1, corr1 = (saved1[0:6], saved1[6], saved1[7]), saved1[8]
    fields2 = (saved2[0:6], saved2[6], saved2[7])
    planes = depth + HALO
    set_level(fine, 1, planes - 1, fluid1, pin1, rhs1, fields1)
    sweep(fine, 2, planes - 2, fields1, fields1[1], other1)
    sweep(fine, 3, planes - 3, fields1, other1, corr1)
    coarse_residual(fine, 4, planes - 4, fields1, corr1, sums)
    count2 = planes // 2
    for source, target, share in ((fluid1, fluid2, 8.0), (pin1, pin2, 4.0)):
        target[NEAR : NEAR + count2] = in_lanes(pair_sum(source[...]), down1) * (1.0 / share)
    low2, high2 = NEAR + 2, NEAR + count2 - 2
    rhs2[low2:high2] = in_lanes(sums[0 : high2 - low2], down1)
    set_level(coarse, low2, high2, fluid2, pin2, rhs2, fields2)
    fluid3 = in_lanes(pair_sum(fluid2[NEAR : NEAR + depth // 2]), down2) * 0.125
    pin3 = in_lanes(pair_sum(pin2[NEAR : NEAR + depth // 2]), down2) * 0.25
    lane = quotient(iota((depth // 4, LANES), 1), ROWS)
    first = jnp.zeros((depth // 4, LANES), F32)
    second = jnp.zeros((depth // 4, LANES), F32)
    for row in range(ROWS):
        first = jnp.where(lane == ROWS + row, fluid3[:, row, :], first)
        second = jnp.where(remainder(lane, ROWS) == row, pin3[:, row, :], second)
    second = ordered(second)
    fluids[...] = ordered(first)
    pins[...] = jnp.where(lane[0:2] < ROWS, second[0:2], second[2:4])


def down_kernel(
    depth,
    own, outer, near2, near_fluid2, near_pin2, fluids, pins,
    saved1, saved2,
    packed,
    fluid1, rhs1, pin1, other1, fluid2, rhs2, pin2, other2, sums,
):
    planes = fluid1.shape[0]
    row = 0
    for index, target in enumerate((fluid1, rhs1, pin1)):
        count = HALO if index == 0 else HALO - 1
        if count < HALO:
            target[0] = jnp.zeros((ROWS, LANES), F32)
        for plane in range(count):
            target[HALO - count + plane] = outer[row + count - 1 - plane]
        row += count
        target[HALO:planes] = own[index * depth : index * depth + planes - HALO]

    fine, coarse = Level(0), Level(1)
    down1, down2 = lanes_down(0), lanes_down(1)
    fields1, corr1 = (saved1[0:6], saved1[6], saved1[7]), saved1[8]
    fields2, corr2 = (saved2[0:6], saved2[6], saved2[7]), saved2[8]
    set_level(fine, 1, planes - 1, fluid1, pin1, rhs1, fields1)
    sweep(fine, 2, planes - 2, fields1, fields1[1], other1)
    sweep(fine, 3, planes - 3, fields1, other1, corr1)
    count2 = depth // 2 + 2 * NEAR
    low2, done, high2 = 2, NEAR + 2, count2 - 2
    coarse_residual(fine, 2 * low2, 2 * done, fields1, corr1, sums)
    for source, ready, target, share in (
        (fluid1, near_fluid2, fluid2, 8.0), (pin1, near_pin2, pin2, 4.0)
    ):
        target[0:NEAR] = in_lanes(pair_sum(source[0:HALO]), down1) * (1.0 / share)
        target[NEAR : done + 1] = ready[NEAR : done + 1]
    rhs2[low2:done] = in_lanes(sums[0 : done - low2], down1)
    set_level(coarse, low2, done, fluid2, pin2, rhs2, fields2)
    for source, target in zip(near2, saved2[0:8]):
        target[done:high2] = source[done:high2]
    sweep(coarse, low2 + 1, high2 - 1, fields2, fields2[1], other2)
    sweep(coarse, low2 + 2, high2 - 2, fields2, other2, corr2)
    coarse_residual(coarse, NEAR, NEAR + depth // 2, fields2, corr2, sums)
    count3 = depth // 4
    rhs3 = in_lanes(sums[0:count3], down2)
    lane = quotient(iota((count3, LANES), 1), ROWS)
    first = jnp.zeros((count3, LANES), F32)
    for row in range(ROWS):
        first = jnp.where(lane == row, rhs3[:, row, :], first)
    first = jnp.where(lane < ROWS, ordered(first), fluids[...])
    copies = packed.shape[0]

    def put(index, part):
        packed[:, index] = jnp.broadcast_to(part[None], (copies,) + part.shape)

    put(0, first[0:2])
    put(1, first[2:4])
    put(2, pins[...])
    lane = quotient(iota((1, LANES), 1), LANES // 4)
    for index, plane in enumerate((NEAR + depth // 2 - 5, NEAR + 4)):
        both = []
        for half in range(2):
            row = jnp.zeros((1, LANES), F32)
            for quarter in range(4):
                at = half * 4 + quarter
                row = jnp.where(lane == quarter, corr2[plane, at : at + 1, :], row)
            both.append(row)
        put(3 + index, jnp.concatenate(both, axis=0))


def rolled(field, shift):
    count = field.shape[0]
    shift %= count
    if shift % ROWS:
        return pltpu.roll(field, shift, 0)
    return jnp.concatenate([field[count - shift :], field[: count - shift]], axis=0)


def columns(rhs, fluid, pin):
    depth = fluid.shape[0]
    z, lane = iota(fluid.shape, 0), iota(fluid.shape, 1)
    y, x = remainder(lane, ROWS), remainder(quotient(lane, ROWS), ROWS)

    def next_x(field):
        return pltpu.roll(field, LANES - ROWS, 1)

    def next_y(field):
        return pltpu.roll(field, LANES - 1, 1)

    wz = jnp.where(z == depth - 1, 0.0, mean_of(fluid, rolled(fluid, -1), 4.0))
    wy = jnp.where(y == ROWS - 1, 0.0, mean_of(fluid, next_y(fluid), 4.0))
    wx = jnp.where(x == ROWS - 1, 0.0, mean_of(fluid, next_x(fluid), 4.0))
    across = (wx + pltpu.roll(wx, ROWS, 1)) + (wy + pltpu.roll(wy, 1, 1)) + pin
    share = 1.0 / jnp.sum(across, axis=0, keepdims=True)

    above, below, own = rolled(wz, 1), wz, across
    steps = []
    stride, right = 1, rhs
    while stride < depth:
        inverse = inverse_of(above + below + own)
        up = above * rolled(inverse, stride)
        down = below * rolled(inverse, -stride)
        own = own + up * rolled(own, stride) + down * rolled(own, -stride)
        above = up * rolled(above, stride)
        below = down * rolled(below, -stride)
        right = right + up * rolled(right, stride) + down * rolled(right, -stride)
        steps.append((stride, up, down))
        stride *= 2
    inverse = inverse_of(above + below + own)

    def mean(right):
        return jnp.sum(right, axis=0, keepdims=True) * share

    corr = right * inverse + mean(rhs)
    flow_x = wx * (next_x(corr) - corr)
    flow_y = wy * (next_y(corr) - corr)
    flow_z = wz * (rolled(corr, -1) - corr)
    rest = (
        (rhs - pin * corr)
        + (flow_x - pltpu.roll(flow_x, ROWS, 1))
        + (flow_y - pltpu.roll(flow_y, 1, 1))
        + (flow_z - rolled(flow_z, 1))
    )
    right = rest
    for stride, up, down in steps:
        right = right + up * rolled(right, stride) + down * rolled(right, -stride)
    return (corr + mean(rest)) + right * inverse


def up_kernel(
    groups, by, depth,
    packed, near1, far1, far2,
    out_ref,
    one1, two1, one2, two2, lifted, first, second, solved, final,
):
    count3 = depth // 4
    shares = packed.shape[0]
    peers = SPLIT[0] * SPLIT[1]
    slots = slots_of(shares // peers)
    for slab, index in enumerate(slots):
        row = slab * count3
        first[row : row + 2] = packed[index, 0]
        first[row + 2 : row + 4] = packed[index, 1]
        both = packed[index, 2]
        second[row : row + 2] = both
        second[row + 2 : row + 4] = pltpu.roll(both, LANES // 2, 1)
    half = iota((shares * count3, LANES), 1) < LANES // 2

    def low_half(field):
        return jnp.where(half, field, pltpu.roll(field, LANES // 2, 1))

    def high_half(field):
        return jnp.where(half, pltpu.roll(field, LANES // 2, 1), field)

    solved[NEAR : NEAR + shares * count3] = columns(
        low_half(first[...]), high_half(first[...]), low_half(second[...])
    )
    solved[0:NEAR] = jnp.zeros((NEAR, LANES), F32)
    solved[NEAR + shares * count3 :] = jnp.zeros((2 * NEAR, LANES), F32)

    nx, ny = SPLIT
    part = own_slab()
    count = count3 + 2 * NEAR
    tall = solved[pl.ds(part * count3, count + count3), :]
    fine, coarse = Level(0), Level(1)
    cell = iota((LANES, LANES), 0)
    lane = iota((LANES, LANES), 1)
    spread = where01((cell < ROWS) & (cell == quotient(remainder(lane, coarse.ny), 2)))
    rows = tall.shape[0]
    turned = [tall] + [pltpu.roll(tall, LANES - ROWS * row, 1) for row in range(1, ROWS)]
    wide = dot01(jnp.concatenate(turned, axis=0), spread)
    for row in range(ROWS):
        lifted[0:rows, row, :] = wide[row * rows : (row + 1) * rows]

    odd = part % 2 == 1

    def lifted_to(plane):
        parent = plane // 2 + NEAR // 2
        return lifted[jnp.where(odd, count - 1 - parent, parent)]

    near_fields, near_corr1 = (near1[0:6], near1[6], near1[7]), near1[8]
    far_fields, far_corr1 = (far1[0:6], far1[6], far1[7]), far1[8]
    fields2, corr2 = (far2[0:6], far2[6], far2[7]), far2[8]
    low, high = NEAR - 4, NEAR + depth // 2 + 4
    reach = depth // 2 + NEAR
    quarter = quotient(iota((ROWS, LANES), 1), LANES // 4)
    row = iota((ROWS, LANES), 0)

    def unpacked(index, which):
        pair = packed[lookup(slots, jnp.clip(index, 0, shares - 1)), which]
        total = None
        for shift in range(4):
            moved = pltpu.roll(pair, shift * (LANES // 4), 1)
            wide = jnp.where(row < 4, moved[0:1, :], moved[1:2, :])
            kept = jnp.where(remainder(quarter - shift, 4) == remainder(row, 4), wide, 0.0)
            total = kept if total is None else total + kept
        return total

    one2[low - 1] = unpacked(jnp.where(odd, part + 1, part - 1), 4) + lifted_to(low - 1)
    for plane in range(low, high):
        one2[plane] = corr2[plane] + lifted_to(plane)
    one2[high] = unpacked(jnp.where(odd, part - 1, part + 1), 3) + lifted_to(high)
    sweep(coarse, NEAR - 4, reach + 4, fields2, one2, two2)
    sweep(coarse, NEAR - 3, reach + 3, fields2, two2, one2)
    sweep(coarse, NEAR - 2, reach + 2, fields2, one2, two2)

    fine_lane, coarse_lane = iota((LANES, LANES), 1), iota((LANES, LANES), 0)
    x_of = quotient(fine_lane, 2 * fine.ny)
    y_of = quotient(remainder(fine_lane, fine.ny), 2)
    up = where01(coarse_lane == x_of * coarse.ny + y_of)
    lifted[0 : depth // 2 + 4] = in_lanes(two2[NEAR - 2 : reach + 2], up)
    parents = lifted[0 : depth // 2 + 4]
    twice = jnp.broadcast_to(parents[:, None], (parents.shape[0], 2, ROWS, LANES))
    low, high = HALO - 4, HALO + depth + 4
    turn = HALO + 3
    for plane in range(low, high):
        corr = far_corr1[plane] if plane < turn else near_corr1[plane - HALO]
        one1[plane] = corr + lifted[(plane - low) // 2]
    reach = depth + HALO
    for more, source, target in ((2, one1, two1), (1, two1, one1)):
        sweep(fine, HALO - more, turn, far_fields, source, target)
        sweep(fine, turn, reach + more, near_fields, source, target, HALO)

    def last(fields, shift):
        def body(plane, count):
            value = swept(fine, plane, count, fields, one1, shift)
            value = value * fields[2][pl.ds(plane - shift, count)]
            for index in range(count):
                at = plane - HALO + index
                final[jnp.where(odd, depth - 1 - at, at)] = value[index]

        return body

    loop(HALO, turn, PIECE, last(far_fields, 0))
    loop(turn, reach, PIECE, last(near_fields, HALO))

    group = remainder(quotient(iota((depth, LANES), 1), by), groups)
    for ix in range(nx):
        scaled = [final[:, ix * groups + part, :] for part in range(groups)]
        for iy in range(ny):
            total = scaled[iy]
            for part in range(groups):
                if part != iy:
                    moved = pltpu.roll(scaled[part], (by * (part - iy)) % LANES, 1)
                    total = jnp.where(group == part, moved, total)
            out_ref[slot_of(ix * ny + iy)] = total


def finish_kernel(blocks, out_ref):
    bx, by, depth = out_ref.shape
    peers = blocks.shape[0]
    ordered = jnp.concatenate([blocks[own_slot_of(rank)] for rank in range(peers)], axis=0)
    turned = ordered.T
    for x in range(bx):
        row = ((x % 4) * (bx // 4) + x // 4) * by
        out_ref[x] = turned[row : row + by]


def whole_planes(residual_q2, viscosity, pinned):
    bx, by, depth = viscosity.shape
    groups = bx // 4
    peers = SPLIT[0] * SPLIT[1]
    share = depth // peers
    planes = share + 2 * HALO
    count2 = share // 2 + 2 * NEAR
    limit = pltpu.CompilerParams(vmem_limit_bytes=32 * 2**20)

    def flat(rows):
        return jax.ShapeDtypeStruct((rows, LANES), F32)

    def blocks(count, rows):
        return jax.ShapeDtypeStruct((count, rows, LANES), F32)

    def room(count):
        return pltpu.VMEM((count, ROWS, LANES), F32)

    fluid = 1.0 / viscosity
    pin = 4.0 * pinned.astype(F32) * fluid
    parcels = pl.pallas_call(
        functools.partial(prepare_kernel, share),
        out_shape=blocks(peers, 3 * share),
        compiler_params=limit,
        name="prepare",
    )(residual_q2.reshape(4 * bx * by, 2 * depth), fluid, pin)
    own, inner, outer = pl.pallas_call(
        functools.partial(spread_kernel, groups, by),
        out_shape=(blocks(3 * share, ROWS),) + (blocks(3 * HALO - 2, ROWS),) * 2,
        scratch_shapes=[room(3 * share)],
        compiler_params=limit,
        name="spread",
    )(exchange(parcels))
    length = lax.axis_size("gz")
    parts = length * peers

    device = devices_of(length)

    def swap(field, first):
        pairs = [(device[i], device[i + 1]) for i in range(first, parts - 1, 2)]
        return lax.ppermute(field, ("gx", "gy", "gz"), pairs + [pair[::-1] for pair in pairs])

    outer, inner = swap(outer, 1), swap(inner, 0)
    count3 = share // 4
    near1, near2, far1, far2 = (
        (blocks(count, ROWS),) * fields
        for count, fields in ((share + HALO, 9), (count2, 8), (HALO + 8, 9), (count2, 9))
    )
    near1, near2, fluid2, pin2, fluids, pins = pl.pallas_call(
        functools.partial(near_kernel, share),
        out_shape=(near1, near2) + (blocks(count2, ROWS),) * 2 + (flat(count3), flat(2)),
        scratch_shapes=[room(share + HALO)] * 4 + [room(count2)] * 2,
        compiler_params=limit,
        name="near",
    )(own, inner)
    far1, far2, parcel = pl.pallas_call(
        functools.partial(down_kernel, share),
        out_shape=(far1, far2, jax.ShapeDtypeStruct((parts, 5, 2, LANES), F32)),
        scratch_shapes=[room(HALO + 8)] * 4 + [room(count2)] * 5,
        compiler_params=limit,
        name="down",
    )(own, outer, near2, fluid2, pin2, fluids, pins)
    packed = exchange_all(parcel)
    depth3 = parts * count3
    mine = pl.pallas_call(
        functools.partial(up_kernel, groups, by, share),
        out_shape=blocks(peers, share),
        scratch_shapes=[room(planes), room(planes), room(count2), room(count2), room(count2)]
        + [pltpu.VMEM((rows, LANES), F32) for rows in (depth3, depth3, depth3 + 3 * NEAR)]
        + [room(share)],
        compiler_params=limit,
        name="up",
    )(packed, near1, far1, far2)
    return pl.pallas_call(
        finish_kernel,
        out_shape=jax.ShapeDtypeStruct((bx, by, depth), F32),
        compiler_params=limit,
        name="finish",
    )(exchange(mine))


def one_tile_planes(mesh, viscosity):
    split = (mesh.shape["gx"], mesh.shape["gy"])
    depth = viscosity.shape[2]
    fits = viscosity.shape[:2] == PLANE and split == SPLIT
    return fits and depth == 4 * LANES and depth // mesh.shape["gz"] == LANES


def solution(mesh):
    placed = (P("gx", "gy", "gz"), P("gx", "gy", "gz"), P("gx", "gy", "gz"))

    def cycle(residual_q2, viscosity, pinned):
        chosen = whole_planes if one_tile_planes(mesh, viscosity) else per_device
        return jax.shard_map(
            chosen, mesh=mesh, in_specs=placed, out_specs=P("gx", "gy", "gz"), check_vma=False
        )(residual_q2, viscosity, pinned)

    return cycle
```
